32 devices in a mesh: ckpt: 4 (over x, core), space: 8 (over z, y).
Axes of the slice: x: 2, y: 2, z: 4, core: 2. Of those that a mesh axis runs over, the one named last changes fastest.
Arguments:
- checkpoint: float32 [8, 6, 16, 16, 128], P('space', None, 'ckpt'), may hold values from -5 to 5
- seeds: float32 [4, 8, 6, 16, 16, 128], P('ckpt', 'space'), may hold values from -6 to 6
- cell_rate: float32 [8, 16, 16, 128], P('space'), may hold values from 0.5 to 2
- flux_mats: float32 [3, 6, 6], replicated, may hold values from -1.25 to 1.25
- owner: int32 [8], replicated, may hold values from 0 to 7, each once
- neighbours: int32 [8, 6], replicated, may hold values from 0 to 7, as said below
- orientation: int32 [8, 6], replicated, may hold values from 0 to 3, as said below
Outputs:
- adjoint: float32 [4, 8, 6, 16, 16, 128], P('ckpt', 'space')
- final_state: float32 [8, 6, 16, 16, 128], P('space')
The draws below stay inside these ranges and needn't reach their ends.
Inputs may be any that keep to these rules, and one draw needn't show every extreme that they name: owner lists each space index once. The block across the -x face of neighbours[b, 0] is b, across the +x face of neighbours[b, 1] is b, and likewise for y and z; a block may be its own neighbour. orientation[b, f] equals the code of the same face seen from the block across it.
All inputs are finite; a program needn't handle non-finite values.
Results may differ from the reference program's by a relative error of at most 0.0001.
Values sent between devices are 32-bit elements; how exact they have to be, the bound alone decides.
No kernel may reach another device: no remote copies, remote signals or barrier semaphores. Data moves between devices by JAX's collectives and lax.ppermute only.
A program may use at most 128 MiB of HBM per device.

```python
import math
import jax
import jax.numpy as jnp
from jax import lax

CX = 16
CY = 16
CZ = 128
VARS = 6
STEPS = 2
NBLK = 8
NOBJ = 4


def glue_links(key):
    subkeys = jax.random.split(jax.random.fold_in(key, 11), 6)
    across = []
    flips = []
    for dimension in range(3):
        forward_map = jax.random.permutation(subkeys[dimension], NBLK).astype(jnp.int32)
        inverse = jnp.argsort(forward_map, stable=True).astype(jnp.int32)
        codes_here = jax.random.randint(subkeys[3 + dimension], (NBLK,), 0, 4, dtype=jnp.int32)
        across = across + [forward_map, inverse]
        flips = flips + [codes_here, codes_here[inverse]]
    return (jnp.stack(across, axis=1), jnp.stack(flips, axis=1))


def draw_neighbours(key, part):
    return glue_links(key)[0]


def draw_orientation(key, part):
    return glue_links(key)[1]


def levels(rng, shape, shards, low, top_value):
    def one(axis_at, parts):
        steps = jax.random.uniform(jax.random.fold_in(jax.random.fold_in(rng, 6), axis_at), (parts,), jnp.float32, low / len(shards), top_value / len(shards))
        return jnp.repeat(jnp.exp(steps), shape[axis_at] // parts).reshape((-1,) + (1,) * (len(shape) - axis_at - 1))

    gain = one(*shards[0])
    for cut in shards[1:]:
        gain = gain * one(*cut)
    return gain


def noise(stream_key, dims, deviation, bound, cuts=(), kind=jnp.bfloat16):
    loudness = levels(stream_key, dims, cuts, -0.22, 0.18) if cuts else 1.0
    entries = jax.random.normal(stream_key, dims, jnp.float32) * deviation * loudness
    return jnp.minimum(jnp.maximum(entries, -bound), bound).astype(kind)


def setup_inputs(seed: int = 0) -> dict:
    key_of = jax.random.split(jax.random.key(seed), 8)
    return {
        "checkpoint": noise(key_of[0], (NBLK, VARS, CX, CY, CZ), 1.0, 5.0, ((0, 8), (2, 4)), jnp.float32),
        "seeds": noise(key_of[1], (NOBJ, NBLK, VARS, CX, CY, CZ), 1.0, 6.0, ((0, 4), (1, 8)), jnp.float32),
        "cell_rate": jnp.clip(jnp.exp(math.log(2.0) - 1.3862944 * jax.random.uniform(key_of[2], (NBLK, CX, CY, CZ), jnp.float32) ** levels(key_of[2], (NBLK, CX, CY, CZ), ((0, 8),), -0.2, 0.2)), 0.5, 2.0),
        "flux_mats": noise(key_of[3], (3, VARS, VARS), 24 ** -0.5, 1.25, (), jnp.float32),
        "owner": jax.random.permutation(key_of[4], NBLK).astype(jnp.int32),
        "neighbours": draw_neighbours(jax.random.fold_in(key_of[7], 71), 0),
        "orientation": draw_orientation(jax.random.fold_in(key_of[7], 71), 0),
    }


time_step = 0.05
damping = 0.015

def boundary(field, side):
    layer_axis = field.ndim - 3 + side // 2
    location = field.shape[layer_axis] - 1 if side % 2 == 0 else 0
    return lax.index_in_dim(field, location, layer_axis, keepdims=False)

def reorient(face, flips):
    face = jnp.where(flips % 2 == 1, jnp.flip(face, -2), face)
    return jnp.where(flips // 2 % 2 == 1, jnp.flip(face, -1), face)

def pad_with(field, ghosts):
    padded = jnp.pad(field, [(0, 0)] * (field.ndim - 3) + [(1, 1)] * 3)
    for side in range(6):
        layer_axis = side // 2
        location = padded.shape[padded.ndim - 3 + layer_axis] - 1 if side % 2 == 0 else 0
        if layer_axis == 0:
            padded = padded.at[..., location, 1:-1, 1:-1].set(ghosts[side])
        elif layer_axis == 1:
            padded = padded.at[..., 1:-1, location, 1:-1].set(ghosts[side])
        else:
            padded = padded.at[..., 1:-1, 1:-1, location].set(ghosts[side])
    return padded

def advance(padded, rates, flux_mats):
    interior = padded[:, 1:-1, 1:-1, 1:-1]
    divergence = jnp.zeros_like(interior)
    for direction in range(3):
        if direction == 0:
            strip = padded[:, :, 1:-1, 1:-1]
        elif direction == 1:
            strip = padded[:, 1:-1, :, 1:-1]
        else:
            strip = padded[:, 1:-1, 1:-1, :]
        length = strip.shape[direction + 1]
        left_cells = lax.slice_in_dim(strip, 0, length - 1, axis=direction + 1)
        right_cells = lax.slice_in_dim(strip, 1, length, axis=direction + 1)
        average = 0.5 * (left_cells + right_cells)
        difference = right_cells - left_cells
        spread = jnp.sqrt(1.0 + average[0] * average[0])
        face_flux = jnp.einsum('ij,jxyz->ixyz', flux_mats[direction], average, precision=lax.Precision.HIGHEST) - 0.5 * spread * difference
        count = face_flux.shape[direction + 1]
        divergence = divergence + lax.slice_in_dim(face_flux, 1, count, axis=direction + 1) - lax.slice_in_dim(face_flux, 0, count - 1, axis=direction + 1)
    return interior - time_step * rates * divergence - damping * jnp.tanh(interior)

def reference(checkpoint, seeds, cell_rate, flux_mats, owner, neighbours, orientation):
    block_count = owner.shape[0]
    indices = jnp.arange(block_count, dtype=jnp.int32)
    blocks = jnp.zeros((block_count,), jnp.int32).at[owner].set(indices)
    source_rows = owner[neighbours[blocks]].astype(jnp.int32)
    flips = orientation[blocks].astype(jnp.int32)

    def with_ghosts(field):
        ghosts = []
        for side in range(6):
            source = boundary(field[source_rows[:, side]], side ^ 1)
            ghosts.append(reorient(source, flips[:, side].reshape((block_count, 1, 1, 1))))
        return pad_with(field, ghosts)

    def forward(initial):
        field = initial
        for section in range(STEPS):
            field = jax.vmap(advance, (0, 0, None))(with_ghosts(field), cell_rate, flux_mats)
        return field
    final_state, pullback = jax.vjp(forward, checkpoint)
    adjoint = jnp.stack([pullback(seeds[objective])[0] for objective in range(seeds.shape[0])])
    return (adjoint, final_state)
```

```python
import functools

import jax
import jax.numpy as jnp
from jax import lax
from jax.experimental import pallas as pl
from jax.experimental.pallas import tpu as pltpu
from jax.sharding import PartitionSpec as P

STEPS = 2
time_step = 0.05
damping = 0.015

PAD = 8
VMEM = pl.BlockSpec(memory_space=pltpu.VMEM)
SMEM = pl.BlockSpec(memory_space=pltpu.SMEM)
VMEM_LIMIT = 32 * 1024 * 1024


class Geometry:
    def __init__(self, nvars, cx, cy, cz, count):
        self.v, self.x, self.y, self.z, self.n = nvars, cx, cy, cz, count
        self.rows = [nvars * cy] * 2 + [nvars * cx] * 2 + [cy] * 2
        self.runs = [-(-rows // count) for rows in self.rows]
        self.starts = [sum(self.runs[:side]) for side in range(6)]
        self.slot = -(-sum(self.runs) // 8) * 8
        self.face_rows = -(-max(run * count for run in self.runs) // 8) * 8
        self.block = (nvars, cx, cy, cz)
        self.padded = (nvars, cx + 2, cy + 2 * PAD, cz)
        self.buffer = (count, self.slot, cz)
        self.faces = (6, self.face_rows, cz)


def pack(geo, source, faces, buffer):
    v, x, y, z = geo.block
    lane = lax.broadcasted_iota(jnp.int32, (y, z), 1)
    faces[0, : v * y] = source[:, x - 1].reshape(v * y, z)
    faces[1, : v * y] = source[:, 0].reshape(v * y, z)
    for var in range(v):
        faces[2, var * x : (var + 1) * x] = source[var, :, y - 1, :]
        faces[3, var * x : (var + 1) * x] = source[var, :, 0, :]
    high = jnp.zeros((y, z), jnp.float32)
    low = jnp.zeros((y, z), jnp.float32)
    for var in range(v):
        for plane in range(x):
            place = var * x + plane
            tile = source[var, plane]
            here = lane == place
            high = jnp.where(here, pltpu.roll(tile, (place + 1) % z, 1), high)
            low = jnp.where(here, pltpu.roll(tile, place, 1) if place else tile, low)
    faces[4, :y] = high
    faces[5, :y] = low
    for side in range(6):
        run, start = geo.runs[side], geo.starts[side]
        for slot in range(geo.n):
            buffer[slot, start : start + run] = faces[side, slot * run : (slot + 1) * run]


def own_codes(geo, place, owner, orientation):
    block = jnp.int32(0)
    for index in range(geo.n):
        block = jnp.where(owner[index] == place[0], index, block)
    return [orientation[block * 6 + side] for side in range(6)]


def flip_rows(values, flag, length):
    rows, z = values.shape
    grouped = values.reshape(rows // length, length // 8, 8, z)
    index = lax.broadcasted_iota(jnp.int32, (8, z), 0)
    index = jnp.where(flag == 1, 7 - index, index)
    tiles = length // 8
    out = []
    for group in range(rows // length):
        for tile in range(tiles):
            picked = jnp.where(flag == 1, grouped[group, tiles - 1 - tile], grouped[group, tile])
            out.append(jnp.take_along_axis(picked, index, axis=0))
    return jnp.stack(out).reshape(rows, z)


def flip_lanes(values, flag, length):
    rows, z = values.shape
    lane = lax.broadcasted_iota(jnp.int32, (8, z), 1)
    within = lax.rem(lane, length)
    index = jnp.where(flag == 1, lane + (length - 1) - 2 * within, lane)
    index = jnp.minimum(index, z - 1)
    tiles = values.reshape(rows // 8, 8, z)
    return jnp.stack(
        [jnp.take_along_axis(tiles[tile], index, axis=1) for tile in range(rows // 8)]
    ).reshape(rows, z)


def unpack(geo, codes, buffer, faces, padded, zfaces):
    v, x, y, z = geo.block
    for side in range(6):
        run, start = geo.runs[side], geo.starts[side]
        for slot in range(geo.n):
            faces[side, slot * run : (slot + 1) * run] = buffer[slot, start : start + run]
    for side in range(6):
        first, second = codes[side] & 1, (codes[side] >> 1) & 1
        layer = faces[side, : geo.rows[side]]
        if side < 2:
            layer = flip_lanes(flip_rows(layer, first, y), second, z)
            where = x + 1 if side == 0 else 0
            padded[:, where, PAD : PAD + y, :] = layer.reshape(v, y, z)
        elif side < 4:
            layer = flip_lanes(flip_rows(layer, first, x), second, z)
            where = PAD + y if side == 2 else PAD - 1
            for var in range(v):
                padded[var, 1 : x + 1, where, :] = layer[var * x : (var + 1) * x]
        else:
            layer = flip_lanes(flip_rows(layer, second, y), first, x)
            zfaces[side - 4] = layer


def around(geo, padded, zfaces, plane):
    v, x, y, z = geo.block
    lane = lax.broadcasted_iota(jnp.int32, (y, z), 1)
    cells, low, high = [], [[], [], []], [[], [], []]
    for var in range(v):
        mid = padded[var, plane + 1, PAD : PAD + y]
        cells.append(mid)
        low[0].append(padded[var, plane, PAD : PAD + y])
        high[0].append(padded[var, plane + 2, PAD : PAD + y])
        low[1].append(padded[var, plane + 1, PAD - 1 : PAD - 1 + y])
        high[1].append(padded[var, plane + 1, PAD + 1 : PAD + 1 + y])
        place = var * x + plane
        ghost_high = pltpu.roll(zfaces[0], lax.rem(2 * z - 1 - place, z), 1)
        ghost_low = pltpu.roll(zfaces[1], lax.rem(z - place, z), 1)
        low[2].append(jnp.where(lane == 0, ghost_low, pltpu.roll(mid, 1, 1)))
        high[2].append(jnp.where(lane == z - 1, ghost_high, pltpu.roll(mid, z - 1, 1)))
    return cells, low, high


def flux_entry(geo, mats, direction, row, column):
    return mats[(direction * geo.v + row) * geo.v + column]


def step_plane(geo, mats, cells, low, high, rate):
    v = geo.v
    total = [None] * v
    for direction in range(3):
        lows, highs = low[direction], high[direction]
        mean_low = 0.5 * (lows[0] + cells[0])
        mean_high = 0.5 * (cells[0] + highs[0])
        square_low = 1.0 + mean_low * mean_low
        square_high = 1.0 + mean_high * mean_high
        spread_low = square_low * lax.rsqrt(square_low)
        spread_high = square_high * lax.rsqrt(square_high)
        slopes = [highs[var] - lows[var] for var in range(v)]
        for var in range(v):
            term = spread_low * (cells[var] - lows[var]) - spread_high * (highs[var] - cells[var])
            for column in range(v):
                term = term + flux_entry(geo, mats, direction, var, column) * slopes[column]
            total[var] = term if total[var] is None else total[var] + term
    scale = (0.5 * time_step) * rate
    return [cells[var] - scale * total[var] - damping * jnp.tanh(cells[var]) for var in range(v)]


def adjoint_plane(geo, mats, cells, low, high, grads, weight, weight_low, weight_high):
    v = geo.v
    total = [None] * v
    extra = None
    for direction in range(3):
        spreads, steps = [], []
        for lower, upper, lower_weight, upper_weight in (
            (low[direction], cells, weight_low[direction], weight),
            (cells, high[direction], weight, weight_high[direction]),
        ):
            mean = 0.5 * (lower[0] + upper[0])
            square = 1.0 + mean * mean
            inverse = lax.rsqrt(square)
            jump = [lower_weight[var] - upper_weight[var] for var in range(v)]
            product = jump[0] * (upper[0] - lower[0])
            for var in range(1, v):
                product = product + jump[var] * (upper[var] - lower[var])
            product = product * (mean * inverse)
            extra = product if extra is None else extra + product
            spreads.append(square * inverse)
            steps.append(jump)
        slopes = [steps[0][var] + steps[1][var] for var in range(v)]
        for var in range(v):
            term = spreads[1] * steps[1][var] - spreads[0] * steps[0][var]
            for row in range(v):
                term = term + flux_entry(geo, mats, direction, row, var) * slopes[row]
            total[var] = term if total[var] is None else total[var] + term
    total[0] = total[0] - 0.5 * extra
    out = []
    for var in range(v):
        bend = jnp.tanh(cells[var])
        slope = (1.0 - damping) + damping * (bend * bend)
        out.append(grads[var] * slope - (0.5 * time_step) * total[var])
    return out


def load_gathered(geo, gathered, padded):
    parts, depth = gathered.shape[0], gathered.shape[2]
    for part in range(parts):
        padded[:, 1 + part * depth : 1 + (part + 1) * depth, PAD : PAD + geo.y, :] = gathered[part]


def pack_state_kernel(geo, gathered, state, buffer, faces):
    parts, depth = gathered.shape[0], gathered.shape[2]
    for part in range(parts):
        state[:, part * depth : (part + 1) * depth] = gathered[part]
    pack(geo, state, faces, buffer)


def pack_weight_kernel(geo, grads, rate, buffer, weight, faces):
    def body(plane, carry):
        for var in range(geo.v):
            weight[var, plane] = rate[plane] * grads[var, plane]
        return carry

    lax.fori_loop(0, geo.x, body, 0)
    pack(geo, weight, faces, buffer)


def route_kernel(geo, owner, neighbours, arrived, leaving):
    for block in range(geo.n):
        target = owner[block]
        for side in range(6):
            source = owner[neighbours[block * 6 + side]]
            run, start, far = geo.runs[side], geo.starts[side], geo.starts[side ^ 1]
            leaving[target, start : start + run] = arrived[source, far : far + run]


def fill(geo, place, owner, orientation, block, buffer, faces, padded, zfaces):
    v, x, y, z = geo.block
    padded[:, 1 : x + 1, PAD : PAD + y, :] = block[...]
    unpack(geo, own_codes(geo, place, owner, orientation), buffer, faces, padded, zfaces)


def step_kernel(geo, packed, place, owner, orientation, mats, block, buffer, rate, *rest):
    if packed:
        result, sent, faces, padded, zfaces = rest
    else:
        result, faces, padded, zfaces = rest
    fill(geo, place, owner, orientation, block, buffer, faces, padded, zfaces)

    def body(plane, carry):
        cells, low, high = around(geo, padded, zfaces, plane)
        for var, value in enumerate(step_plane(geo, mats, cells, low, high, rate[plane])):
            result[var, plane] = value
        return carry

    lax.fori_loop(0, geo.x, body, 0)
    if packed:
        pack(geo, result, faces, sent)


def adjoint_kernel(geo, packed, place, owner, orientation, mats, block, buffer, grads, weight_buffer, rate, *rest):
    if packed:
        result, sent, faces, padded, zfaces, weights, weight_zfaces, weight_block = rest
    else:
        result, faces, padded, zfaces, weights, weight_zfaces = rest
    v, x, y, z = geo.block
    fill(geo, place, owner, orientation, block, buffer, faces, padded, zfaces)
    codes = own_codes(geo, place, owner, orientation)
    unpack(geo, codes, weight_buffer, faces, weights, weight_zfaces)

    def scale(plane, carry):
        for var in range(v):
            weights[var, plane + 1, PAD : PAD + y] = rate[plane] * grads[var, plane]
        return carry

    lax.fori_loop(0, x, scale, 0)

    def body(plane, carry):
        cells, low, high = around(geo, padded, zfaces, plane)
        weight, weight_low, weight_high = around(geo, weights, weight_zfaces, plane)
        here = [grads[var, plane] for var in range(v)]
        values = adjoint_plane(geo, mats, cells, low, high, here, weight, weight_low, weight_high)
        for var, value in enumerate(values):
            result[var, plane] = value
            if packed:
                weight_block[var, plane] = rate[plane] * value
        return carry

    lax.fori_loop(0, x, body, 0)
    if packed:
        pack(geo, weight_block, faces, sent)


def call(kernel, specs, outs, scratch, flops):
    return pl.pallas_call(
        kernel,
        in_specs=specs,
        out_specs=[VMEM] * len(outs),
        out_shape=[jax.ShapeDtypeStruct(shape, jnp.float32) for shape in outs],
        scratch_shapes=[pltpu.VMEM(shape, jnp.float32) for shape in scratch],
        compiler_params=pltpu.CompilerParams(vmem_limit_bytes=VMEM_LIMIT),
        cost_estimate=pl.CostEstimate(flops=flops, bytes_accessed=3 << 20, transcendentals=0),
    )


def on_device(count, checkpoint, seeds, cell_rate, flux_mats, owner, neighbours, orientation):
    nvars, cx, cy, cz = seeds.shape[2:]
    geo = Geometry(nvars, cx, cy, cz, count)
    rate = cell_rate[0]
    grads = seeds[0, 0]
    place = lax.axis_index("space").astype(jnp.int32).reshape(1)
    mats = flux_mats.reshape(-1)
    neighbours = neighbours.reshape(-1)
    orientation = orientation.reshape(-1)
    zfaces = (2, cy, cz)
    work = nvars * nvars * 3 * 4 * cx * cy * cz

    def exchange(buffer):
        arrived = lax.all_to_all(buffer, "space", 0, 0, tiled=True)
        leaving = call(
            functools.partial(route_kernel, geo), [SMEM, SMEM, VMEM], [geo.buffer], [], work // 16
        )(owner, neighbours, arrived)[0]
        return lax.all_to_all(leaving, "space", 0, 0, tiled=True)

    gathered = lax.all_gather(checkpoint, "ckpt", axis=0, tiled=True)
    (sent,) = call(
        functools.partial(pack_weight_kernel, geo), [VMEM, VMEM], [geo.buffer], [geo.block, geo.faces], work // 8
    )(grads, rate)
    weight_ghosts = exchange(sent)
    state, sent = call(
        functools.partial(pack_state_kernel, geo), [VMEM], [geo.block, geo.buffer], [geo.faces], work // 8
    )(gathered)
    ghosts = [exchange(sent)]
    states = [state]
    fixed = (place, owner, orientation, mats)
    step_specs = [SMEM] * 4 + [VMEM] * 3
    next_state, sent = call(
        functools.partial(step_kernel, geo, True),
        step_specs,
        [geo.block, geo.buffer],
        [geo.faces, geo.padded, zfaces],
        work,
    )(*fixed, states[0], ghosts[0], rate)
    states.append(next_state)
    ghosts.append(exchange(sent))
    adjoint_specs = [SMEM] * 4 + [VMEM] * 5
    pads = [geo.faces, geo.padded, zfaces, geo.padded, zfaces]
    grads_now, sent = call(
        functools.partial(adjoint_kernel, geo, True),
        adjoint_specs,
        [geo.block, geo.buffer],
        pads + [geo.block],
        2 * work,
    )(*fixed, states[1], ghosts[1], grads, weight_ghosts, rate)
    weight_ghosts = exchange(sent)
    (final,) = call(
        functools.partial(step_kernel, geo, False),
        step_specs,
        [geo.block],
        [geo.faces, geo.padded, zfaces],
        work,
    )(*fixed, states[1], ghosts[1], rate)
    (adjoint,) = call(
        functools.partial(adjoint_kernel, geo, False),
        adjoint_specs,
        [geo.block],
        pads,
        2 * work,
    )(*fixed, states[0], ghosts[0], grads_now, weight_ghosts, rate)
    return (adjoint[None, None], final[None])


def solution(mesh):
    return jax.shard_map(
        functools.partial(on_device, mesh.shape["space"]),
        mesh=mesh,
        in_specs=(
            P("space", None, "ckpt", None, None),
            P("ckpt", "space", None, None, None, None),
            P("space", None, None, None),
            P(),
            P(),
            P(),
            P(),
        ),
        out_specs=(P("ckpt", "space", None, None, None, None), P("space", None, None, None, None)),
        check_vma=False,
    )
```

```python
import functools

import jax
import jax.numpy as jnp
from jax import lax
from jax.experimental import pallas as pl
from jax.experimental.pallas import tpu as pltpu
from jax.sharding import PartitionSpec as P

STEPS = 2
time_step = 0.05
damping = 0.015

PAD = 8
VMEM = pl.BlockSpec(memory_space=pltpu.VMEM)
SMEM = pl.BlockSpec(memory_space=pltpu.SMEM)
VMEM_LIMIT = 32 * 1024 * 1024


class Geometry:
    def __init__(self, nvars, cx, cy, cz, count):
        self.v, self.x, self.y, self.z, self.n = nvars, cx, cy, cz, count
        self.rows = [nvars * cy] * 2 + [nvars * cx] * 2 + [cy] * 2
        self.runs = [-(-rows // count) for rows in self.rows]
        self.starts = [sum(self.runs[:side]) for side in range(6)]
        self.slot = -(-sum(self.runs) // 8) * 8
        self.face_rows = -(-max(run * count for run in self.runs) // 8) * 8
        self.block = (nvars, cx, cy, cz)
        self.padded = (nvars, cx + 2, cy + 2 * PAD, cz)
        self.buffer = (count, self.slot, cz)
        self.faces = (6, self.face_rows, cz)


def pack(geo, source, faces, buffer):
    v, x, y, z = geo.block
    lane = lax.broadcasted_iota(jnp.int32, (y, z), 1)
    faces[0, : v * y] = source[:, x - 1].reshape(v * y, z)
    faces[1, : v * y] = source[:, 0].reshape(v * y, z)
    for var in range(v):
        faces[2, var * x : (var + 1) * x] = source[var, :, y - 1, :]
        faces[3, var * x : (var + 1) * x] = source[var, :, 0, :]
    high = jnp.zeros((y, z), jnp.float32)
    low = jnp.zeros((y, z), jnp.float32)
    for var in range(v):
        for plane in range(x):
            place = var * x + plane
            tile = source[var, plane]
            here = lane == place
            high = jnp.where(here, pltpu.roll(tile, (place + 1) % z, 1), high)
            low = jnp.where(here, pltpu.roll(tile, place, 1) if place else tile, low)
    faces[4, :y] = high
    faces[5, :y] = low
    for side in range(6):
        run, start = geo.runs[side], geo.starts[side]
        for slot in range(geo.n):
            buffer[slot, start : start + run] = faces[side, slot * run : (slot + 1) * run]


def own_codes(geo, place, owner, orientation):
    block = jnp.int32(0)
    for index in range(geo.n):
        block = jnp.where(owner[index] == place[0], index, block)
    return [orientation[block * 6 + side] for side in range(6)]


def flip_rows(values, flag, length):
    rows, z = values.shape
    grouped = values.reshape(rows // length, length // 8, 8, z)
    index = lax.broadcasted_iota(jnp.int32, (8, z), 0)
    index = jnp.where(flag == 1, 7 - index, index)
    tiles = length // 8
    out = []
    for group in range(rows // length):
        for tile in range(tiles):
            picked = jnp.where(flag == 1, grouped[group, tiles - 1 - tile], grouped[group, tile])
            out.append(jnp.take_along_axis(picked, index, axis=0))
    return jnp.stack(out).reshape(rows, z)


def flip_lanes(values, flag, length):
    rows, z = values.shape
    lane = lax.broadcasted_iota(jnp.int32, (8, z), 1)
    within = lax.rem(lane, length)
    index = jnp.where(flag == 1, lane + (length - 1) - 2 * within, lane)
    index = jnp.minimum(index, z - 1)
    tiles = values.reshape(rows // 8, 8, z)
    return jnp.stack(
        [jnp.take_along_axis(tiles[tile], index, axis=1) for tile in range(rows // 8)]
    ).reshape(rows, z)


def unpack(geo, codes, buffer, faces, padded, zfaces):
    v, x, y, z = geo.block
    for side in range(6):
        run, start = geo.runs[side], geo.starts[side]
        for slot in range(geo.n):
            faces[side, slot * run : (slot + 1) * run] = buffer[slot, start : start + run]
    for side in range(6):
        first, second = codes[side] & 1, (codes[side] >> 1) & 1
        layer = faces[side, : geo.rows[side]]
        if side < 2:
            layer = flip_lanes(flip_rows(layer, first, y), second, z)
            where = x + 1 if side == 0 else 0
            padded[:, where, PAD : PAD + y, :] = layer.reshape(v, y, z)
        elif side < 4:
            layer = flip_lanes(flip_rows(layer, first, x), second, z)
            where = PAD + y if side == 2 else PAD - 1
            for var in range(v):
                padded[var, 1 : x + 1, where, :] = layer[var * x : (var + 1) * x]
        else:
            layer = flip_lanes(flip_rows(layer, second, y), first, x)
            zfaces[side - 4] = layer


def around(geo, padded, zfaces, plane):
    v, x, y, z = geo.block
    lane = lax.broadcasted_iota(jnp.int32, (y, z), 1)
    cells, low, high = [], [[], [], []], [[], [], []]
    for var in range(v):
        mid = padded[var, plane + 1, PAD : PAD + y]
        cells.append(mid)
        low[0].append(padded[var, plane, PAD : PAD + y])
        high[0].append(padded[var, plane + 2, PAD : PAD + y])
        low[1].append(padded[var, plane + 1, PAD - 1 : PAD - 1 + y])
        high[1].append(padded[var, plane + 1, PAD + 1 : PAD + 1 + y])
        place = var * x + plane
        ghost_high = pltpu.roll(zfaces[0], lax.rem(2 * z - 1 - place, z), 1)
        ghost_low = pltpu.roll(zfaces[1], lax.rem(z - place, z), 1)
        low[2].append(jnp.where(lane == 0, ghost_low, pltpu.roll(mid, 1, 1)))
        high[2].append(jnp.where(lane == z - 1, ghost_high, pltpu.roll(mid, z - 1, 1)))
    return cells, low, high


def flux_entry(geo, mats, direction, row, column):
    return mats[(direction * geo.v + row) * geo.v + column]


def step_plane(geo, mats, cells, low, high, rate):
    v = geo.v
    total = [None] * v
    for direction in range(3):
        lows, highs = low[direction], high[direction]
        mean_low = 0.5 * (lows[0] + cells[0])
        mean_high = 0.5 * (cells[0] + highs[0])
        square_low = 1.0 + mean_low * mean_low
        square_high = 1.0 + mean_high * mean_high
        spread_low = square_low * lax.rsqrt(square_low)
        spread_high = square_high * lax.rsqrt(square_high)
        slopes = [highs[var] - lows[var] for var in range(v)]
        for var in range(v):
            term = spread_low * (cells[var] - lows[var]) - spread_high * (highs[var] - cells[var])
            for column in range(v):
                term = term + flux_entry(geo, mats, direction, var, column) * slopes[column]
            total[var] = term if total[var] is None else total[var] + term
    scale = (0.5 * time_step) * rate
    return [cells[var] - scale * total[var] - damping * jnp.tanh(cells[var]) for var in range(v)]


def adjoint_plane(geo, mats, cells, low, high, grads, weight, weight_low, weight_high):
    v = geo.v
    total = [None] * v
    extra = None
    for direction in range(3):
        spreads, steps = [], []
        for lower, upper, lower_weight, upper_weight in (
            (low[direction], cells, weight_low[direction], weight),
            (cells, high[direction], weight, weight_high[direction]),
        ):
            mean = 0.5 * (lower[0] + upper[0])
            square = 1.0 + mean * mean
            inverse = lax.rsqrt(square)
            jump = [lower_weight[var] - upper_weight[var] for var in range(v)]
            product = jump[0] * (upper[0] - lower[0])
            for var in range(1, v):
                product = product + jump[var] * (upper[var] - lower[var])
            product = product * (mean * inverse)
            extra = product if extra is None else extra + product
            spreads.append(square * inverse)
            steps.append(jump)
        slopes = [steps[0][var] + steps[1][var] for var in range(v)]
        for var in range(v):
            term = spreads[1] * steps[1][var] - spreads[0] * steps[0][var]
            for row in range(v):
                term = term + flux_entry(geo, mats, direction, row, var) * slopes[row]
            total[var] = term if total[var] is None else total[var] + term
    total[0] = total[0] - 0.5 * extra
    out = []
    for var in range(v):
        bend = jnp.tanh(cells[var])
        slope = (1.0 - damping) + damping * (bend * bend)
        out.append(grads[var] * slope - (0.5 * time_step) * total[var])
    return out


def partner(count, place, distance):
    if count & (count - 1) == 0:
        return place ^ distance
    return lax.rem(distance - place + 2 * count, count) if not isinstance(place, int) else (distance - place) % count


def scatter_slots(geo, place, parts, buffer):
    for distance in range(geo.n):
        buffer[partner(geo.n, place[0], jnp.int32(distance))] = parts[distance][...]


def collect_slots(geo, place, buffer, parts):
    for distance in range(geo.n):
        parts[distance][...] = buffer[partner(geo.n, place[0], jnp.int32(distance))]


def pack_state_kernel(geo, place, gathered, state, *rest):
    sent, (buffer, faces) = rest[: geo.n], rest[geo.n :]
    parts, depth = gathered.shape[0], gathered.shape[2]
    for part in range(parts):
        state[:, part * depth : (part + 1) * depth] = gathered[part]
    pack(geo, state, faces, buffer)
    collect_slots(geo, place, buffer, sent)


def pack_weight_kernel(geo, place, grads, rate, *rest):
    sent, (buffer, weight, faces) = rest[: geo.n], rest[geo.n :]

    def body(plane, carry):
        for var in range(geo.v):
            weight[var, plane] = rate[plane] * grads[var, plane]
        return carry

    lax.fori_loop(0, geo.x, body, 0)
    pack(geo, weight, faces, buffer)
    collect_slots(geo, place, buffer, sent)


def route_kernel(geo, place, owner, neighbours, *rest):
    parts, sent, (arrived, leaving) = rest[: geo.n], rest[geo.n : 2 * geo.n], rest[2 * geo.n :]
    scatter_slots(geo, place, parts, arrived)
    for block in range(geo.n):
        target = owner[block]
        for side in range(6):
            source = owner[neighbours[block * 6 + side]]
            run, start, far = geo.runs[side], geo.starts[side], geo.starts[side ^ 1]
            leaving[target, start : start + run] = arrived[source, far : far + run]
    collect_slots(geo, place, leaving, sent)


def fill(geo, place, owner, orientation, block, parts, buffer, faces, padded, zfaces):
    v, x, y, z = geo.block
    padded[:, 1 : x + 1, PAD : PAD + y, :] = block[...]
    scatter_slots(geo, place, parts, buffer)
    unpack(geo, own_codes(geo, place, owner, orientation), buffer, faces, padded, zfaces)


def step_kernel(geo, packed, place, owner, orientation, mats, block, rate, *rest):
    parts, result, rest = rest[: geo.n], rest[geo.n], rest[geo.n + 1 :]
    if packed:
        sent, rest = rest[: geo.n], rest[geo.n :]
    buffer, faces, padded, zfaces = rest
    fill(geo, place, owner, orientation, block, parts, buffer, faces, padded, zfaces)

    def body(plane, carry):
        cells, low, high = around(geo, padded, zfaces, plane)
        for var, value in enumerate(step_plane(geo, mats, cells, low, high, rate[plane])):
            result[var, plane] = value
        return carry

    lax.fori_loop(0, geo.x, body, 0)
    if packed:
        pack(geo, result, faces, buffer)
        collect_slots(geo, place, buffer, sent)


def adjoint_kernel(geo, packed, place, owner, orientation, mats, block, grads, rate, *rest):
    v, x, y, z = geo.block
    parts, weight_parts, result = rest[: geo.n], rest[geo.n : 2 * geo.n], rest[2 * geo.n]
    rest = rest[2 * geo.n + 1 :]
    if packed:
        sent, rest = rest[: geo.n], rest[geo.n :]
    buffer, faces, padded, zfaces, weights, weight_zfaces = rest[:6]
    if packed:
        weight_block = rest[6]
    fill(geo, place, owner, orientation, block, parts, buffer, faces, padded, zfaces)
    codes = own_codes(geo, place, owner, orientation)
    scatter_slots(geo, place, weight_parts, buffer)
    unpack(geo, codes, buffer, faces, weights, weight_zfaces)

    def scale(plane, carry):
        for var in range(v):
            weights[var, plane + 1, PAD : PAD + y] = rate[plane] * grads[var, plane]
        return carry

    lax.fori_loop(0, x, scale, 0)

    def body(plane, carry):
        cells, low, high = around(geo, padded, zfaces, plane)
        weight, weight_low, weight_high = around(geo, weights, weight_zfaces, plane)
        here = [grads[var, plane] for var in range(v)]
        values = adjoint_plane(geo, mats, cells, low, high, here, weight, weight_low, weight_high)
        for var, value in enumerate(values):
            result[var, plane] = value
            if packed:
                weight_block[var, plane] = rate[plane] * value
        return carry

    lax.fori_loop(0, x, body, 0)
    if packed:
        pack(geo, weight_block, faces, buffer)
        collect_slots(geo, place, buffer, sent)


def call(kernel, specs, outs, scratch, flops):
    return pl.pallas_call(
        kernel,
        in_specs=specs,
        out_specs=[VMEM] * len(outs),
        out_shape=[jax.ShapeDtypeStruct(shape, jnp.float32) for shape in outs],
        scratch_shapes=[pltpu.VMEM(shape, jnp.float32) for shape in scratch],
        compiler_params=pltpu.CompilerParams(vmem_limit_bytes=VMEM_LIMIT),
        cost_estimate=pl.CostEstimate(flops=flops, bytes_accessed=3 << 20, transcendentals=0),
    )


def on_device(count, checkpoint, seeds, cell_rate, flux_mats, owner, neighbours, orientation):
    nvars, cx, cy, cz = seeds.shape[2:]
    geo = Geometry(nvars, cx, cy, cz, count)
    rate = cell_rate[0]
    grads = seeds[0, 0]
    place = lax.axis_index("space").astype(jnp.int32).reshape(1)
    mats = flux_mats.reshape(-1)
    neighbours = neighbours.reshape(-1)
    orientation = orientation.reshape(-1)
    zfaces = (2, cy, cz)
    work = nvars * nvars * 3 * 4 * cx * cy * cz

    parts = [geo.buffer[1:]] * count

    def swap(sent):
        out = [sent[0]]
        for distance in range(1, count):
            pairs = [(index, partner(count, index, distance)) for index in range(count)]
            out.append(lax.ppermute(sent[distance], "space", pairs))
        return out

    def exchange(sent):
        leaving = call(
            functools.partial(route_kernel, geo), [SMEM] * 3 + [VMEM] * count, parts, [geo.buffer] * 2, work // 16
        )(place, owner, neighbours, *swap(sent))
        return swap(leaving)

    gathered = lax.all_gather(checkpoint, "ckpt", axis=0, tiled=True)
    sent = call(
        functools.partial(pack_weight_kernel, geo),
        [SMEM, VMEM, VMEM],
        parts,
        [geo.buffer, geo.block, geo.faces],
        work // 8,
    )(place, grads, rate)
    weight_ghosts = exchange(sent)
    state, *sent = call(
        functools.partial(pack_state_kernel, geo),
        [SMEM, VMEM],
        [geo.block] + parts,
        [geo.buffer, geo.faces],
        work // 8,
    )(place, gathered)
    ghosts = exchange(sent)
    fixed = (place, owner, orientation, mats)
    step_specs = [SMEM] * 4 + [VMEM] * (2 + count)
    pads = [geo.buffer, geo.faces, geo.padded, zfaces]
    next_state, *sent = call(
        functools.partial(step_kernel, geo, True), step_specs, [geo.block] + parts, pads, work
    )(*fixed, state, rate, *ghosts)
    next_ghosts = exchange(sent)
    adjoint_specs = [SMEM] * 4 + [VMEM] * (3 + 2 * count)
    grads_now, *sent = call(
        functools.partial(adjoint_kernel, geo, True),
        adjoint_specs,
        [geo.block] + parts,
        pads + [geo.padded, zfaces, geo.block],
        2 * work,
    )(*fixed, next_state, grads, rate, *next_ghosts, *weight_ghosts)
    weight_ghosts = exchange(sent)
    (final,) = call(functools.partial(step_kernel, geo, False), step_specs, [geo.block], pads, work)(
        *fixed, next_state, rate, *next_ghosts
    )
    (adjoint,) = call(
        functools.partial(adjoint_kernel, geo, False), adjoint_specs, [geo.block], pads + [geo.padded, zfaces], 2 * work
    )(*fixed, state, grads_now, rate, *ghosts, *weight_ghosts)
    return (adjoint[None, None], final[None])


def solution(mesh):
    return jax.shard_map(
        functools.partial(on_device, mesh.shape["space"]),
        mesh=mesh,
        in_specs=(
            P("space", None, "ckpt", None, None),
            P("ckpt", "space", None, None, None, None),
            P("space", None, None, None),
            P(),
            P(),
            P(),
            P(),
        ),
        out_specs=(P("ckpt", "space", None, None, None, None), P("space", None, None, None, None)),
        check_vma=False,
    )
```

```python
import functools

import jax
import jax.numpy as jnp
from jax import lax
from jax.experimental import pallas as pl
from jax.experimental.pallas import tpu as pltpu
from jax.sharding import PartitionSpec as P

STEPS = 2
time_step = 0.05
damping = 0.015

PAD = 8
VMEM = pl.BlockSpec(memory_space=pltpu.VMEM)
SMEM = pl.BlockSpec(memory_space=pltpu.SMEM)
VMEM_LIMIT = 32 * 1024 * 1024


class Geometry:
    def __init__(self, nvars, cx, cy, cz, count):
        self.v, self.x, self.y, self.z, self.n = nvars, cx, cy, cz, count
        self.rows = [nvars * cy] * 2 + [nvars * cx] * 2 + [cy] * 2
        self.runs = [-(-rows // count) for rows in self.rows]
        self.starts = [sum(self.runs[:side]) for side in range(6)]
        self.field = sum(self.runs)
        self.face_rows = -(-max(run * count for run in self.runs) // 8) * 8
        self.block = (nvars, cx, cy, cz)
        self.tall = (nvars, cx, cy + 2 * PAD, cz)
        self.faces = (6, self.face_rows, cz)
        self.rate_faces = (6, max(cx, cy), cz)

    def buffer(self, fields):
        return (self.n, -(-fields * self.field // 8) * 8, self.z)


def take_z_faces(geo, load):
    v, x, y, z = geo.block
    lane = lax.broadcasted_iota(jnp.int32, (y, z), 1)
    high = jnp.zeros((y, z), jnp.float32)
    low = jnp.zeros((y, z), jnp.float32)
    for var in range(v):
        for plane in range(x):
            place = var * x + plane
            tile = load(var, plane)
            here = lane == place
            high = jnp.where(here, pltpu.roll(tile, (place + 1) % z, 1), high)
            low = jnp.where(here, pltpu.roll(tile, place, 1) if place else tile, low)
    return high, low


def take_xy_faces(geo, source, faces):
    v, x, y, z = geo.block
    faces[0, : v * y] = source[:, x - 1].reshape(v * y, z)
    faces[1, : v * y] = source[:, 0].reshape(v * y, z)
    for var in range(v):
        faces[2, var * x : (var + 1) * x] = source[var, :, y - 1, :]
        faces[3, var * x : (var + 1) * x] = source[var, :, 0, :]


def cut(geo, faces, buffer, field):
    for side in range(6):
        run, start = geo.runs[side], field * geo.field + geo.starts[side]
        for slot in range(geo.n):
            buffer[slot, start : start + run] = faces[side, slot * run : (slot + 1) * run]


def own_codes(geo, place, owner, orientation):
    block = jnp.int32(0)
    for index in range(geo.n):
        block = jnp.where(owner[index] == place[0], index, block)
    return [orientation[block * 6 + side] for side in range(6)]


def flip_rows(values, flag, length):
    rows, z = values.shape
    grouped = values.reshape(rows // length, length // 8, 8, z)
    index = lax.broadcasted_iota(jnp.int32, (8, z), 0)
    index = jnp.where(flag == 1, 7 - index, index)
    tiles = length // 8
    out = []
    for group in range(rows // length):
        for tile in range(tiles):
            picked = jnp.where(flag == 1, grouped[group, tiles - 1 - tile], grouped[group, tile])
            out.append(jnp.take_along_axis(picked, index, axis=0))
    return jnp.stack(out).reshape(rows, z)


def flip_lanes(values, flag, length):
    rows, z = values.shape
    lane = lax.broadcasted_iota(jnp.int32, (8, z), 1)
    within = lax.rem(lane, length)
    index = jnp.where(flag == 1, lane + (length - 1) - 2 * within, lane)
    index = jnp.minimum(index, z - 1)
    tiles = values.reshape(rows // 8, 8, z)
    return jnp.stack(
        [jnp.take_along_axis(tiles[tile], index, axis=1) for tile in range(rows // 8)]
    ).reshape(rows, z)


def unpack(geo, codes, buffer, field, raw, ghosts):
    v, x, y, z = geo.block
    for side in range(6):
        run, start = geo.runs[side], field * geo.field + geo.starts[side]
        for slot in range(geo.n):
            raw[side, slot * run : (slot + 1) * run] = buffer[slot, start : start + run]
    for side in range(6):
        first, second = codes[side] & 1, (codes[side] >> 1) & 1
        layer = raw[side, : geo.rows[side]]
        if side < 4:
            layer = flip_lanes(flip_rows(layer, first, y if side < 2 else x), second, z)
        else:
            layer = flip_lanes(flip_rows(layer, second, y), first, x)
        ghosts[side, : geo.rows[side]] = layer


def face_values(geo, faces, side):
    v, x, y, z = geo.block
    if side < 4:
        depth = y if side < 2 else x
        return [faces[side, var * depth : (var + 1) * depth] for var in range(v)]
    layer = faces[side, :y]
    return [layer] + [pltpu.roll(layer, z - var * x, 1) for var in range(1, v)]


def add_xy_terms(geo, side, terms, result):
    v, x, y, z = geo.block
    for var in range(v):
        if side < 2:
            plane = x - 1 if side == 0 else 0
            result[var, plane] = result[var, plane] + terms[var]
        else:
            row = y - 1 if side == 2 else 0
            result[var, :, row, :] = result[var, :, row, :] + terms[var]


def add_z_terms(geo, high_terms, low_terms, result):
    v, x, y, z = geo.block
    lane = lax.broadcasted_iota(jnp.int32, (y, z), 1)
    zero = jnp.zeros((y, z), jnp.float32)
    for var in range(v):
        for plane in range(x):
            high = pltpu.roll(high_terms[var], z - 1 - plane, 1)
            low = pltpu.roll(low_terms[var], z - plane, 1) if plane else low_terms[var]
            change = jnp.where(lane == z - 1, high, jnp.where(lane == 0, low, zero))
            result[var, plane] = result[var, plane] + change


def fill_tall(geo, source, tall):
    v, x, y, z = geo.block
    tall[:, :, PAD : PAD + y, :] = source[...]
    for var in range(v):
        tall[var, :, PAD - 1, :] = source[var, :, 0, :]
        tall[var, :, PAD + y, :] = source[var, :, y - 1, :]


def around(geo, tall, plane):
    v, x, y, z = geo.block
    lane = lax.broadcasted_iota(jnp.int32, (y, z), 1)
    before, after = jnp.maximum(plane - 1, 0), jnp.minimum(plane + 1, x - 1)
    cells, low, high = [], [[], [], []], [[], [], []]
    for var in range(v):
        mid = tall[var, plane, PAD : PAD + y]
        cells.append(mid)
        low[0].append(tall[var, before, PAD : PAD + y])
        high[0].append(tall[var, after, PAD : PAD + y])
        low[1].append(tall[var, plane, PAD - 1 : PAD - 1 + y])
        high[1].append(tall[var, plane, PAD + 1 : PAD + 1 + y])
        low[2].append(jnp.where(lane == 0, mid, pltpu.roll(mid, 1, 1)))
        high[2].append(jnp.where(lane == z - 1, mid, pltpu.roll(mid, z - 1, 1)))
    return cells, low, high


def flux_entry(geo, mats, direction, row, column):
    return mats[(direction * geo.v + row) * geo.v + column]


def step_plane(geo, mats, cells, low, high, rate):
    v = geo.v
    total = [None] * v
    for direction in range(3):
        lows, highs = low[direction], high[direction]
        mean_low = 0.5 * (lows[0] + cells[0])
        mean_high = 0.5 * (cells[0] + highs[0])
        square_low = 1.0 + mean_low * mean_low
        square_high = 1.0 + mean_high * mean_high
        spread_low = square_low * lax.rsqrt(square_low)
        spread_high = square_high * lax.rsqrt(square_high)
        slopes = [highs[var] - lows[var] for var in range(v)]
        for var in range(v):
            term = spread_low * (cells[var] - lows[var]) - spread_high * (highs[var] - cells[var])
            for column in range(v):
                term = term + flux_entry(geo, mats, direction, var, column) * slopes[column]
            total[var] = term if total[var] is None else total[var] + term
    scale = (0.5 * time_step) * rate
    return [cells[var] - scale * total[var] - damping * jnp.tanh(cells[var]) for var in range(v)]


def adjoint_plane(geo, mats, cells, low, high, grads, weight, weight_low, weight_high):
    v = geo.v
    total = [None] * v
    extra = None
    for direction in range(3):
        spreads, steps = [], []
        for lower, upper, lower_weight, upper_weight in (
            (low[direction], cells, weight_low[direction], weight),
            (cells, high[direction], weight, weight_high[direction]),
        ):
            mean = 0.5 * (lower[0] + upper[0])
            square = 1.0 + mean * mean
            inverse = lax.rsqrt(square)
            jump = [lower_weight[var] - upper_weight[var] for var in range(v)]
            product = jump[0] * (upper[0] - lower[0])
            for var in range(1, v):
                product = product + jump[var] * (upper[var] - lower[var])
            product = product * (mean * inverse)
            extra = product if extra is None else extra + product
            spreads.append(square * inverse)
            steps.append(jump)
        slopes = [steps[0][var] + steps[1][var] for var in range(v)]
        for var in range(v):
            term = spreads[1] * steps[1][var] - spreads[0] * steps[0][var]
            for row in range(v):
                term = term + flux_entry(geo, mats, direction, row, var) * slopes[row]
            total[var] = term if total[var] is None else total[var] + term
    total[0] = total[0] - 0.5 * extra
    out = []
    for var in range(v):
        bend = jnp.tanh(cells[var])
        slope = (1.0 - damping) + damping * (bend * bend)
        out.append(grads[var] * slope - (0.5 * time_step) * total[var])
    return out


def step_face(geo, mats, side, cells, ghosts, rate):
    v = geo.v
    mean = 0.5 * (cells[0] + ghosts[0])
    square = 1.0 + mean * mean
    spread = square * lax.rsqrt(square)
    gap = [ghosts[var] - cells[var] for var in range(v)]
    scale = (0.5 * time_step) * rate
    out = []
    for var in range(v):
        total = flux_entry(geo, mats, side // 2, var, 0) * gap[0]
        for column in range(1, v):
            total = total + flux_entry(geo, mats, side // 2, var, column) * gap[column]
        if side % 2 == 0:
            out.append(scale * (spread * gap[var] - total))
        else:
            out.append(scale * (spread * gap[var] + total))
    return out


def adjoint_face(geo, mats, side, cells, ghosts, weight, ghost_weight):
    v = geo.v
    mean = 0.5 * (cells[0] + ghosts[0])
    square = 1.0 + mean * mean
    inverse = lax.rsqrt(square)
    spread = square * inverse
    jump = [weight[var] - ghost_weight[var] for var in range(v)]
    product = jump[0] * (ghosts[0] - cells[0])
    for var in range(1, v):
        product = product + jump[var] * (ghosts[var] - cells[var])
    product = (0.5 * product) * (mean * inverse)
    out = []
    for var in range(v):
        total = flux_entry(geo, mats, side // 2, 0, var) * jump[0]
        for row in range(1, v):
            total = total + flux_entry(geo, mats, side // 2, row, var) * jump[row]
        if side % 2 == 0:
            total = spread * jump[var] + total
        else:
            total = spread * jump[var] - total
        if var == 0:
            total = total - product
        out.append((-0.5 * time_step) * total)
    return out


def pack_kernel(geo, gathered, grads, rate, state, faces, weight_faces, rate_faces, buffer, weight):
    v, x, y, z = geo.block
    parts, depth = gathered.shape[0], gathered.shape[2]
    for part in range(parts):
        state[:, part * depth : (part + 1) * depth] = gathered[part]
    take_xy_faces(geo, state, faces)
    high, low = take_z_faces(geo, lambda var, plane: state[var, plane])
    faces[4, :y] = high
    faces[5, :y] = low
    cut(geo, faces, buffer, 0)
    rate_faces[0, :y] = rate[x - 1]
    rate_faces[1, :y] = rate[0]
    rate_faces[2, :x] = rate[:, y - 1, :]
    rate_faces[3, :x] = rate[:, 0, :]
    high, low = take_z_faces(geo, lambda var, plane: rate[plane])
    rate_faces[4, :y] = high
    rate_faces[5, :y] = low

    def body(plane, carry):
        for var in range(v):
            weight[var, plane] = rate[plane] * grads[var, plane]
        return carry

    lax.fori_loop(0, x, body, 0)
    take_xy_faces(geo, weight, weight_faces)
    high, low = take_z_faces(geo, lambda var, plane: weight[var, plane])
    weight_faces[4, :y] = high
    weight_faces[5, :y] = low
    cut(geo, weight_faces, buffer, 1)


def route_kernel(geo, fields, owner, neighbours, arrived, leaving):
    for block in range(geo.n):
        target = owner[block]
        for side in range(6):
            source = owner[neighbours[block * 6 + side]]
            for field in range(fields):
                run, base = geo.runs[side], field * geo.field
                start, far = base + geo.starts[side], base + geo.starts[side ^ 1]
                leaving[target, start : start + run] = arrived[source, far : far + run]


def step_inner_kernel(geo, mats, block, rate, result, tall):
    fill_tall(geo, block, tall)

    def body(plane, carry):
        cells, low, high = around(geo, tall, plane)
        for var, value in enumerate(step_plane(geo, mats, cells, low, high, rate[plane])):
            result[var, plane] = value
        return carry

    lax.fori_loop(0, geo.x, body, 0)


def adjoint_inner_kernel(geo, mats, block, grads, rate, result, tall, weights):
    v, x, y, z = geo.block
    fill_tall(geo, block, tall)

    def scale(plane, carry):
        for var in range(v):
            weights[var, plane, PAD : PAD + y] = rate[plane] * grads[var, plane]
        return carry

    lax.fori_loop(0, x, scale, 0)
    for var in range(v):
        weights[var, :, PAD - 1, :] = weights[var, :, PAD, :]
        weights[var, :, PAD + y, :] = weights[var, :, PAD + y - 1, :]

    def body(plane, carry):
        cells, low, high = around(geo, tall, plane)
        weight, weight_low, weight_high = around(geo, weights, plane)
        here = [grads[var, plane] for var in range(v)]
        values = adjoint_plane(geo, mats, cells, low, high, here, weight, weight_low, weight_high)
        for var, value in enumerate(values):
            result[var, plane] = value
        return carry

    lax.fori_loop(0, x, body, 0)


def step_edge_kernel(geo, packed, place, owner, orientation, mats, inner, faces, rate_faces, buffer, result, *rest):
    if packed:
        new_faces, sent, raw, ghosts = rest
    else:
        raw, ghosts = rest
    v, x, y, z = geo.block
    unpack(geo, own_codes(geo, place, owner, orientation), buffer, 0, raw, ghosts)
    result[...] = inner[...]
    terms = []
    for side in range(6):
        depth = y if side < 2 or side > 3 else x
        cells, outer = face_values(geo, faces, side), face_values(geo, ghosts, side)
        values = step_face(geo, mats, side, cells, outer, rate_faces[side, :depth])
        if side < 4:
            add_xy_terms(geo, side, values, result)
        else:
            terms.append(values)
    add_z_terms(geo, *terms, result)
    if packed:
        take_xy_faces(geo, result, new_faces)
        high, low = take_z_faces(geo, lambda var, plane: result[var, plane])
        new_faces[4, :y] = high
        new_faces[5, :y] = low
        cut(geo, new_faces, sent, 0)


def adjoint_edge_kernel(
    geo, packed, weight_field, place, owner, orientation, mats, inner, faces, weight_faces, *rest
):
    rate_faces, buffer, weight_buffer, result = rest[:4]
    if packed:
        new_faces, sent, raw, ghosts, weight_ghosts = rest[4:]
    else:
        raw, ghosts, weight_ghosts = rest[4:]
    v, x, y, z = geo.block
    codes = own_codes(geo, place, owner, orientation)
    unpack(geo, codes, buffer, 0, raw, ghosts)
    unpack(geo, codes, weight_buffer, weight_field, raw, weight_ghosts)
    result[...] = inner[...]
    terms = []
    for side in range(6):
        views = [face_values(geo, field, side) for field in (faces, ghosts, weight_faces, weight_ghosts)]
        values = adjoint_face(geo, mats, side, *views)
        if side < 4:
            add_xy_terms(geo, side, values, result)
        else:
            terms.append(values)
    add_z_terms(geo, *terms, result)
    if packed:
        take_xy_faces(geo, result, new_faces)
        high, low = take_z_faces(geo, lambda var, plane: result[var, plane])
        for side in range(4):
            depth = y if side < 2 else x
            for var in range(v):
                here = slice(var * depth, (var + 1) * depth)
                new_faces[side, here] = new_faces[side, here] * rate_faces[side, :depth]
        new_faces[4, :y] = high * rate_faces[4, :y]
        new_faces[5, :y] = low * rate_faces[5, :y]
        cut(geo, new_faces, sent, 0)


def call(kernel, specs, outs, scratch, flops):
    return pl.pallas_call(
        kernel,
        in_specs=specs,
        out_specs=[VMEM] * len(outs),
        out_shape=[jax.ShapeDtypeStruct(shape, jnp.float32) for shape in outs],
        scratch_shapes=[pltpu.VMEM(shape, jnp.float32) for shape in scratch],
        compiler_params=pltpu.CompilerParams(vmem_limit_bytes=VMEM_LIMIT),
        cost_estimate=pl.CostEstimate(flops=flops, bytes_accessed=3 << 20, transcendentals=0),
    )


def on_device(count, checkpoint, seeds, cell_rate, flux_mats, owner, neighbours, orientation):
    nvars, cx, cy, cz = seeds.shape[2:]
    geo = Geometry(nvars, cx, cy, cz, count)
    rate = cell_rate[0]
    grads = seeds[0, 0]
    place = lax.axis_index("space").astype(jnp.int32).reshape(1)
    mats = flux_mats.reshape(-1)
    neighbours = neighbours.reshape(-1)
    orientation = orientation.reshape(-1)
    work = nvars * nvars * 3 * 4 * cx * cy * cz
    few = work // 16

    def exchange(buffer, fields):
        arrived = lax.all_to_all(buffer, "space", 0, 0, tiled=True)
        (leaving,) = call(
            functools.partial(route_kernel, geo, fields), [SMEM, SMEM, VMEM], [geo.buffer(fields)], [], few
        )(owner, neighbours, arrived)
        return lax.all_to_all(leaving, "space", 0, 0, tiled=True)

    def step_inner(block):
        return call(
            functools.partial(step_inner_kernel, geo), [SMEM, VMEM, VMEM], [geo.block], [geo.tall], work
        )(mats, block, rate)[0]

    def adjoint_inner(block, grads):
        return call(
            functools.partial(adjoint_inner_kernel, geo), [SMEM] + [VMEM] * 3, [geo.block], [geo.tall] * 2, 2 * work
        )(mats, block, grads, rate)[0]

    def step_edge(inner, faces, buffer, packed):
        outs = [geo.block, geo.faces, geo.buffer(1)] if packed else [geo.block]
        return call(
            functools.partial(step_edge_kernel, geo, packed), [SMEM] * 4 + [VMEM] * 4, outs, [geo.faces] * 2, few
        )(*fixed, inner, faces, rate_faces, buffer)

    def adjoint_edge(inner, faces, weight_faces, buffer, weight_buffer, field, packed):
        outs = [geo.block, geo.faces, geo.buffer(1)] if packed else [geo.block]
        return call(
            functools.partial(adjoint_edge_kernel, geo, packed, field),
            [SMEM] * 4 + [VMEM] * 6,
            outs,
            [geo.faces] * 3,
            few,
        )(*fixed, inner, faces, weight_faces, rate_faces, buffer, weight_buffer)

    fixed = (place, owner, orientation, mats)
    gathered = lax.all_gather(checkpoint, "ckpt", axis=0, tiled=True)
    state, faces, weight_faces, rate_faces, sent = call(
        functools.partial(pack_kernel, geo),
        [VMEM] * 3,
        [geo.block, geo.faces, geo.faces, geo.rate_faces, geo.buffer(2)],
        [geo.block],
        few,
    )(gathered, grads, rate)
    ghosts = exchange(sent, 2)
    next_state, next_faces, sent = step_edge(step_inner(state), faces, ghosts, True)
    next_ghosts = exchange(sent, 1)
    inner = adjoint_inner(next_state, grads)
    grads_now, next_weight_faces, sent = adjoint_edge(
        inner, next_faces, weight_faces, next_ghosts, ghosts, 1, True
    )
    weight_ghosts = exchange(sent, 1)
    (final,) = step_edge(step_inner(next_state), next_faces, next_ghosts, False)
    inner = adjoint_inner(state, grads_now)
    (adjoint,) = adjoint_edge(inner, faces, next_weight_faces, ghosts, weight_ghosts, 0, False)
    return (adjoint[None, None], final[None])


def solution(mesh):
    return jax.shard_map(
        functools.partial(on_device, mesh.shape["space"]),
        mesh=mesh,
        in_specs=(
            P("space", None, "ckpt", None, None),
            P("ckpt", "space", None, None, None, None),
            P("space", None, None, None),
            P(),
            P(),
            P(),
            P(),
        ),
        out_specs=(P("ckpt", "space", None, None, None, None), P("space", None, None, None, None)),
        check_vma=False,
    )
```

```python
import functools

import jax
import jax.numpy as jnp
from jax import lax
from jax.experimental import pallas as pl
from jax.experimental.pallas import tpu as pltpu
from jax.sharding import PartitionSpec as P

STEPS = 2
time_step = 0.05
damping = 0.015

PAD = 8
VMEM = pl.BlockSpec(memory_space=pltpu.VMEM)
SMEM = pl.BlockSpec(memory_space=pltpu.SMEM)
VMEM_LIMIT = 12 * 1024 * 1024


class Pieces:
    def __init__(self, rows, count):
        self.rows = rows
        self.runs = [-(-length // count) for length in rows]
        self.starts = [sum(self.runs[:index]) for index in range(len(rows))]
        self.total = sum(self.runs)


class Geometry:
    def __init__(self, nvars, cx, cy, cz, count, parts):
        self.v, self.x, self.y, self.z, self.n, self.parts = nvars, cx, cy, cz, count, parts
        self.depth = cx // parts
        self.rows = [nvars * cy] * 2 + [nvars * cx] * 2 + [cy] * 2
        self.whole = Pieces(self.rows, count)
        self.part = Pieces([nvars * cy] + [nvars * self.depth] * 2 + [cy] * 2, count)
        self.face_rows = -(-max(run * count for run in self.whole.runs) // 8) * 8
        self.block = (nvars, cx, cy, cz)
        self.tall = (nvars, cx, cy + 2 * PAD, cz)
        self.faces = (6, self.face_rows, cz)
        self.rate_faces = (6, max(cx, cy), cz)

    def buffer(self, rows):
        return (self.n, -(-rows // 8) * 8, self.z)


def take_z_faces(geo, load):
    v, x, y, z = geo.block
    lane = lax.broadcasted_iota(jnp.int32, (y, z), 1)
    high = jnp.zeros((y, z), jnp.float32)
    low = jnp.zeros((y, z), jnp.float32)
    for var in range(v):
        for plane in range(x):
            place = var * x + plane
            tile = load(var, plane)
            here = lane == place
            high = jnp.where(here, pltpu.roll(tile, (place + 1) % z, 1), high)
            low = jnp.where(here, pltpu.roll(tile, place, 1) if place else tile, low)
    return high, low


def take_xy_faces(geo, source, faces):
    v, x, y, z = geo.block
    faces[0, : v * y] = source[:, x - 1].reshape(v * y, z)
    faces[1, : v * y] = source[:, 0].reshape(v * y, z)
    for var in range(v):
        faces[2, var * x : (var + 1) * x] = source[var, :, y - 1, :]
        faces[3, var * x : (var + 1) * x] = source[var, :, 0, :]


def cut(geo, pieces, faces, buffer, base):
    for index, (run, start) in enumerate(zip(pieces.runs, pieces.starts)):
        for slot in range(geo.n):
            buffer[slot, base + start : base + start + run] = faces[index, slot * run : (slot + 1) * run]


def own_codes(geo, place, owner, orientation):
    block = jnp.int32(0)
    for index in range(geo.n):
        block = jnp.where(owner[index] == place[0], index, block)
    return [orientation[block * 6 + side] for side in range(6)]


def flip_rows(values, flag, length):
    rows, z = values.shape
    grouped = values.reshape(rows // length, length // 8, 8, z)
    index = lax.broadcasted_iota(jnp.int32, (8, z), 0)
    index = jnp.where(flag == 1, 7 - index, index)
    tiles = length // 8
    out = []
    for group in range(rows // length):
        for tile in range(tiles):
            picked = jnp.where(flag == 1, grouped[group, tiles - 1 - tile], grouped[group, tile])
            out.append(jnp.take_along_axis(picked, index, axis=0))
    return jnp.stack(out).reshape(rows, z)


def flip_lanes(values, flag, length):
    rows, z = values.shape
    lane = lax.broadcasted_iota(jnp.int32, (8, z), 1)
    within = lax.rem(lane, length)
    index = jnp.where(flag == 1, lane + (length - 1) - 2 * within, lane)
    index = jnp.minimum(index, z - 1)
    tiles = values.reshape(rows // 8, 8, z)
    return jnp.stack(
        [jnp.take_along_axis(tiles[tile], index, axis=1) for tile in range(rows // 8)]
    ).reshape(rows, z)


def join(geo, buffer, raw):
    for side in range(6):
        run, start = geo.whole.runs[side], geo.whole.starts[side]
        for slot in range(geo.n):
            raw[side, slot * run : (slot + 1) * run] = buffer[slot, start : start + run]


def join_parts(geo, buffer, raw, piece):
    for side in range(6):
        index = 0 if side < 2 else side - 1
        run, start = geo.part.runs[index], geo.part.starts[index]
        if side < 2:
            part = 0 if side == 0 else geo.parts - 1
            for slot in range(geo.n):
                raw[side, slot * run : (slot + 1) * run] = buffer[part, slot, start : start + run]
        elif side < 4:
            for part in range(geo.parts):
                for slot in range(geo.n):
                    piece[slot * run : (slot + 1) * run] = buffer[part, slot, start : start + run]
                for var in range(geo.v):
                    row = var * geo.x + part * geo.depth
                    raw[side, row : row + geo.depth] = piece[var * geo.depth : (var + 1) * geo.depth]
        else:
            for slot in range(geo.n):
                total = buffer[0, slot, start : start + run]
                for part in range(1, geo.parts):
                    total = total + buffer[part, slot, start : start + run]
                raw[side, slot * run : (slot + 1) * run] = total


def turn(geo, codes, raw, ghosts):
    v, x, y, z = geo.block
    for side in range(6):
        first, second = codes[side] & 1, (codes[side] >> 1) & 1
        layer = raw[side, : geo.rows[side]]
        if side < 4:
            layer = flip_lanes(flip_rows(layer, first, y if side < 2 else x), second, z)
        else:
            layer = flip_lanes(flip_rows(layer, second, y), first, x)
        ghosts[side, : geo.rows[side]] = layer


def face_values(geo, faces, side):
    v, x, y, z = geo.block
    if side < 4:
        depth = y if side < 2 else x
        return [faces[side, var * depth : (var + 1) * depth] for var in range(v)]
    layer = faces[side, :y]
    return [layer] + [pltpu.roll(layer, z - var * x, 1) for var in range(1, v)]


def add_xy_terms(geo, side, terms, result):
    v, x, y, z = geo.block
    for var in range(v):
        if side < 2:
            plane = x - 1 if side == 0 else 0
            result[var, plane] = result[var, plane] + terms[var]
        else:
            row = y - 1 if side == 2 else 0
            result[var, :, row, :] = result[var, :, row, :] + terms[var]


def add_z_terms(geo, high_terms, low_terms, result):
    v, x, y, z = geo.block
    lane = lax.broadcasted_iota(jnp.int32, (y, z), 1)
    zero = jnp.zeros((y, z), jnp.float32)
    for var in range(v):
        for plane in range(x):
            high = pltpu.roll(high_terms[var], z - 1 - plane, 1)
            low = pltpu.roll(low_terms[var], z - plane, 1) if plane else low_terms[var]
            change = jnp.where(lane == z - 1, high, jnp.where(lane == 0, low, zero))
            result[var, plane] = result[var, plane] + change


def fill_tall(geo, source, tall):
    v, x, y, z = geo.block
    if len(source.shape) == 5:
        depth = geo.depth
        for part in range(geo.parts):
            tall[:, part * depth : (part + 1) * depth, PAD : PAD + y, :] = source[part]
    else:
        tall[:, :, PAD : PAD + y, :] = source[...]
    for var in range(v):
        tall[var, :, PAD - 1, :] = tall[var, :, PAD, :]
        tall[var, :, PAD + y, :] = tall[var, :, PAD + y - 1, :]


def around(geo, tall, plane):
    v, x, y, z = geo.block
    lane = lax.broadcasted_iota(jnp.int32, (y, z), 1)
    before, after = jnp.maximum(plane - 1, 0), jnp.minimum(plane + 1, x - 1)
    cells, low, high = [], [[], [], []], [[], [], []]
    for var in range(v):
        mid = tall[var, plane, PAD : PAD + y]
        cells.append(mid)
        low[0].append(tall[var, before, PAD : PAD + y])
        high[0].append(tall[var, after, PAD : PAD + y])
        low[1].append(tall[var, plane, PAD - 1 : PAD - 1 + y])
        high[1].append(tall[var, plane, PAD + 1 : PAD + 1 + y])
        low[2].append(jnp.where(lane == 0, mid, pltpu.roll(mid, 1, 1)))
        high[2].append(jnp.where(lane == z - 1, mid, pltpu.roll(mid, z - 1, 1)))
    return cells, low, high


def flux_entry(geo, mats, direction, row, column):
    return mats[(direction * geo.v + row) * geo.v + column]


def step_plane(geo, mats, cells, low, high, rate):
    v = geo.v
    total = [None] * v
    for direction in range(3):
        lows, highs = low[direction], high[direction]
        mean_low = 0.5 * (lows[0] + cells[0])
        mean_high = 0.5 * (cells[0] + highs[0])
        square_low = 1.0 + mean_low * mean_low
        square_high = 1.0 + mean_high * mean_high
        spread_low = square_low * lax.rsqrt(square_low)
        spread_high = square_high * lax.rsqrt(square_high)
        slopes = [highs[var] - lows[var] for var in range(v)]
        for var in range(v):
            term = spread_low * (cells[var] - lows[var]) - spread_high * (highs[var] - cells[var])
            for column in range(v):
                term = term + flux_entry(geo, mats, direction, var, column) * slopes[column]
            total[var] = term if total[var] is None else total[var] + term
    scale = (0.5 * time_step) * rate
    return [cells[var] - scale * total[var] - damping * jnp.tanh(cells[var]) for var in range(v)]


def adjoint_plane(geo, mats, cells, low, high, grads, weight, weight_low, weight_high):
    v = geo.v
    total = [None] * v
    extra = None
    for direction in range(3):
        spreads, steps = [], []
        for lower, upper, lower_weight, upper_weight in (
            (low[direction], cells, weight_low[direction], weight),
            (cells, high[direction], weight, weight_high[direction]),
        ):
            mean = 0.5 * (lower[0] + upper[0])
            square = 1.0 + mean * mean
            inverse = lax.rsqrt(square)
            jump = [lower_weight[var] - upper_weight[var] for var in range(v)]
            product = jump[0] * (upper[0] - lower[0])
            for var in range(1, v):
                product = product + jump[var] * (upper[var] - lower[var])
            product = product * (mean * inverse)
            extra = product if extra is None else extra + product
            spreads.append(square * inverse)
            steps.append(jump)
        slopes = [steps[0][var] + steps[1][var] for var in range(v)]
        for var in range(v):
            term = spreads[1] * steps[1][var] - spreads[0] * steps[0][var]
            for row in range(v):
                term = term + flux_entry(geo, mats, direction, row, var) * slopes[row]
            total[var] = term if total[var] is None else total[var] + term
    total[0] = total[0] - 0.5 * extra
    out = []
    for var in range(v):
        bend = jnp.tanh(cells[var])
        slope = (1.0 - damping) + damping * (bend * bend)
        out.append(grads[var] * slope - (0.5 * time_step) * total[var])
    return out


def step_face(geo, mats, side, cells, ghosts, rate):
    v = geo.v
    mean = 0.5 * (cells[0] + ghosts[0])
    square = 1.0 + mean * mean
    spread = square * lax.rsqrt(square)
    gap = [ghosts[var] - cells[var] for var in range(v)]
    scale = (0.5 * time_step) * rate
    out = []
    for var in range(v):
        total = flux_entry(geo, mats, side // 2, var, 0) * gap[0]
        for column in range(1, v):
            total = total + flux_entry(geo, mats, side // 2, var, column) * gap[column]
        if side % 2 == 0:
            out.append(scale * (spread * gap[var] - total))
        else:
            out.append(scale * (spread * gap[var] + total))
    return out


def adjoint_face(geo, mats, side, cells, ghosts, weight, ghost_weight):
    v = geo.v
    mean = 0.5 * (cells[0] + ghosts[0])
    square = 1.0 + mean * mean
    inverse = lax.rsqrt(square)
    spread = square * inverse
    jump = [weight[var] - ghost_weight[var] for var in range(v)]
    product = jump[0] * (ghosts[0] - cells[0])
    for var in range(1, v):
        product = product + jump[var] * (ghosts[var] - cells[var])
    product = (0.5 * product) * (mean * inverse)
    out = []
    for var in range(v):
        total = flux_entry(geo, mats, side // 2, 0, var) * jump[0]
        for row in range(1, v):
            total = total + flux_entry(geo, mats, side // 2, row, var) * jump[row]
        if side % 2 == 0:
            total = spread * jump[var] + total
        else:
            total = spread * jump[var] - total
        if var == 0:
            total = total - product
        out.append((-0.5 * time_step) * total)
    return out


def pack_kernel(geo, part, stored, grads, rate, kept, weight_faces, rate_faces, buffer, pieces):
    v, x, y, z = geo.block
    depth = geo.depth
    kept[...] = stored[...]
    lane = lax.broadcasted_iota(jnp.int32, (y, z), 1)
    plane = jnp.where(part[0] == geo.parts - 1, depth - 1, 0)
    high = jnp.zeros((y, z), jnp.float32)
    low = jnp.zeros((y, z), jnp.float32)
    for var in range(v):
        pieces[0, var * y : (var + 1) * y] = stored[var, plane]
        pieces[1, var * depth : (var + 1) * depth] = stored[var, :, y - 1, :]
        pieces[2, var * depth : (var + 1) * depth] = stored[var, :, 0, :]
        for step in range(depth):
            place = var * x + part[0] * depth + step
            tile = stored[var, step]
            here = lane == place
            high = jnp.where(here, pltpu.roll(tile, lax.rem(place + 1, z), 1), high)
            low = jnp.where(here, pltpu.roll(tile, place, 1), low)
    pieces[3, :y] = high
    pieces[4, :y] = low
    cut(geo, geo.part, pieces, buffer, 0)
    rate_faces[0, :y] = rate[x - 1]
    rate_faces[1, :y] = rate[0]
    rate_faces[2, :x] = rate[:, y - 1, :]
    rate_faces[3, :x] = rate[:, 0, :]
    high, low = take_z_faces(geo, lambda var, plane: rate[plane])
    rate_faces[4, :y] = high
    rate_faces[5, :y] = low
    take_weight_faces(geo, grads, rate_faces, weight_faces)
    cut(geo, geo.whole, weight_faces, buffer, geo.part.total)


def take_weight_faces(geo, grads, rate_faces, faces):
    v, x, y, z = geo.block
    take_xy_faces(geo, grads, faces)
    for side in range(4):
        depth = y if side < 2 else x
        for var in range(v):
            here = slice(var * depth, (var + 1) * depth)
            faces[side, here] = faces[side, here] * rate_faces[side, :depth]
    high, low = take_z_faces(geo, lambda var, plane: grads[var, plane])
    faces[4, :y] = high * rate_faces[4, :y]
    faces[5, :y] = low * rate_faces[5, :y]


def route_whole(geo, owner, neighbours, arrived, base, leaving):
    for block in range(geo.n):
        target = owner[block]
        for side in range(6):
            source = owner[neighbours[block * 6 + side]]
            run, start, far = geo.whole.runs[side], geo.whole.starts[side], base + geo.whole.starts[side ^ 1]
            leaving[target, start : start + run] = arrived[source, far : far + run]


def route_kernel(geo, owner, neighbours, arrived, leaving):
    route_whole(geo, owner, neighbours, arrived, 0, leaving)


def route_first_kernel(geo, part, owner, neighbours, arrived, leaving, weight_leaving):
    route_whole(geo, owner, neighbours, arrived, geo.part.total, weight_leaving)
    x_side = jnp.where(part[0] == geo.parts - 1, 1, 0)
    for block in range(geo.n):
        target = owner[block]
        for index in range(5):
            side, far_index = (x_side, 0) if index == 0 else (index + 1, ((index + 1) ^ 1) - 1)
            source = owner[neighbours[block * 6 + side]]
            run, start, far = geo.part.runs[index], geo.part.starts[index], geo.part.starts[far_index]
            leaving[target, start : start + run] = arrived[source, far : far + run]


def step_inner_kernel(geo, mats, block, rate, result, *rest):
    tall = rest[-1]
    fill_tall(geo, block, tall)

    def body(plane, carry):
        cells, low, high = around(geo, tall, plane)
        for var, value in enumerate(step_plane(geo, mats, cells, low, high, rate[plane])):
            result[var, plane] = value
        return carry

    lax.fori_loop(0, geo.x, body, 0)
    if len(rest) == 2:
        faces = rest[0]
        v, x, y, z = geo.block
        for var in range(v):
            faces[0, var * y : (var + 1) * y] = tall[var, x - 1, PAD : PAD + y]
            faces[1, var * y : (var + 1) * y] = tall[var, 0, PAD : PAD + y]
            faces[2, var * x : (var + 1) * x] = tall[var, :, PAD + y - 1, :]
            faces[3, var * x : (var + 1) * x] = tall[var, :, PAD, :]
        high, low = take_z_faces(geo, lambda var, plane: tall[var, plane, PAD : PAD + y])
        faces[4, :y] = high
        faces[5, :y] = low


def adjoint_inner_kernel(geo, mats, block, grads, rate, result, tall, weights):
    v, x, y, z = geo.block
    fill_tall(geo, block, tall)

    def scale(plane, carry):
        for var in range(v):
            weights[var, plane, PAD : PAD + y] = rate[plane] * grads[var, plane]
        return carry

    lax.fori_loop(0, x, scale, 0)
    for var in range(v):
        weights[var, :, PAD - 1, :] = weights[var, :, PAD, :]
        weights[var, :, PAD + y, :] = weights[var, :, PAD + y - 1, :]

    def body(plane, carry):
        cells, low, high = around(geo, tall, plane)
        weight, weight_low, weight_high = around(geo, weights, plane)
        here = [grads[var, plane] for var in range(v)]
        values = adjoint_plane(geo, mats, cells, low, high, here, weight, weight_low, weight_high)
        for var, value in enumerate(values):
            result[var, plane] = value
        return carry

    lax.fori_loop(0, x, body, 0)


def step_edge_kernel(geo, first, place, owner, orientation, mats, inner, faces, rate_faces, buffer, result, *rest):
    if first:
        new_faces, sent, ghosts, raw, piece = rest
        join_parts(geo, buffer, raw, piece)
    else:
        ghosts, raw = rest
        join(geo, buffer, raw)
    v, x, y, z = geo.block
    turn(geo, own_codes(geo, place, owner, orientation), raw, ghosts)
    result[...] = inner[...]
    terms = []
    for side in range(6):
        depth = y if side < 2 or side > 3 else x
        cells, outer = face_values(geo, faces, side), face_values(geo, ghosts, side)
        values = step_face(geo, mats, side, cells, outer, rate_faces[side, :depth])
        if side < 4:
            add_xy_terms(geo, side, values, result)
        else:
            terms.append(values)
    add_z_terms(geo, *terms, result)
    if first:
        take_xy_faces(geo, result, new_faces)
        high, low = take_z_faces(geo, lambda var, plane: result[var, plane])
        new_faces[4, :y] = high
        new_faces[5, :y] = low
        cut(geo, geo.whole, new_faces, sent, 0)


def adjoint_edge_kernel(geo, last, place, owner, orientation, mats, inner, faces, weight_faces, *rest):
    v, x, y, z = geo.block
    codes = own_codes(geo, place, owner, orientation)
    if last:
        ghosts, weight_buffer, result, raw, weight_ghosts = rest
    else:
        rate_faces, buffer, weight_buffer, result, new_faces, sent, raw, ghosts, weight_ghosts = rest
        join(geo, buffer, raw)
        turn(geo, codes, raw, ghosts)
    join(geo, weight_buffer, raw)
    turn(geo, codes, raw, weight_ghosts)
    result[...] = inner[...]
    terms = []
    for side in range(6):
        views = [face_values(geo, field, side) for field in (faces, ghosts, weight_faces, weight_ghosts)]
        values = adjoint_face(geo, mats, side, *views)
        if side < 4:
            add_xy_terms(geo, side, values, result)
        else:
            terms.append(values)
    add_z_terms(geo, *terms, result)
    if not last:
        take_weight_faces(geo, result, rate_faces, new_faces)
        cut(geo, geo.whole, new_faces, sent, 0)


def call(kernel, specs, outs, scratch, flops):
    return pl.pallas_call(
        kernel,
        in_specs=specs,
        out_specs=[VMEM] * len(outs),
        out_shape=[jax.ShapeDtypeStruct(shape, jnp.float32) for shape in outs],
        scratch_shapes=[pltpu.VMEM(shape, jnp.float32) for shape in scratch],
        compiler_params=pltpu.CompilerParams(vmem_limit_bytes=VMEM_LIMIT),
        cost_estimate=pl.CostEstimate(flops=flops, bytes_accessed=3 << 20, transcendentals=0),
    )


def on_device(count, parts, checkpoint, seeds, cell_rate, flux_mats, owner, neighbours, orientation):
    nvars, cx, cy, cz = seeds.shape[2:]
    geo = Geometry(nvars, cx, cy, cz, count, parts)
    rate = cell_rate[0]
    grads = seeds[0, 0]
    place = lax.axis_index("space").astype(jnp.int32).reshape(1)
    part = lax.axis_index("ckpt").astype(jnp.int32).reshape(1)
    mats = flux_mats.reshape(-1)
    neighbours = neighbours.reshape(-1)
    orientation = orientation.reshape(-1)
    fixed = (place, owner, orientation, mats)
    work = nvars * nvars * 3 * 4 * cx * cy * cz
    few = work // 16
    whole, some = geo.buffer(geo.whole.total), geo.buffer(geo.part.total)

    def swap(buffer):
        return lax.all_to_all(buffer, "space", 0, 0, tiled=True)

    def route(arrived):
        return call(functools.partial(route_kernel, geo), [SMEM, SMEM, VMEM], [whole], [], few)(
            owner, neighbours, arrived
        )[0]

    def step_inner(block, faces):
        outs = [geo.block, geo.faces] if faces else [geo.block]
        return call(functools.partial(step_inner_kernel, geo), [SMEM, VMEM, VMEM], outs, [geo.tall], work)(
            mats, block, rate
        )

    def adjoint_inner(block, grads):
        return call(
            functools.partial(adjoint_inner_kernel, geo), [SMEM] + [VMEM] * 3, [geo.block], [geo.tall] * 2, 2 * work
        )(mats, block, grads, rate)[0]

    kept, weight_faces, rate_faces, sent = call(
        functools.partial(pack_kernel, geo),
        [SMEM] + [VMEM] * 3,
        [checkpoint.shape[1:], geo.faces, geo.rate_faces, geo.buffer(geo.part.total + geo.whole.total)],
        [geo.faces],
        few,
    )(part, checkpoint[0], grads, rate)
    arrived = swap(sent)
    state = lax.all_gather(kept, "ckpt", axis=0)
    arrived, state = lax.optimization_barrier((arrived, state))
    leaving, weight_leaving = call(
        functools.partial(route_first_kernel, geo), [SMEM] * 3 + [VMEM], [some, whole], [], few
    )(part, owner, neighbours, arrived)
    part_ghosts = swap(leaving)
    inner, faces = step_inner(state, True)
    part_ghosts, inner, faces = lax.optimization_barrier((part_ghosts, inner, faces))
    weight_ghosts = swap(weight_leaving)
    gathered = lax.all_gather(part_ghosts, "ckpt", axis=0)
    next_state, next_faces, sent, ghosts = call(
        functools.partial(step_edge_kernel, geo, True),
        [SMEM] * 4 + [VMEM] * 4,
        [geo.block, geo.faces, whole, geo.faces],
        [geo.faces, geo.faces[1:]],
        few,
    )(*fixed, inner, faces, rate_faces, gathered)

    arrived = swap(sent)
    inner = adjoint_inner(next_state, grads)
    arrived, inner = lax.optimization_barrier((arrived, inner))
    leaving = route(arrived)
    later_state, leaving = lax.optimization_barrier((next_state, leaving))
    next_ghosts = swap(leaving)
    (final_inner,) = step_inner(later_state, False)
    next_ghosts, final_inner = lax.optimization_barrier((next_ghosts, final_inner))
    grads_now, next_weight_faces, sent = call(
        functools.partial(adjoint_edge_kernel, geo, False),
        [SMEM] * 4 + [VMEM] * 6,
        [geo.block, geo.faces, whole],
        [geo.faces] * 3,
        few,
    )(*fixed, inner, next_faces, weight_faces, rate_faces, next_ghosts, weight_ghosts)

    arrived = swap(sent)
    inner = adjoint_inner(state, grads_now)
    arrived, inner = lax.optimization_barrier((arrived, inner))
    leaving = route(arrived)
    final_inner, leaving = lax.optimization_barrier((final_inner, leaving))
    last_ghosts = swap(leaving)
    (final,) = call(
        functools.partial(step_edge_kernel, geo, False),
        [SMEM] * 4 + [VMEM] * 4,
        [geo.block],
        [geo.faces] * 2,
        work,
    )(*fixed, final_inner, next_faces, rate_faces, next_ghosts)
    last_ghosts, final = lax.optimization_barrier((last_ghosts, final))
    (adjoint,) = call(
        functools.partial(adjoint_edge_kernel, geo, True),
        [SMEM] * 4 + [VMEM] * 5,
        [geo.block],
        [geo.faces] * 2,
        few,
    )(*fixed, inner, faces, next_weight_faces, ghosts, last_ghosts)
    return (adjoint[None, None], final[None])


def solution(mesh):
    return jax.shard_map(
        functools.partial(on_device, mesh.shape["space"], mesh.shape["ckpt"]),
        mesh=mesh,
        in_specs=(
            P("space", None, "ckpt", None, None),
            P("ckpt", "space", None, None, None, None),
            P("space", None, None, None),
            P(),
            P(),
            P(),
            P(),
        ),
        out_specs=(P("ckpt", "space", None, None, None, None), P("space", None, None, None, None)),
        check_vma=False,
    )
```

```python
import functools

import jax
import jax.numpy as jnp
from jax import lax
from jax.experimental import pallas as pl
from jax.experimental.pallas import tpu as pltpu
from jax.sharding import PartitionSpec as P

STEPS = 2
time_step = 0.05
damping = 0.015

PAD = 8
VMEM = pl.BlockSpec(memory_space=pltpu.VMEM)
SMEM = pl.BlockSpec(memory_space=pltpu.SMEM)
VMEM_LIMIT = 16 * 1024 * 1024


class Pieces:
    def __init__(self, rows, count):
        self.rows = rows
        self.runs = [-(-length // count) for length in rows]
        self.starts = [sum(self.runs[:index]) for index in range(len(rows))]
        self.total = sum(self.runs)


class Geometry:
    def __init__(self, nvars, cx, cy, cz, count, parts):
        self.v, self.x, self.y, self.z, self.n, self.parts = nvars, cx, cy, cz, count, parts
        self.depth = cx // parts
        self.rows = [nvars * cy] * 2 + [nvars * cx] * 2 + [cy] * 2
        self.whole = Pieces(self.rows, count)
        self.part = Pieces([nvars * cy] + [nvars * self.depth] * 2 + [cy] * 2, count)
        self.face_rows = -(-max(run * count for run in self.whole.runs) // 8) * 8
        self.block = (nvars, cx, cy, cz)
        self.tall = (nvars, cx, cy + 2 * PAD, cz)
        self.faces = (6, self.face_rows, cz)
        self.rate_faces = (6, max(cx, cy), cz)

    def buffer(self, rows):
        return (self.n, -(-rows // 8) * 8, self.z)


def take_z_faces(geo, load):
    v, x, y, z = geo.block
    lane = lax.broadcasted_iota(jnp.int32, (y, z), 1)
    high = jnp.zeros((y, z), jnp.float32)
    low = jnp.zeros((y, z), jnp.float32)
    for var in range(v):
        for plane in range(x):
            place = var * x + plane
            tile = load(var, plane)
            here = lane == place
            high = jnp.where(here, pltpu.roll(tile, (place + 1) % z, 1), high)
            low = jnp.where(here, pltpu.roll(tile, place, 1) if place else tile, low)
    return high, low


def take_xy_faces(geo, source, faces):
    v, x, y, z = geo.block
    faces[0, : v * y] = source[:, x - 1].reshape(v * y, z)
    faces[1, : v * y] = source[:, 0].reshape(v * y, z)
    for var in range(v):
        faces[2, var * x : (var + 1) * x] = source[var, :, y - 1, :]
        faces[3, var * x : (var + 1) * x] = source[var, :, 0, :]


def cut(geo, pieces, faces, buffer, base):
    for index, (run, start) in enumerate(zip(pieces.runs, pieces.starts)):
        for slot in range(geo.n):
            buffer[slot, base + start : base + start + run] = faces[index, slot * run : (slot + 1) * run]


def own_codes(geo, place, owner, orientation):
    block = jnp.int32(0)
    for index in range(geo.n):
        block = jnp.where(owner[index] == place[0], index, block)
    return [orientation[block * 6 + side] for side in range(6)]


def flip_rows(values, flag, length):
    rows, z = values.shape
    grouped = values.reshape(rows // length, length // 8, 8, z)
    index = lax.broadcasted_iota(jnp.int32, (8, z), 0)
    index = jnp.where(flag == 1, 7 - index, index)
    tiles = length // 8
    out = []
    for group in range(rows // length):
        for tile in range(tiles):
            picked = jnp.where(flag == 1, grouped[group, tiles - 1 - tile], grouped[group, tile])
            out.append(jnp.take_along_axis(picked, index, axis=0))
    return jnp.stack(out).reshape(rows, z)


def flip_lanes(values, flag, length):
    rows, z = values.shape
    lane = lax.broadcasted_iota(jnp.int32, (8, z), 1)
    within = lax.rem(lane, length)
    index = jnp.where(flag == 1, lane + (length - 1) - 2 * within, lane)
    index = jnp.minimum(index, z - 1)
    tiles = values.reshape(rows // 8, 8, z)
    return jnp.stack(
        [jnp.take_along_axis(tiles[tile], index, axis=1) for tile in range(rows // 8)]
    ).reshape(rows, z)


def join(geo, buffer, raw):
    for side in range(6):
        run, start = geo.whole.runs[side], geo.whole.starts[side]
        for slot in range(geo.n):
            raw[side, slot * run : (slot + 1) * run] = buffer[slot, start : start + run]


def join_parts(geo, buffer, raw, piece):
    for side in range(6):
        index = 0 if side < 2 else side - 1
        run, start = geo.part.runs[index], geo.part.starts[index]
        if side < 2:
            part = 0 if side == 0 else geo.parts - 1
            for slot in range(geo.n):
                raw[side, slot * run : (slot + 1) * run] = buffer[part, slot, start : start + run]
        elif side < 4:
            for part in range(geo.parts):
                for slot in range(geo.n):
                    piece[slot * run : (slot + 1) * run] = buffer[part, slot, start : start + run]
                for var in range(geo.v):
                    row = var * geo.x + part * geo.depth
                    raw[side, row : row + geo.depth] = piece[var * geo.depth : (var + 1) * geo.depth]
        else:
            for slot in range(geo.n):
                total = buffer[0, slot, start : start + run]
                for part in range(1, geo.parts):
                    total = total + buffer[part, slot, start : start + run]
                raw[side, slot * run : (slot + 1) * run] = total


def turn(geo, codes, raw, ghosts):
    v, x, y, z = geo.block
    for side in range(6):
        first, second = codes[side] & 1, (codes[side] >> 1) & 1
        layer = raw[side, : geo.rows[side]]
        if side < 4:
            layer = flip_lanes(flip_rows(layer, first, y if side < 2 else x), second, z)
        else:
            layer = flip_lanes(flip_rows(layer, second, y), first, x)
        ghosts[side, : geo.rows[side]] = layer


def face_values(geo, faces, side):
    v, x, y, z = geo.block
    if side < 4:
        depth = y if side < 2 else x
        return [faces[side, var * depth : (var + 1) * depth] for var in range(v)]
    layer = faces[side, :y]
    return [layer] + [pltpu.roll(layer, z - var * x, 1) for var in range(1, v)]


def add_xy_terms(geo, side, terms, result):
    v, x, y, z = geo.block
    for var in range(v):
        if side < 2:
            plane = x - 1 if side == 0 else 0
            result[var, plane] = result[var, plane] + terms[var]
        else:
            row = y - 1 if side == 2 else 0
            result[var, :, row, :] = result[var, :, row, :] + terms[var]


def add_z_terms(geo, high_terms, low_terms, result):
    v, x, y, z = geo.block
    lane = lax.broadcasted_iota(jnp.int32, (y, z), 1)
    zero = jnp.zeros((y, z), jnp.float32)
    for var in range(v):
        for plane in range(x):
            high = pltpu.roll(high_terms[var], z - 1 - plane, 1)
            low = pltpu.roll(low_terms[var], z - plane, 1) if plane else low_terms[var]
            change = jnp.where(lane == z - 1, high, jnp.where(lane == 0, low, zero))
            result[var, plane] = result[var, plane] + change


def fill_tall(geo, source, tall):
    v, x, y, z = geo.block
    if len(source.shape) == 5:
        depth = geo.depth
        for part in range(geo.parts):
            tall[:, part * depth : (part + 1) * depth, PAD : PAD + y, :] = source[part]
    else:
        tall[:, :, PAD : PAD + y, :] = source[...]
    for var in range(v):
        tall[var, :, PAD - 1, :] = tall[var, :, PAD, :]
        tall[var, :, PAD + y, :] = tall[var, :, PAD + y - 1, :]


def around(geo, tall, plane):
    v, x, y, z = geo.block
    lane = lax.broadcasted_iota(jnp.int32, (y, z), 1)
    before, after = jnp.maximum(plane - 1, 0), jnp.minimum(plane + 1, x - 1)
    cells, low, high = [], [[], [], []], [[], [], []]
    for var in range(v):
        mid = tall[var, plane, PAD : PAD + y]
        cells.append(mid)
        low[0].append(tall[var, before, PAD : PAD + y])
        high[0].append(tall[var, after, PAD : PAD + y])
        low[1].append(tall[var, plane, PAD - 1 : PAD - 1 + y])
        high[1].append(tall[var, plane, PAD + 1 : PAD + 1 + y])
        low[2].append(jnp.where(lane == 0, mid, pltpu.roll(mid, 1, 1)))
        high[2].append(jnp.where(lane == z - 1, mid, pltpu.roll(mid, z - 1, 1)))
    return cells, low, high


def flux_entry(geo, mats, direction, row, column):
    return mats[(direction * geo.v + row) * geo.v + column]


def step_plane(geo, mats, cells, low, high, rate):
    v = geo.v
    total = [None] * v
    for direction in range(3):
        lows, highs = low[direction], high[direction]
        mean_low = 0.5 * (lows[0] + cells[0])
        mean_high = 0.5 * (cells[0] + highs[0])
        square_low = 1.0 + mean_low * mean_low
        square_high = 1.0 + mean_high * mean_high
        spread_low = square_low * lax.rsqrt(square_low)
        spread_high = square_high * lax.rsqrt(square_high)
        slopes = [highs[var] - lows[var] for var in range(v)]
        for var in range(v):
            term = spread_low * (cells[var] - lows[var]) - spread_high * (highs[var] - cells[var])
            for column in range(v):
                term = term + flux_entry(geo, mats, direction, var, column) * slopes[column]
            total[var] = term if total[var] is None else total[var] + term
    scale = (0.5 * time_step) * rate
    return [cells[var] - scale * total[var] - damping * jnp.tanh(cells[var]) for var in range(v)]


def adjoint_plane(geo, mats, cells, low, high, grads, weight, weight_low, weight_high):
    v = geo.v
    total = [None] * v
    extra = None
    for direction in range(3):
        spreads, steps = [], []
        for lower, upper, lower_weight, upper_weight in (
            (low[direction], cells, weight_low[direction], weight),
            (cells, high[direction], weight, weight_high[direction]),
        ):
            mean = 0.5 * (lower[0] + upper[0])
            square = 1.0 + mean * mean
            inverse = lax.rsqrt(square)
            jump = [lower_weight[var] - upper_weight[var] for var in range(v)]
            product = jump[0] * (upper[0] - lower[0])
            for var in range(1, v):
                product = product + jump[var] * (upper[var] - lower[var])
            product = product * (mean * inverse)
            extra = product if extra is None else extra + product
            spreads.append(square * inverse)
            steps.append(jump)
        slopes = [steps[0][var] + steps[1][var] for var in range(v)]
        for var in range(v):
            term = spreads[1] * steps[1][var] - spreads[0] * steps[0][var]
            for row in range(v):
                term = term + flux_entry(geo, mats, direction, row, var) * slopes[row]
            total[var] = term if total[var] is None else total[var] + term
    total[0] = total[0] - 0.5 * extra
    out = []
    for var in range(v):
        bend = jnp.tanh(cells[var])
        slope = (1.0 - damping) + damping * (bend * bend)
        out.append(grads[var] * slope - (0.5 * time_step) * total[var])
    return out


def step_face(geo, mats, side, cells, ghosts, rate):
    v = geo.v
    mean = 0.5 * (cells[0] + ghosts[0])
    square = 1.0 + mean * mean
    spread = square * lax.rsqrt(square)
    gap = [ghosts[var] - cells[var] for var in range(v)]
    scale = (0.5 * time_step) * rate
    out = []
    for var in range(v):
        total = flux_entry(geo, mats, side // 2, var, 0) * gap[0]
        for column in range(1, v):
            total = total + flux_entry(geo, mats, side // 2, var, column) * gap[column]
        if side % 2 == 0:
            out.append(scale * (spread * gap[var] - total))
        else:
            out.append(scale * (spread * gap[var] + total))
    return out


def adjoint_face(geo, mats, side, cells, ghosts, weight, ghost_weight):
    v = geo.v
    mean = 0.5 * (cells[0] + ghosts[0])
    square = 1.0 + mean * mean
    inverse = lax.rsqrt(square)
    spread = square * inverse
    jump = [weight[var] - ghost_weight[var] for var in range(v)]
    product = jump[0] * (ghosts[0] - cells[0])
    for var in range(1, v):
        product = product + jump[var] * (ghosts[var] - cells[var])
    product = (0.5 * product) * (mean * inverse)
    out = []
    for var in range(v):
        total = flux_entry(geo, mats, side // 2, 0, var) * jump[0]
        for row in range(1, v):
            total = total + flux_entry(geo, mats, side // 2, row, var) * jump[row]
        if side % 2 == 0:
            total = spread * jump[var] + total
        else:
            total = spread * jump[var] - total
        if var == 0:
            total = total - product
        out.append((-0.5 * time_step) * total)
    return out


def pack_kernel(geo, late, part, stored, grads, rate, weight_faces, rate_faces, buffer, pieces):
    v, x, y, z = geo.block
    depth = geo.depth
    late.wait(1)
    lane = lax.broadcasted_iota(jnp.int32, (y, z), 1)
    plane = jnp.where(part[0] == geo.parts - 1, depth - 1, 0)
    high = jnp.zeros((y, z), jnp.float32)
    low = jnp.zeros((y, z), jnp.float32)
    for var in range(v):
        pieces[0, var * y : (var + 1) * y] = stored[var, plane]
        pieces[1, var * depth : (var + 1) * depth] = stored[var, :, y - 1, :]
        pieces[2, var * depth : (var + 1) * depth] = stored[var, :, 0, :]
        for step in range(depth):
            place = var * x + part[0] * depth + step
            tile = stored[var, step]
            here = lane == place
            high = jnp.where(here, pltpu.roll(tile, lax.rem(place + 1, z), 1), high)
            low = jnp.where(here, pltpu.roll(tile, place, 1), low)
    pieces[3, :y] = high
    pieces[4, :y] = low
    cut(geo, geo.part, pieces, buffer, 0)
    late.wait(2)
    late.wait(3)
    rate_faces[0, :y] = rate[x - 1]
    rate_faces[1, :y] = rate[0]
    rate_faces[2, :x] = rate[:, y - 1, :]
    rate_faces[3, :x] = rate[:, 0, :]
    high, low = take_z_faces(geo, lambda var, plane: rate[plane])
    rate_faces[4, :y] = high
    rate_faces[5, :y] = low
    late.leave(1)
    take_weight_faces(geo, grads, rate_faces, weight_faces)
    late.leave(0)
    cut(geo, geo.whole, weight_faces, buffer, geo.part.total)


def take_weight_faces(geo, grads, rate_faces, faces):
    v, x, y, z = geo.block
    take_xy_faces(geo, grads, faces)
    for side in range(4):
        depth = y if side < 2 else x
        for var in range(v):
            here = slice(var * depth, (var + 1) * depth)
            faces[side, here] = faces[side, here] * rate_faces[side, :depth]
    high, low = take_z_faces(geo, lambda var, plane: grads[var, plane])
    faces[4, :y] = high * rate_faces[4, :y]
    faces[5, :y] = low * rate_faces[5, :y]


def route_whole(geo, owner, neighbours, arrived, base, leaving):
    for block in range(geo.n):
        target = owner[block]
        for side in range(6):
            source = owner[neighbours[block * 6 + side]]
            run, start, far = geo.whole.runs[side], geo.whole.starts[side], base + geo.whole.starts[side ^ 1]
            leaving[target, start : start + run] = arrived[source, far : far + run]


def route_kernel(geo, late, owner, neighbours, arrived, leaving):
    route_whole(geo, owner, neighbours, arrived, 0, leaving)


def route_first_kernel(geo, late, part, owner, neighbours, arrived, leaving, weight_leaving):
    route_whole(geo, owner, neighbours, arrived, geo.part.total, weight_leaving)
    x_side = jnp.where(part[0] == geo.parts - 1, 1, 0)
    for block in range(geo.n):
        target = owner[block]
        for index in range(5):
            side, far_index = (x_side, 0) if index == 0 else (index + 1, ((index + 1) ^ 1) - 1)
            source = owner[neighbours[block * 6 + side]]
            run, start, far = geo.part.runs[index], geo.part.starts[index], geo.part.starts[far_index]
            leaving[target, start : start + run] = arrived[source, far : far + run]


def step_inner_kernel(geo, late, mats, block, rate, result, *rest):
    tall = rest[-1]
    late.wait(1)
    late.wait(2)
    fill_tall(geo, block, tall)

    def body(plane, carry):
        cells, low, high = around(geo, tall, plane)
        for var, value in enumerate(step_plane(geo, mats, cells, low, high, rate[plane])):
            result[var, plane] = value
        return carry

    lax.fori_loop(0, geo.x, body, 0)
    if len(rest) == 2:
        faces = rest[0]
        v, x, y, z = geo.block
        for var in range(v):
            faces[0, var * y : (var + 1) * y] = tall[var, x - 1, PAD : PAD + y]
            faces[1, var * y : (var + 1) * y] = tall[var, 0, PAD : PAD + y]
            faces[2, var * x : (var + 1) * x] = tall[var, :, PAD + y - 1, :]
            faces[3, var * x : (var + 1) * x] = tall[var, :, PAD, :]
        high, low = take_z_faces(geo, lambda var, plane: tall[var, plane, PAD : PAD + y])
        faces[4, :y] = high
        faces[5, :y] = low


def adjoint_inner_kernel(geo, late, mats, block, grads, rate, result, tall, weights):
    v, x, y, z = geo.block
    for index in range(1, 4):
        late.wait(index)
    fill_tall(geo, block, tall)

    def scale(plane, carry):
        for var in range(v):
            weights[var, plane, PAD : PAD + y] = rate[plane] * grads[var, plane]
        return carry

    lax.fori_loop(0, x, scale, 0)
    for var in range(v):
        weights[var, :, PAD - 1, :] = weights[var, :, PAD, :]
        weights[var, :, PAD + y, :] = weights[var, :, PAD + y - 1, :]

    def body(plane, carry):
        cells, low, high = around(geo, tall, plane)
        weight, weight_low, weight_high = around(geo, weights, plane)
        here = [grads[var, plane] for var in range(v)]
        values = adjoint_plane(geo, mats, cells, low, high, here, weight, weight_low, weight_high)
        for var, value in enumerate(values):
            result[var, plane] = value
        return carry

    lax.fori_loop(0, x, body, 0)


def step_edge_kernel(geo, first, late, place, owner, orientation, mats, inner, faces, rate_faces, arrived, result, *rest):
    v, x, y, z = geo.block
    if first:
        new_faces, sent, ghosts, raw, piece = rest
        join_parts(geo, arrived, raw, piece)
        turn(geo, own_codes(geo, place, owner, orientation), raw, ghosts)
        late.leave(2)
    else:
        ghosts = arrived
    result[...] = inner[...]
    terms = []
    for side in range(6):
        depth = y if side < 2 or side > 3 else x
        cells, outer = face_values(geo, faces, side), face_values(geo, ghosts, side)
        values = step_face(geo, mats, side, cells, outer, rate_faces[side, :depth])
        if side < 4:
            add_xy_terms(geo, side, values, result)
        else:
            terms.append(values)
    add_z_terms(geo, *terms, result)
    late.leave(0)
    if first:
        take_xy_faces(geo, result, new_faces)
        high, low = take_z_faces(geo, lambda var, plane: result[var, plane])
        new_faces[4, :y] = high
        new_faces[5, :y] = low
        late.leave(1)
        cut(geo, geo.whole, new_faces, sent, 0)


def adjoint_edge_kernel(geo, last, late, place, owner, orientation, mats, inner, faces, weight_faces, *rest):
    v, x, y, z = geo.block
    codes = own_codes(geo, place, owner, orientation)
    if last:
        ghosts, weight_buffer, result, raw, weight_ghosts = rest
        join(geo, weight_buffer, raw)
        turn(geo, codes, raw, weight_ghosts)
    else:
        rate_faces, buffer, weight_buffer, result, new_faces, sent, ghosts, raw, weight_ghosts = rest
        join(geo, buffer, raw)
        turn(geo, codes, raw, ghosts)
        late.leave(2)
        join(geo, weight_buffer, raw)
        turn(geo, codes, raw, weight_ghosts)
    result[...] = inner[...]
    terms = []
    for side in range(6):
        views = [face_values(geo, field, side) for field in (faces, ghosts, weight_faces, weight_ghosts)]
        values = adjoint_face(geo, mats, side, *views)
        if side < 4:
            add_xy_terms(geo, side, values, result)
        else:
            terms.append(values)
    add_z_terms(geo, *terms, result)
    late.leave(0)
    if not last:
        take_weight_faces(geo, result, rate_faces, new_faces)
        late.leave(1)
        cut(geo, geo.whole, new_faces, sent, 0)


class Late:
    def __init__(self, arrivals, departures):
        self.arrivals, self.departures = arrivals, departures

    def wait(self, index):
        if index in self.arrivals:
            self.arrivals[index].wait()

    def leave(self, index):
        if index in self.departures:
            self.departures[index].start()


def call(kernel, ins, outs, scratch, flops):
    late_in = [(index, shape) for index, (kind, shape) in enumerate(ins) if kind == "H"]
    late_out = [(index, shape) for index, (kind, shape) in enumerate(outs) if kind == "H"]
    count_in, count_out = len(late_in), len(late_out)

    def body(*refs):
        given = list(refs[: len(ins)])
        made = list(refs[len(ins) : len(ins) + len(outs)])
        rest = list(refs[len(ins) + len(outs) :])
        own = rest[: len(scratch)]
        stage = rest[len(scratch) : len(scratch) + count_in + count_out]
        sems = rest[-1] if count_in + count_out else None
        arrivals, departures = {}, {}
        for slot, (index, _) in enumerate(late_in):
            copy = pltpu.make_async_copy(given[index], stage[slot], sems.at[slot])
            copy.start()
            arrivals[index] = copy
            given[index] = stage[slot]
        for slot, (index, _) in enumerate(late_out):
            spot = count_in + slot
            departures[index] = pltpu.make_async_copy(stage[spot], made[index], sems.at[spot])
            made[index] = stage[spot]
        kernel(Late(arrivals, departures), *given, *made, *own)
        for copy in departures.values():
            copy.wait()

    hbm = pl.BlockSpec(memory_space=pltpu.HBM)
    specs = {"S": SMEM, "V": VMEM, "R": VMEM, "H": hbm}
    scratch_shapes = [pltpu.VMEM(shape, jnp.float32) for shape in scratch]
    scratch_shapes += [pltpu.VMEM(shape, jnp.float32) for _, shape in late_in + late_out]
    if count_in + count_out:
        scratch_shapes.append(pltpu.SemaphoreType.DMA((count_in + count_out,)))
    shapes = {"V": jax.ShapeDtypeStruct, "R": pltpu.VMEM, "H": pltpu.HBM}
    invoke = pl.pallas_call(
        body,
        in_specs=[specs[kind] for kind, _ in ins],
        out_specs=[specs[kind] for kind, _ in outs],
        out_shape=[shapes[kind](shape, jnp.float32) for kind, shape in outs],
        scratch_shapes=scratch_shapes,
        compiler_params=pltpu.CompilerParams(vmem_limit_bytes=VMEM_LIMIT),
        cost_estimate=pl.CostEstimate(flops=flops, bytes_accessed=3 << 20, transcendentals=0),
    )

    def run(*operands):
        placed = {"H": pltpu.HBM, "R": pltpu.VMEM}
        return invoke(
            *[
                pltpu.with_memory_space_constraint(operand, placed[kind]) if kind in placed else operand
                for operand, (kind, _) in zip(operands, ins)
            ]
        )

    return run


def on_device(count, parts, checkpoint, seeds, cell_rate, flux_mats, owner, neighbours, orientation):
    nvars, cx, cy, cz = seeds.shape[2:]
    geo = Geometry(nvars, cx, cy, cz, count, parts)
    rate = cell_rate[0]
    grads = seeds[0, 0]
    place = lax.axis_index("space").astype(jnp.int32).reshape(1)
    part = lax.axis_index("ckpt").astype(jnp.int32).reshape(1)
    mats = flux_mats.reshape(-1)
    neighbours = neighbours.reshape(-1)
    orientation = orientation.reshape(-1)
    fixed = (place, owner, orientation, mats)
    work = nvars * nvars * 3 * 4 * cx * cy * cz
    few = work // 16
    whole, some = geo.buffer(geo.whole.total), geo.buffer(geo.part.total)

    stored_shape, block, faces_shape = checkpoint.shape[1:], geo.block, geo.faces
    rate_block = cell_rate.shape[1:]
    scalar, near, kept_near = ("S", None), ("V", None), ("R", None)

    def far(shape):
        return ("H", shape)

    def swap(buffer):
        return lax.all_to_all(buffer, "space", 0, 0, tiled=True)

    def route(arrived):
        return call(functools.partial(route_kernel, geo), [scalar, scalar, near], [("V", whole)], [], few)(
            owner, neighbours, arrived
        )[0]

    def adjoint_inner(state, state_kind, grads, grads_kind):
        return call(
            functools.partial(adjoint_inner_kernel, geo),
            [scalar, state_kind, grads_kind, far(rate_block)],
            [("R", block)],
            [geo.tall] * 2,
            2 * work,
        )(mats, state, grads, rate)[0]

    weight_faces, rate_faces, sent = call(
        functools.partial(pack_kernel, geo),
        [scalar, far(stored_shape), far(block), far(rate_block)],
        [("R", faces_shape), ("R", geo.rate_faces), ("V", geo.buffer(geo.part.total + geo.whole.total))],
        [faces_shape],
        few,
    )(part, checkpoint[0], grads, rate)
    kept, sent = lax.optimization_barrier((checkpoint[0], sent))
    arrived = swap(sent)
    state = lax.all_gather(kept, "ckpt", axis=0)
    arrived, state = lax.optimization_barrier((arrived, state))
    leaving, weight_leaving = call(
        functools.partial(route_first_kernel, geo), [scalar] * 3 + [near], [("V", some), ("V", whole)], [], few
    )(part, owner, neighbours, arrived)
    part_ghosts = swap(leaving)
    inner, faces = call(
        functools.partial(step_inner_kernel, geo),
        [scalar, far(state.shape), far(rate_block)],
        [("R", block), ("R", faces_shape)],
        [geo.tall],
        work,
    )(mats, state, rate)
    part_ghosts, inner, faces = lax.optimization_barrier((part_ghosts, inner, faces))
    weight_ghosts = swap(weight_leaving)
    gathered = lax.all_gather(part_ghosts, "ckpt", axis=0)
    next_state, next_faces, sent, ghosts = call(
        functools.partial(step_edge_kernel, geo, True),
        [scalar] * 4 + [kept_near] * 3 + [near],
        [("R", block), ("R", faces_shape), ("V", whole), ("R", faces_shape)],
        [faces_shape, faces_shape[1:]],
        few,
    )(*fixed, inner, faces, rate_faces, gathered)

    sent, weight_ghosts = lax.optimization_barrier((sent, weight_ghosts))
    arrived = swap(sent)
    inner = adjoint_inner(next_state, kept_near, grads, far(block))
    arrived, inner = lax.optimization_barrier((arrived, inner))
    leaving = route(arrived)
    later_state, leaving = lax.optimization_barrier((next_state, leaving))
    next_ghosts = swap(leaving)
    (final_inner,) = call(
        functools.partial(step_inner_kernel, geo),
        [scalar, kept_near, far(rate_block)],
        [("R", block)],
        [geo.tall],
        work,
    )(mats, later_state, rate)
    next_ghosts, final_inner = lax.optimization_barrier((next_ghosts, final_inner))
    grads_now, next_weight_faces, sent, turned = call(
        functools.partial(adjoint_edge_kernel, geo, False),
        [scalar] * 4 + [kept_near] * 4 + [near, near],
        [("R", block), ("R", faces_shape), ("V", whole), ("R", faces_shape)],
        [faces_shape] * 2,
        few,
    )(*fixed, inner, next_faces, weight_faces, rate_faces, next_ghosts, weight_ghosts)

    arrived = swap(sent)
    inner = adjoint_inner(state, far(state.shape), grads_now, kept_near)
    arrived, inner = lax.optimization_barrier((arrived, inner))
    leaving = route(arrived)
    final_inner, leaving = lax.optimization_barrier((final_inner, leaving))
    last_ghosts = swap(leaving)
    (final,) = call(
        functools.partial(step_edge_kernel, geo, False),
        [scalar] * 4 + [kept_near] * 4,
        [("V", block)],
        [],
        work,
    )(*fixed, final_inner, next_faces, rate_faces, turned)
    last_ghosts, final = lax.optimization_barrier((last_ghosts, final))
    (adjoint,) = call(
        functools.partial(adjoint_edge_kernel, geo, True),
        [scalar] * 4 + [kept_near] * 4 + [near],
        [("V", block)],
        [faces_shape] * 2,
        few,
    )(*fixed, inner, faces, next_weight_faces, ghosts, last_ghosts)
    return (adjoint[None, None], final[None])


def solution(mesh):
    return jax.shard_map(
        functools.partial(on_device, mesh.shape["space"], mesh.shape["ckpt"]),
        mesh=mesh,
        in_specs=(
            P("space", None, "ckpt", None, None),
            P("ckpt", "space", None, None, None, None),
            P("space", None, None, None),
            P(),
            P(),
            P(),
            P(),
        ),
        out_specs=(P("ckpt", "space", None, None, None, None), P("space", None, None, None, None)),
        check_vma=False,
    )
```

```python
import functools

import jax
import jax.numpy as jnp
from jax import lax
from jax.experimental import pallas as pl
from jax.experimental.pallas import tpu as pltpu
from jax.sharding import PartitionSpec as P

STEPS = 2
time_step = 0.05
damping = 0.015

PAD = 8
VMEM = pl.BlockSpec(memory_space=pltpu.VMEM)
SMEM = pl.BlockSpec(memory_space=pltpu.SMEM)
VMEM_LIMIT = 16 * 1024 * 1024


class Pieces:
    def __init__(self, rows, count):
        self.rows = rows
        self.runs = [-(-length // count) for length in rows]
        self.starts = [sum(self.runs[:index]) for index in range(len(rows))]
        self.total = sum(self.runs)


class Geometry:
    def __init__(self, nvars, cx, cy, cz, count, parts):
        self.v, self.x, self.y, self.z, self.n, self.parts = nvars, cx, cy, cz, count, parts
        self.depth = cx // parts
        self.rows = [nvars * cy] * 2 + [nvars * cx] * 2 + [cy] * 2
        self.whole = Pieces(self.rows, count)
        self.part = Pieces([nvars * cy] + [nvars * self.depth] * 2 + [cy] * 2, count)
        self.face_rows = -(-max(run * count for run in self.whole.runs) // 8) * 8
        self.block = (nvars, cx, cy, cz)
        self.tall = (nvars, cx, cy + 2 * PAD, cz)
        self.faces = (6, self.face_rows, cz)
        self.rate_faces = (6, max(cx, cy), cz)

    def buffer(self, rows):
        return (self.n, -(-rows // 8) * 8, self.z)


def take_z_faces(geo, load):
    v, x, y, z = geo.block
    lane = lax.broadcasted_iota(jnp.int32, (y, z), 1)
    high = jnp.zeros((y, z), jnp.float32)
    low = jnp.zeros((y, z), jnp.float32)
    for var in range(v):
        for plane in range(x):
            place = var * x + plane
            tile = load(var, plane)
            here = lane == place
            high = jnp.where(here, pltpu.roll(tile, (place + 1) % z, 1), high)
            low = jnp.where(here, pltpu.roll(tile, place, 1) if place else tile, low)
    return high, low


def take_xy_faces(geo, source, faces):
    v, x, y, z = geo.block
    faces[0, : v * y] = source[:, x - 1].reshape(v * y, z)
    faces[1, : v * y] = source[:, 0].reshape(v * y, z)
    for var in range(v):
        faces[2, var * x : (var + 1) * x] = source[var, :, y - 1, :]
        faces[3, var * x : (var + 1) * x] = source[var, :, 0, :]


def cut(geo, pieces, faces, buffer, base):
    for index, (run, start) in enumerate(zip(pieces.runs, pieces.starts)):
        for slot in range(geo.n):
            buffer[slot, base + start : base + start + run] = faces[index, slot * run : (slot + 1) * run]


def own_codes(geo, place, owner, orientation):
    block = jnp.int32(0)
    for index in range(geo.n):
        block = jnp.where(owner[index] == place[0], index, block)
    return [orientation[block * 6 + side] for side in range(6)]


def flip_rows(values, flag, length):
    rows, z = values.shape
    grouped = values.reshape(rows // length, length // 8, 8, z)
    index = lax.broadcasted_iota(jnp.int32, (8, z), 0)
    index = jnp.where(flag == 1, 7 - index, index)
    tiles = length // 8
    out = []
    for group in range(rows // length):
        for tile in range(tiles):
            picked = jnp.where(flag == 1, grouped[group, tiles - 1 - tile], grouped[group, tile])
            out.append(jnp.take_along_axis(picked, index, axis=0))
    return jnp.stack(out).reshape(rows, z)


def flip_lanes(values, flag, length):
    rows, z = values.shape
    lane = lax.broadcasted_iota(jnp.int32, (8, z), 1)
    within = lax.rem(lane, length)
    index = jnp.where(flag == 1, lane + (length - 1) - 2 * within, lane)
    index = jnp.minimum(index, z - 1)
    tiles = values.reshape(rows // 8, 8, z)
    return jnp.stack(
        [jnp.take_along_axis(tiles[tile], index, axis=1) for tile in range(rows // 8)]
    ).reshape(rows, z)


def join(geo, buffer, raw, base=0):
    for side in range(6):
        run, start = geo.whole.runs[side], base + geo.whole.starts[side]
        for slot in range(geo.n):
            raw[side, slot * run : (slot + 1) * run] = buffer[slot, start : start + run]


def join_parts(geo, buffer, raw, piece):
    for side in range(6):
        index = 0 if side < 2 else side - 1
        run, start = geo.part.runs[index], geo.part.starts[index]
        if side < 2:
            part = 0 if side == 0 else geo.parts - 1
            for slot in range(geo.n):
                raw[side, slot * run : (slot + 1) * run] = buffer[part, slot, start : start + run]
        elif side < 4:
            for part in range(geo.parts):
                for slot in range(geo.n):
                    piece[slot * run : (slot + 1) * run] = buffer[part, slot, start : start + run]
                for var in range(geo.v):
                    row = var * geo.x + part * geo.depth
                    raw[side, row : row + geo.depth] = piece[var * geo.depth : (var + 1) * geo.depth]
        else:
            for slot in range(geo.n):
                total = buffer[0, slot, start : start + run]
                for part in range(1, geo.parts):
                    total = total + buffer[part, slot, start : start + run]
                raw[side, slot * run : (slot + 1) * run] = total


def turn(geo, codes, raw, ghosts):
    v, x, y, z = geo.block
    for side in range(6):
        first, second = codes[side] & 1, (codes[side] >> 1) & 1
        layer = raw[side, : geo.rows[side]]
        if side < 4:
            layer = flip_lanes(flip_rows(layer, first, y if side < 2 else x), second, z)
        else:
            layer = flip_lanes(flip_rows(layer, second, y), first, x)
        ghosts[side, : geo.rows[side]] = layer


def face_values(geo, faces, side):
    v, x, y, z = geo.block
    if side < 4:
        depth = y if side < 2 else x
        return [faces[side, var * depth : (var + 1) * depth] for var in range(v)]
    layer = faces[side, :y]
    return [layer] + [pltpu.roll(layer, z - var * x, 1) for var in range(1, v)]


def add_xy_terms(geo, side, terms, result):
    v, x, y, z = geo.block
    for var in range(v):
        if side < 2:
            plane = x - 1 if side == 0 else 0
            result[var, plane] = result[var, plane] + terms[var]
        else:
            row = y - 1 if side == 2 else 0
            result[var, :, row, :] = result[var, :, row, :] + terms[var]


def add_z_terms(geo, high_terms, low_terms, result):
    v, x, y, z = geo.block
    lane = lax.broadcasted_iota(jnp.int32, (y, z), 1)
    zero = jnp.zeros((y, z), jnp.float32)
    for var in range(v):
        for plane in range(x):
            high = pltpu.roll(high_terms[var], z - 1 - plane, 1)
            low = pltpu.roll(low_terms[var], z - plane, 1) if plane else low_terms[var]
            change = jnp.where(lane == z - 1, high, jnp.where(lane == 0, low, zero))
            result[var, plane] = result[var, plane] + change


def fill_tall(geo, source, tall):
    v, x, y, z = geo.block
    if len(source.shape) == 5:
        depth = geo.depth
        for part in range(geo.parts):
            tall[:, part * depth : (part + 1) * depth, PAD : PAD + y, :] = source[part]
    else:
        tall[:, :, PAD : PAD + y, :] = source[...]
    for var in range(v):
        tall[var, :, PAD - 1, :] = tall[var, :, PAD, :]
        tall[var, :, PAD + y, :] = tall[var, :, PAD + y - 1, :]


def around(geo, tall, plane):
    v, x, y, z = geo.block
    lane = lax.broadcasted_iota(jnp.int32, (y, z), 1)
    before, after = jnp.maximum(plane - 1, 0), jnp.minimum(plane + 1, x - 1)
    cells, low, high = [], [[], [], []], [[], [], []]
    for var in range(v):
        mid = tall[var, plane, PAD : PAD + y]
        cells.append(mid)
        low[0].append(tall[var, before, PAD : PAD + y])
        high[0].append(tall[var, after, PAD : PAD + y])
        low[1].append(tall[var, plane, PAD - 1 : PAD - 1 + y])
        high[1].append(tall[var, plane, PAD + 1 : PAD + 1 + y])
        low[2].append(jnp.where(lane == 0, mid, pltpu.roll(mid, 1, 1)))
        high[2].append(jnp.where(lane == z - 1, mid, pltpu.roll(mid, z - 1, 1)))
    return cells, low, high


def flux_entry(geo, mats, direction, row, column):
    return mats[(direction * geo.v + row) * geo.v + column]


def step_plane(geo, mats, cells, low, high, rate):
    v = geo.v
    total = [None] * v
    for direction in range(3):
        lows, highs = low[direction], high[direction]
        mean_low = 0.5 * (lows[0] + cells[0])
        mean_high = 0.5 * (cells[0] + highs[0])
        square_low = 1.0 + mean_low * mean_low
        square_high = 1.0 + mean_high * mean_high
        spread_low = square_low * lax.rsqrt(square_low)
        spread_high = square_high * lax.rsqrt(square_high)
        slopes = [highs[var] - lows[var] for var in range(v)]
        for var in range(v):
            term = spread_low * (cells[var] - lows[var]) - spread_high * (highs[var] - cells[var])
            for column in range(v):
                term = term + flux_entry(geo, mats, direction, var, column) * slopes[column]
            total[var] = term if total[var] is None else total[var] + term
    scale = (0.5 * time_step) * rate
    return [cells[var] - scale * total[var] - damping * jnp.tanh(cells[var]) for var in range(v)]


def adjoint_plane(geo, mats, cells, low, high, grads, weight, weight_low, weight_high):
    v = geo.v
    total = [None] * v
    extra = None
    for direction in range(3):
        spreads, steps = [], []
        for lower, upper, lower_weight, upper_weight in (
            (low[direction], cells, weight_low[direction], weight),
            (cells, high[direction], weight, weight_high[direction]),
        ):
            mean = 0.5 * (lower[0] + upper[0])
            square = 1.0 + mean * mean
            inverse = lax.rsqrt(square)
            jump = [lower_weight[var] - upper_weight[var] for var in range(v)]
            product = jump[0] * (upper[0] - lower[0])
            for var in range(1, v):
                product = product + jump[var] * (upper[var] - lower[var])
            product = product * (mean * inverse)
            extra = product if extra is None else extra + product
            spreads.append(square * inverse)
            steps.append(jump)
        slopes = [steps[0][var] + steps[1][var] for var in range(v)]
        for var in range(v):
            term = spreads[1] * steps[1][var] - spreads[0] * steps[0][var]
            for row in range(v):
                term = term + flux_entry(geo, mats, direction, row, var) * slopes[row]
            total[var] = term if total[var] is None else total[var] + term
    total[0] = total[0] - 0.5 * extra
    out = []
    for var in range(v):
        bend = jnp.tanh(cells[var])
        slope = (1.0 - damping) + damping * (bend * bend)
        out.append(grads[var] * slope - (0.5 * time_step) * total[var])
    return out


def step_face(geo, mats, side, cells, ghosts, rate):
    v = geo.v
    mean = 0.5 * (cells[0] + ghosts[0])
    square = 1.0 + mean * mean
    spread = square * lax.rsqrt(square)
    gap = [ghosts[var] - cells[var] for var in range(v)]
    scale = (0.5 * time_step) * rate
    out = []
    for var in range(v):
        total = flux_entry(geo, mats, side // 2, var, 0) * gap[0]
        for column in range(1, v):
            total = total + flux_entry(geo, mats, side // 2, var, column) * gap[column]
        if side % 2 == 0:
            out.append(scale * (spread * gap[var] - total))
        else:
            out.append(scale * (spread * gap[var] + total))
    return out


def adjoint_face(geo, mats, side, cells, ghosts, weight, ghost_weight):
    v = geo.v
    mean = 0.5 * (cells[0] + ghosts[0])
    square = 1.0 + mean * mean
    inverse = lax.rsqrt(square)
    spread = square * inverse
    jump = [weight[var] - ghost_weight[var] for var in range(v)]
    product = jump[0] * (ghosts[0] - cells[0])
    for var in range(1, v):
        product = product + jump[var] * (ghosts[var] - cells[var])
    product = (0.5 * product) * (mean * inverse)
    out = []
    for var in range(v):
        total = flux_entry(geo, mats, side // 2, 0, var) * jump[0]
        for row in range(1, v):
            total = total + flux_entry(geo, mats, side // 2, row, var) * jump[row]
        if side % 2 == 0:
            total = spread * jump[var] + total
        else:
            total = spread * jump[var] - total
        if var == 0:
            total = total - product
        out.append((-0.5 * time_step) * total)
    return out


def pack_kernel(geo, late, part, stored, grads, rate, weight_faces, rate_faces, buffer, pieces):
    v, x, y, z = geo.block
    depth = geo.depth
    late.wait(1)
    lane = lax.broadcasted_iota(jnp.int32, (y, z), 1)
    plane = jnp.where(part[0] == geo.parts - 1, depth - 1, 0)
    high = jnp.zeros((y, z), jnp.float32)
    low = jnp.zeros((y, z), jnp.float32)
    for var in range(v):
        pieces[0, var * y : (var + 1) * y] = stored[var, plane]
        pieces[1, var * depth : (var + 1) * depth] = stored[var, :, y - 1, :]
        pieces[2, var * depth : (var + 1) * depth] = stored[var, :, 0, :]
        for step in range(depth):
            place = var * x + part[0] * depth + step
            tile = stored[var, step]
            here = lane == place
            high = jnp.where(here, pltpu.roll(tile, lax.rem(place + 1, z), 1), high)
            low = jnp.where(here, pltpu.roll(tile, place, 1), low)
    pieces[3, :y] = high
    pieces[4, :y] = low
    cut(geo, geo.part, pieces, buffer, 0)
    late.wait(2)
    late.wait(3)
    rate_faces[0, :y] = rate[x - 1]
    rate_faces[1, :y] = rate[0]
    rate_faces[2, :x] = rate[:, y - 1, :]
    rate_faces[3, :x] = rate[:, 0, :]
    high, low = take_z_faces(geo, lambda var, plane: rate[plane])
    rate_faces[4, :y] = high
    rate_faces[5, :y] = low
    late.leave(1)
    take_weight_faces(geo, grads, rate_faces, weight_faces)
    late.leave(0)
    cut(geo, geo.whole, weight_faces, buffer, geo.part.total)
    late.leave(2)


def take_weight_faces(geo, grads, rate_faces, faces):
    v, x, y, z = geo.block
    take_xy_faces(geo, grads, faces)
    for side in range(4):
        depth = y if side < 2 else x
        for var in range(v):
            here = slice(var * depth, (var + 1) * depth)
            faces[side, here] = faces[side, here] * rate_faces[side, :depth]
    high, low = take_z_faces(geo, lambda var, plane: grads[var, plane])
    faces[4, :y] = high * rate_faces[4, :y]
    faces[5, :y] = low * rate_faces[5, :y]


def route_whole(geo, owner, neighbours, arrived, leaving, base):
    for block in range(geo.n):
        target = owner[block]
        for side in range(6):
            source = owner[neighbours[block * 6 + side]]
            run, start, far = geo.whole.runs[side], base + geo.whole.starts[side], base + geo.whole.starts[side ^ 1]
            leaving[target, start : start + run] = arrived[source, far : far + run]


def route_kernel(geo, late, owner, neighbours, arrived, leaving):
    route_whole(geo, owner, neighbours, arrived, leaving, 0)
    late.leave(0)


def route_first_kernel(geo, late, part, owner, neighbours, arrived, leaving):
    route_whole(geo, owner, neighbours, arrived, leaving, geo.part.total)
    x_side = jnp.where(part[0] == geo.parts - 1, 1, 0)
    for block in range(geo.n):
        target = owner[block]
        for index in range(5):
            side, far_index = (x_side, 0) if index == 0 else (index + 1, ((index + 1) ^ 1) - 1)
            source = owner[neighbours[block * 6 + side]]
            run, start, far = geo.part.runs[index], geo.part.starts[index], geo.part.starts[far_index]
            leaving[target, start : start + run] = arrived[source, far : far + run]
    late.leave(0)


def step_inner_kernel(geo, late, mats, block, rate, result, *rest):
    tall = rest[-1]
    late.wait(1)
    late.wait(2)
    fill_tall(geo, block, tall)

    def body(plane, carry):
        cells, low, high = around(geo, tall, plane)
        for var, value in enumerate(step_plane(geo, mats, cells, low, high, rate[plane])):
            result[var, plane] = value
        return carry

    lax.fori_loop(0, geo.x, body, 0)
    late.leave(0)
    if len(rest) == 2:
        faces = rest[0]
        v, x, y, z = geo.block
        for var in range(v):
            faces[0, var * y : (var + 1) * y] = tall[var, x - 1, PAD : PAD + y]
            faces[1, var * y : (var + 1) * y] = tall[var, 0, PAD : PAD + y]
            faces[2, var * x : (var + 1) * x] = tall[var, :, PAD + y - 1, :]
            faces[3, var * x : (var + 1) * x] = tall[var, :, PAD, :]
        high, low = take_z_faces(geo, lambda var, plane: tall[var, plane, PAD : PAD + y])
        faces[4, :y] = high
        faces[5, :y] = low
        late.leave(1)


def adjoint_inner_kernel(geo, late, mats, block, grads, rate, result, tall, weights):
    v, x, y, z = geo.block
    for index in range(1, 4):
        late.wait(index)
    fill_tall(geo, block, tall)

    def scale(plane, carry):
        for var in range(v):
            weights[var, plane, PAD : PAD + y] = rate[plane] * grads[var, plane]
        return carry

    lax.fori_loop(0, x, scale, 0)
    for var in range(v):
        weights[var, :, PAD - 1, :] = weights[var, :, PAD, :]
        weights[var, :, PAD + y, :] = weights[var, :, PAD + y - 1, :]

    def body(plane, carry):
        cells, low, high = around(geo, tall, plane)
        weight, weight_low, weight_high = around(geo, weights, plane)
        here = [grads[var, plane] for var in range(v)]
        values = adjoint_plane(geo, mats, cells, low, high, here, weight, weight_low, weight_high)
        for var, value in enumerate(values):
            result[var, plane] = value
        return carry

    lax.fori_loop(0, x, body, 0)


def step_edge_kernel(geo, first, late, place, owner, orientation, mats, inner, faces, rate_faces, arrived, result, *rest):
    v, x, y, z = geo.block
    if first:
        new_faces, sent, ghosts, raw, piece = rest
        join_parts(geo, arrived, raw, piece)
        turn(geo, own_codes(geo, place, owner, orientation), raw, ghosts)
        late.leave(3)
    else:
        ghosts = arrived
        late.wait(4)
        late.wait(7)
    late.wait(5)
    result[...] = inner[...]
    terms = []
    for side in range(6):
        depth = y if side < 2 or side > 3 else x
        cells, outer = face_values(geo, faces, side), face_values(geo, ghosts, side)
        values = step_face(geo, mats, side, cells, outer, rate_faces[side, :depth])
        if side < 4:
            add_xy_terms(geo, side, values, result)
        else:
            terms.append(values)
    add_z_terms(geo, *terms, result)
    late.leave(0)
    if first:
        take_xy_faces(geo, result, new_faces)
        high, low = take_z_faces(geo, lambda var, plane: result[var, plane])
        new_faces[4, :y] = high
        new_faces[5, :y] = low
        late.leave(1)
        cut(geo, geo.whole, new_faces, sent, 0)
        late.leave(2)


def adjoint_edge_kernel(geo, last, late, place, owner, orientation, mats, inner, faces, weight_faces, *rest):
    v, x, y, z = geo.block
    codes = own_codes(geo, place, owner, orientation)
    if last:
        ghosts, weight_buffer, result, raw, weight_ghosts = rest
        join(geo, weight_buffer, raw)
        turn(geo, codes, raw, weight_ghosts)
    else:
        rate_faces, buffer, weight_buffer, result, new_faces, sent, ghosts, raw, weight_ghosts = rest
        join(geo, buffer, raw)
        turn(geo, codes, raw, ghosts)
        late.leave(3)
        join(geo, weight_buffer, raw, geo.part.total)
        turn(geo, codes, raw, weight_ghosts)
    for index in range(5, 8):
        late.wait(index)
    result[...] = inner[...]
    terms = []
    for side in range(6):
        views = [face_values(geo, field, side) for field in (faces, ghosts, weight_faces, weight_ghosts)]
        values = adjoint_face(geo, mats, side, *views)
        if side < 4:
            add_xy_terms(geo, side, values, result)
        else:
            terms.append(values)
    add_z_terms(geo, *terms, result)
    late.leave(0)
    if not last:
        take_weight_faces(geo, result, rate_faces, new_faces)
        late.leave(1)
        cut(geo, geo.whole, new_faces, sent, 0)
        late.leave(2)


class Late:
    def __init__(self, arrivals, departures):
        self.arrivals, self.departures = arrivals, departures

    def wait(self, index):
        if index in self.arrivals:
            self.arrivals[index].wait()

    def leave(self, index):
        if index in self.departures:
            self.departures[index].start()


def call(kernel, ins, outs, scratch, flops):
    late_in = [(index, shape) for index, (kind, shape) in enumerate(ins) if kind == "H"]
    late_out = [(index, shape) for index, (kind, shape) in enumerate(outs) if kind == "H"]
    count_in, count_out = len(late_in), len(late_out)

    def body(*refs):
        given = list(refs[: len(ins)])
        made = list(refs[len(ins) : len(ins) + len(outs)])
        rest = list(refs[len(ins) + len(outs) :])
        own = rest[: len(scratch)]
        stage = rest[len(scratch) : len(scratch) + count_in + count_out]
        sems = rest[-1] if count_in + count_out else None
        arrivals, departures = {}, {}
        for slot, (index, _) in enumerate(late_in):
            copy = pltpu.make_async_copy(given[index], stage[slot], sems.at[slot])
            copy.start()
            arrivals[index] = copy
            given[index] = stage[slot]
        for slot, (index, _) in enumerate(late_out):
            spot = count_in + slot
            departures[index] = pltpu.make_async_copy(stage[spot], made[index], sems.at[spot])
            made[index] = stage[spot]
        kernel(Late(arrivals, departures), *given, *made, *own)
        for copy in departures.values():
            copy.wait()

    hbm = pl.BlockSpec(memory_space=pltpu.HBM)
    specs = {"S": SMEM, "V": VMEM, "R": VMEM, "H": hbm}
    scratch_shapes = [pltpu.VMEM(shape, jnp.float32) for shape in scratch]
    scratch_shapes += [pltpu.VMEM(shape, jnp.float32) for _, shape in late_in + late_out]
    if count_in + count_out:
        scratch_shapes.append(pltpu.SemaphoreType.DMA((count_in + count_out,)))
    shapes = {"V": jax.ShapeDtypeStruct, "R": pltpu.VMEM, "H": pltpu.HBM}
    invoke = pl.pallas_call(
        body,
        in_specs=[specs[kind] for kind, _ in ins],
        out_specs=[specs[kind] for kind, _ in outs],
        out_shape=[shapes[kind](shape, jnp.float32) for kind, shape in outs],
        scratch_shapes=scratch_shapes,
        compiler_params=pltpu.CompilerParams(vmem_limit_bytes=VMEM_LIMIT),
        cost_estimate=pl.CostEstimate(flops=flops, bytes_accessed=3 << 20, transcendentals=0),
    )

    def run(*operands):
        placed = {"H": pltpu.HBM, "R": pltpu.VMEM}
        return invoke(
            *[
                pltpu.with_memory_space_constraint(operand, placed[kind]) if kind in placed else operand
                for operand, (kind, _) in zip(operands, ins)
            ]
        )

    return run


def on_device(count, parts, checkpoint, seeds, cell_rate, flux_mats, owner, neighbours, orientation):
    nvars, cx, cy, cz = seeds.shape[2:]
    geo = Geometry(nvars, cx, cy, cz, count, parts)
    rate = cell_rate[0]
    grads = seeds[0, 0]
    place = lax.axis_index("space").astype(jnp.int32).reshape(1)
    part = lax.axis_index("ckpt").astype(jnp.int32).reshape(1)
    mats = flux_mats.reshape(-1)
    neighbours = neighbours.reshape(-1)
    orientation = orientation.reshape(-1)
    fixed = (place, owner, orientation, mats)
    work = nvars * nvars * 3 * 4 * cx * cy * cz
    few = work // 16
    whole, both = geo.buffer(geo.whole.total), geo.buffer(geo.part.total + geo.whole.total)
    some = -(-geo.part.total // 8) * 8

    stored_shape, block, faces_shape = checkpoint.shape[1:], geo.block, geo.faces
    rate_block = cell_rate.shape[1:]
    scalar, near, kept_near = ("S", None), ("V", None), ("R", None)

    def far(shape):
        return ("H", shape)

    def swap(buffer):
        return lax.all_to_all(buffer, "space", 0, 0, tiled=True)

    def route(arrived):
        return call(functools.partial(route_kernel, geo), [scalar, scalar, near], [far(whole)], [], few)(
            owner, neighbours, arrived
        )[0]

    def adjoint_inner(state, state_kind, grads, grads_kind):
        return call(
            functools.partial(adjoint_inner_kernel, geo),
            [scalar, state_kind, grads_kind, far(rate_block)],
            [("R", block)],
            [geo.tall] * 2,
            2 * work,
        )(mats, state, grads, rate)[0]

    weight_faces, rate_faces, sent = call(
        functools.partial(pack_kernel, geo),
        [scalar, far(stored_shape), far(block), far(rate_block)],
        [far(faces_shape), ("R", geo.rate_faces), far(both)],
        [faces_shape],
        few,
    )(part, checkpoint[0], grads, rate)
    kept, sent = lax.optimization_barrier((checkpoint[0], sent))
    arrived = swap(sent)
    state = lax.all_gather(kept, "ckpt", axis=0)
    arrived, state = lax.optimization_barrier((arrived, state))
    (leaving,) = call(functools.partial(route_first_kernel, geo), [scalar] * 3 + [near], [far(both)], [], few)(
        part, owner, neighbours, arrived
    )
    first_ghosts = swap(leaving)
    inner, faces = call(
        functools.partial(step_inner_kernel, geo),
        [scalar, far(state.shape), far(rate_block)],
        [("R", block), far(faces_shape)],
        [geo.tall],
        work,
    )(mats, state, rate)
    first_ghosts, inner, faces = lax.optimization_barrier((first_ghosts, inner, faces))
    gathered = lax.all_gather(first_ghosts[:, :some], "ckpt", axis=0)
    next_state, next_faces, sent, ghosts = call(
        functools.partial(step_edge_kernel, geo, True),
        [scalar] * 4 + [kept_near, far(faces_shape), kept_near, near],
        [far(block), far(faces_shape), far(whole), far(faces_shape)],
        [faces_shape, faces_shape[1:]],
        few,
    )(*fixed, inner, faces, rate_faces, gathered)

    arrived = swap(sent)
    inner = adjoint_inner(next_state, far(block), grads, far(block))
    arrived, inner = lax.optimization_barrier((arrived, inner))
    leaving = route(arrived)
    later_state, leaving = lax.optimization_barrier((next_state, leaving))
    next_ghosts = swap(leaving)
    (final_inner,) = call(
        functools.partial(step_inner_kernel, geo),
        [scalar, far(block), far(rate_block)],
        [far(block)],
        [geo.tall],
        work,
    )(mats, later_state, rate)
    next_ghosts, final_inner = lax.optimization_barrier((next_ghosts, final_inner))
    grads_now, next_weight_faces, sent, turned = call(
        functools.partial(adjoint_edge_kernel, geo, False),
        [scalar] * 4 + [kept_near, far(faces_shape), far(faces_shape), kept_near, near, near],
        [far(block), far(faces_shape), far(whole), far(faces_shape)],
        [faces_shape] * 2,
        few,
    )(*fixed, inner, next_faces, weight_faces, rate_faces, next_ghosts, first_ghosts)

    arrived = swap(sent)
    inner = adjoint_inner(state, far(state.shape), grads_now, far(block))
    arrived, inner = lax.optimization_barrier((arrived, inner))
    leaving = route(arrived)
    final_inner, leaving = lax.optimization_barrier((final_inner, leaving))
    last_ghosts = swap(leaving)
    (final,) = call(
        functools.partial(step_edge_kernel, geo, False),
        [scalar] * 4 + [far(block), far(faces_shape), kept_near, far(faces_shape)],
        [("V", block)],
        [],
        work,
    )(*fixed, final_inner, next_faces, rate_faces, turned)
    last_ghosts, final = lax.optimization_barrier((last_ghosts, final))
    (adjoint,) = call(
        functools.partial(adjoint_edge_kernel, geo, True),
        [scalar] * 4 + [kept_near] + [far(faces_shape)] * 3 + [near],
        [("V", block)],
        [faces_shape] * 2,
        few,
    )(*fixed, inner, faces, next_weight_faces, ghosts, last_ghosts)
    return (adjoint[None, None], final[None])


def solution(mesh):
    return jax.shard_map(
        functools.partial(on_device, mesh.shape["space"], mesh.shape["ckpt"]),
        mesh=mesh,
        in_specs=(
            P("space", None, "ckpt", None, None),
            P("ckpt", "space", None, None, None, None),
            P("space", None, None, None),
            P(),
            P(),
            P(),
            P(),
        ),
        out_specs=(P("ckpt", "space", None, None, None, None), P("space", None, None, None, None)),
        check_vma=False,
    )
```

```python
import functools

import jax
import jax.numpy as jnp
from jax import lax
from jax.experimental import pallas as pl
from jax.experimental.pallas import tpu as pltpu
from jax.sharding import PartitionSpec as P

STEPS = 2
time_step = 0.05
damping = 0.015

PAD = 8
VMEM = pl.BlockSpec(memory_space=pltpu.VMEM)
SMEM = pl.BlockSpec(memory_space=pltpu.SMEM)
VMEM_LIMIT = 16 * 1024 * 1024


class Pieces:
    def __init__(self, rows, count):
        self.rows = rows
        self.runs = [-(-length // count) for length in rows]
        self.starts = [sum(self.runs[:index]) for index in range(len(rows))]
        self.total = sum(self.runs)


class Geometry:
    def __init__(self, nvars, cx, cy, cz, count, parts):
        self.v, self.x, self.y, self.z, self.n, self.parts = nvars, cx, cy, cz, count, parts
        self.depth = cx // parts
        self.rows = [nvars * cy] * 2 + [nvars * cx] * 2 + [cy] * 2
        self.whole = Pieces(self.rows, count)
        self.part = Pieces([nvars * cy] + [nvars * self.depth] * 2 + [cy] * 2, count)
        self.face_rows = -(-max(run * count for run in self.whole.runs) // 8) * 8
        self.block = (nvars, cx, cy, cz)
        self.tall = (nvars, cx, cy + 2 * PAD, cz)
        self.faces = (6, self.face_rows, cz)
        self.rate_faces = (6, max(cx, cy), cz)

    def buffer(self, rows):
        return (self.n, -(-rows // 8) * 8, self.z)


def take_z_faces(geo, load):
    v, x, y, z = geo.block
    lane = lax.broadcasted_iota(jnp.int32, (y, z), 1)
    high = jnp.zeros((y, z), jnp.float32)
    low = jnp.zeros((y, z), jnp.float32)
    for var in range(v):
        for plane in range(x):
            place = var * x + plane
            tile = load(var, plane)
            here = lane == place
            high = jnp.where(here, pltpu.roll(tile, (place + 1) % z, 1), high)
            low = jnp.where(here, pltpu.roll(tile, place, 1) if place else tile, low)
    return high, low


def take_xy_faces(geo, source, faces):
    v, x, y, z = geo.block
    faces[0, : v * y] = source[:, x - 1].reshape(v * y, z)
    faces[1, : v * y] = source[:, 0].reshape(v * y, z)
    for var in range(v):
        faces[2, var * x : (var + 1) * x] = source[var, :, y - 1, :]
        faces[3, var * x : (var + 1) * x] = source[var, :, 0, :]


def cut(geo, pieces, faces, buffer, base, leave=None):
    for slot in range(geo.n):
        for index, (run, start) in enumerate(zip(pieces.runs, pieces.starts)):
            buffer[slot, base + start : base + start + run] = faces[index, slot * run : (slot + 1) * run]
        if leave:
            leave(slot)


def own_codes(geo, place, owner, orientation):
    block = jnp.int32(0)
    for index in range(geo.n):
        block = jnp.where(owner[index] == place[0], index, block)
    return [orientation[block * 6 + side] for side in range(6)]


def flip_rows(values, flag, length):
    rows, z = values.shape
    grouped = values.reshape(rows // length, length // 8, 8, z)
    index = lax.broadcasted_iota(jnp.int32, (8, z), 0)
    index = jnp.where(flag == 1, 7 - index, index)
    tiles = length // 8
    out = []
    for group in range(rows // length):
        for tile in range(tiles):
            picked = jnp.where(flag == 1, grouped[group, tiles - 1 - tile], grouped[group, tile])
            out.append(jnp.take_along_axis(picked, index, axis=0))
    return jnp.stack(out).reshape(rows, z)


def flip_lanes(values, flag, length):
    rows, z = values.shape
    lane = lax.broadcasted_iota(jnp.int32, (8, z), 1)
    within = lax.rem(lane, length)
    index = jnp.where(flag == 1, lane + (length - 1) - 2 * within, lane)
    index = jnp.minimum(index, z - 1)
    tiles = values.reshape(rows // 8, 8, z)
    return jnp.stack(
        [jnp.take_along_axis(tiles[tile], index, axis=1) for tile in range(rows // 8)]
    ).reshape(rows, z)


def join(geo, buffer, raw, base=0):
    for side in range(6):
        run, start = geo.whole.runs[side], base + geo.whole.starts[side]
        for slot in range(geo.n):
            raw[side, slot * run : (slot + 1) * run] = buffer[slot, start : start + run]


def join_parts(geo, buffer, raw, piece):
    for side in range(6):
        index = 0 if side < 2 else side - 1
        run, start = geo.part.runs[index], geo.part.starts[index]
        if side < 2:
            part = 0 if side == 0 else geo.parts - 1
            for slot in range(geo.n):
                raw[side, slot * run : (slot + 1) * run] = buffer[part, slot, start : start + run]
        elif side < 4:
            for part in range(geo.parts):
                for slot in range(geo.n):
                    piece[slot * run : (slot + 1) * run] = buffer[part, slot, start : start + run]
                for var in range(geo.v):
                    row = var * geo.x + part * geo.depth
                    raw[side, row : row + geo.depth] = piece[var * geo.depth : (var + 1) * geo.depth]
        else:
            for slot in range(geo.n):
                total = buffer[0, slot, start : start + run]
                for part in range(1, geo.parts):
                    total = total + buffer[part, slot, start : start + run]
                raw[side, slot * run : (slot + 1) * run] = total


def turn(geo, codes, raw, ghosts):
    v, x, y, z = geo.block
    for side in range(6):
        first, second = codes[side] & 1, (codes[side] >> 1) & 1
        layer = raw[side, : geo.rows[side]]
        if side < 4:
            layer = flip_lanes(flip_rows(layer, first, y if side < 2 else x), second, z)
        else:
            layer = flip_lanes(flip_rows(layer, second, y), first, x)
        ghosts[side, : geo.rows[side]] = layer


def face_values(geo, faces, side):
    v, x, y, z = geo.block
    if side < 4:
        depth = y if side < 2 else x
        return [faces[side, var * depth : (var + 1) * depth] for var in range(v)]
    layer = faces[side, :y]
    return [layer] + [pltpu.roll(layer, z - var * x, 1) for var in range(1, v)]


def add_xy_terms(geo, side, terms, result):
    v, x, y, z = geo.block
    for var in range(v):
        if side < 2:
            plane = x - 1 if side == 0 else 0
            result[var, plane] = result[var, plane] + terms[var]
        else:
            row = y - 1 if side == 2 else 0
            result[var, :, row, :] = result[var, :, row, :] + terms[var]


def add_z_terms(geo, high_terms, low_terms, inner, result):
    v, x, y, z = geo.block
    lane = lax.broadcasted_iota(jnp.int32, (y, z), 1)
    zero = jnp.zeros((y, z), jnp.float32)
    for var in range(v):
        for plane in range(x):
            high = pltpu.roll(high_terms[var], z - 1 - plane, 1)
            low = pltpu.roll(low_terms[var], z - plane, 1) if plane else low_terms[var]
            change = jnp.where(lane == z - 1, high, jnp.where(lane == 0, low, zero))
            result[var, plane] = inner[var, plane] + change


def fill_tall(geo, source, tall):
    v, x, y, z = geo.block
    if len(source.shape) == 5:
        depth = geo.depth
        for part in range(geo.parts):
            tall[:, part * depth : (part + 1) * depth, PAD : PAD + y, :] = source[part]
    else:
        tall[:, :, PAD : PAD + y, :] = source[...]
    for var in range(v):
        tall[var, :, PAD - 1, :] = tall[var, :, PAD, :]
        tall[var, :, PAD + y, :] = tall[var, :, PAD + y - 1, :]


def around(geo, tall, plane):
    v, x, y, z = geo.block
    lane = lax.broadcasted_iota(jnp.int32, (y, z), 1)
    before, after = jnp.maximum(plane - 1, 0), jnp.minimum(plane + 1, x - 1)
    cells, low, high = [], [[], [], []], [[], [], []]
    for var in range(v):
        mid = tall[var, plane, PAD : PAD + y]
        cells.append(mid)
        low[0].append(tall[var, before, PAD : PAD + y])
        high[0].append(tall[var, after, PAD : PAD + y])
        low[1].append(tall[var, plane, PAD - 1 : PAD - 1 + y])
        high[1].append(tall[var, plane, PAD + 1 : PAD + 1 + y])
        low[2].append(jnp.where(lane == 0, mid, pltpu.roll(mid, 1, 1)))
        high[2].append(jnp.where(lane == z - 1, mid, pltpu.roll(mid, z - 1, 1)))
    return cells, low, high


def flux_entry(geo, mats, direction, row, column):
    return mats[(direction * geo.v + row) * geo.v + column]


def step_plane(geo, mats, cells, low, high, rate):
    v = geo.v
    total = [None] * v
    for direction in range(3):
        lows, highs = low[direction], high[direction]
        mean_low = 0.5 * (lows[0] + cells[0])
        mean_high = 0.5 * (cells[0] + highs[0])
        square_low = 1.0 + mean_low * mean_low
        square_high = 1.0 + mean_high * mean_high
        spread_low = square_low * lax.rsqrt(square_low)
        spread_high = square_high * lax.rsqrt(square_high)
        slopes = [highs[var] - lows[var] for var in range(v)]
        for var in range(v):
            term = spread_low * (cells[var] - lows[var]) - spread_high * (highs[var] - cells[var])
            for column in range(v):
                term = term + flux_entry(geo, mats, direction, var, column) * slopes[column]
            total[var] = term if total[var] is None else total[var] + term
    scale = (0.5 * time_step) * rate
    return [cells[var] - scale * total[var] - damping * jnp.tanh(cells[var]) for var in range(v)]


def adjoint_plane(geo, mats, cells, low, high, grads, weight, weight_low, weight_high):
    v = geo.v
    total = [None] * v
    extra = None
    for direction in range(3):
        spreads, steps = [], []
        for lower, upper, lower_weight, upper_weight in (
            (low[direction], cells, weight_low[direction], weight),
            (cells, high[direction], weight, weight_high[direction]),
        ):
            mean = 0.5 * (lower[0] + upper[0])
            square = 1.0 + mean * mean
            inverse = lax.rsqrt(square)
            jump = [lower_weight[var] - upper_weight[var] for var in range(v)]
            product = jump[0] * (upper[0] - lower[0])
            for var in range(1, v):
                product = product + jump[var] * (upper[var] - lower[var])
            product = product * (mean * inverse)
            extra = product if extra is None else extra + product
            spreads.append(square * inverse)
            steps.append(jump)
        slopes = [steps[0][var] + steps[1][var] for var in range(v)]
        for var in range(v):
            term = spreads[1] * steps[1][var] - spreads[0] * steps[0][var]
            for row in range(v):
                term = term + flux_entry(geo, mats, direction, row, var) * slopes[row]
            total[var] = term if total[var] is None else total[var] + term
    total[0] = total[0] - 0.5 * extra
    out = []
    for var in range(v):
        bend = jnp.tanh(cells[var])
        slope = (1.0 - damping) + damping * (bend * bend)
        out.append(grads[var] * slope - (0.5 * time_step) * total[var])
    return out


def step_face(geo, mats, side, cells, ghosts, rate):
    v = geo.v
    mean = 0.5 * (cells[0] + ghosts[0])
    square = 1.0 + mean * mean
    spread = square * lax.rsqrt(square)
    gap = [ghosts[var] - cells[var] for var in range(v)]
    scale = (0.5 * time_step) * rate
    out = []
    for var in range(v):
        total = flux_entry(geo, mats, side // 2, var, 0) * gap[0]
        for column in range(1, v):
            total = total + flux_entry(geo, mats, side // 2, var, column) * gap[column]
        if side % 2 == 0:
            out.append(scale * (spread * gap[var] - total))
        else:
            out.append(scale * (spread * gap[var] + total))
    return out


def adjoint_face(geo, mats, side, cells, ghosts, weight, ghost_weight):
    v = geo.v
    mean = 0.5 * (cells[0] + ghosts[0])
    square = 1.0 + mean * mean
    inverse = lax.rsqrt(square)
    spread = square * inverse
    jump = [weight[var] - ghost_weight[var] for var in range(v)]
    product = jump[0] * (ghosts[0] - cells[0])
    for var in range(1, v):
        product = product + jump[var] * (ghosts[var] - cells[var])
    product = (0.5 * product) * (mean * inverse)
    out = []
    for var in range(v):
        total = flux_entry(geo, mats, side // 2, 0, var) * jump[0]
        for row in range(1, v):
            total = total + flux_entry(geo, mats, side // 2, row, var) * jump[row]
        if side % 2 == 0:
            total = spread * jump[var] + total
        else:
            total = spread * jump[var] - total
        if var == 0:
            total = total - product
        out.append((-0.5 * time_step) * total)
    return out


def pack_kernel(geo, late, part, stored, grads, rate, weight_faces, rate_faces, buffer, pieces):
    v, x, y, z = geo.block
    depth = geo.depth
    late.wait(1)
    lane = lax.broadcasted_iota(jnp.int32, (y, z), 1)
    plane = jnp.where(part[0] == geo.parts - 1, depth - 1, 0)
    high = jnp.zeros((y, z), jnp.float32)
    low = jnp.zeros((y, z), jnp.float32)
    for var in range(v):
        pieces[0, var * y : (var + 1) * y] = stored[var, plane]
        pieces[1, var * depth : (var + 1) * depth] = stored[var, :, y - 1, :]
        pieces[2, var * depth : (var + 1) * depth] = stored[var, :, 0, :]
        for step in range(depth):
            place = var * x + part[0] * depth + step
            tile = stored[var, step]
            here = lane == place
            high = jnp.where(here, pltpu.roll(tile, lax.rem(place + 1, z), 1), high)
            low = jnp.where(here, pltpu.roll(tile, place, 1), low)
    pieces[3, :y] = high
    pieces[4, :y] = low
    cut(geo, geo.part, pieces, buffer, 0)
    late.wait(2)
    late.wait(3)
    rate_faces[0, :y] = rate[x - 1]
    rate_faces[1, :y] = rate[0]
    rate_faces[2, :x] = rate[:, y - 1, :]
    rate_faces[3, :x] = rate[:, 0, :]
    high, low = take_z_faces(geo, lambda var, plane: rate[plane])
    rate_faces[4, :y] = high
    rate_faces[5, :y] = low
    late.leave(1)
    take_weight_faces(geo, grads, rate_faces, weight_faces)
    late.leave(0)
    cut(geo, geo.whole, weight_faces, buffer, geo.part.total, functools.partial(late.leave, 2))


def take_weight_faces(geo, grads, rate_faces, faces):
    v, x, y, z = geo.block
    take_xy_faces(geo, grads, faces)
    for side in range(4):
        depth = y if side < 2 else x
        for var in range(v):
            here = slice(var * depth, (var + 1) * depth)
            faces[side, here] = faces[side, here] * rate_faces[side, :depth]
    high, low = take_z_faces(geo, lambda var, plane: grads[var, plane])
    faces[4, :y] = high * rate_faces[4, :y]
    faces[5, :y] = low * rate_faces[5, :y]


def route_whole(geo, owner, neighbours, block, arrived, leaving, base):
    for side in range(6):
        source = owner[neighbours[block * 6 + side]]
        run, start, far = geo.whole.runs[side], base + geo.whole.starts[side], base + geo.whole.starts[side ^ 1]
        leaving[owner[block], start : start + run] = arrived[source, far : far + run]


def route_kernel(geo, late, owner, neighbours, arrived, leaving):
    for block in range(geo.n):
        route_whole(geo, owner, neighbours, block, arrived, leaving, 0)
        late.leave(0, owner[block])


def route_first_kernel(geo, late, part, owner, neighbours, arrived, leaving):
    x_side = jnp.where(part[0] == geo.parts - 1, 1, 0)
    for block in range(geo.n):
        route_whole(geo, owner, neighbours, block, arrived, leaving, geo.part.total)
        for index in range(5):
            side, far_index = (x_side, 0) if index == 0 else (index + 1, ((index + 1) ^ 1) - 1)
            source = owner[neighbours[block * 6 + side]]
            run, start, far = geo.part.runs[index], geo.part.starts[index], geo.part.starts[far_index]
            leaving[owner[block], start : start + run] = arrived[source, far : far + run]
        late.leave(0, owner[block])


def step_inner_kernel(geo, late, mats, block, rate, result, *rest):
    tall = rest[-1]
    late.wait(1)
    late.wait(2)
    fill_tall(geo, block, tall)

    def body(plane, carry):
        cells, low, high = around(geo, tall, plane)
        for var, value in enumerate(step_plane(geo, mats, cells, low, high, rate[plane])):
            result[var, plane] = value
        return carry

    lax.fori_loop(0, geo.x, body, 0)
    late.leave(0)
    if len(rest) == 2:
        faces = rest[0]
        v, x, y, z = geo.block
        for var in range(v):
            faces[0, var * y : (var + 1) * y] = tall[var, x - 1, PAD : PAD + y]
            faces[1, var * y : (var + 1) * y] = tall[var, 0, PAD : PAD + y]
            faces[2, var * x : (var + 1) * x] = tall[var, :, PAD + y - 1, :]
            faces[3, var * x : (var + 1) * x] = tall[var, :, PAD, :]
        high, low = take_z_faces(geo, lambda var, plane: tall[var, plane, PAD : PAD + y])
        faces[4, :y] = high
        faces[5, :y] = low
        late.leave(1)


def adjoint_inner_kernel(geo, late, mats, block, grads, rate, result, tall, weights):
    v, x, y, z = geo.block
    for index in range(1, 4):
        late.wait(index)
    fill_tall(geo, block, tall)

    def scale(plane, carry):
        for var in range(v):
            weights[var, plane, PAD : PAD + y] = rate[plane] * grads[var, plane]
        return carry

    lax.fori_loop(0, x, scale, 0)
    for var in range(v):
        weights[var, :, PAD - 1, :] = weights[var, :, PAD, :]
        weights[var, :, PAD + y, :] = weights[var, :, PAD + y - 1, :]

    def body(plane, carry):
        cells, low, high = around(geo, tall, plane)
        weight, weight_low, weight_high = around(geo, weights, plane)
        here = [grads[var, plane] for var in range(v)]
        values = adjoint_plane(geo, mats, cells, low, high, here, weight, weight_low, weight_high)
        for var, value in enumerate(values):
            result[var, plane] = value
        return carry

    lax.fori_loop(0, x, body, 0)


def step_edge_kernel(geo, first, late, place, owner, orientation, mats, inner, faces, rate_faces, arrived, result, *rest):
    v, x, y, z = geo.block
    if first:
        new_faces, sent, ghosts, raw, piece = rest
        join_parts(geo, arrived, raw, piece)
        turn(geo, own_codes(geo, place, owner, orientation), raw, ghosts)
        late.leave(3)
    else:
        ghosts = arrived
        late.wait(4)
        late.wait(7)
    late.wait(5)
    terms = []
    for side in (4, 5, 0, 1, 2, 3):
        depth = y if side < 2 or side > 3 else x
        cells, outer = face_values(geo, faces, side), face_values(geo, ghosts, side)
        values = step_face(geo, mats, side, cells, outer, rate_faces[side, :depth])
        if side < 4:
            add_xy_terms(geo, side, values, result)
        else:
            terms.append(values)
            if side == 5:
                add_z_terms(geo, *terms, inner, result)
    late.leave(0)
    if first:
        take_xy_faces(geo, result, new_faces)
        high, low = take_z_faces(geo, lambda var, plane: result[var, plane])
        new_faces[4, :y] = high
        new_faces[5, :y] = low
        late.leave(1)
        cut(geo, geo.whole, new_faces, sent, 0, functools.partial(late.leave, 2))


def adjoint_edge_kernel(geo, last, late, place, owner, orientation, mats, inner, faces, weight_faces, *rest):
    v, x, y, z = geo.block
    codes = own_codes(geo, place, owner, orientation)
    if last:
        ghosts, weight_buffer, result, raw, weight_ghosts = rest
        join(geo, weight_buffer, raw)
        turn(geo, codes, raw, weight_ghosts)
    else:
        rate_faces, buffer, weight_buffer, result, new_faces, sent, ghosts, raw, weight_ghosts = rest
        join(geo, buffer, raw)
        turn(geo, codes, raw, ghosts)
        late.leave(3)
        join(geo, weight_buffer, raw, geo.part.total)
        turn(geo, codes, raw, weight_ghosts)
    for index in range(5, 8):
        late.wait(index)
    terms = []
    for side in (4, 5, 0, 1, 2, 3):
        views = [face_values(geo, field, side) for field in (faces, ghosts, weight_faces, weight_ghosts)]
        values = adjoint_face(geo, mats, side, *views)
        if side < 4:
            add_xy_terms(geo, side, values, result)
        else:
            terms.append(values)
            if side == 5:
                add_z_terms(geo, *terms, inner, result)
    late.leave(0)
    if not last:
        take_weight_faces(geo, result, rate_faces, new_faces)
        late.leave(1)
        cut(geo, geo.whole, new_faces, sent, 0, functools.partial(late.leave, 2))


class Late:
    def __init__(self, arrivals, departures, sems):
        self.arrivals, self.departures, self.sems, self.started = arrivals, departures, sems, []

    def wait(self, index):
        if index in self.arrivals:
            self.arrivals[index].wait()

    def leave(self, index, slot=None):
        if index in self.departures:
            source, target = self.departures[index]
            if slot is not None:
                source, target = source.at[slot], target.at[slot]
            copy = pltpu.make_async_copy(source, target, self.sems.at[len(self.started)])
            copy.start()
            self.started.append(copy)


def call(kernel, ins, outs, scratch, flops):
    late_in = [(index, shape) for index, (kind, shape) in enumerate(ins) if kind == "H"]
    late_out = [(index, shape) for index, (kind, shape) in enumerate(outs) if kind in "HB"]
    count_in, count_out = len(late_in), len(late_out)
    sends = sum(shape[0] if kind == "B" else 1 for kind, shape in outs if kind in "HB")

    def body(*refs):
        given = list(refs[: len(ins)])
        made = list(refs[len(ins) : len(ins) + len(outs)])
        rest = list(refs[len(ins) + len(outs) :])
        own = rest[: len(scratch)]
        stage = rest[len(scratch) : len(scratch) + count_in + count_out]
        sems_in = rest[len(scratch) + count_in + count_out] if count_in else None
        sems_out = rest[-1] if count_out else None
        arrivals, departures = {}, {}
        for slot, (index, _) in enumerate(late_in):
            copy = pltpu.make_async_copy(given[index], stage[slot], sems_in.at[slot])
            copy.start()
            arrivals[index] = copy
            given[index] = stage[slot]
        for slot, (index, _) in enumerate(late_out):
            departures[index] = (stage[count_in + slot], made[index])
            made[index] = stage[count_in + slot]
        late = Late(arrivals, departures, sems_out)
        kernel(late, *given, *made, *own)
        assert len(late.started) == sends
        for copy in late.started:
            copy.wait()

    hbm = pl.BlockSpec(memory_space=pltpu.HBM)
    specs = {"S": SMEM, "V": VMEM, "R": VMEM, "H": hbm, "B": hbm}
    scratch_shapes = [pltpu.VMEM(shape, jnp.float32) for shape in scratch]
    scratch_shapes += [pltpu.VMEM(shape, jnp.float32) for _, shape in late_in + late_out]
    if count_in:
        scratch_shapes.append(pltpu.SemaphoreType.DMA((count_in,)))
    if count_out:
        scratch_shapes.append(pltpu.SemaphoreType.DMA((sends,)))
    shapes = {"V": jax.ShapeDtypeStruct, "R": pltpu.VMEM, "H": pltpu.HBM, "B": pltpu.HBM}
    invoke = pl.pallas_call(
        body,
        in_specs=[specs[kind] for kind, _ in ins],
        out_specs=[specs[kind] for kind, _ in outs],
        out_shape=[shapes[kind](shape, jnp.float32) for kind, shape in outs],
        scratch_shapes=scratch_shapes,
        compiler_params=pltpu.CompilerParams(vmem_limit_bytes=VMEM_LIMIT),
        cost_estimate=pl.CostEstimate(flops=flops, bytes_accessed=3 << 20, transcendentals=0),
    )

    def run(*operands):
        placed = {"H": pltpu.HBM, "R": pltpu.VMEM}
        return invoke(
            *[
                pltpu.with_memory_space_constraint(operand, placed[kind]) if kind in placed else operand
                for operand, (kind, _) in zip(operands, ins)
            ]
        )

    return run


def on_device(count, parts, checkpoint, seeds, cell_rate, flux_mats, owner, neighbours, orientation):
    nvars, cx, cy, cz = seeds.shape[2:]
    geo = Geometry(nvars, cx, cy, cz, count, parts)
    rate = cell_rate[0]
    grads = seeds[0, 0]
    place = lax.axis_index("space").astype(jnp.int32).reshape(1)
    part = lax.axis_index("ckpt").astype(jnp.int32).reshape(1)
    mats = flux_mats.reshape(-1)
    neighbours = neighbours.reshape(-1)
    orientation = orientation.reshape(-1)
    fixed = (place, owner, orientation, mats)
    work = nvars * nvars * 3 * 4 * cx * cy * cz
    few = work // 16
    whole, both = geo.buffer(geo.whole.total), geo.buffer(geo.part.total + geo.whole.total)
    some = -(-geo.part.total // 8) * 8

    stored_shape, block, faces_shape = checkpoint.shape[1:], geo.block, geo.faces
    rate_block = cell_rate.shape[1:]
    scalar, near, kept_near = ("S", None), ("V", None), ("R", None)

    def far(shape):
        return ("H", shape)

    def swap(buffer):
        return lax.all_to_all(buffer, "space", 0, 0, tiled=True)

    def route(arrived):
        return call(functools.partial(route_kernel, geo), [scalar, scalar, near], [("B", whole)], [], few)(
            owner, neighbours, arrived
        )[0]

    def adjoint_inner(state, state_kind, grads, grads_kind):
        return call(
            functools.partial(adjoint_inner_kernel, geo),
            [scalar, state_kind, grads_kind, far(rate_block)],
            [("R", block)],
            [geo.tall] * 2,
            2 * work,
        )(mats, state, grads, rate)[0]

    weight_faces, rate_faces, sent = call(
        functools.partial(pack_kernel, geo),
        [scalar, far(stored_shape), far(block), far(rate_block)],
        [far(faces_shape), ("R", geo.rate_faces), ("B", both)],
        [faces_shape],
        few,
    )(part, checkpoint[0], grads, rate)
    kept, sent = lax.optimization_barrier((checkpoint[0], sent))
    arrived = swap(sent)
    state = lax.all_gather(kept, "ckpt", axis=0)
    arrived, state = lax.optimization_barrier((arrived, state))
    (leaving,) = call(functools.partial(route_first_kernel, geo), [scalar] * 3 + [near], [("B", both)], [], few)(
        part, owner, neighbours, arrived
    )
    first_ghosts = swap(leaving)
    inner, faces = call(
        functools.partial(step_inner_kernel, geo),
        [scalar, far(state.shape), far(rate_block)],
        [("R", block), far(faces_shape)],
        [geo.tall],
        work,
    )(mats, state, rate)
    first_ghosts, inner, faces = lax.optimization_barrier((first_ghosts, inner, faces))
    gathered = lax.all_gather(first_ghosts[:, :some], "ckpt", axis=0)
    next_state, next_faces, sent, ghosts = call(
        functools.partial(step_edge_kernel, geo, True),
        [scalar] * 4 + [kept_near, far(faces_shape), kept_near, near],
        [("R", block), far(faces_shape), ("B", whole), far(faces_shape)],
        [faces_shape, faces_shape[1:]],
        few,
    )(*fixed, inner, faces, rate_faces, gathered)

    arrived = swap(sent)
    inner = adjoint_inner(next_state, kept_near, grads, far(block))
    arrived, inner = lax.optimization_barrier((arrived, inner))
    leaving = route(arrived)
    later_state, leaving = lax.optimization_barrier((next_state, leaving))
    next_ghosts = swap(leaving)
    (final_inner,) = call(
        functools.partial(step_inner_kernel, geo),
        [scalar, kept_near, far(rate_block)],
        [far(block)],
        [geo.tall],
        work,
    )(mats, later_state, rate)
    next_ghosts, final_inner = lax.optimization_barrier((next_ghosts, final_inner))
    grads_now, next_weight_faces, sent, turned = call(
        functools.partial(adjoint_edge_kernel, geo, False),
        [scalar] * 4 + [kept_near, far(faces_shape), far(faces_shape), kept_near, near, near],
        [("R", block), far(faces_shape), ("B", whole), far(faces_shape)],
        [faces_shape] * 2,
        few,
    )(*fixed, inner, next_faces, weight_faces, rate_faces, next_ghosts, first_ghosts)

    arrived = swap(sent)
    inner = adjoint_inner(state, far(state.shape), grads_now, kept_near)
    arrived, inner = lax.optimization_barrier((arrived, inner))
    leaving = route(arrived)
    final_inner, leaving = lax.optimization_barrier((final_inner, leaving))
    last_ghosts = swap(leaving)
    (final,) = call(
        functools.partial(step_edge_kernel, geo, False),
        [scalar] * 4 + [far(block), far(faces_shape), kept_near, far(faces_shape)],
        [("V", block)],
        [],
        work,
    )(*fixed, final_inner, next_faces, rate_faces, turned)
    last_ghosts, final = lax.optimization_barrier((last_ghosts, final))
    (adjoint,) = call(
        functools.partial(adjoint_edge_kernel, geo, True),
        [scalar] * 4 + [kept_near] + [far(faces_shape)] * 3 + [near],
        [("V", block)],
        [faces_shape] * 2,
        few,
    )(*fixed, inner, faces, next_weight_faces, ghosts, last_ghosts)
    return (adjoint[None, None], final[None])


def solution(mesh):
    return jax.shard_map(
        functools.partial(on_device, mesh.shape["space"], mesh.shape["ckpt"]),
        mesh=mesh,
        in_specs=(
            P("space", None, "ckpt", None, None),
            P("ckpt", "space", None, None, None, None),
            P("space", None, None, None),
            P(),
            P(),
            P(),
            P(),
        ),
        out_specs=(P("ckpt", "space", None, None, None, None), P("space", None, None, None, None)),
        check_vma=False,
    )
```

```python
import functools

import jax
import jax.numpy as jnp
from jax import lax
from jax.experimental import pallas as pl
from jax.experimental.pallas import tpu as pltpu
from jax.sharding import PartitionSpec as P

STEPS = 2
time_step = 0.05
damping = 0.015

PAD = 8
VMEM = pl.BlockSpec(memory_space=pltpu.VMEM)
SMEM = pl.BlockSpec(memory_space=pltpu.SMEM)
VMEM_LIMIT = 16 * 1024 * 1024


class Pieces:
    def __init__(self, rows, count):
        self.rows = rows
        self.runs = [-(-length // count) for length in rows]
        self.starts = [sum(self.runs[:index]) for index in range(len(rows))]
        self.total = sum(self.runs)


class Geometry:
    def __init__(self, nvars, cx, cy, cz, count, parts):
        self.v, self.x, self.y, self.z, self.n, self.parts = nvars, cx, cy, cz, count, parts
        self.depth = cx // parts
        self.rows = [nvars * cy] * 2 + [nvars * cx] * 2 + [cy] * 2
        self.whole = Pieces(self.rows, count)
        self.part = Pieces([nvars * cy] + [nvars * self.depth] * 2 + [cy] * 2, count)
        self.face_rows = -(-max(run * count for run in self.whole.runs) // 8) * 8
        self.block = (nvars, cx, cy, cz)
        self.tall = (nvars, cx, cy + 2 * PAD, cz)
        self.faces = (6, self.face_rows, cz)
        self.rate_faces = (6, max(cx, cy), cz)

    def buffer(self, rows):
        return (self.n, -(-rows // 8) * 8, self.z)


def take_z_faces(geo, load):
    v, x, y, z = geo.block
    lane = lax.broadcasted_iota(jnp.int32, (y, z), 1)
    high = jnp.zeros((y, z), jnp.float32)
    low = jnp.zeros((y, z), jnp.float32)
    for var in range(v):
        for plane in range(x):
            place = var * x + plane
            tile = load(var, plane)
            here = lane == place
            high = jnp.where(here, pltpu.roll(tile, (place + 1) % z, 1), high)
            low = jnp.where(here, pltpu.roll(tile, place, 1) if place else tile, low)
    return high, low


def take_xy_faces(geo, source, faces):
    v, x, y, z = geo.block
    faces[0, : v * y] = source[:, x - 1].reshape(v * y, z)
    faces[1, : v * y] = source[:, 0].reshape(v * y, z)
    for var in range(v):
        faces[2, var * x : (var + 1) * x] = source[var, :, y - 1, :]
        faces[3, var * x : (var + 1) * x] = source[var, :, 0, :]


def cut(geo, pieces, faces, buffer, base, leave=None):
    for slot in range(geo.n):
        for index, (run, start) in enumerate(zip(pieces.runs, pieces.starts)):
            buffer[slot, base + start : base + start + run] = faces[index, slot * run : (slot + 1) * run]
        if leave:
            leave(slot)


def own_codes(geo, place, owner, orientation):
    block = jnp.int32(0)
    for index in range(geo.n):
        block = jnp.where(owner[index] == place[0], index, block)
    return [orientation[block * 6 + side] for side in range(6)]


def flip_rows(values, flag, length):
    rows, z = values.shape
    grouped = values.reshape(rows // length, length // 8, 8, z)
    index = lax.broadcasted_iota(jnp.int32, (8, z), 0)
    index = jnp.where(flag == 1, 7 - index, index)
    tiles = length // 8
    out = []
    for group in range(rows // length):
        for tile in range(tiles):
            picked = jnp.where(flag == 1, grouped[group, tiles - 1 - tile], grouped[group, tile])
            out.append(jnp.take_along_axis(picked, index, axis=0))
    return jnp.stack(out).reshape(rows, z)


def flip_lanes(values, flag, length):
    rows, z = values.shape
    lane = lax.broadcasted_iota(jnp.int32, (8, z), 1)
    within = lax.rem(lane, length)
    index = jnp.where(flag == 1, lane + (length - 1) - 2 * within, lane)
    index = jnp.minimum(index, z - 1)
    tiles = values.reshape(rows // 8, 8, z)
    return jnp.stack(
        [jnp.take_along_axis(tiles[tile], index, axis=1) for tile in range(rows // 8)]
    ).reshape(rows, z)


def join(geo, buffer, raw, base=0):
    for side in range(6):
        run, start = geo.whole.runs[side], base + geo.whole.starts[side]
        for slot in range(geo.n):
            raw[side, slot * run : (slot + 1) * run] = buffer[slot, start : start + run]


def join_parts(geo, buffer, raw, piece):
    for side in range(6):
        index = 0 if side < 2 else side - 1
        run, start = geo.part.runs[index], geo.part.starts[index]
        if side < 2:
            part = 0 if side == 0 else geo.parts - 1
            for slot in range(geo.n):
                raw[side, slot * run : (slot + 1) * run] = buffer[part, slot, start : start + run]
        elif side < 4:
            for part in range(geo.parts):
                for slot in range(geo.n):
                    piece[slot * run : (slot + 1) * run] = buffer[part, slot, start : start + run]
                for var in range(geo.v):
                    row = var * geo.x + part * geo.depth
                    raw[side, row : row + geo.depth] = piece[var * geo.depth : (var + 1) * geo.depth]
        else:
            for slot in range(geo.n):
                total = buffer[0, slot, start : start + run]
                for part in range(1, geo.parts):
                    total = total + buffer[part, slot, start : start + run]
                raw[side, slot * run : (slot + 1) * run] = total


def turn(geo, codes, raw, ghosts):
    v, x, y, z = geo.block
    for side in range(6):
        first, second = codes[side] & 1, (codes[side] >> 1) & 1
        layer = raw[side, : geo.rows[side]]
        if side < 4:
            layer = flip_lanes(flip_rows(layer, first, y if side < 2 else x), second, z)
        else:
            layer = flip_lanes(flip_rows(layer, second, y), first, x)
        ghosts[side, : geo.rows[side]] = layer


def face_values(geo, faces, side):
    v, x, y, z = geo.block
    if side < 4:
        depth = y if side < 2 else x
        return [faces[side, var * depth : (var + 1) * depth] for var in range(v)]
    layer = faces[side, :y]
    return [layer] + [pltpu.roll(layer, z - var * x, 1) for var in range(1, v)]


def fill_tall(geo, source, tall):
    v, x, y, z = geo.block
    if len(source.shape) == 5:
        depth = geo.depth
        for part in range(geo.parts):
            tall[:, part * depth : (part + 1) * depth, PAD : PAD + y, :] = source[part]
    else:
        tall[:, :, PAD : PAD + y, :] = source[...]
    for var in range(v):
        tall[var, :, PAD - 1, :] = tall[var, :, PAD, :]
        tall[var, :, PAD + y, :] = tall[var, :, PAD + y - 1, :]


def around(geo, tall, plane):
    v, x, y, z = geo.block
    lane = lax.broadcasted_iota(jnp.int32, (y, z), 1)
    before, after = jnp.maximum(plane - 1, 0), jnp.minimum(plane + 1, x - 1)
    cells, low, high = [], [[], [], []], [[], [], []]
    for var in range(v):
        mid = tall[var, plane, PAD : PAD + y]
        cells.append(mid)
        low[0].append(tall[var, before, PAD : PAD + y])
        high[0].append(tall[var, after, PAD : PAD + y])
        low[1].append(tall[var, plane, PAD - 1 : PAD - 1 + y])
        high[1].append(tall[var, plane, PAD + 1 : PAD + 1 + y])
        low[2].append(jnp.where(lane == 0, mid, pltpu.roll(mid, 1, 1)))
        high[2].append(jnp.where(lane == z - 1, mid, pltpu.roll(mid, z - 1, 1)))
    return cells, low, high


def flux_entry(geo, mats, direction, row, column):
    return mats[(direction * geo.v + row) * geo.v + column]


def step_plane(geo, mats, cells, low, high, rate):
    v = geo.v
    total = [None] * v
    for direction in range(3):
        lows, highs = low[direction], high[direction]
        mean_low = 0.5 * (lows[0] + cells[0])
        mean_high = 0.5 * (cells[0] + highs[0])
        square_low = 1.0 + mean_low * mean_low
        square_high = 1.0 + mean_high * mean_high
        spread_low = square_low * lax.rsqrt(square_low)
        spread_high = square_high * lax.rsqrt(square_high)
        slopes = [highs[var] - lows[var] for var in range(v)]
        for var in range(v):
            term = spread_low * (cells[var] - lows[var]) - spread_high * (highs[var] - cells[var])
            for column in range(v):
                term = term + flux_entry(geo, mats, direction, var, column) * slopes[column]
            total[var] = term if total[var] is None else total[var] + term
    scale = (0.5 * time_step) * rate
    return [cells[var] - scale * total[var] - damping * jnp.tanh(cells[var]) for var in range(v)]


def adjoint_plane(geo, mats, cells, low, high, grads, weight, weight_low, weight_high):
    v = geo.v
    total = [None] * v
    extra = None
    for direction in range(3):
        spreads, steps = [], []
        for lower, upper, lower_weight, upper_weight in (
            (low[direction], cells, weight_low[direction], weight),
            (cells, high[direction], weight, weight_high[direction]),
        ):
            mean = 0.5 * (lower[0] + upper[0])
            square = 1.0 + mean * mean
            inverse = lax.rsqrt(square)
            jump = [lower_weight[var] - upper_weight[var] for var in range(v)]
            product = jump[0] * (upper[0] - lower[0])
            for var in range(1, v):
                product = product + jump[var] * (upper[var] - lower[var])
            product = product * (mean * inverse)
            extra = product if extra is None else extra + product
            spreads.append(square * inverse)
            steps.append(jump)
        slopes = [steps[0][var] + steps[1][var] for var in range(v)]
        for var in range(v):
            term = spreads[1] * steps[1][var] - spreads[0] * steps[0][var]
            for row in range(v):
                term = term + flux_entry(geo, mats, direction, row, var) * slopes[row]
            total[var] = term if total[var] is None else total[var] + term
    total[0] = total[0] - 0.5 * extra
    out = []
    for var in range(v):
        bend = jnp.tanh(cells[var])
        slope = (1.0 - damping) + damping * (bend * bend)
        out.append(grads[var] * slope - (0.5 * time_step) * total[var])
    return out


def step_face(geo, mats, side, cells, ghosts, rate):
    v = geo.v
    mean = 0.5 * (cells[0] + ghosts[0])
    square = 1.0 + mean * mean
    spread = square * lax.rsqrt(square)
    gap = [ghosts[var] - cells[var] for var in range(v)]
    scale = (0.5 * time_step) * rate
    out = []
    for var in range(v):
        total = flux_entry(geo, mats, side // 2, var, 0) * gap[0]
        for column in range(1, v):
            total = total + flux_entry(geo, mats, side // 2, var, column) * gap[column]
        if side % 2 == 0:
            out.append(scale * (spread * gap[var] - total))
        else:
            out.append(scale * (spread * gap[var] + total))
    return out


def adjoint_face(geo, mats, side, cells, ghosts, weight, ghost_weight):
    v = geo.v
    mean = 0.5 * (cells[0] + ghosts[0])
    square = 1.0 + mean * mean
    inverse = lax.rsqrt(square)
    spread = square * inverse
    jump = [weight[var] - ghost_weight[var] for var in range(v)]
    product = jump[0] * (ghosts[0] - cells[0])
    for var in range(1, v):
        product = product + jump[var] * (ghosts[var] - cells[var])
    product = (0.5 * product) * (mean * inverse)
    out = []
    for var in range(v):
        total = flux_entry(geo, mats, side // 2, 0, var) * jump[0]
        for row in range(1, v):
            total = total + flux_entry(geo, mats, side // 2, row, var) * jump[row]
        if side % 2 == 0:
            total = spread * jump[var] + total
        else:
            total = spread * jump[var] - total
        if var == 0:
            total = total - product
        out.append((-0.5 * time_step) * total)
    return out


def pack_kernel(geo, late, part, stored, grads, rate, weight_faces, rate_faces, buffer, pieces):
    v, x, y, z = geo.block
    depth = geo.depth
    late.wait(1)
    lane = lax.broadcasted_iota(jnp.int32, (y, z), 1)
    plane = jnp.where(part[0] == geo.parts - 1, depth - 1, 0)
    high = jnp.zeros((y, z), jnp.float32)
    low = jnp.zeros((y, z), jnp.float32)
    for var in range(v):
        pieces[0, var * y : (var + 1) * y] = stored[var, plane]
        pieces[1, var * depth : (var + 1) * depth] = stored[var, :, y - 1, :]
        pieces[2, var * depth : (var + 1) * depth] = stored[var, :, 0, :]
        for step in range(depth):
            place = var * x + part[0] * depth + step
            tile = stored[var, step]
            here = lane == place
            high = jnp.where(here, pltpu.roll(tile, lax.rem(place + 1, z), 1), high)
            low = jnp.where(here, pltpu.roll(tile, place, 1), low)
    pieces[3, :y] = high
    pieces[4, :y] = low
    cut(geo, geo.part, pieces, buffer, 0)
    late.wait(2)
    late.wait(3)
    rate_faces[0, :y] = rate[x - 1]
    rate_faces[1, :y] = rate[0]
    rate_faces[2, :x] = rate[:, y - 1, :]
    rate_faces[3, :x] = rate[:, 0, :]
    high, low = take_z_faces(geo, lambda var, plane: rate[plane])
    rate_faces[4, :y] = high
    rate_faces[5, :y] = low
    late.leave(1)
    take_weight_faces(geo, grads, rate_faces, weight_faces)
    late.leave(0)
    cut(geo, geo.whole, weight_faces, buffer, geo.part.total, functools.partial(late.leave, 2))


def take_weight_faces(geo, grads, rate_faces, faces):
    v, x, y, z = geo.block
    take_xy_faces(geo, grads, faces)
    for side in range(4):
        depth = y if side < 2 else x
        for var in range(v):
            here = slice(var * depth, (var + 1) * depth)
            faces[side, here] = faces[side, here] * rate_faces[side, :depth]
    high, low = take_z_faces(geo, lambda var, plane: grads[var, plane])
    faces[4, :y] = high * rate_faces[4, :y]
    faces[5, :y] = low * rate_faces[5, :y]


def route_whole(geo, owner, neighbours, block, arrived, leaving, base):
    for side in range(6):
        source = owner[neighbours[block * 6 + side]]
        run, start, far = geo.whole.runs[side], base + geo.whole.starts[side], base + geo.whole.starts[side ^ 1]
        leaving[owner[block], start : start + run] = arrived[source, far : far + run]


def route_kernel(geo, late, owner, neighbours, arrived, leaving):
    for block in range(geo.n):
        route_whole(geo, owner, neighbours, block, arrived, leaving, 0)
        late.leave(0, owner[block])


def route_first_kernel(geo, late, part, owner, neighbours, arrived, leaving):
    x_side = jnp.where(part[0] == geo.parts - 1, 1, 0)
    for block in range(geo.n):
        route_whole(geo, owner, neighbours, block, arrived, leaving, geo.part.total)
        for index in range(5):
            side, far_index = (x_side, 0) if index == 0 else (index + 1, ((index + 1) ^ 1) - 1)
            source = owner[neighbours[block * 6 + side]]
            run, start, far = geo.part.runs[index], geo.part.starts[index], geo.part.starts[far_index]
            leaving[owner[block], start : start + run] = arrived[source, far : far + run]
        late.leave(0, owner[block])


def step_inner_kernel(geo, late, mats, block, rate, result, *rest):
    tall = rest[-1]
    late.wait(1)
    late.wait(2)
    fill_tall(geo, block, tall)

    def body(plane, carry):
        cells, low, high = around(geo, tall, plane)
        for var, value in enumerate(step_plane(geo, mats, cells, low, high, rate[plane])):
            result[var, plane] = value
        return carry

    lax.fori_loop(0, geo.x, body, 0)
    late.leave(0)
    if len(rest) == 2:
        faces = rest[0]
        v, x, y, z = geo.block
        for var in range(v):
            faces[0, var * y : (var + 1) * y] = tall[var, x - 1, PAD : PAD + y]
            faces[1, var * y : (var + 1) * y] = tall[var, 0, PAD : PAD + y]
            faces[2, var * x : (var + 1) * x] = tall[var, :, PAD + y - 1, :]
            faces[3, var * x : (var + 1) * x] = tall[var, :, PAD, :]
        high, low = take_z_faces(geo, lambda var, plane: tall[var, plane, PAD : PAD + y])
        faces[4, :y] = high
        faces[5, :y] = low
        late.leave(2)


def adjoint_inner_kernel(geo, late, mats, block, grads, rate, result, tall, weights):
    v, x, y, z = geo.block
    for index in range(1, 4):
        late.wait(index)
    fill_tall(geo, block, tall)

    def scale(plane, carry):
        for var in range(v):
            weights[var, plane, PAD : PAD + y] = rate[plane] * grads[var, plane]
        return carry

    lax.fori_loop(0, x, scale, 0)
    for var in range(v):
        weights[var, :, PAD - 1, :] = weights[var, :, PAD, :]
        weights[var, :, PAD + y, :] = weights[var, :, PAD + y - 1, :]

    def body(plane, carry):
        cells, low, high = around(geo, tall, plane)
        weight, weight_low, weight_high = around(geo, weights, plane)
        here = [grads[var, plane] for var in range(v)]
        values = adjoint_plane(geo, mats, cells, low, high, here, weight, weight_low, weight_high)
        for var, value in enumerate(values):
            result[var, plane] = value
        return carry

    lax.fori_loop(0, x, body, 0)


def add_terms(geo, values, inner, result, leave=None):
    v, x, y, z = geo.block
    lane = lax.broadcasted_iota(jnp.int32, (y, z), 1)
    zero = jnp.zeros((y, z), jnp.float32)
    for var in range(v):
        for plane in range(x):
            high = pltpu.roll(values[4][var], z - 1 - plane, 1)
            low = pltpu.roll(values[5][var], z - plane, 1) if plane else values[5][var]
            change = jnp.where(lane == z - 1, high, jnp.where(lane == 0, low, zero))
            if plane == 0:
                change = change + values[1][var]
            if plane == x - 1:
                change = change + values[0][var]
            result[var, plane] = inner[var, plane] + change
        result[var, :, y - 1, :] = result[var, :, y - 1, :] + values[2][var]
        result[var, :, 0, :] = result[var, :, 0, :] + values[3][var]
        if leave:
            leave(var)


def step_edge_kernel(geo, first, late, place, owner, orientation, mats, inner, faces, rate_faces, arrived, result, *rest):
    v, x, y, z = geo.block
    if first:
        new_faces, sent, ghosts, raw, piece = rest
        join_parts(geo, arrived, raw, piece)
        turn(geo, own_codes(geo, place, owner, orientation), raw, ghosts)
        late.leave(4)
    else:
        ghosts = arrived
        late.wait(4)
        late.wait(7)
    late.wait(5)
    values = []
    for side in range(6):
        depth = y if side < 2 or side > 3 else x
        cells, outer = face_values(geo, faces, side), face_values(geo, ghosts, side)
        values.append(step_face(geo, mats, side, cells, outer, rate_faces[side, :depth]))
    add_terms(geo, values, inner, result)
    if first:
        take_xy_faces(geo, result, new_faces)
        high, low = take_z_faces(geo, lambda var, plane: result[var, plane])
        new_faces[4, :y] = high
        new_faces[5, :y] = low
        cut(geo, geo.whole, new_faces, sent, 0, functools.partial(late.leave, 3))
        late.leave(2)


def adjoint_edge_kernel(geo, last, late, place, owner, orientation, mats, inner, faces, weight_faces, *rest):
    v, x, y, z = geo.block
    codes = own_codes(geo, place, owner, orientation)
    if last:
        ghosts, weight_buffer, result, raw, weight_ghosts = rest
        join(geo, weight_buffer, raw)
        turn(geo, codes, raw, weight_ghosts)
    else:
        rate_faces, buffer, weight_buffer, result, new_faces, sent, ghosts, raw, weight_ghosts = rest
        join(geo, buffer, raw)
        turn(geo, codes, raw, ghosts)
        late.leave(3)
        join(geo, weight_buffer, raw, geo.part.total)
        turn(geo, codes, raw, weight_ghosts)
    values = []
    for side in range(6):
        views = [face_values(geo, field, side) for field in (faces, ghosts, weight_faces, weight_ghosts)]
        values.append(adjoint_face(geo, mats, side, *views))
    add_terms(geo, values, inner, result, functools.partial(late.leave, 0) if last else None)
    if not last:
        take_weight_faces(geo, result, rate_faces, new_faces)
        cut(geo, geo.whole, new_faces, sent, 0, functools.partial(late.leave, 2))


class Late:
    def __init__(self, arrivals, departures, sems):
        self.arrivals, self.departures, self.sems, self.started = arrivals, departures, sems, []

    def wait(self, index):
        if index in self.arrivals:
            self.arrivals[index].wait()

    def leave(self, index, slot=None):
        if index in self.departures:
            source, target = self.departures[index]
            if slot is not None:
                source, target = source.at[slot], target.at[slot]
            copy = pltpu.make_async_copy(source, target, self.sems.at[len(self.started)])
            copy.start()
            self.started.append(copy)


def call(kernel, ins, outs, scratch, flops, fetch=()):
    late_in = [(index, shape) for index, (kind, shape) in enumerate(ins) if kind == "H"]
    late_out = [(index, shape) for index, (kind, shape) in enumerate(outs) if kind in "HB"]
    count_in, count_out = len(late_in), len(late_out)
    sends = sum(shape[0] if kind == "B" else 1 for kind, shape in outs if kind in "HBD")

    def body(*refs):
        given = list(refs[: len(ins)])
        made = list(refs[len(ins) : len(ins) + len(outs)])
        rest = list(refs[len(ins) + len(outs) :])
        own = rest[: len(scratch)]
        stage = rest[len(scratch) : len(scratch) + count_in + count_out]
        sems_in = rest[len(scratch) + count_in + count_out] if count_in or fetch else None
        sems_out = rest[-1] if sends else None
        arrivals, departures = {}, {}
        for slot, (index, _) in enumerate(late_in):
            copy = pltpu.make_async_copy(given[index], stage[slot], sems_in.at[slot])
            copy.start()
            arrivals[index] = copy
            given[index] = stage[slot]
        for slot, (index, _) in enumerate(late_out):
            departures[index] = (stage[count_in + slot], made[index])
            made[index] = stage[count_in + slot]
        for index, (kind, _) in enumerate(outs):
            if kind == "D":
                departures[index] = (made[index - 1], made[index])
        fetched = []
        for slot, (source, target) in enumerate(fetch):
            copy = pltpu.make_async_copy(given[source], made[target], sems_in.at[count_in + slot])
            copy.start()
            fetched.append(copy)
        late = Late(arrivals, departures, sems_out)
        hidden_in = {source for source, _ in fetch}
        hidden_out = {target for _, target in fetch}
        kernel(
            late,
            *[ref for index, ref in enumerate(given) if index not in hidden_in],
            *[ref for index, ref in enumerate(made) if index not in hidden_out and outs[index][0] != "D"],
            *own,
        )
        assert len(late.started) == sends
        for copy in fetched + late.started:
            copy.wait()

    hbm = pl.BlockSpec(memory_space=pltpu.HBM)
    specs = {"S": SMEM, "V": VMEM, "R": VMEM, "H": hbm, "B": hbm, "D": hbm, "P": hbm}
    scratch_shapes = [pltpu.VMEM(shape, jnp.float32) for shape in scratch]
    scratch_shapes += [pltpu.VMEM(shape, jnp.float32) for _, shape in late_in + late_out]
    if count_in or fetch:
        scratch_shapes.append(pltpu.SemaphoreType.DMA((count_in + len(fetch),)))
    if sends:
        scratch_shapes.append(pltpu.SemaphoreType.DMA((sends,)))
    shapes = {"V": jax.ShapeDtypeStruct, "R": pltpu.VMEM, "H": pltpu.HBM, "B": pltpu.HBM, "D": pltpu.HBM}
    invoke = pl.pallas_call(
        body,
        in_specs=[specs[kind] for kind, _ in ins],
        out_specs=[specs[kind] for kind, _ in outs],
        out_shape=[shapes[kind](shape, jnp.float32) for kind, shape in outs],
        scratch_shapes=scratch_shapes,
        compiler_params=pltpu.CompilerParams(vmem_limit_bytes=VMEM_LIMIT),
        cost_estimate=pl.CostEstimate(flops=flops, bytes_accessed=3 << 20, transcendentals=0),
    )

    def run(*operands):
        placed = {"H": pltpu.HBM, "R": pltpu.VMEM, "P": pltpu.HBM}
        return invoke(
            *[
                pltpu.with_memory_space_constraint(operand, placed[kind]) if kind in placed else operand
                for operand, (kind, _) in zip(operands, ins)
            ]
        )

    return run


def on_device(count, parts, checkpoint, seeds, cell_rate, flux_mats, owner, neighbours, orientation):
    nvars, cx, cy, cz = seeds.shape[2:]
    geo = Geometry(nvars, cx, cy, cz, count, parts)
    rate = cell_rate[0]
    grads = seeds[0, 0]
    place = lax.axis_index("space").astype(jnp.int32).reshape(1)
    part = lax.axis_index("ckpt").astype(jnp.int32).reshape(1)
    mats = flux_mats.reshape(-1)
    neighbours = neighbours.reshape(-1)
    orientation = orientation.reshape(-1)
    fixed = (place, owner, orientation, mats)
    work = nvars * nvars * 3 * 4 * cx * cy * cz
    few = work // 16
    whole, both = geo.buffer(geo.whole.total), geo.buffer(geo.part.total + geo.whole.total)
    some = -(-geo.part.total // 8) * 8

    stored_shape, block, faces_shape = checkpoint.shape[1:], geo.block, geo.faces
    rate_block = cell_rate.shape[1:]
    scalar, near, kept_near = ("S", None), ("V", None), ("R", None)

    def far(shape):
        return ("H", shape)

    def swap(buffer):
        return lax.all_to_all(buffer, "space", 0, 0, tiled=True)

    def route(arrived):
        return call(functools.partial(route_kernel, geo), [scalar, scalar, near], [("B", whole)], [], few)(
            owner, neighbours, arrived
        )[0]

    def adjoint_inner(state, state_kind, grads, grads_kind):
        return call(
            functools.partial(adjoint_inner_kernel, geo),
            [scalar, state_kind, grads_kind, far(rate_block)],
            [("R", block)],
            [geo.tall] * 2,
            2 * work,
        )(mats, state, grads, rate)[0]

    weight_faces, rate_faces, sent = call(
        functools.partial(pack_kernel, geo),
        [scalar, far(stored_shape), far(block), far(rate_block)],
        [far(faces_shape), ("R", geo.rate_faces), ("B", both)],
        [faces_shape],
        few,
    )(part, checkpoint[0], grads, rate)
    kept, sent = lax.optimization_barrier((checkpoint[0], sent))
    arrived = swap(sent)
    state = lax.all_gather(kept, "ckpt", axis=0)
    arrived, state = lax.optimization_barrier((arrived, state))
    (leaving,) = call(functools.partial(route_first_kernel, geo), [scalar] * 3 + [near], [("B", both)], [], few)(
        part, owner, neighbours, arrived
    )
    first_ghosts = swap(leaving)
    inner, faces, kept_faces = call(
        functools.partial(step_inner_kernel, geo),
        [scalar, far(state.shape), far(rate_block)],
        [("R", block), ("R", faces_shape), ("D", faces_shape)],
        [geo.tall],
        work,
    )(mats, state, rate)
    first_ghosts, inner, faces = lax.optimization_barrier((first_ghosts, inner, faces))
    gathered = lax.all_gather(first_ghosts[:, :some], "ckpt", axis=0)
    next_state, next_faces, kept_next_faces, sent, ghosts = call(
        functools.partial(step_edge_kernel, geo, True),
        [scalar] * 4 + [kept_near] * 3 + [near],
        [("R", block), ("R", faces_shape), ("D", faces_shape), ("B", whole), far(faces_shape)],
        [faces_shape, faces_shape[1:]],
        few,
    )(*fixed, inner, faces, rate_faces, gathered)

    arrived = swap(sent)
    inner = adjoint_inner(next_state, kept_near, grads, far(block))
    arrived, inner = lax.optimization_barrier((arrived, inner))
    leaving = route(arrived)
    later_state, leaving = lax.optimization_barrier((next_state, leaving))
    next_ghosts = swap(leaving)
    final_inner, weight_faces = call(
        functools.partial(step_inner_kernel, geo),
        [scalar, kept_near, far(rate_block), ("P", None)],
        [far(block), ("R", faces_shape)],
        [geo.tall],
        work,
        fetch=((3, 1),),
    )(mats, later_state, rate, weight_faces)
    next_ghosts, final_inner, weight_faces = lax.optimization_barrier((next_ghosts, final_inner, weight_faces))
    grads_now, next_weight_faces, sent, turned = call(
        functools.partial(adjoint_edge_kernel, geo, False),
        [scalar] * 4 + [kept_near] * 4 + [near, near],
        [("R", block), ("R", faces_shape), ("B", whole), far(faces_shape)],
        [faces_shape] * 2,
        few,
    )(*fixed, inner, next_faces, weight_faces, rate_faces, next_ghosts, first_ghosts)

    arrived = swap(sent)
    inner = adjoint_inner(state, far(state.shape), grads_now, kept_near)
    arrived, inner = lax.optimization_barrier((arrived, inner))
    leaving = route(arrived)
    final_inner, leaving = lax.optimization_barrier((final_inner, leaving))
    last_ghosts = swap(leaving)
    final, faces, ghosts = call(
        functools.partial(step_edge_kernel, geo, False),
        [scalar] * 4 + [far(block), far(faces_shape), kept_near, far(faces_shape), ("P", None), ("P", None)],
        [("V", block), ("R", faces_shape), ("R", faces_shape)],
        [],
        work,
        fetch=((8, 1), (9, 2)),
    )(*fixed, final_inner, kept_next_faces, rate_faces, turned, kept_faces, ghosts)
    last_ghosts, final, faces, ghosts = lax.optimization_barrier((last_ghosts, final, faces, ghosts))
    (adjoint,) = call(
        functools.partial(adjoint_edge_kernel, geo, True),
        [scalar] * 4 + [kept_near] * 4 + [near],
        [("B", block)],
        [faces_shape] * 2,
        few,
    )(*fixed, inner, faces, next_weight_faces, ghosts, last_ghosts)
    return (adjoint[None, None], final[None])


def solution(mesh):
    return jax.shard_map(
        functools.partial(on_device, mesh.shape["space"], mesh.shape["ckpt"]),
        mesh=mesh,
        in_specs=(
            P("space", None, "ckpt", None, None),
            P("ckpt", "space", None, None, None, None),
            P("space", None, None, None),
            P(),
            P(),
            P(),
            P(),
        ),
        out_specs=(P("ckpt", "space", None, None, None, None), P("space", None, None, None, None)),
        check_vma=False,
    )
```

```python
import functools

import jax
import jax.numpy as jnp
from jax import lax
from jax.experimental import pallas as pl
from jax.experimental.pallas import tpu as pltpu
from jax.sharding import PartitionSpec as P

STEPS = 2
time_step = 0.05
damping = 0.015

PAD = 8
VMEM = pl.BlockSpec(memory_space=pltpu.VMEM)
SMEM = pl.BlockSpec(memory_space=pltpu.SMEM)
VMEM_LIMIT = 16 * 1024 * 1024


class Pieces:
    def __init__(self, rows, count):
        self.rows = rows
        self.runs = [-(-length // count) for length in rows]
        self.starts = [sum(self.runs[:index]) for index in range(len(rows))]
        self.total = sum(self.runs)


class Geometry:
    def __init__(self, nvars, cx, cy, cz, count, parts):
        self.v, self.x, self.y, self.z, self.n, self.parts = nvars, cx, cy, cz, count, parts
        self.depth = cx // parts
        self.rows = [nvars * cy] * 2 + [nvars * cx] * 2 + [cy] * 2
        self.whole = Pieces(self.rows, count)
        self.part = Pieces([nvars * cy] + [nvars * self.depth] * 2 + [cy] * 2, count)
        self.face_rows = -(-max(run * count for run in self.whole.runs) // 8) * 8
        self.block = (nvars, cx, cy, cz)
        self.tall = (nvars, cx, cy + 2 * PAD, cz)
        self.faces = (6, self.face_rows, cz)
        self.rate_faces = (6, max(cx, cy), cz)

    def buffer(self, rows):
        return (self.n, -(-rows // 8) * 8, self.z)


def take_z_faces(geo, load, variables=None):
    v, x, y, z = geo.block
    lane = lax.broadcasted_iota(jnp.int32, (y, z), 1)
    high = jnp.zeros((y, z), jnp.float32)
    low = jnp.zeros((y, z), jnp.float32)
    for var in range(variables or v):
        for plane in range(x):
            place = var * x + plane
            tile = pltpu.roll(load(var, plane), place + 1, 1)
            high = jnp.where(lane == place, tile, high)
            low = jnp.where(lane == place + 1, tile, low)
    return high, pltpu.roll(low, z - 1, 1)


def repeat_lanes(geo, layer):
    total = layer
    for var in range(1, geo.v):
        total = total + pltpu.roll(layer, var * geo.x, 1)
    return total


def take_xy_faces(geo, source, faces):
    v, x, y, z = geo.block
    faces[0, : v * y] = source[:, x - 1].reshape(v * y, z)
    faces[1, : v * y] = source[:, 0].reshape(v * y, z)
    for var in range(v):
        faces[2, var * x : (var + 1) * x] = source[var, :, y - 1, :]
        faces[3, var * x : (var + 1) * x] = source[var, :, 0, :]


def cut(geo, pieces, faces, buffer, base, leave=None):
    for slot in range(geo.n):
        for index, (run, start) in enumerate(zip(pieces.runs, pieces.starts)):
            buffer[slot, base + start : base + start + run] = faces[index, slot * run : (slot + 1) * run]
        if leave:
            leave(slot)


def own_codes(geo, place, owner, orientation):
    block = jnp.int32(0)
    for index in range(geo.n):
        block = jnp.where(owner[index] == place[0], index, block)
    return [orientation[block * 6 + side] for side in range(6)]


def flip_rows(values, flag, length):
    rows, z = values.shape
    grouped = values.reshape(rows // length, length // 8, 8, z)
    index = lax.broadcasted_iota(jnp.int32, (8, z), 0)
    index = jnp.where(flag == 1, 7 - index, index)
    tiles = length // 8
    out = []
    for group in range(rows // length):
        for tile in range(tiles):
            picked = jnp.where(flag == 1, grouped[group, tiles - 1 - tile], grouped[group, tile])
            out.append(jnp.take_along_axis(picked, index, axis=0))
    return jnp.stack(out).reshape(rows, z)


def flip_lanes(values, flag, length):
    rows, z = values.shape
    lane = lax.broadcasted_iota(jnp.int32, (8, z), 1)
    within = lax.rem(lane, length)
    index = jnp.where(flag == 1, lane + (length - 1) - 2 * within, lane)
    index = jnp.minimum(index, z - 1)
    tiles = values.reshape(rows // 8, 8, z)
    return jnp.stack(
        [jnp.take_along_axis(tiles[tile], index, axis=1) for tile in range(rows // 8)]
    ).reshape(rows, z)


def join(geo, buffer, raw, base=0):
    for side in range(6):
        run, start = geo.whole.runs[side], base + geo.whole.starts[side]
        for slot in range(geo.n):
            raw[side, slot * run : (slot + 1) * run] = buffer[slot, start : start + run]


def join_parts(geo, buffer, raw, piece):
    for side in range(6):
        index = 0 if side < 2 else side - 1
        run, start = geo.part.runs[index], geo.part.starts[index]
        if side < 2:
            part = 0 if side == 0 else geo.parts - 1
            for slot in range(geo.n):
                raw[side, slot * run : (slot + 1) * run] = buffer[part, slot, start : start + run]
        elif side < 4:
            for part in range(geo.parts):
                for slot in range(geo.n):
                    piece[slot * run : (slot + 1) * run] = buffer[part, slot, start : start + run]
                for var in range(geo.v):
                    row = var * geo.x + part * geo.depth
                    raw[side, row : row + geo.depth] = piece[var * geo.depth : (var + 1) * geo.depth]
        else:
            for slot in range(geo.n):
                total = buffer[0, slot, start : start + run]
                for part in range(1, geo.parts):
                    total = total + buffer[part, slot, start : start + run]
                raw[side, slot * run : (slot + 1) * run] = total


def turn(geo, codes, raw, ghosts):
    v, x, y, z = geo.block
    for side in range(6):
        first, second = codes[side] & 1, (codes[side] >> 1) & 1
        layer = raw[side, : geo.rows[side]]
        if side < 4:
            layer = flip_lanes(flip_rows(layer, first, y if side < 2 else x), second, z)
        else:
            layer = flip_lanes(flip_rows(layer, second, y), first, x)
        ghosts[side, : geo.rows[side]] = layer


def face_values(geo, faces, side):
    v, x, y, z = geo.block
    if side < 4:
        depth = y if side < 2 else x
        return [faces[side, var * depth : (var + 1) * depth] for var in range(v)]
    layer = faces[side, :y]
    return [layer] + [pltpu.roll(layer, z - var * x, 1) for var in range(1, v)]


def fill_tall(geo, source, tall):
    v, x, y, z = geo.block
    if len(source.shape) == 5:
        depth = geo.depth
        for part in range(geo.parts):
            tall[:, part * depth : (part + 1) * depth, PAD : PAD + y, :] = source[part]
    else:
        tall[:, :, PAD : PAD + y, :] = source[...]
    for var in range(v):
        tall[var, :, PAD - 1, :] = tall[var, :, PAD, :]
        tall[var, :, PAD + y, :] = tall[var, :, PAD + y - 1, :]


def around(geo, tall, plane):
    v, x, y, z = geo.block
    lane = lax.broadcasted_iota(jnp.int32, (y, z), 1)
    before, after = jnp.maximum(plane - 1, 0), jnp.minimum(plane + 1, x - 1)
    cells, low, high = [], [[], [], []], [[], [], []]
    for var in range(v):
        mid = tall[var, plane, PAD : PAD + y]
        cells.append(mid)
        low[0].append(tall[var, before, PAD : PAD + y])
        high[0].append(tall[var, after, PAD : PAD + y])
        low[1].append(tall[var, plane, PAD - 1 : PAD - 1 + y])
        high[1].append(tall[var, plane, PAD + 1 : PAD + 1 + y])
        low[2].append(jnp.where(lane == 0, mid, pltpu.roll(mid, 1, 1)))
        high[2].append(jnp.where(lane == z - 1, mid, pltpu.roll(mid, z - 1, 1)))
    return cells, low, high


def flux_entry(geo, mats, direction, row, column):
    return mats[(direction * geo.v + row) * geo.v + column]


def step_plane(geo, mats, cells, low, high, rate):
    v = geo.v
    total = [None] * v
    for direction in range(3):
        lows, highs = low[direction], high[direction]
        mean_low = 0.5 * (lows[0] + cells[0])
        mean_high = 0.5 * (cells[0] + highs[0])
        square_low = 1.0 + mean_low * mean_low
        square_high = 1.0 + mean_high * mean_high
        spread_low = square_low * lax.rsqrt(square_low)
        spread_high = square_high * lax.rsqrt(square_high)
        slopes = [highs[var] - lows[var] for var in range(v)]
        for var in range(v):
            term = spread_low * (cells[var] - lows[var]) - spread_high * (highs[var] - cells[var])
            for column in range(v):
                term = term + flux_entry(geo, mats, direction, var, column) * slopes[column]
            total[var] = term if total[var] is None else total[var] + term
    scale = (0.5 * time_step) * rate
    return [cells[var] - scale * total[var] - damping * jnp.tanh(cells[var]) for var in range(v)]


def adjoint_plane(geo, mats, cells, low, high, grads, weight, weight_low, weight_high):
    v = geo.v
    total = [None] * v
    extra = None
    for direction in range(3):
        spreads, steps = [], []
        for lower, upper, lower_weight, upper_weight in (
            (low[direction], cells, weight_low[direction], weight),
            (cells, high[direction], weight, weight_high[direction]),
        ):
            mean = 0.5 * (lower[0] + upper[0])
            square = 1.0 + mean * mean
            inverse = lax.rsqrt(square)
            jump = [lower_weight[var] - upper_weight[var] for var in range(v)]
            product = jump[0] * (upper[0] - lower[0])
            for var in range(1, v):
                product = product + jump[var] * (upper[var] - lower[var])
            product = product * (mean * inverse)
            extra = product if extra is None else extra + product
            spreads.append(square * inverse)
            steps.append(jump)
        slopes = [steps[0][var] + steps[1][var] for var in range(v)]
        for var in range(v):
            term = spreads[1] * steps[1][var] - spreads[0] * steps[0][var]
            for row in range(v):
                term = term + flux_entry(geo, mats, direction, row, var) * slopes[row]
            total[var] = term if total[var] is None else total[var] + term
    total[0] = total[0] - 0.5 * extra
    out = []
    for var in range(v):
        bend = jnp.tanh(cells[var])
        slope = (1.0 - damping) + damping * (bend * bend)
        out.append(grads[var] * slope - (0.5 * time_step) * total[var])
    return out


def step_face(geo, mats, side, cells, ghosts, rate):
    v = geo.v
    mean = 0.5 * (cells[0] + ghosts[0])
    square = 1.0 + mean * mean
    spread = square * lax.rsqrt(square)
    gap = [ghosts[var] - cells[var] for var in range(v)]
    scale = (0.5 * time_step) * rate
    out = []
    for var in range(v):
        total = flux_entry(geo, mats, side // 2, var, 0) * gap[0]
        for column in range(1, v):
            total = total + flux_entry(geo, mats, side // 2, var, column) * gap[column]
        if side % 2 == 0:
            out.append(scale * (spread * gap[var] - total))
        else:
            out.append(scale * (spread * gap[var] + total))
    return out


def adjoint_face(geo, mats, side, cells, ghosts, weight, ghost_weight):
    v = geo.v
    mean = 0.5 * (cells[0] + ghosts[0])
    square = 1.0 + mean * mean
    inverse = lax.rsqrt(square)
    spread = square * inverse
    jump = [weight[var] - ghost_weight[var] for var in range(v)]
    product = jump[0] * (ghosts[0] - cells[0])
    for var in range(1, v):
        product = product + jump[var] * (ghosts[var] - cells[var])
    product = (0.5 * product) * (mean * inverse)
    out = []
    for var in range(v):
        total = flux_entry(geo, mats, side // 2, 0, var) * jump[0]
        for row in range(1, v):
            total = total + flux_entry(geo, mats, side // 2, row, var) * jump[row]
        if side % 2 == 0:
            total = spread * jump[var] + total
        else:
            total = spread * jump[var] - total
        if var == 0:
            total = total - product
        out.append((-0.5 * time_step) * total)
    return out


def pack_kernel(geo, late, part, stored, grads, rate, weight_faces, rate_faces, buffer, pieces):
    v, x, y, z = geo.block
    depth = geo.depth
    late.wait(1)
    lane = lax.broadcasted_iota(jnp.int32, (y, z), 1)
    plane = jnp.where(part[0] == geo.parts - 1, depth - 1, 0)
    high = jnp.zeros((y, z), jnp.float32)
    low = jnp.zeros((y, z), jnp.float32)
    for var in range(v):
        pieces[0, var * y : (var + 1) * y] = stored[var, plane]
        pieces[1, var * depth : (var + 1) * depth] = stored[var, :, y - 1, :]
        pieces[2, var * depth : (var + 1) * depth] = stored[var, :, 0, :]
        for step in range(depth):
            place = var * x + part[0] * depth + step
            tile = stored[var, step]
            here = lane == place
            high = jnp.where(here, pltpu.roll(tile, lax.rem(place + 1, z), 1), high)
            low = jnp.where(here, pltpu.roll(tile, place, 1), low)
    pieces[3, :y] = high
    pieces[4, :y] = low
    cut(geo, geo.part, pieces, buffer, 0)
    late.wait(2)
    late.wait(3)
    rate_faces[0, :y] = rate[x - 1]
    rate_faces[1, :y] = rate[0]
    rate_faces[2, :x] = rate[:, y - 1, :]
    rate_faces[3, :x] = rate[:, 0, :]
    high, low = take_z_faces(geo, lambda var, plane: rate[plane], 1)
    rate_faces[4, :y] = repeat_lanes(geo, high)
    rate_faces[5, :y] = repeat_lanes(geo, low)
    late.leave(1)
    take_weight_faces(geo, grads, rate_faces, weight_faces)
    late.leave(0)
    cut(geo, geo.whole, weight_faces, buffer, geo.part.total, functools.partial(late.leave, 2))


def take_weight_faces(geo, grads, rate_faces, faces):
    v, x, y, z = geo.block
    take_xy_faces(geo, grads, faces)
    for side in range(4):
        depth = y if side < 2 else x
        for var in range(v):
            here = slice(var * depth, (var + 1) * depth)
            faces[side, here] = faces[side, here] * rate_faces[side, :depth]
    high, low = take_z_faces(geo, lambda var, plane: grads[var, plane])
    faces[4, :y] = high * rate_faces[4, :y]
    faces[5, :y] = low * rate_faces[5, :y]


def route_whole(geo, owner, neighbours, block, arrived, leaving, base):
    for side in range(6):
        source = owner[neighbours[block * 6 + side]]
        run, start, far = geo.whole.runs[side], base + geo.whole.starts[side], base + geo.whole.starts[side ^ 1]
        leaving[owner[block], start : start + run] = arrived[source, far : far + run]


def route_kernel(geo, late, owner, neighbours, arrived, leaving):
    for block in range(geo.n):
        route_whole(geo, owner, neighbours, block, arrived, leaving, 0)
        late.leave(0, owner[block])


def route_first_kernel(geo, late, part, owner, neighbours, arrived, leaving):
    x_side = jnp.where(part[0] == geo.parts - 1, 1, 0)
    for block in range(geo.n):
        route_whole(geo, owner, neighbours, block, arrived, leaving, geo.part.total)
        for index in range(5):
            side, far_index = (x_side, 0) if index == 0 else (index + 1, ((index + 1) ^ 1) - 1)
            source = owner[neighbours[block * 6 + side]]
            run, start, far = geo.part.runs[index], geo.part.starts[index], geo.part.starts[far_index]
            leaving[owner[block], start : start + run] = arrived[source, far : far + run]
        late.leave(0, owner[block])


def turn_weights_kernel(geo, late, mats, block, rate, place, owner, orientation, buffer, result, ghosts, tall, raw):
    join(geo, buffer, raw, geo.part.total)
    turn(geo, own_codes(geo, place, owner, orientation), raw, ghosts)
    step_inner_kernel(geo, late, mats, block, rate, result, tall)


def step_inner_kernel(geo, late, mats, block, rate, result, *rest):
    tall = rest[-1]
    late.wait(1)
    late.wait(2)
    fill_tall(geo, block, tall)

    def body(plane, carry):
        cells, low, high = around(geo, tall, plane)
        for var, value in enumerate(step_plane(geo, mats, cells, low, high, rate[plane])):
            result[var, plane] = value
        return carry

    lax.fori_loop(0, geo.x, body, 0)
    late.leave(0)
    if len(rest) == 2:
        faces = rest[0]
        v, x, y, z = geo.block
        for var in range(v):
            faces[0, var * y : (var + 1) * y] = tall[var, x - 1, PAD : PAD + y]
            faces[1, var * y : (var + 1) * y] = tall[var, 0, PAD : PAD + y]
            faces[2, var * x : (var + 1) * x] = tall[var, :, PAD + y - 1, :]
            faces[3, var * x : (var + 1) * x] = tall[var, :, PAD, :]
        high, low = take_z_faces(geo, lambda var, plane: tall[var, plane, PAD : PAD + y])
        faces[4, :y] = high
        faces[5, :y] = low
        late.leave(2)


def adjoint_inner_kernel(geo, late, mats, block, grads, rate, result, tall, weights):
    v, x, y, z = geo.block
    for index in range(1, 4):
        late.wait(index)
    fill_tall(geo, block, tall)

    def scale(plane, carry):
        for var in range(v):
            weights[var, plane, PAD : PAD + y] = rate[plane] * grads[var, plane]
        return carry

    lax.fori_loop(0, x, scale, 0)
    for var in range(v):
        weights[var, :, PAD - 1, :] = weights[var, :, PAD, :]
        weights[var, :, PAD + y, :] = weights[var, :, PAD + y - 1, :]

    def body(plane, carry):
        cells, low, high = around(geo, tall, plane)
        weight, weight_low, weight_high = around(geo, weights, plane)
        here = [grads[var, plane] for var in range(v)]
        values = adjoint_plane(geo, mats, cells, low, high, here, weight, weight_low, weight_high)
        for var, value in enumerate(values):
            result[var, plane] = value
        return carry

    lax.fori_loop(0, x, body, 0)


def add_terms(geo, values, inner, result, leave=None):
    v, x, y, z = geo.block
    lane = lax.broadcasted_iota(jnp.int32, (y, z), 1)
    zero = jnp.zeros((y, z), jnp.float32)
    ends = (lane == 0) | (lane == z - 1)
    even = lane % 2 == 0
    for var in range(v):
        high, low = values[4][var], pltpu.roll(values[5][var], 1, 1)
        mixed = (jnp.where(even, high, low), jnp.where(even, low, high))
        for plane in range(x):
            change = jnp.where(ends, pltpu.roll(mixed[plane % 2], z - 1 - plane, 1), zero)
            if plane == 0:
                change = change + values[1][var]
            if plane == x - 1:
                change = change + values[0][var]
            result[var, plane] = inner[var, plane] + change
        result[var, :, y - 1, :] = result[var, :, y - 1, :] + values[2][var]
        result[var, :, 0, :] = result[var, :, 0, :] + values[3][var]
        if leave:
            leave(var)


def step_edge_kernel(geo, first, late, place, owner, orientation, mats, inner, faces, rate_faces, arrived, result, *rest):
    v, x, y, z = geo.block
    if first:
        new_faces, sent, ghosts, raw, piece = rest
        join_parts(geo, arrived, raw, piece)
        turn(geo, own_codes(geo, place, owner, orientation), raw, ghosts)
        late.leave(4)
    else:
        ghosts = arrived
        late.wait(4)
        late.wait(7)
    late.wait(5)
    values = []
    for side in range(6):
        depth = y if side < 2 or side > 3 else x
        cells, outer = face_values(geo, faces, side), face_values(geo, ghosts, side)
        values.append(step_face(geo, mats, side, cells, outer, rate_faces[side, :depth]))
    add_terms(geo, values, inner, result)
    if first:
        take_xy_faces(geo, result, new_faces)
        high, low = take_z_faces(geo, lambda var, plane: result[var, plane])
        new_faces[4, :y] = high
        new_faces[5, :y] = low
        cut(geo, geo.whole, new_faces, sent, 0, functools.partial(late.leave, 3))
        late.leave(2)


def adjoint_edge_kernel(geo, last, late, place, owner, orientation, mats, inner, faces, weight_faces, *rest):
    v, x, y, z = geo.block
    codes = own_codes(geo, place, owner, orientation)
    if last:
        ghosts, weight_buffer, result, raw, weight_ghosts = rest
        join(geo, weight_buffer, raw)
        turn(geo, codes, raw, weight_ghosts)
    else:
        rate_faces, buffer, weight_ghosts, result, new_faces, sent, ghosts, raw = rest
        join(geo, buffer, raw)
        turn(geo, codes, raw, ghosts)
        late.leave(3)
    values = []
    for side in range(6):
        views = [face_values(geo, field, side) for field in (faces, ghosts, weight_faces, weight_ghosts)]
        values.append(adjoint_face(geo, mats, side, *views))
    add_terms(geo, values, inner, result, functools.partial(late.leave, 0) if last else None)
    if not last:
        take_weight_faces(geo, result, rate_faces, new_faces)
        cut(geo, geo.whole, new_faces, sent, 0, functools.partial(late.leave, 2))


class Late:
    def __init__(self, arrivals, departures, sems):
        self.arrivals, self.departures, self.sems, self.started = arrivals, departures, sems, []

    def wait(self, index):
        if index in self.arrivals:
            self.arrivals[index].wait()

    def leave(self, index, slot=None):
        if index in self.departures:
            source, target = self.departures[index]
            if slot is not None:
                source, target = source.at[slot], target.at[slot]
            copy = pltpu.make_async_copy(source, target, self.sems.at[len(self.started)])
            copy.start()
            self.started.append(copy)


def call(kernel, ins, outs, scratch, flops, fetch=()):
    late_in = [(index, shape) for index, (kind, shape) in enumerate(ins) if kind == "H"]
    late_out = [(index, shape) for index, (kind, shape) in enumerate(outs) if kind in "HB"]
    count_in, count_out = len(late_in), len(late_out)
    sends = sum(shape[0] if kind == "B" else 1 for kind, shape in outs if kind in "HBD")

    def body(*refs):
        given = list(refs[: len(ins)])
        made = list(refs[len(ins) : len(ins) + len(outs)])
        rest = list(refs[len(ins) + len(outs) :])
        own = rest[: len(scratch)]
        stage = rest[len(scratch) : len(scratch) + count_in + count_out]
        sems_in = rest[len(scratch) + count_in + count_out] if count_in or fetch else None
        sems_out = rest[-1] if sends else None
        arrivals, departures = {}, {}
        for slot, (index, _) in enumerate(late_in):
            copy = pltpu.make_async_copy(given[index], stage[slot], sems_in.at[slot])
            copy.start()
            arrivals[index] = copy
            given[index] = stage[slot]
        for slot, (index, _) in enumerate(late_out):
            departures[index] = (stage[count_in + slot], made[index])
            made[index] = stage[count_in + slot]
        for index, (kind, _) in enumerate(outs):
            if kind == "D":
                departures[index] = (made[index - 1], made[index])
        fetched = []
        for slot, (source, target) in enumerate(fetch):
            copy = pltpu.make_async_copy(given[source], made[target], sems_in.at[count_in + slot])
            copy.start()
            fetched.append(copy)
        late = Late(arrivals, departures, sems_out)
        hidden_in = {source for source, _ in fetch}
        hidden_out = {target for _, target in fetch}
        kernel(
            late,
            *[ref for index, ref in enumerate(given) if index not in hidden_in],
            *[ref for index, ref in enumerate(made) if index not in hidden_out and outs[index][0] != "D"],
            *own,
        )
        assert len(late.started) == sends
        for copy in fetched + late.started:
            copy.wait()

    hbm = pl.BlockSpec(memory_space=pltpu.HBM)
    specs = {"S": SMEM, "V": VMEM, "R": VMEM, "H": hbm, "B": hbm, "D": hbm, "P": hbm}
    scratch_shapes = [pltpu.VMEM(shape, jnp.float32) for shape in scratch]
    scratch_shapes += [pltpu.VMEM(shape, jnp.float32) for _, shape in late_in + late_out]
    if count_in or fetch:
        scratch_shapes.append(pltpu.SemaphoreType.DMA((count_in + len(fetch),)))
    if sends:
        scratch_shapes.append(pltpu.SemaphoreType.DMA((sends,)))
    shapes = {"V": jax.ShapeDtypeStruct, "R": pltpu.VMEM, "H": pltpu.HBM, "B": pltpu.HBM, "D": pltpu.HBM}
    invoke = pl.pallas_call(
        body,
        in_specs=[specs[kind] for kind, _ in ins],
        out_specs=[specs[kind] for kind, _ in outs],
        out_shape=[shapes[kind](shape, jnp.float32) for kind, shape in outs],
        scratch_shapes=scratch_shapes,
        compiler_params=pltpu.CompilerParams(vmem_limit_bytes=VMEM_LIMIT),
        cost_estimate=pl.CostEstimate(flops=flops, bytes_accessed=3 << 20, transcendentals=0),
    )

    def run(*operands):
        placed = {"H": pltpu.HBM, "R": pltpu.VMEM, "P": pltpu.HBM}
        return invoke(
            *[
                pltpu.with_memory_space_constraint(operand, placed[kind]) if kind in placed else operand
                for operand, (kind, _) in zip(operands, ins)
            ]
        )

    return run


def on_device(count, parts, checkpoint, seeds, cell_rate, flux_mats, owner, neighbours, orientation):
    nvars, cx, cy, cz = seeds.shape[2:]
    geo = Geometry(nvars, cx, cy, cz, count, parts)
    rate = cell_rate[0]
    grads = seeds[0, 0]
    place = lax.axis_index("space").astype(jnp.int32).reshape(1)
    part = lax.axis_index("ckpt").astype(jnp.int32).reshape(1)
    mats = flux_mats.reshape(-1)
    neighbours = neighbours.reshape(-1)
    orientation = orientation.reshape(-1)
    fixed = (place, owner, orientation, mats)
    work = nvars * nvars * 3 * 4 * cx * cy * cz
    few = work // 16
    whole, both = geo.buffer(geo.whole.total), geo.buffer(geo.part.total + geo.whole.total)
    some = -(-geo.part.total // 8) * 8

    stored_shape, block, faces_shape = checkpoint.shape[1:], geo.block, geo.faces
    rate_block = cell_rate.shape[1:]
    scalar, near, kept_near = ("S", None), ("V", None), ("R", None)

    def far(shape):
        return ("H", shape)

    def swap(buffer):
        return lax.all_to_all(buffer, "space", 0, 0, tiled=True)

    def route(arrived):
        return call(functools.partial(route_kernel, geo), [scalar, scalar, near], [("B", whole)], [], few)(
            owner, neighbours, arrived
        )[0]

    def adjoint_inner(state, state_kind, grads, grads_kind):
        return call(
            functools.partial(adjoint_inner_kernel, geo),
            [scalar, state_kind, grads_kind, far(rate_block)],
            [("R", block)],
            [geo.tall] * 2,
            2 * work,
        )(mats, state, grads, rate)[0]

    weight_faces, rate_faces, sent = call(
        functools.partial(pack_kernel, geo),
        [scalar, far(stored_shape), far(block), far(rate_block)],
        [far(faces_shape), ("R", geo.rate_faces), ("B", both)],
        [faces_shape],
        few,
    )(part, checkpoint[0], grads, rate)
    kept, sent = lax.optimization_barrier((checkpoint[0], sent))
    arrived = swap(sent)
    state = lax.all_gather(kept, "ckpt", axis=0)
    arrived, state = lax.optimization_barrier((arrived, state))
    (leaving,) = call(functools.partial(route_first_kernel, geo), [scalar] * 3 + [near], [("B", both)], [], few)(
        part, owner, neighbours, arrived
    )
    first_ghosts = swap(leaving)
    inner, faces, kept_faces = call(
        functools.partial(step_inner_kernel, geo),
        [scalar, far(state.shape), far(rate_block)],
        [("R", block), ("R", faces_shape), ("D", faces_shape)],
        [geo.tall],
        work,
    )(mats, state, rate)
    first_ghosts, inner, faces = lax.optimization_barrier((first_ghosts, inner, faces))
    gathered = lax.all_gather(first_ghosts[:, :some], "ckpt", axis=0)
    next_state, next_faces, kept_next_faces, sent, ghosts = call(
        functools.partial(step_edge_kernel, geo, True),
        [scalar] * 4 + [kept_near] * 3 + [near],
        [("R", block), ("R", faces_shape), ("D", faces_shape), ("B", whole), far(faces_shape)],
        [faces_shape, faces_shape[1:]],
        few,
    )(*fixed, inner, faces, rate_faces, gathered)

    arrived = swap(sent)
    inner = adjoint_inner(next_state, kept_near, grads, far(block))
    arrived, inner = lax.optimization_barrier((arrived, inner))
    leaving = route(arrived)
    later_state, leaving = lax.optimization_barrier((next_state, leaving))
    next_ghosts = swap(leaving)
    final_inner, weight_ghosts, weight_faces = call(
        functools.partial(turn_weights_kernel, geo),
        [scalar, kept_near, far(rate_block)] + [scalar] * 3 + [near, ("P", None)],
        [far(block), ("R", faces_shape), ("R", faces_shape)],
        [geo.tall, faces_shape],
        work,
        fetch=((7, 2),),
    )(mats, later_state, rate, place, owner, orientation, first_ghosts, weight_faces)
    next_ghosts, final_inner, weight_ghosts, weight_faces = lax.optimization_barrier(
        (next_ghosts, final_inner, weight_ghosts, weight_faces)
    )
    grads_now, next_weight_faces, sent, turned = call(
        functools.partial(adjoint_edge_kernel, geo, False),
        [scalar] * 4 + [kept_near] * 4 + [near, kept_near],
        [("R", block), ("R", faces_shape), ("B", whole), far(faces_shape)],
        [faces_shape],
        few,
    )(*fixed, inner, next_faces, weight_faces, rate_faces, next_ghosts, weight_ghosts)

    arrived = swap(sent)
    inner = adjoint_inner(state, far(state.shape), grads_now, kept_near)
    arrived, inner = lax.optimization_barrier((arrived, inner))
    leaving = route(arrived)
    final_inner, leaving = lax.optimization_barrier((final_inner, leaving))
    last_ghosts = swap(leaving)
    final, faces, ghosts = call(
        functools.partial(step_edge_kernel, geo, False),
        [scalar] * 4 + [far(block), far(faces_shape), kept_near, far(faces_shape), ("P", None), ("P", None)],
        [("V", block), ("R", faces_shape), ("R", faces_shape)],
        [],
        work,
        fetch=((8, 1), (9, 2)),
    )(*fixed, final_inner, kept_next_faces, rate_faces, turned, kept_faces, ghosts)
    last_ghosts, final, faces, ghosts = lax.optimization_barrier((last_ghosts, final, faces, ghosts))
    (adjoint,) = call(
        functools.partial(adjoint_edge_kernel, geo, True),
        [scalar] * 4 + [kept_near] * 4 + [near],
        [("B", block)],
        [faces_shape] * 2,
        few,
    )(*fixed, inner, faces, next_weight_faces, ghosts, last_ghosts)
    return (adjoint[None, None], final[None])


def solution(mesh):
    return jax.shard_map(
        functools.partial(on_device, mesh.shape["space"], mesh.shape["ckpt"]),
        mesh=mesh,
        in_specs=(
            P("space", None, "ckpt", None, None),
            P("ckpt", "space", None, None, None, None),
            P("space", None, None, None),
            P(),
            P(),
            P(),
            P(),
        ),
        out_specs=(P("ckpt", "space", None, None, None, None), P("space", None, None, None, None)),
        check_vma=False,
    )
```

```python
import functools

import jax
import jax.numpy as jnp
from jax import lax
from jax.experimental import pallas as pl
from jax.experimental.pallas import tpu as pltpu
from jax.sharding import PartitionSpec as P

STEPS = 2
time_step = 0.05
damping = 0.015

PAD = 8
VMEM = pl.BlockSpec(memory_space=pltpu.VMEM)
SMEM = pl.BlockSpec(memory_space=pltpu.SMEM)
VMEM_LIMIT = 16 * 1024 * 1024


class Pieces:
    def __init__(self, rows, count):
        self.rows = rows
        self.runs = [-(-length // count) for length in rows]
        self.starts = [sum(self.runs[:index]) for index in range(len(rows))]
        self.total = sum(self.runs)


class Geometry:
    def __init__(self, nvars, cx, cy, cz, count, parts):
        self.v, self.x, self.y, self.z, self.n, self.parts = nvars, cx, cy, cz, count, parts
        self.depth = cx // parts
        self.rows = [nvars * cy] * 2 + [nvars * cx] * 2 + [cy] * 2
        self.whole = Pieces(self.rows, count)
        self.part = Pieces([nvars * cy] + [nvars * self.depth] * 2 + [cy] * 2, count)
        self.face_rows = -(-max(run * count for run in self.whole.runs) // 8) * 8
        self.block = (nvars, cx, cy, cz)
        self.tall = (nvars, cx, cy + 2 * PAD, cz)
        self.faces = (6, self.face_rows, cz)
        self.rate_faces = (6, max(cx, cy), cz)

    def buffer(self, rows):
        return (self.n, -(-rows // 8) * 8, self.z)


def take_z_faces(geo, load, variables=None):
    v, x, y, z = geo.block
    lane = lax.broadcasted_iota(jnp.int32, (y, z), 1)
    high = jnp.zeros((y, z), jnp.float32)
    low = jnp.zeros((y, z), jnp.float32)
    for var in range(variables or v):
        for plane in range(x):
            place = var * x + plane
            tile = pltpu.roll(load(var, plane), place + 1, 1)
            high = jnp.where(lane == place, tile, high)
            low = jnp.where(lane == place + 1, tile, low)
    return high, pltpu.roll(low, z - 1, 1)


def repeat_lanes(geo, layer):
    total = layer
    for var in range(1, geo.v):
        total = total + pltpu.roll(layer, var * geo.x, 1)
    return total


def take_xy_faces(geo, source, faces):
    v, x, y, z = geo.block
    faces[0, : v * y] = source[:, x - 1].reshape(v * y, z)
    faces[1, : v * y] = source[:, 0].reshape(v * y, z)
    for var in range(v):
        faces[2, var * x : (var + 1) * x] = source[var, :, y - 1, :]
        faces[3, var * x : (var + 1) * x] = source[var, :, 0, :]


def cut(geo, pieces, faces, buffer, base, leave=None):
    for slot in range(geo.n):
        for index, (run, start) in enumerate(zip(pieces.runs, pieces.starts)):
            buffer[slot, base + start : base + start + run] = faces[index, slot * run : (slot + 1) * run]
        if leave:
            leave(slot)


class Table:
    def __init__(self, geo, ref):
        self.ref, self.n = ref, geo.n

    def place(self):
        return self.ref[0]

    def part(self):
        return self.ref[1]

    def owner(self, block):
        return self.ref[2 + block]

    def neighbour(self, block, side):
        return self.ref[2 + self.n + block * 6 + side]

    def orientation(self, block, side):
        return self.ref[2 + 7 * self.n + block * 6 + side]


def own_codes(geo, table):
    table = Table(geo, table)
    block = jnp.int32(0)
    for index in range(geo.n):
        block = jnp.where(table.owner(index) == table.place(), index, block)
    return [table.orientation(block, side) for side in range(6)]


def flip_rows(values, flag, length):
    rows, z = values.shape
    grouped = values.reshape(rows // length, length // 8, 8, z)
    index = lax.broadcasted_iota(jnp.int32, (8, z), 0)
    index = jnp.where(flag == 1, 7 - index, index)
    tiles = length // 8
    out = []
    for group in range(rows // length):
        for tile in range(tiles):
            picked = jnp.where(flag == 1, grouped[group, tiles - 1 - tile], grouped[group, tile])
            out.append(jnp.take_along_axis(picked, index, axis=0))
    return jnp.stack(out).reshape(rows, z)


def flip_lanes(values, flag, length):
    rows, z = values.shape
    lane = lax.broadcasted_iota(jnp.int32, (8, z), 1)
    within = lax.rem(lane, length)
    index = jnp.where(flag == 1, lane + (length - 1) - 2 * within, lane)
    index = jnp.minimum(index, z - 1)
    tiles = values.reshape(rows // 8, 8, z)
    return jnp.stack(
        [jnp.take_along_axis(tiles[tile], index, axis=1) for tile in range(rows // 8)]
    ).reshape(rows, z)


def join(geo, buffer, raw, base=0):
    for side in range(6):
        run, start = geo.whole.runs[side], base + geo.whole.starts[side]
        for slot in range(geo.n):
            raw[side, slot * run : (slot + 1) * run] = buffer[slot, start : start + run]


def join_parts(geo, buffer, raw, piece):
    for side in range(6):
        index = 0 if side < 2 else side - 1
        run, start = geo.part.runs[index], geo.part.starts[index]
        if side < 2:
            part = 0 if side == 0 else geo.parts - 1
            for slot in range(geo.n):
                raw[side, slot * run : (slot + 1) * run] = buffer[part, slot, start : start + run]
        elif side < 4:
            for part in range(geo.parts):
                for slot in range(geo.n):
                    piece[slot * run : (slot + 1) * run] = buffer[part, slot, start : start + run]
                for var in range(geo.v):
                    row = var * geo.x + part * geo.depth
                    raw[side, row : row + geo.depth] = piece[var * geo.depth : (var + 1) * geo.depth]
        else:
            for slot in range(geo.n):
                total = buffer[0, slot, start : start + run]
                for part in range(1, geo.parts):
                    total = total + buffer[part, slot, start : start + run]
                raw[side, slot * run : (slot + 1) * run] = total


def turn(geo, codes, raw, ghosts):
    v, x, y, z = geo.block
    for side in range(6):
        first, second = codes[side] & 1, (codes[side] >> 1) & 1
        layer = raw[side, : geo.rows[side]]
        if side < 4:
            layer = flip_lanes(flip_rows(layer, first, y if side < 2 else x), second, z)
        else:
            layer = flip_lanes(flip_rows(layer, second, y), first, x)
        ghosts[side, : geo.rows[side]] = layer


def face_values(geo, faces, side):
    v, x, y, z = geo.block
    if side < 4:
        depth = y if side < 2 else x
        return [faces[side, var * depth : (var + 1) * depth] for var in range(v)]
    layer = faces[side, :y]
    return [layer] + [pltpu.roll(layer, z - var * x, 1) for var in range(1, v)]


def fill_tall(geo, source, tall):
    v, x, y, z = geo.block
    if len(source.shape) == 5:
        depth = geo.depth
        for part in range(geo.parts):
            tall[:, part * depth : (part + 1) * depth, PAD : PAD + y, :] = source[part]
    else:
        tall[:, :, PAD : PAD + y, :] = source[...]
    for var in range(v):
        tall[var, :, PAD - 1, :] = tall[var, :, PAD, :]
        tall[var, :, PAD + y, :] = tall[var, :, PAD + y - 1, :]


def around(geo, tall, plane):
    v, x, y, z = geo.block
    lane = lax.broadcasted_iota(jnp.int32, (y, z), 1)
    before, after = jnp.maximum(plane - 1, 0), jnp.minimum(plane + 1, x - 1)
    cells, low, high = [], [[], [], []], [[], [], []]
    for var in range(v):
        mid = tall[var, plane, PAD : PAD + y]
        cells.append(mid)
        low[0].append(tall[var, before, PAD : PAD + y])
        high[0].append(tall[var, after, PAD : PAD + y])
        low[1].append(tall[var, plane, PAD - 1 : PAD - 1 + y])
        high[1].append(tall[var, plane, PAD + 1 : PAD + 1 + y])
        low[2].append(jnp.where(lane == 0, mid, pltpu.roll(mid, 1, 1)))
        high[2].append(jnp.where(lane == z - 1, mid, pltpu.roll(mid, z - 1, 1)))
    return cells, low, high


def flux_entry(geo, mats, direction, row, column):
    return mats[(direction * geo.v + row) * geo.v + column]


def step_plane(geo, mats, cells, low, high, rate):
    v = geo.v
    total = [None] * v
    for direction in range(3):
        lows, highs = low[direction], high[direction]
        mean_low = 0.5 * (lows[0] + cells[0])
        mean_high = 0.5 * (cells[0] + highs[0])
        square_low = 1.0 + mean_low * mean_low
        square_high = 1.0 + mean_high * mean_high
        spread_low = square_low * lax.rsqrt(square_low)
        spread_high = square_high * lax.rsqrt(square_high)
        slopes = [highs[var] - lows[var] for var in range(v)]
        for var in range(v):
            term = spread_low * (cells[var] - lows[var]) - spread_high * (highs[var] - cells[var])
            for column in range(v):
                term = term + flux_entry(geo, mats, direction, var, column) * slopes[column]
            total[var] = term if total[var] is None else total[var] + term
    scale = (0.5 * time_step) * rate
    return [cells[var] - scale * total[var] - damping * jnp.tanh(cells[var]) for var in range(v)]


def adjoint_plane(geo, mats, cells, low, high, grads, weight, weight_low, weight_high):
    v = geo.v
    total = [None] * v
    extra = None
    for direction in range(3):
        spreads, steps = [], []
        for lower, upper, lower_weight, upper_weight in (
            (low[direction], cells, weight_low[direction], weight),
            (cells, high[direction], weight, weight_high[direction]),
        ):
            mean = 0.5 * (lower[0] + upper[0])
            square = 1.0 + mean * mean
            inverse = lax.rsqrt(square)
            jump = [lower_weight[var] - upper_weight[var] for var in range(v)]
            product = jump[0] * (upper[0] - lower[0])
            for var in range(1, v):
                product = product + jump[var] * (upper[var] - lower[var])
            product = product * (mean * inverse)
            extra = product if extra is None else extra + product
            spreads.append(square * inverse)
            steps.append(jump)
        slopes = [steps[0][var] + steps[1][var] for var in range(v)]
        for var in range(v):
            term = spreads[1] * steps[1][var] - spreads[0] * steps[0][var]
            for row in range(v):
                term = term + flux_entry(geo, mats, direction, row, var) * slopes[row]
            total[var] = term if total[var] is None else total[var] + term
    total[0] = total[0] - 0.5 * extra
    out = []
    for var in range(v):
        bend = jnp.tanh(cells[var])
        slope = (1.0 - damping) + damping * (bend * bend)
        out.append(grads[var] * slope - (0.5 * time_step) * total[var])
    return out


def step_face(geo, mats, side, cells, ghosts, rate):
    v = geo.v
    mean = 0.5 * (cells[0] + ghosts[0])
    square = 1.0 + mean * mean
    spread = square * lax.rsqrt(square)
    gap = [ghosts[var] - cells[var] for var in range(v)]
    scale = (0.5 * time_step) * rate
    out = []
    for var in range(v):
        total = flux_entry(geo, mats, side // 2, var, 0) * gap[0]
        for column in range(1, v):
            total = total + flux_entry(geo, mats, side // 2, var, column) * gap[column]
        if side % 2 == 0:
            out.append(scale * (spread * gap[var] - total))
        else:
            out.append(scale * (spread * gap[var] + total))
    return out


def adjoint_face(geo, mats, side, cells, ghosts, weight, ghost_weight):
    v = geo.v
    mean = 0.5 * (cells[0] + ghosts[0])
    square = 1.0 + mean * mean
    inverse = lax.rsqrt(square)
    spread = square * inverse
    jump = [weight[var] - ghost_weight[var] for var in range(v)]
    product = jump[0] * (ghosts[0] - cells[0])
    for var in range(1, v):
        product = product + jump[var] * (ghosts[var] - cells[var])
    product = (0.5 * product) * (mean * inverse)
    out = []
    for var in range(v):
        total = flux_entry(geo, mats, side // 2, 0, var) * jump[0]
        for row in range(1, v):
            total = total + flux_entry(geo, mats, side // 2, row, var) * jump[row]
        if side % 2 == 0:
            total = spread * jump[var] + total
        else:
            total = spread * jump[var] - total
        if var == 0:
            total = total - product
        out.append((-0.5 * time_step) * total)
    return out


def pack_kernel(geo, late, part, stored, grads, rate, weight_faces, rate_faces, buffer, pieces):
    v, x, y, z = geo.block
    depth = geo.depth
    late.wait(1)
    lane = lax.broadcasted_iota(jnp.int32, (y, z), 1)
    plane = jnp.where(part[0] == geo.parts - 1, depth - 1, 0)
    high = jnp.zeros((y, z), jnp.float32)
    low = jnp.zeros((y, z), jnp.float32)
    for var in range(v):
        pieces[0, var * y : (var + 1) * y] = stored[var, plane]
        pieces[1, var * depth : (var + 1) * depth] = stored[var, :, y - 1, :]
        pieces[2, var * depth : (var + 1) * depth] = stored[var, :, 0, :]
        for step in range(depth):
            place = var * x + part[0] * depth + step
            tile = stored[var, step]
            here = lane == place
            high = jnp.where(here, pltpu.roll(tile, lax.rem(place + 1, z), 1), high)
            low = jnp.where(here, pltpu.roll(tile, place, 1), low)
    pieces[3, :y] = high
    pieces[4, :y] = low
    cut(geo, geo.part, pieces, buffer, 0)
    late.wait(2)
    late.wait(3)
    rate_faces[0, :y] = rate[x - 1]
    rate_faces[1, :y] = rate[0]
    rate_faces[2, :x] = rate[:, y - 1, :]
    rate_faces[3, :x] = rate[:, 0, :]
    high, low = take_z_faces(geo, lambda var, plane: rate[plane], 1)
    rate_faces[4, :y] = repeat_lanes(geo, high)
    rate_faces[5, :y] = repeat_lanes(geo, low)
    late.leave(1)
    take_weight_faces(geo, grads, rate_faces, weight_faces)
    late.leave(0)
    cut(geo, geo.whole, weight_faces, buffer, geo.part.total, functools.partial(late.leave, 2))


def take_weight_faces(geo, grads, rate_faces, faces):
    v, x, y, z = geo.block
    take_xy_faces(geo, grads, faces)
    for side in range(4):
        depth = y if side < 2 else x
        for var in range(v):
            here = slice(var * depth, (var + 1) * depth)
            faces[side, here] = faces[side, here] * rate_faces[side, :depth]
    high, low = take_z_faces(geo, lambda var, plane: grads[var, plane])
    faces[4, :y] = high * rate_faces[4, :y]
    faces[5, :y] = low * rate_faces[5, :y]


def route_whole(geo, table, block, arrived, leaving, base):
    for side in range(6):
        source = table.owner(table.neighbour(block, side))
        run, start, far = geo.whole.runs[side], base + geo.whole.starts[side], base + geo.whole.starts[side ^ 1]
        leaving[table.owner(block), start : start + run] = arrived[source, far : far + run]


def route_kernel(geo, late, table, arrived, leaving):
    table = Table(geo, table)
    for block in range(geo.n):
        route_whole(geo, table, block, arrived, leaving, 0)
        late.leave(0, table.owner(block))


def route_first_kernel(geo, late, table, arrived, leaving):
    table = Table(geo, table)
    x_side = jnp.where(table.part() == geo.parts - 1, 1, 0)
    for block in range(geo.n):
        route_whole(geo, table, block, arrived, leaving, geo.part.total)
        for index in range(5):
            side, far_index = (x_side, 0) if index == 0 else (index + 1, ((index + 1) ^ 1) - 1)
            source = table.owner(table.neighbour(block, side))
            run, start, far = geo.part.runs[index], geo.part.starts[index], geo.part.starts[far_index]
            leaving[table.owner(block), start : start + run] = arrived[source, far : far + run]
        late.leave(0, table.owner(block))


def turn_weights_kernel(geo, late, mats, block, rate, table, buffer, result, ghosts, tall, raw):
    join(geo, buffer, raw, geo.part.total)
    turn(geo, own_codes(geo, table), raw, ghosts)
    step_inner_kernel(geo, late, mats, block, rate, result, tall)


def step_inner_kernel(geo, late, mats, block, rate, result, *rest):
    tall = rest[-1]
    late.wait(1)
    late.wait(2)
    fill_tall(geo, block, tall)

    def body(plane, carry):
        cells, low, high = around(geo, tall, plane)
        for var, value in enumerate(step_plane(geo, mats, cells, low, high, rate[plane])):
            result[var, plane] = value
        return carry

    lax.fori_loop(0, geo.x, body, 0)
    late.leave(0)
    if len(rest) == 2:
        faces = rest[0]
        v, x, y, z = geo.block
        for var in range(v):
            faces[0, var * y : (var + 1) * y] = tall[var, x - 1, PAD : PAD + y]
            faces[1, var * y : (var + 1) * y] = tall[var, 0, PAD : PAD + y]
            faces[2, var * x : (var + 1) * x] = tall[var, :, PAD + y - 1, :]
            faces[3, var * x : (var + 1) * x] = tall[var, :, PAD, :]
        high, low = take_z_faces(geo, lambda var, plane: tall[var, plane, PAD : PAD + y])
        faces[4, :y] = high
        faces[5, :y] = low
        late.leave(2)


def adjoint_inner_kernel(geo, late, mats, block, grads, rate, result, tall, weights):
    v, x, y, z = geo.block
    for index in range(1, 4):
        late.wait(index)
    fill_tall(geo, block, tall)

    def scale(plane, carry):
        for var in range(v):
            weights[var, plane, PAD : PAD + y] = rate[plane] * grads[var, plane]
        return carry

    lax.fori_loop(0, x, scale, 0)
    for var in range(v):
        weights[var, :, PAD - 1, :] = weights[var, :, PAD, :]
        weights[var, :, PAD + y, :] = weights[var, :, PAD + y - 1, :]

    def body(plane, carry):
        cells, low, high = around(geo, tall, plane)
        weight, weight_low, weight_high = around(geo, weights, plane)
        here = [grads[var, plane] for var in range(v)]
        values = adjoint_plane(geo, mats, cells, low, high, here, weight, weight_low, weight_high)
        for var, value in enumerate(values):
            result[var, plane] = value
        return carry

    lax.fori_loop(0, x, body, 0)


def add_terms(geo, values, inner, result, leave=None):
    v, x, y, z = geo.block
    lane = lax.broadcasted_iota(jnp.int32, (y, z), 1)
    zero = jnp.zeros((y, z), jnp.float32)
    ends = (lane == 0) | (lane == z - 1)
    even = lane % 2 == 0
    for var in range(v):
        high, low = values[4][var], pltpu.roll(values[5][var], 1, 1)
        mixed = (jnp.where(even, high, low), jnp.where(even, low, high))
        for plane in range(x):
            change = jnp.where(ends, pltpu.roll(mixed[plane % 2], z - 1 - plane, 1), zero)
            if plane == 0:
                change = change + values[1][var]
            if plane == x - 1:
                change = change + values[0][var]
            result[var, plane] = inner[var, plane] + change
        result[var, :, y - 1, :] = result[var, :, y - 1, :] + values[2][var]
        result[var, :, 0, :] = result[var, :, 0, :] + values[3][var]
        if leave:
            leave(var)


def step_edge_kernel(geo, first, late, table, mats, inner, faces, rate_faces, arrived, result, *rest):
    v, x, y, z = geo.block
    if first:
        new_faces, sent, ghosts, raw, piece = rest
        join_parts(geo, arrived, raw, piece)
        turn(geo, own_codes(geo, table), raw, ghosts)
        late.leave(4)
    else:
        ghosts = arrived
        late.wait(2)
        late.wait(5)
    late.wait(3)
    values = []
    for side in range(6):
        depth = y if side < 2 or side > 3 else x
        cells, outer = face_values(geo, faces, side), face_values(geo, ghosts, side)
        values.append(step_face(geo, mats, side, cells, outer, rate_faces[side, :depth]))
    add_terms(geo, values, inner, result)
    if first:
        take_xy_faces(geo, result, new_faces)
        high, low = take_z_faces(geo, lambda var, plane: result[var, plane])
        new_faces[4, :y] = high
        new_faces[5, :y] = low
        cut(geo, geo.whole, new_faces, sent, 0, functools.partial(late.leave, 3))
        late.leave(2)


def adjoint_edge_kernel(geo, last, late, table, mats, inner, faces, weight_faces, *rest):
    v, x, y, z = geo.block
    codes = own_codes(geo, table)
    if last:
        ghosts, weight_buffer, result, raw, weight_ghosts = rest
        join(geo, weight_buffer, raw)
        turn(geo, codes, raw, weight_ghosts)
    else:
        rate_faces, buffer, weight_ghosts, result, new_faces, sent, ghosts, raw = rest
        join(geo, buffer, raw)
        turn(geo, codes, raw, ghosts)
        late.leave(3)
    values = []
    for side in range(6):
        views = [face_values(geo, field, side) for field in (faces, ghosts, weight_faces, weight_ghosts)]
        values.append(adjoint_face(geo, mats, side, *views))
    add_terms(geo, values, inner, result, functools.partial(late.leave, 0) if last else None)
    if not last:
        take_weight_faces(geo, result, rate_faces, new_faces)
        cut(geo, geo.whole, new_faces, sent, 0, functools.partial(late.leave, 2))


class Late:
    def __init__(self, arrivals, departures, sems):
        self.arrivals, self.departures, self.sems, self.started = arrivals, departures, sems, []

    def wait(self, index):
        if index in self.arrivals:
            self.arrivals[index].wait()

    def leave(self, index, slot=None):
        if index in self.departures:
            source, target = self.departures[index]
            if slot is not None:
                source, target = source.at[slot], target.at[slot]
            copy = pltpu.make_async_copy(source, target, self.sems.at[len(self.started)])
            copy.start()
            self.started.append(copy)


def call(kernel, ins, outs, scratch, flops, fetch=(), aliases=None):
    late_in = [(index, shape) for index, (kind, shape) in enumerate(ins) if kind == "H"]
    late_out = [(index, shape) for index, (kind, shape) in enumerate(outs) if kind in "HB"]
    count_in, count_out = len(late_in), len(late_out)
    sends = sum(shape[0] if kind == "B" else 1 for kind, shape in outs if kind in "HBD")

    def body(*refs):
        given = list(refs[: len(ins)])
        made = list(refs[len(ins) : len(ins) + len(outs)])
        rest = list(refs[len(ins) + len(outs) :])
        own = rest[: len(scratch)]
        stage = rest[len(scratch) : len(scratch) + count_in + count_out]
        sems_in = rest[len(scratch) + count_in + count_out] if count_in or fetch else None
        sems_out = rest[-1] if sends else None
        arrivals, departures = {}, {}
        for slot, (index, _) in enumerate(late_in):
            copy = pltpu.make_async_copy(given[index], stage[slot], sems_in.at[slot])
            copy.start()
            arrivals[index] = copy
            given[index] = stage[slot]
        for slot, (index, _) in enumerate(late_out):
            departures[index] = (stage[count_in + slot], made[index])
            made[index] = stage[count_in + slot]
        for index, (kind, _) in enumerate(outs):
            if kind == "D":
                departures[index] = (made[index - 1], made[index])
        fetched = []
        for slot, (source, target) in enumerate(fetch):
            copy = pltpu.make_async_copy(given[source], made[target], sems_in.at[count_in + slot])
            copy.start()
            fetched.append(copy)
        late = Late(arrivals, departures, sems_out)
        hidden_in = {source for source, _ in fetch}
        hidden_out = {target for _, target in fetch}
        kernel(
            late,
            *[ref for index, ref in enumerate(given) if index not in hidden_in],
            *[ref for index, ref in enumerate(made) if index not in hidden_out and outs[index][0] != "D"],
            *own,
        )
        assert len(late.started) == sends
        for copy in fetched + late.started:
            copy.wait()

    hbm = pl.BlockSpec(memory_space=pltpu.HBM)
    specs = {"S": SMEM, "V": VMEM, "R": VMEM, "H": hbm, "B": hbm, "D": hbm, "P": hbm}
    scratch_shapes = [pltpu.VMEM(shape, jnp.float32) for shape in scratch]
    scratch_shapes += [pltpu.VMEM(shape, jnp.float32) for _, shape in late_in + late_out]
    if count_in or fetch:
        scratch_shapes.append(pltpu.SemaphoreType.DMA((count_in + len(fetch),)))
    if sends:
        scratch_shapes.append(pltpu.SemaphoreType.DMA((sends,)))
    shapes = {"V": jax.ShapeDtypeStruct, "R": pltpu.VMEM, "H": pltpu.HBM, "B": pltpu.HBM, "D": pltpu.HBM}
    invoke = pl.pallas_call(
        body,
        in_specs=[specs[kind] for kind, _ in ins],
        out_specs=[specs[kind] for kind, _ in outs],
        out_shape=[shapes[kind](shape, jnp.float32) for kind, shape in outs],
        scratch_shapes=scratch_shapes,
        input_output_aliases=aliases or {},
        compiler_params=pltpu.CompilerParams(vmem_limit_bytes=VMEM_LIMIT),
        cost_estimate=pl.CostEstimate(flops=flops, bytes_accessed=3 << 20, transcendentals=0),
    )

    def run(*operands):
        placed = {"S": pltpu.HBM, "H": pltpu.HBM, "R": pltpu.VMEM, "P": pltpu.HBM}
        return invoke(
            *[
                pltpu.with_memory_space_constraint(operand, placed[kind]) if kind in placed else operand
                for operand, (kind, _) in zip(operands, ins)
            ]
        )

    return run


def on_device(count, parts, checkpoint, seeds, cell_rate, flux_mats, owner, neighbours, orientation):
    nvars, cx, cy, cz = seeds.shape[2:]
    geo = Geometry(nvars, cx, cy, cz, count, parts)
    rate = cell_rate[0]
    grads = seeds[0, 0]
    place = lax.axis_index("space").astype(jnp.int32).reshape(1)
    part = lax.axis_index("ckpt").astype(jnp.int32).reshape(1)
    mats = flux_mats.reshape(-1)
    table = jnp.concatenate([place, part, owner, neighbours.reshape(-1), orientation.reshape(-1)])
    fixed = (table, mats)
    work = nvars * nvars * 3 * 4 * cx * cy * cz
    few = work // 16
    whole, both = geo.buffer(geo.whole.total), geo.buffer(geo.part.total + geo.whole.total)
    some = -(-geo.part.total // 8) * 8

    stored_shape, block, faces_shape = checkpoint.shape[1:], geo.block, geo.faces
    rate_block = cell_rate.shape[1:]
    scalar, near, kept_near = ("S", None), ("V", None), ("R", None)

    def far(shape):
        return ("H", shape)

    def swap(buffer):
        return lax.all_to_all(buffer, "space", 0, 0, tiled=True)

    def route(arrived):
        return call(functools.partial(route_kernel, geo), [scalar, near], [("B", whole)], [], few)(
            table, arrived
        )[0]

    def adjoint_inner(state, state_kind, grads, grads_kind):
        return call(
            functools.partial(adjoint_inner_kernel, geo),
            [scalar, state_kind, grads_kind, far(rate_block)],
            [("R", block)],
            [geo.tall] * 2,
            2 * work,
        )(mats, state, grads, rate)[0]

    weight_faces, rate_faces, sent = call(
        functools.partial(pack_kernel, geo),
        [scalar, far(stored_shape), far(block), far(rate_block)],
        [far(faces_shape), ("R", geo.rate_faces), ("B", both)],
        [faces_shape],
        few,
    )(part, checkpoint[0], grads, rate)
    kept, sent = lax.optimization_barrier((checkpoint[0], sent))
    arrived = swap(sent)
    state = lax.all_gather(kept, "ckpt", axis=0)
    arrived, state = lax.optimization_barrier((arrived, state))
    (leaving,) = call(functools.partial(route_first_kernel, geo), [scalar, near], [("B", both)], [], few)(
        table, arrived
    )
    first_ghosts = swap(leaving)
    inner, faces, kept_faces = call(
        functools.partial(step_inner_kernel, geo),
        [scalar, far(state.shape), far(rate_block)],
        [("R", block), ("R", faces_shape), ("D", faces_shape)],
        [geo.tall],
        work,
    )(mats, state, rate)
    first_ghosts, inner, faces = lax.optimization_barrier((first_ghosts, inner, faces))
    gathered = lax.all_gather(first_ghosts[:, :some], "ckpt", axis=0)
    next_state, next_faces, kept_next_faces, sent, ghosts = call(
        functools.partial(step_edge_kernel, geo, True),
        [scalar] * 2 + [kept_near] * 3 + [near],
        [("R", block), ("R", faces_shape), ("D", faces_shape), ("B", whole), far(faces_shape)],
        [faces_shape, faces_shape[1:]],
        few,
        aliases={2: 0},
    )(*fixed, inner, faces, rate_faces, gathered)

    arrived = swap(sent)
    inner = adjoint_inner(next_state, kept_near, grads, far(block))
    arrived, inner = lax.optimization_barrier((arrived, inner))
    leaving = route(arrived)
    later_state, leaving = lax.optimization_barrier((next_state, leaving))
    next_ghosts = swap(leaving)
    final_inner, weight_ghosts, weight_faces = call(
        functools.partial(turn_weights_kernel, geo),
        [scalar, kept_near, far(rate_block), scalar, near, ("P", None)],
        [far(block), ("R", faces_shape), ("R", faces_shape)],
        [geo.tall, faces_shape],
        work,
        fetch=((5, 2),),
    )(mats, later_state, rate, table, first_ghosts, weight_faces)
    next_ghosts, final_inner, weight_ghosts, weight_faces = lax.optimization_barrier(
        (next_ghosts, final_inner, weight_ghosts, weight_faces)
    )
    grads_now, next_weight_faces, sent, turned = call(
        functools.partial(adjoint_edge_kernel, geo, False),
        [scalar] * 2 + [kept_near] * 4 + [near, kept_near],
        [("R", block), ("R", faces_shape), ("B", whole), far(faces_shape)],
        [faces_shape],
        few,
        aliases={2: 0},
    )(*fixed, inner, next_faces, weight_faces, rate_faces, next_ghosts, weight_ghosts)

    arrived = swap(sent)
    inner = adjoint_inner(state, far(state.shape), grads_now, kept_near)
    arrived, inner = lax.optimization_barrier((arrived, inner))
    leaving = route(arrived)
    final_inner, leaving = lax.optimization_barrier((final_inner, leaving))
    last_ghosts = swap(leaving)
    final, faces, ghosts = call(
        functools.partial(step_edge_kernel, geo, False),
        [scalar] * 2 + [far(block), far(faces_shape), kept_near, far(faces_shape), ("P", None), ("P", None)],
        [("V", block), ("R", faces_shape), ("R", faces_shape)],
        [],
        work,
        fetch=((6, 1), (7, 2)),
    )(*fixed, final_inner, kept_next_faces, rate_faces, turned, kept_faces, ghosts)
    last_ghosts, final, faces, ghosts = lax.optimization_barrier((last_ghosts, final, faces, ghosts))
    (adjoint,) = call(
        functools.partial(adjoint_edge_kernel, geo, True),
        [scalar] * 2 + [kept_near] * 4 + [near],
        [("B", block)],
        [faces_shape] * 2,
        few,
    )(*fixed, inner, faces, next_weight_faces, ghosts, last_ghosts)
    return (adjoint[None, None], final[None])


def solution(mesh):
    return jax.shard_map(
        functools.partial(on_device, mesh.shape["space"], mesh.shape["ckpt"]),
        mesh=mesh,
        in_specs=(
            P("space", None, "ckpt", None, None),
            P("ckpt", "space", None, None, None, None),
            P("space", None, None, None),
            P(),
            P(),
            P(),
            P(),
        ),
        out_specs=(P("ckpt", "space", None, None, None, None), P("space", None, None, None, None)),
        check_vma=False,
    )
```

```python
import functools

import jax
import jax.numpy as jnp
from jax import lax
from jax.experimental import pallas as pl
from jax.experimental.pallas import tpu as pltpu
from jax.sharding import PartitionSpec as P

STEPS = 2
time_step = 0.05
damping = 0.015

PAD = 8
VMEM = pl.BlockSpec(memory_space=pltpu.VMEM)
SMEM = pl.BlockSpec(memory_space=pltpu.SMEM)
VMEM_LIMIT = 16 * 1024 * 1024


class Pieces:
    def __init__(self, rows, count):
        self.rows = rows
        self.runs = [-(-length // count) for length in rows]
        self.starts = [sum(self.runs[:index]) for index in range(len(rows))]
        self.total = sum(self.runs)


class Geometry:
    def __init__(self, nvars, cx, cy, cz, count, parts):
        self.v, self.x, self.y, self.z, self.n, self.parts = nvars, cx, cy, cz, count, parts
        self.depth = cx // parts
        self.rows = [nvars * cy] * 2 + [nvars * cx] * 2 + [cy] * 2
        self.whole = Pieces(self.rows, count)
        self.part = Pieces([nvars * cy] + [nvars * self.depth] * 2 + [cy] * 2, count)
        self.face_rows = -(-max(run * count for run in self.whole.runs) // 8) * 8
        self.block = (nvars, cx, cy, cz)
        self.tall = (nvars, cx, cy + 2 * PAD, cz)
        self.faces = (6, self.face_rows, cz)
        self.rate_faces = (6, max(cx, cy), cz)

    def buffer(self, rows):
        return (self.n, -(-rows // 8) * 8, self.z)


def take_z_faces(geo, load, variables=None):
    v, x, y, z = geo.block
    lane = lax.broadcasted_iota(jnp.int32, (y, z), 1)
    high = jnp.zeros((y, z), jnp.float32)
    low = jnp.zeros((y, z), jnp.float32)
    for var in range(variables or v):
        for plane in range(x):
            place = var * x + plane
            tile = pltpu.roll(load(var, plane), place + 1, 1)
            high = jnp.where(lane == place, tile, high)
            low = jnp.where(lane == place + 1, tile, low)
    return high, pltpu.roll(low, z - 1, 1)


def repeat_lanes(geo, layer):
    total = layer
    for var in range(1, geo.v):
        total = total + pltpu.roll(layer, var * geo.x, 1)
    return total


def take_xy_faces(geo, source, faces):
    v, x, y, z = geo.block
    faces[0, : v * y] = source[:, x - 1].reshape(v * y, z)
    faces[1, : v * y] = source[:, 0].reshape(v * y, z)
    for var in range(v):
        faces[2, var * x : (var + 1) * x] = source[var, :, y - 1, :]
        faces[3, var * x : (var + 1) * x] = source[var, :, 0, :]


def cut(geo, pieces, faces, buffer, base, leave=None):
    for slot in range(geo.n):
        for index, (run, start) in enumerate(zip(pieces.runs, pieces.starts)):
            buffer[slot, base + start : base + start + run] = faces[index, slot * run : (slot + 1) * run]
        if leave:
            leave(slot)


class Links:
    def __init__(self, owner, neighbours):
        self.owner, self.neighbours = owner, neighbours

    def target(self, block):
        return self.owner[block]

    def source(self, block, side):
        return self.owner[self.neighbours[block, side]]


class Table:
    def __init__(self, geo, ref):
        self.ref, self.n = ref, geo.n

    def codes(self):
        return [self.ref[side] for side in range(6)]

    def target(self, block):
        return self.ref[6 + block]

    def source(self, block, side):
        return self.ref[6 + self.n + block * 6 + side]


def fill_table(geo, place, owner, neighbours, orientation, table):
    links = Links(owner, neighbours)
    own = jnp.int32(0)
    for block in range(geo.n):
        own = jnp.where(owner[block] == place[0], block, own)
        table[6 + block] = links.target(block)
        for side in range(6):
            table[6 + geo.n + block * 6 + side] = links.source(block, side)
    for side in range(6):
        table[side] = orientation[own, side]


def flip_rows(values, flag, length):
    rows, z = values.shape
    grouped = values.reshape(rows // length, length // 8, 8, z)
    index = lax.broadcasted_iota(jnp.int32, (8, z), 0)
    index = jnp.where(flag == 1, 7 - index, index)
    tiles = length // 8
    out = []
    for group in range(rows // length):
        for tile in range(tiles):
            picked = jnp.where(flag == 1, grouped[group, tiles - 1 - tile], grouped[group, tile])
            out.append(jnp.take_along_axis(picked, index, axis=0))
    return jnp.stack(out).reshape(rows, z)


def flip_lanes(values, flag, length):
    rows, z = values.shape
    lane = lax.broadcasted_iota(jnp.int32, (8, z), 1)
    within = lax.rem(lane, length)
    index = jnp.where(flag == 1, lane + (length - 1) - 2 * within, lane)
    index = jnp.minimum(index, z - 1)
    tiles = values.reshape(rows // 8, 8, z)
    return jnp.stack(
        [jnp.take_along_axis(tiles[tile], index, axis=1) for tile in range(rows // 8)]
    ).reshape(rows, z)


def join(geo, buffer, raw, base=0):
    for side in range(6):
        run, start = geo.whole.runs[side], base + geo.whole.starts[side]
        for slot in range(geo.n):
            raw[side, slot * run : (slot + 1) * run] = buffer[slot, start : start + run]


def join_parts(geo, buffer, raw, piece):
    for side in range(6):
        index = 0 if side < 2 else side - 1
        run, start = geo.part.runs[index], geo.part.starts[index]
        if side < 2:
            part = 0 if side == 0 else geo.parts - 1
            for slot in range(geo.n):
                raw[side, slot * run : (slot + 1) * run] = buffer[part, slot, start : start + run]
        elif side < 4:
            for part in range(geo.parts):
                for slot in range(geo.n):
                    piece[slot * run : (slot + 1) * run] = buffer[part, slot, start : start + run]
                for var in range(geo.v):
                    row = var * geo.x + part * geo.depth
                    raw[side, row : row + geo.depth] = piece[var * geo.depth : (var + 1) * geo.depth]
        else:
            for slot in range(geo.n):
                total = buffer[0, slot, start : start + run]
                for part in range(1, geo.parts):
                    total = total + buffer[part, slot, start : start + run]
                raw[side, slot * run : (slot + 1) * run] = total


def turn(geo, codes, raw, ghosts):
    v, x, y, z = geo.block
    for side in range(6):
        first, second = codes[side] & 1, (codes[side] >> 1) & 1
        layer = raw[side, : geo.rows[side]]
        if side < 4:
            layer = flip_lanes(flip_rows(layer, first, y if side < 2 else x), second, z)
        else:
            layer = flip_lanes(flip_rows(layer, second, y), first, x)
        ghosts[side, : geo.rows[side]] = layer


def face_values(geo, faces, side):
    v, x, y, z = geo.block
    if side < 4:
        depth = y if side < 2 else x
        return [faces[side, var * depth : (var + 1) * depth] for var in range(v)]
    layer = faces[side, :y]
    return [layer] + [pltpu.roll(layer, z - var * x, 1) for var in range(1, v)]


def fill_tall(geo, source, tall):
    v, x, y, z = geo.block
    if len(source.shape) == 5:
        depth = geo.depth
        for part in range(geo.parts):
            tall[:, part * depth : (part + 1) * depth, PAD : PAD + y, :] = source[part]
    else:
        tall[:, :, PAD : PAD + y, :] = source[...]
    for var in range(v):
        tall[var, :, PAD - 1, :] = tall[var, :, PAD, :]
        tall[var, :, PAD + y, :] = tall[var, :, PAD + y - 1, :]


def around(geo, tall, plane):
    v, x, y, z = geo.block
    lane = lax.broadcasted_iota(jnp.int32, (y, z), 1)
    before, after = jnp.maximum(plane - 1, 0), jnp.minimum(plane + 1, x - 1)
    cells, low, high = [], [[], [], []], [[], [], []]
    for var in range(v):
        mid = tall[var, plane, PAD : PAD + y]
        cells.append(mid)
        low[0].append(tall[var, before, PAD : PAD + y])
        high[0].append(tall[var, after, PAD : PAD + y])
        low[1].append(tall[var, plane, PAD - 1 : PAD - 1 + y])
        high[1].append(tall[var, plane, PAD + 1 : PAD + 1 + y])
        low[2].append(jnp.where(lane == 0, mid, pltpu.roll(mid, 1, 1)))
        high[2].append(jnp.where(lane == z - 1, mid, pltpu.roll(mid, z - 1, 1)))
    return cells, low, high


def flux_entry(geo, mats, direction, row, column):
    return mats[(direction * geo.v + row) * geo.v + column]


def step_plane(geo, mats, cells, low, high, rate):
    v = geo.v
    total = [None] * v
    for direction in range(3):
        lows, highs = low[direction], high[direction]
        mean_low = 0.5 * (lows[0] + cells[0])
        mean_high = 0.5 * (cells[0] + highs[0])
        square_low = 1.0 + mean_low * mean_low
        square_high = 1.0 + mean_high * mean_high
        spread_low = square_low * lax.rsqrt(square_low)
        spread_high = square_high * lax.rsqrt(square_high)
        slopes = [highs[var] - lows[var] for var in range(v)]
        for var in range(v):
            term = spread_low * (cells[var] - lows[var]) - spread_high * (highs[var] - cells[var])
            for column in range(v):
                term = term + flux_entry(geo, mats, direction, var, column) * slopes[column]
            total[var] = term if total[var] is None else total[var] + term
    scale = (0.5 * time_step) * rate
    return [cells[var] - scale * total[var] - damping * jnp.tanh(cells[var]) for var in range(v)]


def adjoint_plane(geo, mats, cells, low, high, grads, weight, weight_low, weight_high):
    v = geo.v
    total = [None] * v
    extra = None
    for direction in range(3):
        spreads, steps = [], []
        for lower, upper, lower_weight, upper_weight in (
            (low[direction], cells, weight_low[direction], weight),
            (cells, high[direction], weight, weight_high[direction]),
        ):
            mean = 0.5 * (lower[0] + upper[0])
            square = 1.0 + mean * mean
            inverse = lax.rsqrt(square)
            jump = [lower_weight[var] - upper_weight[var] for var in range(v)]
            product = jump[0] * (upper[0] - lower[0])
            for var in range(1, v):
                product = product + jump[var] * (upper[var] - lower[var])
            product = product * (mean * inverse)
            extra = product if extra is None else extra + product
            spreads.append(square * inverse)
            steps.append(jump)
        slopes = [steps[0][var] + steps[1][var] for var in range(v)]
        for var in range(v):
            term = spreads[1] * steps[1][var] - spreads[0] * steps[0][var]
            for row in range(v):
                term = term + flux_entry(geo, mats, direction, row, var) * slopes[row]
            total[var] = term if total[var] is None else total[var] + term
    total[0] = total[0] - 0.5 * extra
    out = []
    for var in range(v):
        bend = jnp.tanh(cells[var])
        slope = (1.0 - damping) + damping * (bend * bend)
        out.append(grads[var] * slope - (0.5 * time_step) * total[var])
    return out


def step_face(geo, mats, side, cells, ghosts, rate):
    v = geo.v
    mean = 0.5 * (cells[0] + ghosts[0])
    square = 1.0 + mean * mean
    spread = square * lax.rsqrt(square)
    gap = [ghosts[var] - cells[var] for var in range(v)]
    scale = (0.5 * time_step) * rate
    out = []
    for var in range(v):
        total = flux_entry(geo, mats, side // 2, var, 0) * gap[0]
        for column in range(1, v):
            total = total + flux_entry(geo, mats, side // 2, var, column) * gap[column]
        if side % 2 == 0:
            out.append(scale * (spread * gap[var] - total))
        else:
            out.append(scale * (spread * gap[var] + total))
    return out


def adjoint_face(geo, mats, side, cells, ghosts, weight, ghost_weight):
    v = geo.v
    mean = 0.5 * (cells[0] + ghosts[0])
    square = 1.0 + mean * mean
    inverse = lax.rsqrt(square)
    spread = square * inverse
    jump = [weight[var] - ghost_weight[var] for var in range(v)]
    product = jump[0] * (ghosts[0] - cells[0])
    for var in range(1, v):
        product = product + jump[var] * (ghosts[var] - cells[var])
    product = (0.5 * product) * (mean * inverse)
    out = []
    for var in range(v):
        total = flux_entry(geo, mats, side // 2, 0, var) * jump[0]
        for row in range(1, v):
            total = total + flux_entry(geo, mats, side // 2, row, var) * jump[row]
        if side % 2 == 0:
            total = spread * jump[var] + total
        else:
            total = spread * jump[var] - total
        if var == 0:
            total = total - product
        out.append((-0.5 * time_step) * total)
    return out


def pack_kernel(geo, late, part, stored, grads, rate, weight_faces, rate_faces, buffer, pieces):
    v, x, y, z = geo.block
    depth = geo.depth
    late.wait(1)
    lane = lax.broadcasted_iota(jnp.int32, (y, z), 1)
    plane = jnp.where(part[0] == geo.parts - 1, depth - 1, 0)
    high = jnp.zeros((y, z), jnp.float32)
    low = jnp.zeros((y, z), jnp.float32)
    for var in range(v):
        pieces[0, var * y : (var + 1) * y] = stored[var, plane]
        pieces[1, var * depth : (var + 1) * depth] = stored[var, :, y - 1, :]
        pieces[2, var * depth : (var + 1) * depth] = stored[var, :, 0, :]
        for step in range(depth):
            place = var * x + part[0] * depth + step
            tile = stored[var, step]
            here = lane == place
            high = jnp.where(here, pltpu.roll(tile, lax.rem(place + 1, z), 1), high)
            low = jnp.where(here, pltpu.roll(tile, place, 1), low)
    pieces[3, :y] = high
    pieces[4, :y] = low
    cut(geo, geo.part, pieces, buffer, 0)
    late.wait(2)
    late.wait(3)
    rate_faces[0, :y] = rate[x - 1]
    rate_faces[1, :y] = rate[0]
    rate_faces[2, :x] = rate[:, y - 1, :]
    rate_faces[3, :x] = rate[:, 0, :]
    high, low = take_z_faces(geo, lambda var, plane: rate[plane], 1)
    rate_faces[4, :y] = repeat_lanes(geo, high)
    rate_faces[5, :y] = repeat_lanes(geo, low)
    late.leave(1)
    take_weight_faces(geo, grads, rate_faces, weight_faces)
    late.leave(0)
    cut(geo, geo.whole, weight_faces, buffer, geo.part.total, functools.partial(late.leave, 2))


def take_weight_faces(geo, grads, rate_faces, faces):
    v, x, y, z = geo.block
    take_xy_faces(geo, grads, faces)
    for side in range(4):
        depth = y if side < 2 else x
        for var in range(v):
            here = slice(var * depth, (var + 1) * depth)
            faces[side, here] = faces[side, here] * rate_faces[side, :depth]
    high, low = take_z_faces(geo, lambda var, plane: grads[var, plane])
    faces[4, :y] = high * rate_faces[4, :y]
    faces[5, :y] = low * rate_faces[5, :y]


def route_whole(geo, links, block, arrived, leaving, base):
    for side in range(6):
        source = links.source(block, side)
        run, start, far = geo.whole.runs[side], base + geo.whole.starts[side], base + geo.whole.starts[side ^ 1]
        leaving[links.target(block), start : start + run] = arrived[source, far : far + run]


def route_kernel(geo, late, table, arrived, leaving):
    links = Table(geo, table)
    for block in range(geo.n):
        route_whole(geo, links, block, arrived, leaving, 0)
        late.leave(0, links.target(block))


def route_first_kernel(geo, late, part, owner, neighbours, arrived, leaving):
    links = Links(owner, neighbours)
    x_side = jnp.where(part[0] == geo.parts - 1, 1, 0)
    for block in range(geo.n):
        route_whole(geo, links, block, arrived, leaving, geo.part.total)
        for index in range(5):
            side, far_index = (x_side, 0) if index == 0 else (index + 1, ((index + 1) ^ 1) - 1)
            source = links.source(block, side)
            run, start, far = geo.part.runs[index], geo.part.starts[index], geo.part.starts[far_index]
            leaving[links.target(block), start : start + run] = arrived[source, far : far + run]
        late.leave(0, links.target(block))


def first_inner_kernel(
    geo, late, mats, block, rate, place, owner, neighbours, orientation, result, faces, table, flat, tall
):
    fill_table(geo, place, owner, neighbours, orientation, table)
    for direction in range(3):
        for row in range(geo.v):
            for column in range(geo.v):
                flat[(direction * geo.v + row) * geo.v + column] = mats[direction, row, column]
    step_inner_kernel(geo, late, flat, block, rate, result, faces, tall)


def turn_weights_kernel(geo, late, mats, block, rate, table, buffer, result, ghosts, tall, raw):
    join(geo, buffer, raw, geo.part.total)
    turn(geo, Table(geo, table).codes(), raw, ghosts)
    step_inner_kernel(geo, late, mats, block, rate, result, tall)


def step_inner_kernel(geo, late, mats, block, rate, result, *rest):
    tall = rest[-1]
    late.wait(1)
    late.wait(2)
    fill_tall(geo, block, tall)

    def body(plane, carry):
        cells, low, high = around(geo, tall, plane)
        for var, value in enumerate(step_plane(geo, mats, cells, low, high, rate[plane])):
            result[var, plane] = value
        return carry

    lax.fori_loop(0, geo.x, body, 0)
    late.leave(0)
    if len(rest) == 2:
        faces = rest[0]
        v, x, y, z = geo.block
        for var in range(v):
            faces[0, var * y : (var + 1) * y] = tall[var, x - 1, PAD : PAD + y]
            faces[1, var * y : (var + 1) * y] = tall[var, 0, PAD : PAD + y]
            faces[2, var * x : (var + 1) * x] = tall[var, :, PAD + y - 1, :]
            faces[3, var * x : (var + 1) * x] = tall[var, :, PAD, :]
        high, low = take_z_faces(geo, lambda var, plane: tall[var, plane, PAD : PAD + y])
        faces[4, :y] = high
        faces[5, :y] = low
        late.leave(2)


def adjoint_inner_kernel(geo, late, mats, block, grads, rate, result, tall, weights):
    v, x, y, z = geo.block
    for index in range(1, 4):
        late.wait(index)
    fill_tall(geo, block, tall)

    def scale(plane, carry):
        for var in range(v):
            weights[var, plane, PAD : PAD + y] = rate[plane] * grads[var, plane]
        return carry

    lax.fori_loop(0, x, scale, 0)
    for var in range(v):
        weights[var, :, PAD - 1, :] = weights[var, :, PAD, :]
        weights[var, :, PAD + y, :] = weights[var, :, PAD + y - 1, :]

    def body(plane, carry):
        cells, low, high = around(geo, tall, plane)
        weight, weight_low, weight_high = around(geo, weights, plane)
        here = [grads[var, plane] for var in range(v)]
        values = adjoint_plane(geo, mats, cells, low, high, here, weight, weight_low, weight_high)
        for var, value in enumerate(values):
            result[var, plane] = value
        return carry

    lax.fori_loop(0, x, body, 0)


def add_terms(geo, values, inner, result, leave=None):
    v, x, y, z = geo.block
    lane = lax.broadcasted_iota(jnp.int32, (y, z), 1)
    zero = jnp.zeros((y, z), jnp.float32)
    ends = (lane == 0) | (lane == z - 1)
    even = lane % 2 == 0
    for var in range(v):
        high, low = values[4][var], pltpu.roll(values[5][var], 1, 1)
        mixed = (jnp.where(even, high, low), jnp.where(even, low, high))
        for plane in range(x):
            change = jnp.where(ends, pltpu.roll(mixed[plane % 2], z - 1 - plane, 1), zero)
            if plane == 0:
                change = change + values[1][var]
            if plane == x - 1:
                change = change + values[0][var]
            result[var, plane] = inner[var, plane] + change
        result[var, :, y - 1, :] = result[var, :, y - 1, :] + values[2][var]
        result[var, :, 0, :] = result[var, :, 0, :] + values[3][var]
        if leave:
            leave(var)


def step_edge_kernel(geo, first, late, table, mats, inner, faces, rate_faces, arrived, result, *rest):
    v, x, y, z = geo.block
    if first:
        new_faces, sent, ghosts, raw, piece = rest
        join_parts(geo, arrived, raw, piece)
        turn(geo, Table(geo, table).codes(), raw, ghosts)
        late.leave(4)
    else:
        ghosts = arrived
        late.wait(2)
        late.wait(5)
    late.wait(3)
    values = []
    for side in range(6):
        depth = y if side < 2 or side > 3 else x
        cells, outer = face_values(geo, faces, side), face_values(geo, ghosts, side)
        values.append(step_face(geo, mats, side, cells, outer, rate_faces[side, :depth]))
    add_terms(geo, values, inner, result)
    if first:
        take_xy_faces(geo, result, new_faces)
        high, low = take_z_faces(geo, lambda var, plane: result[var, plane])
        new_faces[4, :y] = high
        new_faces[5, :y] = low
        cut(geo, geo.whole, new_faces, sent, 0, functools.partial(late.leave, 3))
        late.leave(2)


def adjoint_edge_kernel(geo, last, late, table, mats, inner, faces, weight_faces, *rest):
    v, x, y, z = geo.block
    codes = Table(geo, table).codes()
    if last:
        ghosts, weight_buffer, result, raw, weight_ghosts = rest
        join(geo, weight_buffer, raw)
        turn(geo, codes, raw, weight_ghosts)
    else:
        rate_faces, buffer, weight_ghosts, result, new_faces, sent, ghosts, raw = rest
        join(geo, buffer, raw)
        turn(geo, codes, raw, ghosts)
        late.leave(3)
    values = []
    for side in range(6):
        views = [face_values(geo, field, side) for field in (faces, ghosts, weight_faces, weight_ghosts)]
        values.append(adjoint_face(geo, mats, side, *views))
    add_terms(geo, values, inner, result, functools.partial(late.leave, 0) if last else None)
    if not last:
        take_weight_faces(geo, result, rate_faces, new_faces)
        cut(geo, geo.whole, new_faces, sent, 0, functools.partial(late.leave, 2))


class Late:
    def __init__(self, arrivals, departures, sems):
        self.arrivals, self.departures, self.sems, self.started = arrivals, departures, sems, []

    def wait(self, index):
        if index in self.arrivals:
            self.arrivals[index].wait()

    def leave(self, index, slot=None):
        if index in self.departures:
            source, target = self.departures[index]
            if slot is not None:
                source, target = source.at[slot], target.at[slot]
            copy = pltpu.make_async_copy(source, target, self.sems.at[len(self.started)])
            copy.start()
            self.started.append(copy)


def call(kernel, ins, outs, scratch, flops, fetch=(), aliases=None):
    late_in = [(index, shape) for index, (kind, shape) in enumerate(ins) if kind == "H"]
    late_out = [(index, shape) for index, (kind, shape) in enumerate(outs) if kind in "HB"]
    count_in, count_out = len(late_in), len(late_out)
    sends = sum(shape[0] if kind == "B" else 1 for kind, shape in outs if kind in "HBD")

    def body(*refs):
        given = list(refs[: len(ins)])
        made = list(refs[len(ins) : len(ins) + len(outs)])
        rest = list(refs[len(ins) + len(outs) :])
        own = rest[: len(scratch)]
        stage = rest[len(scratch) : len(scratch) + count_in + count_out]
        sems_in = rest[len(scratch) + count_in + count_out] if count_in or fetch else None
        sems_out = rest[-1] if sends else None
        arrivals, departures = {}, {}
        for slot, (index, _) in enumerate(late_in):
            copy = pltpu.make_async_copy(given[index], stage[slot], sems_in.at[slot])
            copy.start()
            arrivals[index] = copy
            given[index] = stage[slot]
        for slot, (index, _) in enumerate(late_out):
            departures[index] = (stage[count_in + slot], made[index])
            made[index] = stage[count_in + slot]
        for index, (kind, _) in enumerate(outs):
            if kind == "D":
                departures[index] = (made[index - 1], made[index])
        fetched = []
        for slot, (source, target) in enumerate(fetch):
            copy = pltpu.make_async_copy(given[source], made[target], sems_in.at[count_in + slot])
            copy.start()
            fetched.append(copy)
        late = Late(arrivals, departures, sems_out)
        hidden_in = {source for source, _ in fetch}
        hidden_out = {target for _, target in fetch}
        kernel(
            late,
            *[ref for index, ref in enumerate(given) if index not in hidden_in],
            *[ref for index, ref in enumerate(made) if index not in hidden_out and outs[index][0] != "D"],
            *own,
        )
        assert len(late.started) == sends
        for copy in fetched + late.started:
            copy.wait()

    hbm = pl.BlockSpec(memory_space=pltpu.HBM)
    specs = {"S": SMEM, "V": VMEM, "R": VMEM, "H": hbm, "B": hbm, "D": hbm, "P": hbm, "M": SMEM, "I": SMEM}
    scratch_shapes = [pltpu.VMEM(shape, jnp.float32) for shape in scratch]
    scratch_shapes += [pltpu.VMEM(shape, jnp.float32) for _, shape in late_in + late_out]
    if count_in or fetch:
        scratch_shapes.append(pltpu.SemaphoreType.DMA((count_in + len(fetch),)))
    if sends:
        scratch_shapes.append(pltpu.SemaphoreType.DMA((sends,)))
    shapes = {"V": jax.ShapeDtypeStruct, "R": pltpu.VMEM, "H": pltpu.HBM, "B": pltpu.HBM, "D": pltpu.HBM}
    shapes.update({"M": pltpu.SMEM, "I": pltpu.SMEM})
    invoke = pl.pallas_call(
        body,
        in_specs=[specs[kind] for kind, _ in ins],
        out_specs=[specs[kind] for kind, _ in outs],
        out_shape=[shapes[kind](shape, jnp.int32 if kind == "I" else jnp.float32) for kind, shape in outs],
        scratch_shapes=scratch_shapes,
        input_output_aliases=aliases or {},
        compiler_params=pltpu.CompilerParams(vmem_limit_bytes=VMEM_LIMIT),
        cost_estimate=pl.CostEstimate(flops=flops, bytes_accessed=3 << 20, transcendentals=0),
    )

    def run(*operands):
        placed = {"M": pltpu.SMEM, "H": pltpu.HBM, "R": pltpu.VMEM, "P": pltpu.HBM}
        return invoke(
            *[
                pltpu.with_memory_space_constraint(operand, placed[kind]) if kind in placed else operand
                for operand, (kind, _) in zip(operands, ins)
            ]
        )

    return run


def on_device(count, parts, checkpoint, seeds, cell_rate, flux_mats, owner, neighbours, orientation):
    nvars, cx, cy, cz = seeds.shape[2:]
    geo = Geometry(nvars, cx, cy, cz, count, parts)
    rate = cell_rate[0]
    grads = seeds[0, 0]
    place = lax.axis_index("space").astype(jnp.int32).reshape(1)
    part = lax.axis_index("ckpt").astype(jnp.int32).reshape(1)
    work = nvars * nvars * 3 * 4 * cx * cy * cz
    few = work // 16
    whole, both = geo.buffer(geo.whole.total), geo.buffer(geo.part.total + geo.whole.total)
    some = -(-geo.part.total // 8) * 8

    stored_shape, block, faces_shape = checkpoint.shape[1:], geo.block, geo.faces
    rate_block = cell_rate.shape[1:]
    scalar, near, kept_near, kept_scalar = ("S", None), ("V", None), ("R", None), ("M", None)

    def far(shape):
        return ("H", shape)

    def swap(buffer):
        return lax.all_to_all(buffer, "space", 0, 0, tiled=True)

    def route(arrived):
        return call(functools.partial(route_kernel, geo), [kept_scalar, near], [("B", whole)], [], few)(
            table, arrived
        )[0]

    def adjoint_inner(state, state_kind, grads, grads_kind):
        return call(
            functools.partial(adjoint_inner_kernel, geo),
            [kept_scalar, state_kind, grads_kind, far(rate_block)],
            [("R", block)],
            [geo.tall] * 2,
            2 * work,
        )(mats, state, grads, rate)[0]

    weight_faces, rate_faces, sent = call(
        functools.partial(pack_kernel, geo),
        [scalar, far(stored_shape), far(block), far(rate_block)],
        [far(faces_shape), ("R", geo.rate_faces), ("B", both)],
        [faces_shape],
        few,
    )(part, checkpoint[0], grads, rate)
    kept, sent = lax.optimization_barrier((checkpoint[0], sent))
    arrived = swap(sent)
    state = lax.all_gather(kept, "ckpt", axis=0)
    arrived, state = lax.optimization_barrier((arrived, state))
    (leaving,) = call(functools.partial(route_first_kernel, geo), [scalar] * 3 + [near], [("B", both)], [], few)(
        part, owner, neighbours, arrived
    )
    first_ghosts = swap(leaving)
    inner, faces, kept_faces, table, mats = call(
        functools.partial(first_inner_kernel, geo),
        [scalar, far(state.shape), far(rate_block)] + [scalar] * 4,
        [("R", block), ("R", faces_shape), ("D", faces_shape), ("I", (6 + 7 * count,)), ("M", (3 * nvars * nvars,))],
        [geo.tall],
        work,
    )(flux_mats, state, rate, place, owner, neighbours, orientation)
    fixed = (table, mats)
    first_ghosts, inner, faces = lax.optimization_barrier((first_ghosts, inner, faces))
    gathered = lax.all_gather(first_ghosts[:, :some], "ckpt", axis=0)
    next_state, next_faces, kept_next_faces, sent, ghosts = call(
        functools.partial(step_edge_kernel, geo, True),
        [kept_scalar] * 2 + [kept_near] * 3 + [near],
        [("R", block), ("R", faces_shape), ("D", faces_shape), ("B", whole), far(faces_shape)],
        [faces_shape, faces_shape[1:]],
        few,
        aliases={2: 0},
    )(*fixed, inner, faces, rate_faces, gathered)

    arrived = swap(sent)
    inner = adjoint_inner(next_state, kept_near, grads, far(block))
    arrived, inner = lax.optimization_barrier((arrived, inner))
    leaving = route(arrived)
    later_state, leaving = lax.optimization_barrier((next_state, leaving))
    next_ghosts = swap(leaving)
    final_inner, weight_ghosts, weight_faces = call(
        functools.partial(turn_weights_kernel, geo),
        [kept_scalar, kept_near, far(rate_block), kept_scalar, near, ("P", None)],
        [far(block), ("R", faces_shape), ("R", faces_shape)],
        [geo.tall, faces_shape],
        work,
        fetch=((5, 2),),
    )(mats, later_state, rate, table, first_ghosts, weight_faces)
    next_ghosts, final_inner, weight_ghosts, weight_faces = lax.optimization_barrier(
        (next_ghosts, final_inner, weight_ghosts, weight_faces)
    )
    grads_now, next_weight_faces, sent, turned = call(
        functools.partial(adjoint_edge_kernel, geo, False),
        [kept_scalar] * 2 + [kept_near] * 4 + [near, kept_near],
        [("R", block), ("R", faces_shape), ("B", whole), far(faces_shape)],
        [faces_shape],
        few,
        aliases={2: 0},
    )(*fixed, inner, next_faces, weight_faces, rate_faces, next_ghosts, weight_ghosts)

    arrived = swap(sent)
    inner = adjoint_inner(state, far(state.shape), grads_now, kept_near)
    arrived, inner = lax.optimization_barrier((arrived, inner))
    leaving = route(arrived)
    final_inner, leaving = lax.optimization_barrier((final_inner, leaving))
    last_ghosts = swap(leaving)
    final, faces, ghosts = call(
        functools.partial(step_edge_kernel, geo, False),
        [kept_scalar] * 2 + [far(block), far(faces_shape), kept_near, far(faces_shape), ("P", None), ("P", None)],
        [("V", block), ("R", faces_shape), ("R", faces_shape)],
        [],
        work,
        fetch=((6, 1), (7, 2)),
    )(*fixed, final_inner, kept_next_faces, rate_faces, turned, kept_faces, ghosts)
    last_ghosts, final, faces, ghosts = lax.optimization_barrier((last_ghosts, final, faces, ghosts))
    (adjoint,) = call(
        functools.partial(adjoint_edge_kernel, geo, True),
        [kept_scalar] * 2 + [kept_near] * 4 + [near],
        [("B", block)],
        [faces_shape] * 2,
        few,
    )(*fixed, inner, faces, next_weight_faces, ghosts, last_ghosts)
    return (adjoint[None, None], final[None])


def solution(mesh):
    return jax.shard_map(
        functools.partial(on_device, mesh.shape["space"], mesh.shape["ckpt"]),
        mesh=mesh,
        in_specs=(
            P("space", None, "ckpt", None, None),
            P("ckpt", "space", None, None, None, None),
            P("space", None, None, None),
            P(),
            P(),
            P(),
            P(),
        ),
        out_specs=(P("ckpt", "space", None, None, None, None), P("space", None, None, None, None)),
        check_vma=False,
    )
```

```python
import functools

import jax
import jax.numpy as jnp
from jax import lax
from jax.experimental import pallas as pl
from jax.experimental.pallas import tpu as pltpu
from jax.sharding import PartitionSpec as P

STEPS = 2
time_step = 0.05
damping = 0.015

PAD = 8
VMEM = pl.BlockSpec(memory_space=pltpu.VMEM)
SMEM = pl.BlockSpec(memory_space=pltpu.SMEM)
VMEM_LIMIT = 16 * 1024 * 1024


class Pieces:
    def __init__(self, rows, count):
        self.rows = rows
        self.runs = [-(-length // count) for length in rows]
        self.starts = [sum(self.runs[:index]) for index in range(len(rows))]
        self.total = sum(self.runs)


class Geometry:
    def __init__(self, nvars, cx, cy, cz, count, parts):
        self.v, self.x, self.y, self.z, self.n, self.parts = nvars, cx, cy, cz, count, parts
        self.depth = cx // parts
        self.rows = [nvars * cy] * 2 + [nvars * cx] * 2 + [cy] * 2
        self.whole = Pieces(self.rows, count)
        self.part = Pieces([nvars * cy] + [nvars * self.depth] * 2 + [cy] * 2, count)
        self.face_rows = -(-max(run * count for run in self.whole.runs) // 8) * 8
        self.block = (nvars, cx, cy, cz)
        self.tall = (nvars, cx, cy + 2 * PAD, cz)
        self.faces = (6, self.face_rows, cz)
        self.rate_faces = (6, max(cx, cy), cz)

    def buffer(self, rows):
        return (self.n, -(-rows // 8) * 8, self.z)


def take_z_faces(geo, load, variables=None):
    v, x, y, z = geo.block
    lane = lax.broadcasted_iota(jnp.int32, (y, z), 1)
    high = jnp.zeros((y, z), jnp.float32)
    low = jnp.zeros((y, z), jnp.float32)
    for var in range(variables or v):
        for plane in range(x):
            place = var * x + plane
            tile = pltpu.roll(load(var, plane), place + 1, 1)
            high = jnp.where(lane == place, tile, high)
            low = jnp.where(lane == place + 1, tile, low)
    return high, pltpu.roll(low, z - 1, 1)


def repeat_lanes(geo, layer):
    total = layer
    for var in range(1, geo.v):
        total = total + pltpu.roll(layer, var * geo.x, 1)
    return total


def take_xy_faces(geo, source, faces):
    v, x, y, z = geo.block
    faces[0, : v * y] = source[:, x - 1].reshape(v * y, z)
    faces[1, : v * y] = source[:, 0].reshape(v * y, z)
    for var in range(v):
        faces[2, var * x : (var + 1) * x] = source[var, :, y - 1, :]
        faces[3, var * x : (var + 1) * x] = source[var, :, 0, :]


def cut(geo, pieces, faces, buffer, base, leave=None):
    for slot in range(geo.n):
        for index, (run, start) in enumerate(zip(pieces.runs, pieces.starts)):
            buffer[slot, base + start : base + start + run] = faces[index, slot * run : (slot + 1) * run]
        if leave:
            leave(slot)


class Table:
    def __init__(self, geo, ref):
        self.ref, self.n = ref, geo.n

    def codes(self):
        return [self.ref[side] for side in range(6)]

    def part(self):
        return self.ref[6]

    def target(self, block):
        return self.ref[7 + block]

    def source(self, block, side):
        return self.ref[7 + self.n + block * 6 + side]


def fill_table(geo, place, part, owner, neighbours, orientation, table):
    own = jnp.int32(0)
    table[6] = part[0]
    for block in range(geo.n):
        own = jnp.where(owner[block] == place[0], block, own)
        table[7 + block] = owner[block]
        for side in range(6):
            table[7 + geo.n + block * 6 + side] = owner[neighbours[block, side]]
    for side in range(6):
        table[side] = orientation[own, side]


def flip_rows(values, flag, length):
    rows, z = values.shape
    grouped = values.reshape(rows // length, length // 8, 8, z)
    index = lax.broadcasted_iota(jnp.int32, (8, z), 0)
    index = jnp.where(flag == 1, 7 - index, index)
    tiles = length // 8
    out = []
    for group in range(rows // length):
        for tile in range(tiles):
            picked = jnp.where(flag == 1, grouped[group, tiles - 1 - tile], grouped[group, tile])
            out.append(jnp.take_along_axis(picked, index, axis=0))
    return jnp.stack(out).reshape(rows, z)


def flip_lanes(values, flag, length):
    rows, z = values.shape
    lane = lax.broadcasted_iota(jnp.int32, (8, z), 1)
    within = lax.rem(lane, length)
    index = jnp.where(flag == 1, lane + (length - 1) - 2 * within, lane)
    index = jnp.minimum(index, z - 1)
    tiles = values.reshape(rows // 8, 8, z)
    return jnp.stack(
        [jnp.take_along_axis(tiles[tile], index, axis=1) for tile in range(rows // 8)]
    ).reshape(rows, z)


def join(geo, buffer, raw, base=0):
    for side in range(6):
        run, start = geo.whole.runs[side], base + geo.whole.starts[side]
        for slot in range(geo.n):
            raw[side, slot * run : (slot + 1) * run] = buffer[slot, start : start + run]


def join_parts(geo, buffer, raw, piece):
    for side in range(6):
        index = 0 if side < 2 else side - 1
        run, start = geo.part.runs[index], geo.part.starts[index]
        if side < 2:
            part = 0 if side == 0 else geo.parts - 1
            for slot in range(geo.n):
                raw[side, slot * run : (slot + 1) * run] = buffer[part, slot, start : start + run]
        elif side < 4:
            for part in range(geo.parts):
                for slot in range(geo.n):
                    piece[slot * run : (slot + 1) * run] = buffer[part, slot, start : start + run]
                for var in range(geo.v):
                    row = var * geo.x + part * geo.depth
                    raw[side, row : row + geo.depth] = piece[var * geo.depth : (var + 1) * geo.depth]
        else:
            for slot in range(geo.n):
                total = buffer[0, slot, start : start + run]
                for part in range(1, geo.parts):
                    total = total + buffer[part, slot, start : start + run]
                raw[side, slot * run : (slot + 1) * run] = total


def turn(geo, codes, raw, ghosts):
    v, x, y, z = geo.block
    for side in range(6):
        first, second = codes[side] & 1, (codes[side] >> 1) & 1
        layer = raw[side, : geo.rows[side]]
        if side < 4:
            layer = flip_lanes(flip_rows(layer, first, y if side < 2 else x), second, z)
        else:
            layer = flip_lanes(flip_rows(layer, second, y), first, x)
        ghosts[side, : geo.rows[side]] = layer


def face_values(geo, faces, side):
    v, x, y, z = geo.block
    if side < 4:
        depth = y if side < 2 else x
        return [faces[side, var * depth : (var + 1) * depth] for var in range(v)]
    layer = faces[side, :y]
    return [layer] + [pltpu.roll(layer, z - var * x, 1) for var in range(1, v)]


def fill_tall(geo, source, tall):
    v, x, y, z = geo.block
    if len(source.shape) == 5:
        depth = geo.depth
        for part in range(geo.parts):
            tall[:, part * depth : (part + 1) * depth, PAD : PAD + y, :] = source[part]
    else:
        tall[:, :, PAD : PAD + y, :] = source[...]
    for var in range(v):
        tall[var, :, PAD - 1, :] = tall[var, :, PAD, :]
        tall[var, :, PAD + y, :] = tall[var, :, PAD + y - 1, :]


def around(geo, tall, plane):
    v, x, y, z = geo.block
    lane = lax.broadcasted_iota(jnp.int32, (y, z), 1)
    before, after = jnp.maximum(plane - 1, 0), jnp.minimum(plane + 1, x - 1)
    cells, low, high = [], [[], [], []], [[], [], []]
    for var in range(v):
        mid = tall[var, plane, PAD : PAD + y]
        cells.append(mid)
        low[0].append(tall[var, before, PAD : PAD + y])
        high[0].append(tall[var, after, PAD : PAD + y])
        low[1].append(tall[var, plane, PAD - 1 : PAD - 1 + y])
        high[1].append(tall[var, plane, PAD + 1 : PAD + 1 + y])
        low[2].append(jnp.where(lane == 0, mid, pltpu.roll(mid, 1, 1)))
        high[2].append(jnp.where(lane == z - 1, mid, pltpu.roll(mid, z - 1, 1)))
    return cells, low, high


def flux_entry(geo, mats, direction, row, column):
    return mats[(direction * geo.v + row) * geo.v + column]


def step_plane(geo, mats, cells, low, high, rate):
    v = geo.v
    total = [None] * v
    for direction in range(3):
        lows, highs = low[direction], high[direction]
        mean_low = 0.5 * (lows[0] + cells[0])
        mean_high = 0.5 * (cells[0] + highs[0])
        square_low = 1.0 + mean_low * mean_low
        square_high = 1.0 + mean_high * mean_high
        spread_low = square_low * lax.rsqrt(square_low)
        spread_high = square_high * lax.rsqrt(square_high)
        slopes = [highs[var] - lows[var] for var in range(v)]
        for var in range(v):
            term = spread_low * (cells[var] - lows[var]) - spread_high * (highs[var] - cells[var])
            for column in range(v):
                term = term + flux_entry(geo, mats, direction, var, column) * slopes[column]
            total[var] = term if total[var] is None else total[var] + term
    scale = (0.5 * time_step) * rate
    return [cells[var] - scale * total[var] - damping * jnp.tanh(cells[var]) for var in range(v)]


def adjoint_plane(geo, mats, cells, low, high, grads, weight, weight_low, weight_high):
    v = geo.v
    total = [None] * v
    extra = None
    for direction in range(3):
        spreads, steps = [], []
        for lower, upper, lower_weight, upper_weight in (
            (low[direction], cells, weight_low[direction], weight),
            (cells, high[direction], weight, weight_high[direction]),
        ):
            mean = 0.5 * (lower[0] + upper[0])
            square = 1.0 + mean * mean
            inverse = lax.rsqrt(square)
            jump = [lower_weight[var] - upper_weight[var] for var in range(v)]
            product = jump[0] * (upper[0] - lower[0])
            for var in range(1, v):
                product = product + jump[var] * (upper[var] - lower[var])
            product = product * (mean * inverse)
            extra = product if extra is None else extra + product
            spreads.append(square * inverse)
            steps.append(jump)
        slopes = [steps[0][var] + steps[1][var] for var in range(v)]
        for var in range(v):
            term = spreads[1] * steps[1][var] - spreads[0] * steps[0][var]
            for row in range(v):
                term = term + flux_entry(geo, mats, direction, row, var) * slopes[row]
            total[var] = term if total[var] is None else total[var] + term
    total[0] = total[0] - 0.5 * extra
    out = []
    for var in range(v):
        bend = jnp.tanh(cells[var])
        slope = (1.0 - damping) + damping * (bend * bend)
        out.append(grads[var] * slope - (0.5 * time_step) * total[var])
    return out


def step_face(geo, mats, side, cells, ghosts, rate):
    v = geo.v
    mean = 0.5 * (cells[0] + ghosts[0])
    square = 1.0 + mean * mean
    spread = square * lax.rsqrt(square)
    gap = [ghosts[var] - cells[var] for var in range(v)]
    scale = (0.5 * time_step) * rate
    out = []
    for var in range(v):
        total = flux_entry(geo, mats, side // 2, var, 0) * gap[0]
        for column in range(1, v):
            total = total + flux_entry(geo, mats, side // 2, var, column) * gap[column]
        if side % 2 == 0:
            out.append(scale * (spread * gap[var] - total))
        else:
            out.append(scale * (spread * gap[var] + total))
    return out


def adjoint_face(geo, mats, side, cells, ghosts, weight, ghost_weight):
    v = geo.v
    mean = 0.5 * (cells[0] + ghosts[0])
    square = 1.0 + mean * mean
    inverse = lax.rsqrt(square)
    spread = square * inverse
    jump = [weight[var] - ghost_weight[var] for var in range(v)]
    product = jump[0] * (ghosts[0] - cells[0])
    for var in range(1, v):
        product = product + jump[var] * (ghosts[var] - cells[var])
    product = (0.5 * product) * (mean * inverse)
    out = []
    for var in range(v):
        total = flux_entry(geo, mats, side // 2, 0, var) * jump[0]
        for row in range(1, v):
            total = total + flux_entry(geo, mats, side // 2, row, var) * jump[row]
        if side % 2 == 0:
            total = spread * jump[var] + total
        else:
            total = spread * jump[var] - total
        if var == 0:
            total = total - product
        out.append((-0.5 * time_step) * total)
    return out


def pack_kernel(geo, late, part, place, owner, neighbours, orientation, mats, stored, grads, rate, *rest):
    weight_faces, rate_faces, buffer, table, flat, pieces = rest
    v, x, y, z = geo.block
    depth = geo.depth
    for index in range(2, 6):
        late.wait(index)
    fill_table(geo, place, part, owner, neighbours, orientation, table)
    for direction in range(3):
        for row in range(v):
            for column in range(v):
                flat[(direction * v + row) * v + column] = mats[direction, row, column]
    late.wait(6)
    lane = lax.broadcasted_iota(jnp.int32, (y, z), 1)
    plane = jnp.where(part[0] == geo.parts - 1, depth - 1, 0)
    high = jnp.zeros((y, z), jnp.float32)
    low = jnp.zeros((y, z), jnp.float32)
    for var in range(v):
        pieces[0, var * y : (var + 1) * y] = stored[var, plane]
        pieces[1, var * depth : (var + 1) * depth] = stored[var, :, y - 1, :]
        pieces[2, var * depth : (var + 1) * depth] = stored[var, :, 0, :]
        for step in range(depth):
            place_now = var * x + part[0] * depth + step
            tile = pltpu.roll(stored[var, step], place_now + 1, 1)
            high = jnp.where(lane == place_now, tile, high)
            low = jnp.where(lane == place_now + 1, tile, low)
    pieces[3, :y] = high
    pieces[4, :y] = pltpu.roll(low, z - 1, 1)
    cut(geo, geo.part, pieces, buffer, 0)
    late.wait(8)
    rate_faces[0, :y] = rate[x - 1]
    rate_faces[1, :y] = rate[0]
    rate_faces[2, :x] = rate[:, y - 1, :]
    rate_faces[3, :x] = rate[:, 0, :]
    high, low = take_z_faces(geo, lambda var, plane: rate[plane], 1)
    rate_faces[4, :y] = repeat_lanes(geo, high)
    rate_faces[5, :y] = repeat_lanes(geo, low)
    take_weight_faces(geo, grads, rate_faces, weight_faces, functools.partial(late.wait, 7))
    late.leave(0)
    cut(geo, geo.whole, weight_faces, buffer, geo.part.total, functools.partial(late.leave, 2))


def take_weight_faces(geo, grads, rate_faces, faces, wait=None):
    v, x, y, z = geo.block
    lane = lax.broadcasted_iota(jnp.int32, (y, z), 1)
    high = jnp.zeros((y, z), jnp.float32)
    low = jnp.zeros((y, z), jnp.float32)
    for var in range(v):
        if wait:
            wait(var)
        faces[0, var * y : (var + 1) * y] = grads[var, x - 1] * rate_faces[0, :y]
        faces[1, var * y : (var + 1) * y] = grads[var, 0] * rate_faces[1, :y]
        faces[2, var * x : (var + 1) * x] = grads[var, :, y - 1, :] * rate_faces[2, :x]
        faces[3, var * x : (var + 1) * x] = grads[var, :, 0, :] * rate_faces[3, :x]
        for plane in range(x):
            place = var * x + plane
            tile = pltpu.roll(grads[var, plane], place + 1, 1)
            high = jnp.where(lane == place, tile, high)
            low = jnp.where(lane == place + 1, tile, low)
    faces[4, :y] = high * rate_faces[4, :y]
    faces[5, :y] = pltpu.roll(low, z - 1, 1) * rate_faces[5, :y]


def route_whole(geo, links, block, arrived, leaving, base):
    for side in range(6):
        source = links.source(block, side)
        run, start, far = geo.whole.runs[side], base + geo.whole.starts[side], base + geo.whole.starts[side ^ 1]
        leaving[links.target(block), start : start + run] = arrived[source, far : far + run]


def route_kernel(geo, late, table, arrived, leaving):
    links = Table(geo, table)
    for block in range(geo.n):
        route_whole(geo, links, block, arrived, leaving, 0)
        late.leave(0, links.target(block))


def route_first_kernel(geo, late, table, arrived, leaving):
    links = Table(geo, table)
    x_side = jnp.where(links.part() == geo.parts - 1, 1, 0)
    for block in range(geo.n):
        route_whole(geo, links, block, arrived, leaving, geo.part.total)
        for index in range(5):
            side, far_index = (x_side, 0) if index == 0 else (index + 1, ((index + 1) ^ 1) - 1)
            source = links.source(block, side)
            run, start, far = geo.part.runs[index], geo.part.starts[index], geo.part.starts[far_index]
            leaving[links.target(block), start : start + run] = arrived[source, far : far + run]
        late.leave(0, links.target(block))


def turn_weights_kernel(geo, late, mats, block, rate, table, buffer, result, ghosts, tall, raw):
    join(geo, buffer, raw, geo.part.total)
    turn(geo, Table(geo, table).codes(), raw, ghosts)
    step_inner_kernel(geo, late, mats, block, rate, result, tall)


def step_inner_kernel(geo, late, mats, block, rate, result, *rest):
    tall = rest[-1]
    late.wait(1)
    late.wait(2)
    fill_tall(geo, block, tall)

    def body(plane, carry):
        cells, low, high = around(geo, tall, plane)
        for var, value in enumerate(step_plane(geo, mats, cells, low, high, rate[plane])):
            result[var, plane] = value
        return carry

    lax.fori_loop(0, geo.x, body, 0)
    late.leave(0)
    if len(rest) == 2:
        faces = rest[0]
        v, x, y, z = geo.block
        for var in range(v):
            faces[0, var * y : (var + 1) * y] = tall[var, x - 1, PAD : PAD + y]
            faces[1, var * y : (var + 1) * y] = tall[var, 0, PAD : PAD + y]
            faces[2, var * x : (var + 1) * x] = tall[var, :, PAD + y - 1, :]
            faces[3, var * x : (var + 1) * x] = tall[var, :, PAD, :]
        high, low = take_z_faces(geo, lambda var, plane: tall[var, plane, PAD : PAD + y])
        faces[4, :y] = high
        faces[5, :y] = low
        late.leave(2)


def adjoint_inner_kernel(geo, late, mats, block, grads, rate, result, tall, weights):
    v, x, y, z = geo.block
    for index in range(1, 4):
        late.wait(index)
    fill_tall(geo, block, tall)

    def scale(plane, carry):
        for var in range(v):
            weights[var, plane, PAD : PAD + y] = rate[plane] * grads[var, plane]
        return carry

    lax.fori_loop(0, x, scale, 0)
    for var in range(v):
        weights[var, :, PAD - 1, :] = weights[var, :, PAD, :]
        weights[var, :, PAD + y, :] = weights[var, :, PAD + y - 1, :]

    def body(plane, carry):
        cells, low, high = around(geo, tall, plane)
        weight, weight_low, weight_high = around(geo, weights, plane)
        here = [grads[var, plane] for var in range(v)]
        values = adjoint_plane(geo, mats, cells, low, high, here, weight, weight_low, weight_high)
        for var, value in enumerate(values):
            result[var, plane] = value
        return carry

    lax.fori_loop(0, x, body, 0)


def add_terms(geo, values, inner, result, leave=None):
    v, x, y, z = geo.block
    lane = lax.broadcasted_iota(jnp.int32, (y, z), 1)
    zero = jnp.zeros((y, z), jnp.float32)
    ends = (lane == 0) | (lane == z - 1)
    even = lane % 2 == 0
    for var in range(v):
        high, low = values[4][var], pltpu.roll(values[5][var], 1, 1)
        mixed = (jnp.where(even, high, low), jnp.where(even, low, high))
        for plane in range(x):
            change = jnp.where(ends, pltpu.roll(mixed[plane % 2], z - 1 - plane, 1), zero)
            if plane == 0:
                change = change + values[1][var]
            if plane == x - 1:
                change = change + values[0][var]
            result[var, plane] = inner[var, plane] + change
        result[var, :, y - 1, :] = result[var, :, y - 1, :] + values[2][var]
        result[var, :, 0, :] = result[var, :, 0, :] + values[3][var]
        if leave:
            leave(var)


def step_edge_kernel(geo, first, late, table, mats, inner, faces, rate_faces, arrived, result, *rest):
    v, x, y, z = geo.block
    if first:
        new_faces, sent, ghosts, raw, piece = rest
        join_parts(geo, arrived, raw, piece)
        turn(geo, Table(geo, table).codes(), raw, ghosts)
        late.leave(4)
    else:
        ghosts = arrived
        late.wait(2)
        late.wait(5)
    late.wait(3)
    values = []
    for side in range(6):
        depth = y if side < 2 or side > 3 else x
        cells, outer = face_values(geo, faces, side), face_values(geo, ghosts, side)
        values.append(step_face(geo, mats, side, cells, outer, rate_faces[side, :depth]))
    add_terms(geo, values, inner, result)
    if first:
        take_xy_faces(geo, result, new_faces)
        high, low = take_z_faces(geo, lambda var, plane: result[var, plane])
        new_faces[4, :y] = high
        new_faces[5, :y] = low
        late.leave(2)
        cut(geo, geo.whole, new_faces, sent, 0, functools.partial(late.leave, 3))


def adjoint_edge_kernel(geo, last, late, table, mats, inner, faces, weight_faces, *rest):
    v, x, y, z = geo.block
    codes = Table(geo, table).codes()
    if last:
        ghosts, weight_buffer, result, raw, weight_ghosts = rest
        join(geo, weight_buffer, raw)
        turn(geo, codes, raw, weight_ghosts)
    else:
        rate_faces, buffer, weight_ghosts, result, new_faces, sent, ghosts, raw = rest
        join(geo, buffer, raw)
        turn(geo, codes, raw, ghosts)
        late.leave(3)
    values = []
    for side in range(6):
        views = [face_values(geo, field, side) for field in (faces, ghosts, weight_faces, weight_ghosts)]
        values.append(adjoint_face(geo, mats, side, *views))
    add_terms(geo, values, inner, result, functools.partial(late.leave, 0) if last else None)
    if not last:
        take_weight_faces(geo, result, rate_faces, new_faces)
        cut(geo, geo.whole, new_faces, sent, 0, functools.partial(late.leave, 2))


class Late:
    def __init__(self, arrivals, departures, sems):
        self.arrivals, self.departures, self.sems, self.started = arrivals, departures, sems, []

    def wait(self, index, slot=0):
        if index in self.arrivals:
            self.arrivals[index][slot].wait()

    def leave(self, index, slot=None):
        if index in self.departures:
            source, target = self.departures[index]
            if slot is not None:
                source, target = source.at[slot], target.at[slot]
            copy = pltpu.make_async_copy(source, target, self.sems.at[len(self.started)])
            copy.start()
            self.started.append(copy)


def call(kernel, ins, outs, scratch, flops, fetch=(), aliases=None):
    late_in = [(index, kind, shape) for index, (kind, shape) in enumerate(ins) if kind in "HCTF"]
    arrive = sum(shape[0] if kind == "C" else 1 for _, kind, shape in late_in)
    late_out = [(index, shape) for index, (kind, shape) in enumerate(outs) if kind in "HB"]
    count_in, count_out = len(late_in), len(late_out)
    sends = sum(shape[0] if kind == "B" else 1 for kind, shape in outs if kind in "HBD")

    def body(*refs):
        given = list(refs[: len(ins)])
        made = list(refs[len(ins) : len(ins) + len(outs)])
        rest = list(refs[len(ins) + len(outs) :])
        own = rest[: len(scratch)]
        stage = rest[len(scratch) : len(scratch) + count_in + count_out]
        sems_in = rest[len(scratch) + count_in + count_out] if count_in or fetch else None
        sems_out = rest[-1] if sends else None
        arrivals, departures = {}, {}
        used = 0
        for slot, (index, kind, shape) in enumerate(late_in):
            pairs = [(given[index], stage[slot])]
            if kind == "C":
                pairs = [(given[index].at[chunk], stage[slot].at[chunk]) for chunk in range(shape[0])]
            arrivals[index] = []
            for source, target in pairs:
                copy = pltpu.make_async_copy(source, target, sems_in.at[used])
                copy.start()
                arrivals[index].append(copy)
                used += 1
            given[index] = stage[slot]
        for slot, (index, _) in enumerate(late_out):
            departures[index] = (stage[count_in + slot], made[index])
            made[index] = stage[count_in + slot]
        for index, (kind, _) in enumerate(outs):
            if kind == "D":
                departures[index] = (made[index - 1], made[index])
        fetched = []
        for slot, (source, target) in enumerate(fetch):
            copy = pltpu.make_async_copy(given[source], made[target], sems_in.at[arrive + slot])
            copy.start()
            fetched.append(copy)
        late = Late(arrivals, departures, sems_out)
        hidden_in = {source for source, _ in fetch}
        hidden_out = {target for _, target in fetch}
        kernel(
            late,
            *[ref for index, ref in enumerate(given) if index not in hidden_in],
            *[ref for index, ref in enumerate(made) if index not in hidden_out and outs[index][0] != "D"],
            *own,
        )
        assert len(late.started) == sends
        for copy in fetched + late.started:
            copy.wait()

    hbm = pl.BlockSpec(memory_space=pltpu.HBM)
    specs = {"C": hbm, "T": hbm, "F": hbm, "S": SMEM, "V": VMEM, "R": VMEM, "H": hbm, "B": hbm, "D": hbm, "P": hbm, "M": SMEM, "I": SMEM}
    scratch_shapes = [pltpu.VMEM(shape, jnp.float32) for shape in scratch]
    stages = {"T": (pltpu.SMEM, jnp.int32), "F": (pltpu.SMEM, jnp.float32)}
    for _, kind, shape in late_in:
        memory, dtype = stages.get(kind, (pltpu.VMEM, jnp.float32))
        scratch_shapes.append(memory(shape, dtype))
    scratch_shapes += [pltpu.VMEM(shape, jnp.float32) for _, shape in late_out]
    if count_in or fetch:
        scratch_shapes.append(pltpu.SemaphoreType.DMA((arrive + len(fetch),)))
    if sends:
        scratch_shapes.append(pltpu.SemaphoreType.DMA((sends,)))
    shapes = {"V": jax.ShapeDtypeStruct, "R": pltpu.VMEM, "H": pltpu.HBM, "B": pltpu.HBM, "D": pltpu.HBM}
    shapes.update({"M": pltpu.SMEM, "I": pltpu.SMEM})
    invoke = pl.pallas_call(
        body,
        in_specs=[specs[kind] for kind, _ in ins],
        out_specs=[specs[kind] for kind, _ in outs],
        out_shape=[shapes[kind](shape, jnp.int32 if kind == "I" else jnp.float32) for kind, shape in outs],
        scratch_shapes=scratch_shapes,
        input_output_aliases=aliases or {},
        compiler_params=pltpu.CompilerParams(vmem_limit_bytes=VMEM_LIMIT),
        cost_estimate=pl.CostEstimate(flops=flops, bytes_accessed=3 << 20, transcendentals=0),
    )

    def run(*operands):
        placed = {"C": pltpu.HBM, "T": pltpu.HBM, "F": pltpu.HBM, "M": pltpu.SMEM, "H": pltpu.HBM, "R": pltpu.VMEM, "P": pltpu.HBM}
        return invoke(
            *[
                pltpu.with_memory_space_constraint(operand, placed[kind]) if kind in placed else operand
                for operand, (kind, _) in zip(operands, ins)
            ]
        )

    return run


def on_device(count, parts, checkpoint, seeds, cell_rate, flux_mats, owner, neighbours, orientation):
    nvars, cx, cy, cz = seeds.shape[2:]
    geo = Geometry(nvars, cx, cy, cz, count, parts)
    rate = cell_rate[0]
    grads = seeds[0, 0]
    place = lax.axis_index("space").astype(jnp.int32).reshape(1)
    part = lax.axis_index("ckpt").astype(jnp.int32).reshape(1)
    work = nvars * nvars * 3 * 4 * cx * cy * cz
    few = work // 16
    whole, both = geo.buffer(geo.whole.total), geo.buffer(geo.part.total + geo.whole.total)
    some = -(-geo.part.total // 8) * 8

    stored_shape, block, faces_shape = checkpoint.shape[1:], geo.block, geo.faces
    rate_block = cell_rate.shape[1:]
    scalar, near, kept_near, kept_scalar = ("S", None), ("V", None), ("R", None), ("M", None)

    def far(shape):
        return ("H", shape)

    def swap(buffer):
        return lax.all_to_all(buffer, "space", 0, 0, tiled=True)

    def route(arrived):
        return call(functools.partial(route_kernel, geo), [kept_scalar, near], [("B", whole)], [], few)(
            table, arrived
        )[0]

    def adjoint_inner(state, state_kind, grads, grads_kind):
        return call(
            functools.partial(adjoint_inner_kernel, geo),
            [kept_scalar, state_kind, grads_kind, far(rate_block)],
            [("R", block)],
            [geo.tall] * 2,
            2 * work,
        )(mats, state, grads, rate)[0]

    weight_faces, rate_faces, sent, table, mats = call(
        functools.partial(pack_kernel, geo),
        [scalar] * 2
        + [("T", owner.shape), ("T", neighbours.shape), ("T", orientation.shape), ("F", flux_mats.shape)]
        + [far(stored_shape), ("C", block), far(rate_block)],
        [far(faces_shape), ("R", geo.rate_faces), ("B", both), ("I", (7 + 7 * count,)), ("M", (3 * nvars * nvars,))],
        [faces_shape],
        few,
    )(part, place, owner, neighbours, orientation, flux_mats, checkpoint[0], grads, rate)
    fixed = (table, mats)
    kept, sent = lax.optimization_barrier((checkpoint[0], sent))
    arrived = swap(sent)
    state = lax.all_gather(kept, "ckpt", axis=0)
    arrived, state = lax.optimization_barrier((arrived, state))
    (leaving,) = call(functools.partial(route_first_kernel, geo), [kept_scalar, near], [("B", both)], [], few)(
        table, arrived
    )
    first_ghosts = swap(leaving)
    inner, faces, kept_faces = call(
        functools.partial(step_inner_kernel, geo),
        [kept_scalar, far(state.shape), far(rate_block)],
        [("R", block), ("R", faces_shape), ("D", faces_shape)],
        [geo.tall],
        work,
    )(mats, state, rate)
    first_ghosts, inner, faces = lax.optimization_barrier((first_ghosts, inner, faces))
    gathered = lax.all_gather(first_ghosts[:, :some], "ckpt", axis=0)
    next_state, next_faces, kept_next_faces, sent, ghosts = call(
        functools.partial(step_edge_kernel, geo, True),
        [kept_scalar] * 2 + [kept_near] * 3 + [near],
        [("R", block), ("R", faces_shape), ("D", faces_shape), ("B", whole), far(faces_shape)],
        [faces_shape, faces_shape[1:]],
        few,
        aliases={2: 0},
    )(*fixed, inner, faces, rate_faces, gathered)

    arrived = swap(sent)
    inner = adjoint_inner(next_state, kept_near, grads, far(block))
    arrived, inner = lax.optimization_barrier((arrived, inner))
    leaving = route(arrived)
    later_state, leaving = lax.optimization_barrier((next_state, leaving))
    next_ghosts = swap(leaving)
    final_inner, weight_ghosts, weight_faces = call(
        functools.partial(turn_weights_kernel, geo),
        [kept_scalar, kept_near, far(rate_block), kept_scalar, near, ("P", None)],
        [far(block), ("R", faces_shape), ("R", faces_shape)],
        [geo.tall, faces_shape],
        work,
        fetch=((5, 2),),
    )(mats, later_state, rate, table, first_ghosts, weight_faces)
    next_ghosts, final_inner, weight_ghosts, weight_faces = lax.optimization_barrier(
        (next_ghosts, final_inner, weight_ghosts, weight_faces)
    )
    grads_now, next_weight_faces, sent, turned = call(
        functools.partial(adjoint_edge_kernel, geo, False),
        [kept_scalar] * 2 + [kept_near] * 4 + [near, kept_near],
        [("R", block), ("R", faces_shape), ("B", whole), far(faces_shape)],
        [faces_shape],
        few,
        aliases={2: 0},
    )(*fixed, inner, next_faces, weight_faces, rate_faces, next_ghosts, weight_ghosts)

    arrived = swap(sent)
    inner = adjoint_inner(state, far(state.shape), grads_now, kept_near)
    arrived, inner = lax.optimization_barrier((arrived, inner))
    leaving = route(arrived)
    final_inner, leaving = lax.optimization_barrier((final_inner, leaving))
    last_ghosts = swap(leaving)
    final, faces, ghosts = call(
        functools.partial(step_edge_kernel, geo, False),
        [kept_scalar] * 2 + [far(block), far(faces_shape), kept_near, far(faces_shape), ("P", None), ("P", None)],
        [("V", block), ("R", faces_shape), ("R", faces_shape)],
        [],
        work,
        fetch=((6, 1), (7, 2)),
    )(*fixed, final_inner, kept_next_faces, rate_faces, turned, kept_faces, ghosts)
    last_ghosts, final, faces, ghosts = lax.optimization_barrier((last_ghosts, final, faces, ghosts))
    (adjoint,) = call(
        functools.partial(adjoint_edge_kernel, geo, True),
        [kept_scalar] * 2 + [kept_near] * 4 + [near],
        [("B", block)],
        [faces_shape] * 2,
        few,
    )(*fixed, inner, faces, next_weight_faces, ghosts, last_ghosts)
    return (adjoint[None, None], final[None])


def solution(mesh):
    return jax.shard_map(
        functools.partial(on_device, mesh.shape["space"], mesh.shape["ckpt"]),
        mesh=mesh,
        in_specs=(
            P("space", None, "ckpt", None, None),
            P("ckpt", "space", None, None, None, None),
            P("space", None, None, None),
            P(),
            P(),
            P(),
            P(),
        ),
        out_specs=(P("ckpt", "space", None, None, None, None), P("space", None, None, None, None)),
        check_vma=False,
    )
```

```python
import functools

import jax
import jax.numpy as jnp
from jax import lax
from jax.experimental import pallas as pl
from jax.experimental.pallas import tpu as pltpu
from jax.sharding import PartitionSpec as P

STEPS = 2
time_step = 0.05
damping = 0.015

PAD = 8
VMEM = pl.BlockSpec(memory_space=pltpu.VMEM)
SMEM = pl.BlockSpec(memory_space=pltpu.SMEM)
VMEM_LIMIT = 16 * 1024 * 1024


class Pieces:
    def __init__(self, rows, count):
        self.rows = rows
        self.runs = [-(-length // count) for length in rows]
        self.starts = [sum(self.runs[:index]) for index in range(len(rows))]
        self.total = sum(self.runs)


class Geometry:
    def __init__(self, nvars, cx, cy, cz, count, parts):
        self.v, self.x, self.y, self.z, self.n, self.parts = nvars, cx, cy, cz, count, parts
        self.depth = cx // parts
        self.rows = [nvars * cy] * 2 + [nvars * cx] * 2 + [cy] * 2
        self.whole = Pieces(self.rows, count)
        self.part = Pieces([nvars * cy] + [nvars * self.depth] * 2 + [cy], count)
        self.face_rows = -(-max(run * count for run in self.whole.runs) // 8) * 8
        self.block = (nvars, cx, cy, cz)
        self.tall = (nvars, cx, cy + 2 * PAD, cz)
        self.faces = (6, self.face_rows, cz)
        self.rate_faces = (6, max(cx, cy), cz)

    def buffer(self, rows):
        return (self.n, -(-rows // 8) * 8, self.z)


def take_z_faces(geo, load, variables=None):
    v, x, y, z = geo.block
    lane = lax.broadcasted_iota(jnp.int32, (y, z), 1)
    high = jnp.zeros((y, z), jnp.float32)
    low = jnp.zeros((y, z), jnp.float32)
    for var in range(variables or v):
        for plane in range(x):
            place = var * x + plane
            tile = pltpu.roll(load(var, plane), place + 1, 1)
            high = jnp.where(lane == place, tile, high)
            low = jnp.where(lane == place + 1, tile, low)
    return high, pltpu.roll(low, z - 1, 1)


def repeat_lanes(geo, layer):
    total = layer
    for var in range(1, geo.v):
        total = total + pltpu.roll(layer, var * geo.x, 1)
    return total


def take_xy_faces(geo, source, faces):
    v, x, y, z = geo.block
    faces[0, : v * y] = source[:, x - 1].reshape(v * y, z)
    faces[1, : v * y] = source[:, 0].reshape(v * y, z)
    for var in range(v):
        faces[2, var * x : (var + 1) * x] = source[var, :, y - 1, :]
        faces[3, var * x : (var + 1) * x] = source[var, :, 0, :]


def cut(geo, pieces, faces, buffer, base, leave=None):
    for slot in range(geo.n):
        for index, (run, start) in enumerate(zip(pieces.runs, pieces.starts)):
            buffer[slot, base + start : base + start + run] = faces[index, slot * run : (slot + 1) * run]
        if leave:
            leave(slot)


class Table:
    def __init__(self, geo, ref):
        self.ref, self.n = ref, geo.n

    def codes(self):
        return [self.ref[side] for side in range(6)]

    def part(self):
        return self.ref[6]

    def target(self, block):
        return self.ref[7 + block]

    def source(self, block, side):
        return self.ref[7 + self.n + block * 6 + side]


def fill_table(geo, place, part, owner, neighbours, orientation, table):
    own = jnp.int32(0)
    table[6] = part[0]
    for block in range(geo.n):
        own = jnp.where(owner[block] == place[0], block, own)
        table[7 + block] = owner[block]
        for side in range(6):
            table[7 + geo.n + block * 6 + side] = owner[neighbours[block, side]]
    for side in range(6):
        table[side] = orientation[own, side]


def flip_rows(values, flag, length):
    rows, z = values.shape
    grouped = values.reshape(rows // length, length // 8, 8, z)
    index = lax.broadcasted_iota(jnp.int32, (8, z), 0)
    index = jnp.where(flag == 1, 7 - index, index)
    tiles = length // 8
    out = []
    for group in range(rows // length):
        for tile in range(tiles):
            picked = jnp.where(flag == 1, grouped[group, tiles - 1 - tile], grouped[group, tile])
            out.append(jnp.take_along_axis(picked, index, axis=0))
    return jnp.stack(out).reshape(rows, z)


def flip_lanes(values, flag, length):
    rows, z = values.shape
    lane = lax.broadcasted_iota(jnp.int32, (8, z), 1)
    within = lax.rem(lane, length)
    index = jnp.where(flag == 1, lane + (length - 1) - 2 * within, lane)
    index = jnp.minimum(index, z - 1)
    tiles = values.reshape(rows // 8, 8, z)
    return jnp.stack(
        [jnp.take_along_axis(tiles[tile], index, axis=1) for tile in range(rows // 8)]
    ).reshape(rows, z)


def join(geo, buffer, raw, base=0):
    for side in range(6):
        run, start = geo.whole.runs[side], base + geo.whole.starts[side]
        for slot in range(geo.n):
            raw[side, slot * run : (slot + 1) * run] = buffer[slot, start : start + run]


def part_of_lane(geo, rows):
    lane = lax.broadcasted_iota(jnp.int32, (rows, geo.z), 1)
    return lax.rem(lane, geo.x) // geo.depth


def join_parts(geo, buffer, raw, piece, zpiece):
    for side in range(6):
        index = 0 if side < 2 else min(side - 1, 3)
        run, start = geo.part.runs[index], geo.part.starts[index]
        if side < 2:
            part = 0 if side == 0 else geo.parts - 1
            for slot in range(geo.n):
                raw[side, slot * run : (slot + 1) * run] = buffer[part, slot, start : start + run]
        elif side < 4:
            for part in range(geo.parts):
                for slot in range(geo.n):
                    piece[slot * run : (slot + 1) * run] = buffer[part, slot, start : start + run]
                for var in range(geo.v):
                    row = var * geo.x + part * geo.depth
                    raw[side, row : row + geo.depth] = piece[var * geo.depth : (var + 1) * geo.depth]
        else:
            lanes = part_of_lane(geo, geo.y)
            total = jnp.zeros((geo.y, geo.z), jnp.float32)
            for part in range(geo.parts):
                if side == 4:
                    for slot in range(geo.n):
                        zpiece[part, slot * run : (slot + 1) * run] = buffer[part, slot, start : start + run]
                    rows = zpiece[part, : geo.y]
                    after = (part + 1) % geo.parts
                    rows = jnp.where(lanes == after, rows, 0.0)
                    total = total + pltpu.roll(rows, geo.z - geo.depth if after else geo.x - geo.depth, 1)
                else:
                    total = total + jnp.where(lanes == part, zpiece[part, : geo.y], 0.0)
            raw[side, : geo.y] = total


def turn(geo, codes, raw, ghosts):
    v, x, y, z = geo.block
    for side in range(6):
        first, second = codes[side] & 1, (codes[side] >> 1) & 1
        layer = raw[side, : geo.rows[side]]
        if side < 4:
            layer = flip_lanes(flip_rows(layer, first, y if side < 2 else x), second, z)
        else:
            layer = flip_lanes(flip_rows(layer, second, y), first, x)
        ghosts[side, : geo.rows[side]] = layer


def face_values(geo, faces, side):
    v, x, y, z = geo.block
    if side < 4:
        depth = y if side < 2 else x
        return [faces[side, var * depth : (var + 1) * depth] for var in range(v)]
    layer = faces[side, :y]
    return [layer] + [pltpu.roll(layer, z - var * x, 1) for var in range(1, v)]


def fill_tall(geo, source, tall):
    v, x, y, z = geo.block
    if len(source.shape) == 5:
        depth = geo.depth
        for part in range(geo.parts):
            tall[:, part * depth : (part + 1) * depth, PAD : PAD + y, :] = source[part]
    else:
        tall[:, :, PAD : PAD + y, :] = source[...]
    for var in range(v):
        tall[var, :, PAD - 1, :] = tall[var, :, PAD, :]
        tall[var, :, PAD + y, :] = tall[var, :, PAD + y - 1, :]


def around(geo, tall, plane):
    v, x, y, z = geo.block
    lane = lax.broadcasted_iota(jnp.int32, (y, z), 1)
    before, after = jnp.maximum(plane - 1, 0), jnp.minimum(plane + 1, x - 1)
    cells, low, high = [], [[], [], []], [[], [], []]
    for var in range(v):
        mid = tall[var, plane, PAD : PAD + y]
        cells.append(mid)
        low[0].append(tall[var, before, PAD : PAD + y])
        high[0].append(tall[var, after, PAD : PAD + y])
        low[1].append(tall[var, plane, PAD - 1 : PAD - 1 + y])
        high[1].append(tall[var, plane, PAD + 1 : PAD + 1 + y])
        low[2].append(jnp.where(lane == 0, mid, pltpu.roll(mid, 1, 1)))
        high[2].append(jnp.where(lane == z - 1, mid, pltpu.roll(mid, z - 1, 1)))
    return cells, low, high


def flux_entry(geo, mats, direction, row, column):
    return mats[(direction * geo.v + row) * geo.v + column]


def step_plane(geo, mats, cells, low, high, rate):
    v = geo.v
    total = [None] * v
    for direction in range(3):
        lows, highs = low[direction], high[direction]
        mean_low = 0.5 * (lows[0] + cells[0])
        mean_high = 0.5 * (cells[0] + highs[0])
        square_low = 1.0 + mean_low * mean_low
        square_high = 1.0 + mean_high * mean_high
        spread_low = square_low * lax.rsqrt(square_low)
        spread_high = square_high * lax.rsqrt(square_high)
        slopes = [highs[var] - lows[var] for var in range(v)]
        for var in range(v):
            term = spread_low * (cells[var] - lows[var]) - spread_high * (highs[var] - cells[var])
            for column in range(v):
                term = term + flux_entry(geo, mats, direction, var, column) * slopes[column]
            total[var] = term if total[var] is None else total[var] + term
    scale = (0.5 * time_step) * rate
    return [cells[var] - scale * total[var] - damping * jnp.tanh(cells[var]) for var in range(v)]


def adjoint_plane(geo, mats, cells, low, high, grads, weight, weight_low, weight_high):
    v = geo.v
    total = [None] * v
    extra = None
    for direction in range(3):
        spreads, steps = [], []
        for lower, upper, lower_weight, upper_weight in (
            (low[direction], cells, weight_low[direction], weight),
            (cells, high[direction], weight, weight_high[direction]),
        ):
            mean = 0.5 * (lower[0] + upper[0])
            square = 1.0 + mean * mean
            inverse = lax.rsqrt(square)
            jump = [lower_weight[var] - upper_weight[var] for var in range(v)]
            product = jump[0] * (upper[0] - lower[0])
            for var in range(1, v):
                product = product + jump[var] * (upper[var] - lower[var])
            product = product * (mean * inverse)
            extra = product if extra is None else extra + product
            spreads.append(square * inverse)
            steps.append(jump)
        slopes = [steps[0][var] + steps[1][var] for var in range(v)]
        for var in range(v):
            term = spreads[1] * steps[1][var] - spreads[0] * steps[0][var]
            for row in range(v):
                term = term + flux_entry(geo, mats, direction, row, var) * slopes[row]
            total[var] = term if total[var] is None else total[var] + term
    total[0] = total[0] - 0.5 * extra
    out = []
    for var in range(v):
        bend = jnp.tanh(cells[var])
        slope = (1.0 - damping) + damping * (bend * bend)
        out.append(grads[var] * slope - (0.5 * time_step) * total[var])
    return out


def step_face(geo, mats, side, cells, ghosts, rate):
    v = geo.v
    mean = 0.5 * (cells[0] + ghosts[0])
    square = 1.0 + mean * mean
    spread = square * lax.rsqrt(square)
    gap = [ghosts[var] - cells[var] for var in range(v)]
    scale = (0.5 * time_step) * rate
    out = []
    for var in range(v):
        total = flux_entry(geo, mats, side // 2, var, 0) * gap[0]
        for column in range(1, v):
            total = total + flux_entry(geo, mats, side // 2, var, column) * gap[column]
        if side % 2 == 0:
            out.append(scale * (spread * gap[var] - total))
        else:
            out.append(scale * (spread * gap[var] + total))
    return out


def adjoint_face(geo, mats, side, cells, ghosts, weight, ghost_weight):
    v = geo.v
    mean = 0.5 * (cells[0] + ghosts[0])
    square = 1.0 + mean * mean
    inverse = lax.rsqrt(square)
    spread = square * inverse
    jump = [weight[var] - ghost_weight[var] for var in range(v)]
    product = jump[0] * (ghosts[0] - cells[0])
    for var in range(1, v):
        product = product + jump[var] * (ghosts[var] - cells[var])
    product = (0.5 * product) * (mean * inverse)
    out = []
    for var in range(v):
        total = flux_entry(geo, mats, side // 2, 0, var) * jump[0]
        for row in range(1, v):
            total = total + flux_entry(geo, mats, side // 2, row, var) * jump[row]
        if side % 2 == 0:
            total = spread * jump[var] + total
        else:
            total = spread * jump[var] - total
        if var == 0:
            total = total - product
        out.append((-0.5 * time_step) * total)
    return out


def pack_kernel(geo, late, part, place, owner, neighbours, orientation, mats, stored, grads, rate, *rest):
    weight_faces, rate_faces, buffer, table, flat, pieces = rest
    v, x, y, z = geo.block
    depth = geo.depth
    late.wait(6)
    lane = lax.broadcasted_iota(jnp.int32, (y, z), 1)
    plane = jnp.where(part[0] == geo.parts - 1, depth - 1, 0)
    high = jnp.zeros((y, z), jnp.float32)
    low = jnp.zeros((y, z), jnp.float32)
    for var in range(v):
        pieces[0, var * y : (var + 1) * y] = stored[var, plane]
        pieces[1, var * depth : (var + 1) * depth] = stored[var, :, y - 1, :]
        pieces[2, var * depth : (var + 1) * depth] = stored[var, :, 0, :]
        for step in range(depth):
            place_now = var * x + part[0] * depth + step
            tile = pltpu.roll(stored[var, step], place_now + 1, 1)
            high = jnp.where(lane == place_now, tile, high)
            low = jnp.where(lane == place_now + 1, tile, low)
    shift = jnp.where(part[0] == geo.parts - 1, z - x + depth, depth)
    pieces[3, :y] = high + pltpu.roll(low, lax.rem(shift + z - 1, z), 1)
    cut(geo, geo.part, pieces, buffer, 0)
    late.wait(8)
    rate_faces[0, :y] = rate[x - 1]
    rate_faces[1, :y] = rate[0]
    rate_faces[2, :x] = rate[:, y - 1, :]
    rate_faces[3, :x] = rate[:, 0, :]
    high, low = take_z_faces(geo, lambda var, plane: rate[plane], 1)
    rate_faces[4, :y] = repeat_lanes(geo, high)
    rate_faces[5, :y] = repeat_lanes(geo, low)
    take_weight_faces(geo, grads, rate_faces, weight_faces, functools.partial(late.wait, 7))
    late.leave(0)
    cut(geo, geo.whole, weight_faces, buffer, geo.part.total, functools.partial(late.leave, 2))
    for index in range(2, 6):
        late.wait(index)
    fill_table(geo, place, part, owner, neighbours, orientation, table)
    for direction in range(3):
        for row in range(v):
            for column in range(v):
                flat[(direction * v + row) * v + column] = mats[direction, row, column]


def take_weight_faces(geo, grads, rate_faces, faces, wait=None):
    v, x, y, z = geo.block
    lane = lax.broadcasted_iota(jnp.int32, (y, z), 1)
    high = jnp.zeros((y, z), jnp.float32)
    low = jnp.zeros((y, z), jnp.float32)
    for var in range(v):
        if wait:
            wait(var)
        faces[0, var * y : (var + 1) * y] = grads[var, x - 1] * rate_faces[0, :y]
        faces[1, var * y : (var + 1) * y] = grads[var, 0] * rate_faces[1, :y]
        faces[2, var * x : (var + 1) * x] = grads[var, :, y - 1, :] * rate_faces[2, :x]
        faces[3, var * x : (var + 1) * x] = grads[var, :, 0, :] * rate_faces[3, :x]
        for plane in range(x):
            place = var * x + plane
            tile = pltpu.roll(grads[var, plane], place + 1, 1)
            high = jnp.where(lane == place, tile, high)
            low = jnp.where(lane == place + 1, tile, low)
    faces[4, :y] = high * rate_faces[4, :y]
    faces[5, :y] = pltpu.roll(low, z - 1, 1) * rate_faces[5, :y]


def route_whole(geo, links, block, arrived, leaving, base):
    for side in range(6):
        source = links.source(block, side)
        run, start, far = geo.whole.runs[side], base + geo.whole.starts[side], base + geo.whole.starts[side ^ 1]
        leaving[links.target(block), start : start + run] = arrived[source, far : far + run]


def route_kernel(geo, late, table, arrived, leaving):
    links = Table(geo, table)
    for block in range(geo.n):
        route_whole(geo, links, block, arrived, leaving, 0)
        late.leave(0, links.target(block))


def route_first_kernel(geo, late, table, arrived, leaving):
    links = Table(geo, table)
    x_side = jnp.where(links.part() == geo.parts - 1, 1, 0)
    for block in range(geo.n):
        route_whole(geo, links, block, arrived, leaving, geo.part.total)
        for index in range(3):
            side, far_index = (x_side, 0) if index == 0 else (index + 1, 3 - index)
            source = links.source(block, side)
            run, start, far = geo.part.runs[index], geo.part.starts[index], geo.part.starts[far_index]
            leaving[links.target(block), start : start + run] = arrived[source, far : far + run]
        run, start = geo.part.runs[3], geo.part.starts[3]
        from_low = arrived[links.source(block, 4), start : start + run]
        from_high = arrived[links.source(block, 5), start : start + run]
        own_lanes = part_of_lane(geo, run) == links.part()
        leaving[links.target(block), start : start + run] = jnp.where(own_lanes, from_high, from_low)
        late.leave(0, links.target(block))


def turn_weights_kernel(geo, late, mats, block, rate, table, buffer, result, ghosts, tall, raw):
    join(geo, buffer, raw, geo.part.total)
    turn(geo, Table(geo, table).codes(), raw, ghosts)
    step_inner_kernel(geo, late, mats, block, rate, result, tall)


def step_inner_kernel(geo, late, mats, block, rate, result, *rest):
    tall = rest[-1]
    late.wait(1)
    late.wait(2)
    fill_tall(geo, block, tall)

    def body(plane, carry):
        cells, low, high = around(geo, tall, plane)
        for var, value in enumerate(step_plane(geo, mats, cells, low, high, rate[plane])):
            result[var, plane] = value
        return carry

    lax.fori_loop(0, geo.x, body, 0)
    late.leave(0)
    if len(rest) == 2:
        faces = rest[0]
        v, x, y, z = geo.block
        for var in range(v):
            faces[0, var * y : (var + 1) * y] = tall[var, x - 1, PAD : PAD + y]
            faces[1, var * y : (var + 1) * y] = tall[var, 0, PAD : PAD + y]
            faces[2, var * x : (var + 1) * x] = tall[var, :, PAD + y - 1, :]
            faces[3, var * x : (var + 1) * x] = tall[var, :, PAD, :]
        high, low = take_z_faces(geo, lambda var, plane: tall[var, plane, PAD : PAD + y])
        faces[4, :y] = high
        faces[5, :y] = low
        late.leave(2)


def adjoint_inner_kernel(geo, late, mats, block, grads, rate, result, tall, weights):
    v, x, y, z = geo.block
    for index in range(1, 4):
        late.wait(index)
    fill_tall(geo, block, tall)

    def scale(plane, carry):
        for var in range(v):
            weights[var, plane, PAD : PAD + y] = rate[plane] * grads[var, plane]
        return carry

    lax.fori_loop(0, x, scale, 0)
    for var in range(v):
        weights[var, :, PAD - 1, :] = weights[var, :, PAD, :]
        weights[var, :, PAD + y, :] = weights[var, :, PAD + y - 1, :]

    def body(plane, carry):
        cells, low, high = around(geo, tall, plane)
        weight, weight_low, weight_high = around(geo, weights, plane)
        here = [grads[var, plane] for var in range(v)]
        values = adjoint_plane(geo, mats, cells, low, high, here, weight, weight_low, weight_high)
        for var, value in enumerate(values):
            result[var, plane] = value
        return carry

    lax.fori_loop(0, x, body, 0)


def add_terms(geo, values, inner, result, leave=None):
    v, x, y, z = geo.block
    lane = lax.broadcasted_iota(jnp.int32, (y, z), 1)
    zero = jnp.zeros((y, z), jnp.float32)
    ends = (lane == 0) | (lane == z - 1)
    even = lane % 2 == 0
    for var in range(v):
        high, low = values[4][var], pltpu.roll(values[5][var], 1, 1)
        mixed = (jnp.where(even, high, low), jnp.where(even, low, high))
        for plane in range(x):
            change = jnp.where(ends, pltpu.roll(mixed[plane % 2], z - 1 - plane, 1), zero)
            if plane == 0:
                change = change + values[1][var]
            if plane == x - 1:
                change = change + values[0][var]
            result[var, plane] = inner[var, plane] + change
        result[var, :, y - 1, :] = result[var, :, y - 1, :] + values[2][var]
        result[var, :, 0, :] = result[var, :, 0, :] + values[3][var]
        if leave:
            leave(var)


def step_edge_kernel(geo, first, late, table, mats, inner, faces, rate_faces, arrived, result, *rest):
    v, x, y, z = geo.block
    if first:
        new_faces, sent, ghosts, raw, piece, zpiece = rest
        join_parts(geo, arrived, raw, piece, zpiece)
        turn(geo, Table(geo, table).codes(), raw, ghosts)
        late.leave(4)
    else:
        ghosts = arrived
        late.wait(2)
        late.wait(5)
    late.wait(3)
    values = []
    for side in range(6):
        depth = y if side < 2 or side > 3 else x
        cells, outer = face_values(geo, faces, side), face_values(geo, ghosts, side)
        values.append(step_face(geo, mats, side, cells, outer, rate_faces[side, :depth]))
    add_terms(geo, values, inner, result)
    if first:
        take_xy_faces(geo, result, new_faces)
        high, low = take_z_faces(geo, lambda var, plane: result[var, plane])
        new_faces[4, :y] = high
        new_faces[5, :y] = low
        late.leave(2)
        cut(geo, geo.whole, new_faces, sent, 0, functools.partial(late.leave, 3))


def adjoint_edge_kernel(geo, last, late, table, mats, inner, faces, weight_faces, *rest):
    v, x, y, z = geo.block
    codes = Table(geo, table).codes()
    if last:
        ghosts, weight_buffer, result, raw, weight_ghosts = rest
        join(geo, weight_buffer, raw)
        turn(geo, codes, raw, weight_ghosts)
    else:
        rate_faces, buffer, weight_ghosts, result, new_faces, sent, ghosts, raw = rest
        join(geo, buffer, raw)
        turn(geo, codes, raw, ghosts)
        late.leave(3)
    values = []
    for side in range(6):
        views = [face_values(geo, field, side) for field in (faces, ghosts, weight_faces, weight_ghosts)]
        values.append(adjoint_face(geo, mats, side, *views))
    add_terms(geo, values, inner, result, functools.partial(late.leave, 0) if last else None)
    if not last:
        take_weight_faces(geo, result, rate_faces, new_faces)
        cut(geo, geo.whole, new_faces, sent, 0, functools.partial(late.leave, 2))


class Late:
    def __init__(self, arrivals, departures, sems):
        self.arrivals, self.departures, self.sems, self.started = arrivals, departures, sems, []

    def wait(self, index, slot=0):
        if index in self.arrivals:
            self.arrivals[index][slot].wait()

    def leave(self, index, slot=None):
        if index in self.departures:
            source, target = self.departures[index]
            if slot is not None:
                source, target = source.at[slot], target.at[slot]
            copy = pltpu.make_async_copy(source, target, self.sems.at[len(self.started)])
            copy.start()
            self.started.append(copy)


def call(kernel, ins, outs, scratch, flops, fetch=(), aliases=None):
    late_in = [(index, kind, shape) for index, (kind, shape) in enumerate(ins) if kind in "HCTF"]
    arrive = sum(shape[0] if kind == "C" else 1 for _, kind, shape in late_in)
    late_out = [(index, shape) for index, (kind, shape) in enumerate(outs) if kind in "HB"]
    count_in, count_out = len(late_in), len(late_out)
    sends = sum(shape[0] if kind == "B" else 1 for kind, shape in outs if kind in "HBD")

    def body(*refs):
        given = list(refs[: len(ins)])
        made = list(refs[len(ins) : len(ins) + len(outs)])
        rest = list(refs[len(ins) + len(outs) :])
        own = rest[: len(scratch)]
        stage = rest[len(scratch) : len(scratch) + count_in + count_out]
        sems_in = rest[len(scratch) + count_in + count_out] if count_in or fetch else None
        sems_out = rest[-1] if sends else None
        arrivals, departures = {}, {}
        used = 0
        for slot, (index, kind, shape) in enumerate(late_in):
            pairs = [(given[index], stage[slot])]
            if kind == "C":
                pairs = [(given[index].at[chunk], stage[slot].at[chunk]) for chunk in range(shape[0])]
            arrivals[index] = []
            for source, target in pairs:
                copy = pltpu.make_async_copy(source, target, sems_in.at[used])
                copy.start()
                arrivals[index].append(copy)
                used += 1
            given[index] = stage[slot]
        for slot, (index, _) in enumerate(late_out):
            departures[index] = (stage[count_in + slot], made[index])
            made[index] = stage[count_in + slot]
        for index, (kind, _) in enumerate(outs):
            if kind == "D":
                departures[index] = (made[index - 1], made[index])
        fetched = []
        for slot, (source, target) in enumerate(fetch):
            copy = pltpu.make_async_copy(given[source], made[target], sems_in.at[arrive + slot])
            copy.start()
            fetched.append(copy)
        late = Late(arrivals, departures, sems_out)
        hidden_in = {source for source, _ in fetch}
        hidden_out = {target for _, target in fetch}
        kernel(
            late,
            *[ref for index, ref in enumerate(given) if index not in hidden_in],
            *[ref for index, ref in enumerate(made) if index not in hidden_out and outs[index][0] != "D"],
            *own,
        )
        assert len(late.started) == sends
        for copy in fetched + late.started:
            copy.wait()

    hbm = pl.BlockSpec(memory_space=pltpu.HBM)
    specs = {"C": hbm, "T": hbm, "F": hbm, "S": SMEM, "V": VMEM, "R": VMEM, "H": hbm, "B": hbm, "D": hbm, "P": hbm, "M": SMEM, "I": SMEM}
    scratch_shapes = [pltpu.VMEM(shape, jnp.float32) for shape in scratch]
    stages = {"T": (pltpu.SMEM, jnp.int32), "F": (pltpu.SMEM, jnp.float32)}
    for _, kind, shape in late_in:
        memory, dtype = stages.get(kind, (pltpu.VMEM, jnp.float32))
        scratch_shapes.append(memory(shape, dtype))
    scratch_shapes += [pltpu.VMEM(shape, jnp.float32) for _, shape in late_out]
    if count_in or fetch:
        scratch_shapes.append(pltpu.SemaphoreType.DMA((arrive + len(fetch),)))
    if sends:
        scratch_shapes.append(pltpu.SemaphoreType.DMA((sends,)))
    shapes = {"V": jax.ShapeDtypeStruct, "R": pltpu.VMEM, "H": pltpu.HBM, "B": pltpu.HBM, "D": pltpu.HBM}
    shapes.update({"M": pltpu.SMEM, "I": pltpu.SMEM})
    invoke = pl.pallas_call(
        body,
        in_specs=[specs[kind] for kind, _ in ins],
        out_specs=[specs[kind] for kind, _ in outs],
        out_shape=[shapes[kind](shape, jnp.int32 if kind == "I" else jnp.float32) for kind, shape in outs],
        scratch_shapes=scratch_shapes,
        input_output_aliases=aliases or {},
        compiler_params=pltpu.CompilerParams(vmem_limit_bytes=VMEM_LIMIT),
        cost_estimate=pl.CostEstimate(flops=flops, bytes_accessed=3 << 20, transcendentals=0),
    )

    def run(*operands):
        placed = {"C": pltpu.HBM, "T": pltpu.HBM, "F": pltpu.HBM, "M": pltpu.SMEM, "H": pltpu.HBM, "R": pltpu.VMEM, "P": pltpu.HBM}
        return invoke(
            *[
                pltpu.with_memory_space_constraint(operand, placed[kind]) if kind in placed else operand
                for operand, (kind, _) in zip(operands, ins)
            ]
        )

    return run


def on_device(count, parts, checkpoint, seeds, cell_rate, flux_mats, owner, neighbours, orientation):
    nvars, cx, cy, cz = seeds.shape[2:]
    geo = Geometry(nvars, cx, cy, cz, count, parts)
    rate = cell_rate[0]
    grads = seeds[0, 0]
    place = lax.axis_index("space").astype(jnp.int32).reshape(1)
    part = lax.axis_index("ckpt").astype(jnp.int32).reshape(1)
    work = nvars * nvars * 3 * 4 * cx * cy * cz
    few = work // 16
    whole, both = geo.buffer(geo.whole.total), geo.buffer(geo.part.total + geo.whole.total)
    some = -(-geo.part.total // 8) * 8

    stored_shape, block, faces_shape = checkpoint.shape[1:], geo.block, geo.faces
    rate_block = cell_rate.shape[1:]
    scalar, near, kept_near, kept_scalar = ("S", None), ("V", None), ("R", None), ("M", None)

    def far(shape):
        return ("H", shape)

    def swap(buffer):
        return lax.all_to_all(buffer, "space", 0, 0, tiled=True)

    def route(arrived):
        return call(functools.partial(route_kernel, geo), [kept_scalar, near], [("B", whole)], [], few)(
            table, arrived
        )[0]

    def adjoint_inner(state, state_kind, grads, grads_kind):
        return call(
            functools.partial(adjoint_inner_kernel, geo),
            [kept_scalar, state_kind, grads_kind, far(rate_block)],
            [("R", block)],
            [geo.tall] * 2,
            2 * work,
        )(mats, state, grads, rate)[0]

    weight_faces, rate_faces, sent, table, mats = call(
        functools.partial(pack_kernel, geo),
        [scalar] * 2
        + [("T", owner.shape), ("T", neighbours.shape), ("T", orientation.shape), ("F", flux_mats.shape)]
        + [far(stored_shape), ("C", block), far(rate_block)],
        [far(faces_shape), ("R", geo.rate_faces), ("B", both), ("I", (7 + 7 * count,)), ("M", (3 * nvars * nvars,))],
        [faces_shape],
        few,
    )(part, place, owner, neighbours, orientation, flux_mats, checkpoint[0], grads, rate)
    fixed = (table, mats)
    kept, sent = lax.optimization_barrier((checkpoint[0], sent))
    arrived = swap(sent)
    state = lax.all_gather(kept, "ckpt", axis=0)
    arrived, state = lax.optimization_barrier((arrived, state))
    (leaving,) = call(functools.partial(route_first_kernel, geo), [kept_scalar, near], [("B", both)], [], few)(
        table, arrived
    )
    first_ghosts = swap(leaving)
    inner, faces, kept_faces = call(
        functools.partial(step_inner_kernel, geo),
        [kept_scalar, far(state.shape), far(rate_block)],
        [("R", block), ("R", faces_shape), ("D", faces_shape)],
        [geo.tall],
        work,
    )(mats, state, rate)
    first_ghosts, inner, faces = lax.optimization_barrier((first_ghosts, inner, faces))
    gathered = lax.all_gather(first_ghosts[:, :some], "ckpt", axis=0)
    next_state, next_faces, kept_next_faces, sent, ghosts = call(
        functools.partial(step_edge_kernel, geo, True),
        [kept_scalar] * 2 + [kept_near] * 3 + [near],
        [("R", block), ("R", faces_shape), ("D", faces_shape), ("B", whole), far(faces_shape)],
        [faces_shape, faces_shape[1:], (parts,) + faces_shape[1:]],
        few,
        aliases={2: 0},
    )(*fixed, inner, faces, rate_faces, gathered)

    arrived = swap(sent)
    inner = adjoint_inner(next_state, kept_near, grads, far(block))
    arrived, inner = lax.optimization_barrier((arrived, inner))
    leaving = route(arrived)
    later_state, leaving = lax.optimization_barrier((next_state, leaving))
    next_ghosts = swap(leaving)
    final_inner, weight_ghosts, weight_faces = call(
        functools.partial(turn_weights_kernel, geo),
        [kept_scalar, kept_near, far(rate_block), kept_scalar, near, ("P", None)],
        [far(block), ("R", faces_shape), ("R", faces_shape)],
        [geo.tall, faces_shape],
        work,
        fetch=((5, 2),),
    )(mats, later_state, rate, table, first_ghosts, weight_faces)
    next_ghosts, final_inner, weight_ghosts, weight_faces = lax.optimization_barrier(
        (next_ghosts, final_inner, weight_ghosts, weight_faces)
    )
    grads_now, next_weight_faces, sent, turned = call(
        functools.partial(adjoint_edge_kernel, geo, False),
        [kept_scalar] * 2 + [kept_near] * 4 + [near, kept_near],
        [("R", block), ("R", faces_shape), ("B", whole), far(faces_shape)],
        [faces_shape],
        few,
        aliases={2: 0},
    )(*fixed, inner, next_faces, weight_faces, rate_faces, next_ghosts, weight_ghosts)

    arrived = swap(sent)
    inner = adjoint_inner(state, far(state.shape), grads_now, kept_near)
    arrived, inner = lax.optimization_barrier((arrived, inner))
    leaving = route(arrived)
    final_inner, leaving = lax.optimization_barrier((final_inner, leaving))
    last_ghosts = swap(leaving)
    final, faces, ghosts = call(
        functools.partial(step_edge_kernel, geo, False),
        [kept_scalar] * 2 + [far(block), far(faces_shape), kept_near, far(faces_shape), ("P", None), ("P", None)],
        [("V", block), ("R", faces_shape), ("R", faces_shape)],
        [],
        work,
        fetch=((6, 1), (7, 2)),
    )(*fixed, final_inner, kept_next_faces, rate_faces, turned, kept_faces, ghosts)
    last_ghosts, final, faces, ghosts = lax.optimization_barrier((last_ghosts, final, faces, ghosts))
    (adjoint,) = call(
        functools.partial(adjoint_edge_kernel, geo, True),
        [kept_scalar] * 2 + [kept_near] * 4 + [near],
        [("B", block)],
        [faces_shape] * 2,
        few,
    )(*fixed, inner, faces, next_weight_faces, ghosts, last_ghosts)
    return (adjoint[None, None], final[None])


def solution(mesh):
    return jax.shard_map(
        functools.partial(on_device, mesh.shape["space"], mesh.shape["ckpt"]),
        mesh=mesh,
        in_specs=(
            P("space", None, "ckpt", None, None),
            P("ckpt", "space", None, None, None, None),
            P("space", None, None, None),
            P(),
            P(),
            P(),
            P(),
        ),
        out_specs=(P("ckpt", "space", None, None, None, None), P("space", None, None, None, None)),
        check_vma=False,
    )
```

```python
import functools

import jax
import jax.numpy as jnp
from jax import lax
from jax.experimental import pallas as pl
from jax.experimental.pallas import tpu as pltpu
from jax.sharding import PartitionSpec as P

STEPS = 2
time_step = 0.05
damping = 0.015

PAD = 8
VMEM = pl.BlockSpec(memory_space=pltpu.VMEM)
SMEM = pl.BlockSpec(memory_space=pltpu.SMEM)
VMEM_LIMIT = 16 * 1024 * 1024


class Pieces:
    def __init__(self, rows, count):
        self.rows = rows
        self.runs = [-(-length // count) for length in rows]
        self.starts = [sum(self.runs[:index]) for index in range(len(rows))]
        self.total = sum(self.runs)


class Geometry:
    def __init__(self, nvars, cx, cy, cz, count, parts):
        self.v, self.x, self.y, self.z, self.n, self.parts = nvars, cx, cy, cz, count, parts
        self.depth = cx // parts
        self.rows = [nvars * cy] * 2 + [nvars * cx] * 2 + [cy] * 2
        self.whole = Pieces(self.rows, count)
        self.part = Pieces([nvars * cy] + [nvars * self.depth] * 2 + [cy], count)
        self.face_rows = -(-max(run * count for run in self.whole.runs) // 8) * 8
        self.block = (nvars, cx, cy, cz)
        self.tall = (nvars, cx, cy + 2 * PAD, cz)
        self.faces = (6, self.face_rows, cz)
        self.rate_faces = (6, max(cx, cy), cz)

    def buffer(self, rows):
        return (self.n, -(-rows // 8) * 8, self.z)


def take_z_faces(geo, load, variables=None):
    v, x, y, z = geo.block
    lane = lax.broadcasted_iota(jnp.int32, (y, z), 1)
    high = jnp.zeros((y, z), jnp.float32)
    low = jnp.zeros((y, z), jnp.float32)
    for var in range(variables or v):
        for plane in range(x):
            place = var * x + plane
            tile = pltpu.roll(load(var, plane), place + 1, 1)
            high = jnp.where(lane == place, tile, high)
            low = jnp.where(lane == place + 1, tile, low)
    return high, pltpu.roll(low, z - 1, 1)


def repeat_lanes(geo, layer):
    total = layer
    for var in range(1, geo.v):
        total = total + pltpu.roll(layer, var * geo.x, 1)
    return total


def take_xy_faces(geo, source, faces):
    v, x, y, z = geo.block
    faces[0, : v * y] = source[:, x - 1].reshape(v * y, z)
    faces[1, : v * y] = source[:, 0].reshape(v * y, z)
    for var in range(v):
        faces[2, var * x : (var + 1) * x] = source[var, :, y - 1, :]
        faces[3, var * x : (var + 1) * x] = source[var, :, 0, :]


def cut(geo, pieces, faces, buffer, base, leave=None):
    for slot in range(geo.n):
        for index, (run, start) in enumerate(zip(pieces.runs, pieces.starts)):
            buffer[slot, base + start : base + start + run] = faces[index, slot * run : (slot + 1) * run]
        if leave:
            leave(slot)


class Table:
    def __init__(self, geo, refs):
        self.n = geo.n
        self.places, self.owner, self.neighbours, self.orientation = refs

    def codes(self):
        own = jnp.int32(0)
        for block in range(self.n):
            own = jnp.where(self.owner[block] == self.places[0], block, own)
        return [self.orientation[own, side] for side in range(6)]

    def part(self):
        return self.places[1]

    def target(self, block):
        return self.owner[block]

    def source(self, block, side):
        return self.owner[self.neighbours[block, side]]


def flip_rows(values, flag, length):
    rows, z = values.shape
    grouped = values.reshape(rows // length, length // 8, 8, z)
    index = lax.broadcasted_iota(jnp.int32, (8, z), 0)
    index = jnp.where(flag == 1, 7 - index, index)
    tiles = length // 8
    out = []
    for group in range(rows // length):
        for tile in range(tiles):
            picked = jnp.where(flag == 1, grouped[group, tiles - 1 - tile], grouped[group, tile])
            out.append(jnp.take_along_axis(picked, index, axis=0))
    return jnp.stack(out).reshape(rows, z)


def flip_lanes(values, flag, length):
    rows, z = values.shape
    lane = lax.broadcasted_iota(jnp.int32, (8, z), 1)
    within = lax.rem(lane, length)
    index = jnp.where(flag == 1, lane + (length - 1) - 2 * within, lane)
    index = jnp.minimum(index, z - 1)
    tiles = values.reshape(rows // 8, 8, z)
    return jnp.stack(
        [jnp.take_along_axis(tiles[tile], index, axis=1) for tile in range(rows // 8)]
    ).reshape(rows, z)


def join(geo, buffer, raw, base=0):
    for side in range(6):
        run, start = geo.whole.runs[side], base + geo.whole.starts[side]
        for slot in range(geo.n):
            raw[side, slot * run : (slot + 1) * run] = buffer[slot, start : start + run]


def part_of_lane(geo, rows):
    lane = lax.broadcasted_iota(jnp.int32, (rows, geo.z), 1)
    return lax.rem(lane, geo.x) // geo.depth


def join_parts(geo, buffer, raw, piece, zpiece):
    for side in range(6):
        index = 0 if side < 2 else min(side - 1, 3)
        run, start = geo.part.runs[index], geo.part.starts[index]
        if side < 2:
            part = 0 if side == 0 else geo.parts - 1
            for slot in range(geo.n):
                raw[side, slot * run : (slot + 1) * run] = buffer[part, slot, start : start + run]
        elif side < 4:
            for part in range(geo.parts):
                for slot in range(geo.n):
                    piece[slot * run : (slot + 1) * run] = buffer[part, slot, start : start + run]
                for var in range(geo.v):
                    row = var * geo.x + part * geo.depth
                    raw[side, row : row + geo.depth] = piece[var * geo.depth : (var + 1) * geo.depth]
        else:
            lanes = part_of_lane(geo, geo.y)
            total = jnp.zeros((geo.y, geo.z), jnp.float32)
            for part in range(geo.parts):
                if side == 4:
                    for slot in range(geo.n):
                        zpiece[part, slot * run : (slot + 1) * run] = buffer[part, slot, start : start + run]
                    rows = zpiece[part, : geo.y]
                    after = (part + 1) % geo.parts
                    rows = jnp.where(lanes == after, rows, 0.0)
                    total = total + pltpu.roll(rows, geo.z - geo.depth if after else geo.x - geo.depth, 1)
                else:
                    total = total + jnp.where(lanes == part, zpiece[part, : geo.y], 0.0)
            raw[side, : geo.y] = total


def turn(geo, codes, raw, ghosts):
    v, x, y, z = geo.block
    for side in range(6):
        first, second = codes[side] & 1, (codes[side] >> 1) & 1
        layer = raw[side, : geo.rows[side]]
        if side < 4:
            layer = flip_lanes(flip_rows(layer, first, y if side < 2 else x), second, z)
        else:
            layer = flip_lanes(flip_rows(layer, second, y), first, x)
        ghosts[side, : geo.rows[side]] = layer


def face_values(geo, faces, side):
    v, x, y, z = geo.block
    if side < 4:
        depth = y if side < 2 else x
        return [faces[side, var * depth : (var + 1) * depth] for var in range(v)]
    layer = faces[side, :y]
    return [layer] + [pltpu.roll(layer, z - var * x, 1) for var in range(1, v)]


def fill_tall(geo, source, tall):
    v, x, y, z = geo.block
    if len(source.shape) == 5:
        depth = geo.depth
        for part in range(geo.parts):
            tall[:, part * depth : (part + 1) * depth, PAD : PAD + y, :] = source[part]
    else:
        tall[:, :, PAD : PAD + y, :] = source[...]
    for var in range(v):
        tall[var, :, PAD - 1, :] = tall[var, :, PAD, :]
        tall[var, :, PAD + y, :] = tall[var, :, PAD + y - 1, :]


def around(geo, tall, plane):
    v, x, y, z = geo.block
    lane = lax.broadcasted_iota(jnp.int32, (y, z), 1)
    before, after = jnp.maximum(plane - 1, 0), jnp.minimum(plane + 1, x - 1)
    cells, low, high = [], [[], [], []], [[], [], []]
    for var in range(v):
        mid = tall[var, plane, PAD : PAD + y]
        cells.append(mid)
        low[0].append(tall[var, before, PAD : PAD + y])
        high[0].append(tall[var, after, PAD : PAD + y])
        low[1].append(tall[var, plane, PAD - 1 : PAD - 1 + y])
        high[1].append(tall[var, plane, PAD + 1 : PAD + 1 + y])
        low[2].append(jnp.where(lane == 0, mid, pltpu.roll(mid, 1, 1)))
        high[2].append(jnp.where(lane == z - 1, mid, pltpu.roll(mid, z - 1, 1)))
    return cells, low, high


def flux_entry(geo, mats, direction, row, column):
    return mats[direction, row, column]


def step_plane(geo, mats, cells, low, high, rate):
    v = geo.v
    total = [None] * v
    for direction in range(3):
        lows, highs = low[direction], high[direction]
        mean_low = 0.5 * (lows[0] + cells[0])
        mean_high = 0.5 * (cells[0] + highs[0])
        square_low = 1.0 + mean_low * mean_low
        square_high = 1.0 + mean_high * mean_high
        spread_low = square_low * lax.rsqrt(square_low)
        spread_high = square_high * lax.rsqrt(square_high)
        slopes = [highs[var] - lows[var] for var in range(v)]
        for var in range(v):
            term = spread_low * (cells[var] - lows[var]) - spread_high * (highs[var] - cells[var])
            for column in range(v):
                term = term + flux_entry(geo, mats, direction, var, column) * slopes[column]
            total[var] = term if total[var] is None else total[var] + term
    scale = (0.5 * time_step) * rate
    return [cells[var] - scale * total[var] - damping * jnp.tanh(cells[var]) for var in range(v)]


def adjoint_plane(geo, mats, cells, low, high, grads, weight, weight_low, weight_high):
    v = geo.v
    total = [None] * v
    extra = None
    for direction in range(3):
        spreads, steps = [], []
        for lower, upper, lower_weight, upper_weight in (
            (low[direction], cells, weight_low[direction], weight),
            (cells, high[direction], weight, weight_high[direction]),
        ):
            mean = 0.5 * (lower[0] + upper[0])
            square = 1.0 + mean * mean
            inverse = lax.rsqrt(square)
            jump = [lower_weight[var] - upper_weight[var] for var in range(v)]
            product = jump[0] * (upper[0] - lower[0])
            for var in range(1, v):
                product = product + jump[var] * (upper[var] - lower[var])
            product = product * (mean * inverse)
            extra = product if extra is None else extra + product
            spreads.append(square * inverse)
            steps.append(jump)
        slopes = [steps[0][var] + steps[1][var] for var in range(v)]
        for var in range(v):
            term = spreads[1] * steps[1][var] - spreads[0] * steps[0][var]
            for row in range(v):
                term = term + flux_entry(geo, mats, direction, row, var) * slopes[row]
            total[var] = term if total[var] is None else total[var] + term
    total[0] = total[0] - 0.5 * extra
    out = []
    for var in range(v):
        bend = jnp.tanh(cells[var])
        slope = (1.0 - damping) + damping * (bend * bend)
        out.append(grads[var] * slope - (0.5 * time_step) * total[var])
    return out


def step_face(geo, mats, side, cells, ghosts, rate):
    v = geo.v
    mean = 0.5 * (cells[0] + ghosts[0])
    square = 1.0 + mean * mean
    spread = square * lax.rsqrt(square)
    gap = [ghosts[var] - cells[var] for var in range(v)]
    scale = (0.5 * time_step) * rate
    out = []
    for var in range(v):
        total = flux_entry(geo, mats, side // 2, var, 0) * gap[0]
        for column in range(1, v):
            total = total + flux_entry(geo, mats, side // 2, var, column) * gap[column]
        if side % 2 == 0:
            out.append(scale * (spread * gap[var] - total))
        else:
            out.append(scale * (spread * gap[var] + total))
    return out


def adjoint_face(geo, mats, side, cells, ghosts, weight, ghost_weight):
    v = geo.v
    mean = 0.5 * (cells[0] + ghosts[0])
    square = 1.0 + mean * mean
    inverse = lax.rsqrt(square)
    spread = square * inverse
    jump = [weight[var] - ghost_weight[var] for var in range(v)]
    product = jump[0] * (ghosts[0] - cells[0])
    for var in range(1, v):
        product = product + jump[var] * (ghosts[var] - cells[var])
    product = (0.5 * product) * (mean * inverse)
    out = []
    for var in range(v):
        total = flux_entry(geo, mats, side // 2, 0, var) * jump[0]
        for row in range(1, v):
            total = total + flux_entry(geo, mats, side // 2, row, var) * jump[row]
        if side % 2 == 0:
            total = spread * jump[var] + total
        else:
            total = spread * jump[var] - total
        if var == 0:
            total = total - product
        out.append((-0.5 * time_step) * total)
    return out


def pack_kernel(geo, late, part, place, stored, grads, rate, *rest):
    weight_faces, rate_faces, buffer, places, pieces = rest
    places[0] = place[0]
    places[1] = part[0]
    v, x, y, z = geo.block
    depth = geo.depth
    late.wait(2)
    lane = lax.broadcasted_iota(jnp.int32, (y, z), 1)
    plane = jnp.where(part[0] == geo.parts - 1, depth - 1, 0)
    high = jnp.zeros((y, z), jnp.float32)
    low = jnp.zeros((y, z), jnp.float32)
    for var in range(v):
        pieces[0, var * y : (var + 1) * y] = stored[var, plane]
        pieces[1, var * depth : (var + 1) * depth] = stored[var, :, y - 1, :]
        pieces[2, var * depth : (var + 1) * depth] = stored[var, :, 0, :]
        for step in range(depth):
            place_now = var * x + part[0] * depth + step
            tile = pltpu.roll(stored[var, step], place_now + 1, 1)
            high = jnp.where(lane == place_now, tile, high)
            low = jnp.where(lane == place_now + 1, tile, low)
    shift = jnp.where(part[0] == geo.parts - 1, z - x + depth, depth)
    pieces[3, :y] = high + pltpu.roll(low, lax.rem(shift + z - 1, z), 1)
    cut(geo, geo.part, pieces, buffer, 0)
    late.wait(4)
    rate_faces[0, :y] = rate[x - 1]
    rate_faces[1, :y] = rate[0]
    rate_faces[2, :x] = rate[:, y - 1, :]
    rate_faces[3, :x] = rate[:, 0, :]
    high, low = take_z_faces(geo, lambda var, plane: rate[plane], 1)
    rate_faces[4, :y] = repeat_lanes(geo, high)
    rate_faces[5, :y] = repeat_lanes(geo, low)
    take_weight_faces(geo, grads, rate_faces, weight_faces, functools.partial(late.wait, 3))
    late.leave(0)
    cut(geo, geo.whole, weight_faces, buffer, geo.part.total, functools.partial(late.leave, 2))


def take_weight_faces(geo, grads, rate_faces, faces, wait=None):
    v, x, y, z = geo.block
    lane = lax.broadcasted_iota(jnp.int32, (y, z), 1)
    high = jnp.zeros((y, z), jnp.float32)
    low = jnp.zeros((y, z), jnp.float32)
    for var in range(v):
        if wait:
            wait(var)
        faces[0, var * y : (var + 1) * y] = grads[var, x - 1] * rate_faces[0, :y]
        faces[1, var * y : (var + 1) * y] = grads[var, 0] * rate_faces[1, :y]
        faces[2, var * x : (var + 1) * x] = grads[var, :, y - 1, :] * rate_faces[2, :x]
        faces[3, var * x : (var + 1) * x] = grads[var, :, 0, :] * rate_faces[3, :x]
        for plane in range(x):
            place = var * x + plane
            tile = pltpu.roll(grads[var, plane], place + 1, 1)
            high = jnp.where(lane == place, tile, high)
            low = jnp.where(lane == place + 1, tile, low)
    faces[4, :y] = high * rate_faces[4, :y]
    faces[5, :y] = pltpu.roll(low, z - 1, 1) * rate_faces[5, :y]


def route_whole(geo, links, block, arrived, leaving, base):
    for side in range(6):
        source = links.source(block, side)
        run, start, far = geo.whole.runs[side], base + geo.whole.starts[side], base + geo.whole.starts[side ^ 1]
        leaving[links.target(block), start : start + run] = arrived[source, far : far + run]


def route_kernel(geo, late, table, arrived, leaving):
    links = Table(geo, table)
    for block in range(geo.n):
        route_whole(geo, links, block, arrived, leaving, 0)
        late.leave(0, links.target(block))


def route_first_kernel(geo, late, table, arrived, leaving):
    links = Table(geo, table)
    x_side = jnp.where(links.part() == geo.parts - 1, 1, 0)
    for block in range(geo.n):
        route_whole(geo, links, block, arrived, leaving, geo.part.total)
        for index in range(3):
            side, far_index = (x_side, 0) if index == 0 else (index + 1, 3 - index)
            source = links.source(block, side)
            run, start, far = geo.part.runs[index], geo.part.starts[index], geo.part.starts[far_index]
            leaving[links.target(block), start : start + run] = arrived[source, far : far + run]
        run, start = geo.part.runs[3], geo.part.starts[3]
        from_low = arrived[links.source(block, 4), start : start + run]
        from_high = arrived[links.source(block, 5), start : start + run]
        own_lanes = part_of_lane(geo, run) == links.part()
        leaving[links.target(block), start : start + run] = jnp.where(own_lanes, from_high, from_low)
        late.leave(0, links.target(block))


def turn_weights_kernel(geo, late, mats, block, rate, table, buffer, result, ghosts, tall, raw):
    join(geo, buffer, raw, geo.part.total)
    turn(geo, Table(geo, table).codes(), raw, ghosts)
    step_inner_kernel(geo, late, mats, block, rate, result, tall)


def step_inner_kernel(geo, late, mats, block, rate, result, *rest):
    tall = rest[-1]
    late.wait(1)
    late.wait(2)
    fill_tall(geo, block, tall)

    def body(plane, carry):
        cells, low, high = around(geo, tall, plane)
        for var, value in enumerate(step_plane(geo, mats, cells, low, high, rate[plane])):
            result[var, plane] = value
        return carry

    lax.fori_loop(0, geo.x, body, 0)
    late.leave(0)
    if len(rest) == 2:
        faces = rest[0]
        v, x, y, z = geo.block
        for var in range(v):
            faces[0, var * y : (var + 1) * y] = tall[var, x - 1, PAD : PAD + y]
            faces[1, var * y : (var + 1) * y] = tall[var, 0, PAD : PAD + y]
            faces[2, var * x : (var + 1) * x] = tall[var, :, PAD + y - 1, :]
            faces[3, var * x : (var + 1) * x] = tall[var, :, PAD, :]
        high, low = take_z_faces(geo, lambda var, plane: tall[var, plane, PAD : PAD + y])
        faces[4, :y] = high
        faces[5, :y] = low
        late.leave(2)


def adjoint_inner_kernel(geo, late, mats, block, grads, rate, result, tall, weights):
    v, x, y, z = geo.block
    for index in range(1, 4):
        late.wait(index)
    fill_tall(geo, block, tall)

    def scale(plane, carry):
        for var in range(v):
            weights[var, plane, PAD : PAD + y] = rate[plane] * grads[var, plane]
        return carry

    lax.fori_loop(0, x, scale, 0)
    for var in range(v):
        weights[var, :, PAD - 1, :] = weights[var, :, PAD, :]
        weights[var, :, PAD + y, :] = weights[var, :, PAD + y - 1, :]

    def body(plane, carry):
        cells, low, high = around(geo, tall, plane)
        weight, weight_low, weight_high = around(geo, weights, plane)
        here = [grads[var, plane] for var in range(v)]
        values = adjoint_plane(geo, mats, cells, low, high, here, weight, weight_low, weight_high)
        for var, value in enumerate(values):
            result[var, plane] = value
        return carry

    lax.fori_loop(0, x, body, 0)


def add_terms(geo, values, inner, result, leave=None):
    v, x, y, z = geo.block
    lane = lax.broadcasted_iota(jnp.int32, (y, z), 1)
    zero = jnp.zeros((y, z), jnp.float32)
    ends = (lane == 0) | (lane == z - 1)
    even = lane % 2 == 0
    for var in range(v):
        high, low = values[4][var], pltpu.roll(values[5][var], 1, 1)
        mixed = (jnp.where(even, high, low), jnp.where(even, low, high))
        for plane in range(x):
            change = jnp.where(ends, pltpu.roll(mixed[plane % 2], z - 1 - plane, 1), zero)
            if plane == 0:
                change = change + values[1][var]
            if plane == x - 1:
                change = change + values[0][var]
            result[var, plane] = inner[var, plane] + change
        result[var, :, y - 1, :] = result[var, :, y - 1, :] + values[2][var]
        result[var, :, 0, :] = result[var, :, 0, :] + values[3][var]
        if leave:
            leave(var)


def step_edge_kernel(geo, first, late, table, mats, inner, faces, rate_faces, arrived, result, *rest):
    v, x, y, z = geo.block
    if first:
        new_faces, sent, ghosts, raw, piece, zpiece = rest
        join_parts(geo, arrived, raw, piece, zpiece)
        turn(geo, Table(geo, table).codes(), raw, ghosts)
        late.leave(4)
    else:
        ghosts = arrived
        late.wait(5)
        late.wait(8)
    late.wait(6)
    values = []
    for side in range(6):
        depth = y if side < 2 or side > 3 else x
        cells, outer = face_values(geo, faces, side), face_values(geo, ghosts, side)
        values.append(step_face(geo, mats, side, cells, outer, rate_faces[side, :depth]))
    add_terms(geo, values, inner, result)
    if first:
        take_xy_faces(geo, result, new_faces)
        high, low = take_z_faces(geo, lambda var, plane: result[var, plane])
        new_faces[4, :y] = high
        new_faces[5, :y] = low
        late.leave(2)
        cut(geo, geo.whole, new_faces, sent, 0, functools.partial(late.leave, 3))


def adjoint_edge_kernel(geo, last, late, table, mats, inner, faces, weight_faces, *rest):
    v, x, y, z = geo.block
    codes = Table(geo, table).codes()
    if last:
        ghosts, weight_buffer, result, raw, weight_ghosts = rest
        join(geo, weight_buffer, raw)
        turn(geo, codes, raw, weight_ghosts)
    else:
        rate_faces, buffer, weight_ghosts, result, new_faces, sent, ghosts, raw = rest
        join(geo, buffer, raw)
        turn(geo, codes, raw, ghosts)
        late.leave(3)
    values = []
    for side in range(6):
        views = [face_values(geo, field, side) for field in (faces, ghosts, weight_faces, weight_ghosts)]
        values.append(adjoint_face(geo, mats, side, *views))
    add_terms(geo, values, inner, result, functools.partial(late.leave, 0) if last else None)
    if not last:
        take_weight_faces(geo, result, rate_faces, new_faces)
        cut(geo, geo.whole, new_faces, sent, 0, functools.partial(late.leave, 2))


class Late:
    def __init__(self, arrivals, departures, sems):
        self.arrivals, self.departures, self.sems, self.started = arrivals, departures, sems, []

    def wait(self, index, slot=0):
        if index in self.arrivals:
            self.arrivals[index][slot].wait()

    def leave(self, index, slot=None):
        if index in self.departures:
            source, target = self.departures[index]
            if slot is not None:
                source, target = source.at[slot], target.at[slot]
            copy = pltpu.make_async_copy(source, target, self.sems.at[len(self.started)])
            copy.start()
            self.started.append(copy)


def call(kernel, ins, outs, scratch, flops, fetch=(), aliases=None):
    late_in = [(index, kind, shape) for index, (kind, shape) in enumerate(ins) if kind in "HCTF"]
    arrive = sum(shape[0] if kind == "C" else 1 for _, kind, shape in late_in)
    late_out = [(index, shape) for index, (kind, shape) in enumerate(outs) if kind in "HB"]
    count_in, count_out = len(late_in), len(late_out)
    sends = sum(shape[0] if kind == "B" else 1 for kind, shape in outs if kind in "HBD")

    def body(*refs):
        given = list(refs[: len(ins)])
        made = list(refs[len(ins) : len(ins) + len(outs)])
        rest = list(refs[len(ins) + len(outs) :])
        own = rest[: len(scratch)]
        stage = rest[len(scratch) : len(scratch) + count_in + count_out]
        sems_in = rest[len(scratch) + count_in + count_out] if count_in or fetch else None
        sems_out = rest[-1] if sends else None
        arrivals, departures = {}, {}
        used = 0
        for slot, (index, kind, shape) in enumerate(late_in):
            pairs = [(given[index], stage[slot])]
            if kind == "C":
                pairs = [(given[index].at[chunk], stage[slot].at[chunk]) for chunk in range(shape[0])]
            arrivals[index] = []
            for source, target in pairs:
                copy = pltpu.make_async_copy(source, target, sems_in.at[used])
                copy.start()
                arrivals[index].append(copy)
                used += 1
            given[index] = stage[slot]
        for slot, (index, _) in enumerate(late_out):
            departures[index] = (stage[count_in + slot], made[index])
            made[index] = stage[count_in + slot]
        for index, (kind, _) in enumerate(outs):
            if kind == "D":
                departures[index] = (made[index - 1], made[index])
        fetched = []
        for slot, (source, target) in enumerate(fetch):
            copy = pltpu.make_async_copy(given[source], made[target], sems_in.at[arrive + slot])
            copy.start()
            fetched.append(copy)
        late = Late(arrivals, departures, sems_out)
        hidden_in = {source for source, _ in fetch}
        hidden_out = {target for _, target in fetch}
        operands, group = [], []
        for index, ref in enumerate(given):
            if ins[index][0] == "G":
                group.append(ref)
                if len(group) == 1:
                    operands.append(group)
            elif index not in hidden_in:
                operands.append(ref)
        kernel(
            late,
            *operands,
            *[ref for index, ref in enumerate(made) if index not in hidden_out and outs[index][0] != "D"],
            *own,
        )
        assert len(late.started) == sends
        for copy in fetched + late.started:
            copy.wait()

    hbm = pl.BlockSpec(memory_space=pltpu.HBM)
    specs = {"G": SMEM, "C": hbm, "T": hbm, "F": hbm, "S": SMEM, "V": VMEM, "R": VMEM, "H": hbm, "B": hbm, "D": hbm, "P": hbm, "M": SMEM, "I": SMEM}
    scratch_shapes = [pltpu.VMEM(shape, jnp.float32) for shape in scratch]
    stages = {"T": (pltpu.SMEM, jnp.int32), "F": (pltpu.SMEM, jnp.float32)}
    for _, kind, shape in late_in:
        memory, dtype = stages.get(kind, (pltpu.VMEM, jnp.float32))
        scratch_shapes.append(memory(shape, dtype))
    scratch_shapes += [pltpu.VMEM(shape, jnp.float32) for _, shape in late_out]
    if count_in or fetch:
        scratch_shapes.append(pltpu.SemaphoreType.DMA((arrive + len(fetch),)))
    if sends:
        scratch_shapes.append(pltpu.SemaphoreType.DMA((sends,)))
    shapes = {"V": jax.ShapeDtypeStruct, "R": pltpu.VMEM, "H": pltpu.HBM, "B": pltpu.HBM, "D": pltpu.HBM}
    shapes.update({"M": pltpu.SMEM, "I": pltpu.SMEM})
    invoke = pl.pallas_call(
        body,
        in_specs=[specs[kind] for kind, _ in ins],
        out_specs=[specs[kind] for kind, _ in outs],
        out_shape=[shapes[kind](shape, jnp.int32 if kind == "I" else jnp.float32) for kind, shape in outs],
        scratch_shapes=scratch_shapes,
        input_output_aliases=aliases or {},
        compiler_params=pltpu.CompilerParams(vmem_limit_bytes=VMEM_LIMIT),
        cost_estimate=pl.CostEstimate(flops=flops, bytes_accessed=3 << 20, transcendentals=0),
    )

    def run(*operands):
        placed = {"G": pltpu.SMEM, "C": pltpu.HBM, "T": pltpu.HBM, "F": pltpu.HBM, "M": pltpu.SMEM, "H": pltpu.HBM, "R": pltpu.VMEM, "P": pltpu.HBM}
        return invoke(
            *[
                pltpu.with_memory_space_constraint(operand, placed[kind]) if kind in placed else operand
                for operand, (kind, _) in zip(operands, ins)
            ]
        )

    return run


def on_device(count, parts, checkpoint, seeds, cell_rate, flux_mats, owner, neighbours, orientation):
    nvars, cx, cy, cz = seeds.shape[2:]
    geo = Geometry(nvars, cx, cy, cz, count, parts)
    rate = cell_rate[0]
    grads = seeds[0, 0]
    place = lax.axis_index("space").astype(jnp.int32).reshape(1)
    part = lax.axis_index("ckpt").astype(jnp.int32).reshape(1)
    work = nvars * nvars * 3 * 4 * cx * cy * cz
    few = work // 16
    whole, both = geo.buffer(geo.whole.total), geo.buffer(geo.part.total + geo.whole.total)
    some = -(-geo.part.total // 8) * 8

    stored_shape, block, faces_shape = checkpoint.shape[1:], geo.block, geo.faces
    rate_block = cell_rate.shape[1:]
    scalar, near, kept_near, kept_scalar = ("S", None), ("V", None), ("R", None), ("M", None)

    grouped = [("G", None)] * 4

    def far(shape):
        return ("H", shape)

    def swap(buffer):
        return lax.all_to_all(buffer, "space", 0, 0, tiled=True)

    def route(arrived):
        return call(functools.partial(route_kernel, geo), grouped + [near], [("B", whole)], [], few)(
            *table, arrived
        )[0]

    def adjoint_inner(state, state_kind, grads, grads_kind):
        return call(
            functools.partial(adjoint_inner_kernel, geo),
            [kept_scalar, state_kind, grads_kind, far(rate_block)],
            [("R", block)],
            [geo.tall] * 2,
            2 * work,
        )(mats, state, grads, rate)[0]

    links = (owner, neighbours, orientation)
    weight_faces, rate_faces, sent, *table, mats = call(
        functools.partial(pack_kernel, geo),
        [scalar] * 2 + [far(stored_shape), ("C", block), far(rate_block)] + [("P", None)] * 4,
        [far(faces_shape), ("R", geo.rate_faces), ("B", both), ("I", (2,))]
        + [("I", link.shape) for link in links]
        + [("M", flux_mats.shape)],
        [faces_shape],
        few,
        fetch=((5, 4), (6, 5), (7, 6), (8, 7)),
    )(part, place, checkpoint[0], grads, rate, *links, flux_mats)
    fixed = (*table, mats)
    kept, sent = lax.optimization_barrier((checkpoint[0], sent))
    arrived = swap(sent)
    state = lax.all_gather(kept, "ckpt", axis=0)
    arrived, state = lax.optimization_barrier((arrived, state))
    (leaving,) = call(functools.partial(route_first_kernel, geo), grouped + [near], [("B", both)], [], few)(
        *table, arrived
    )
    first_ghosts = swap(leaving)
    inner, faces, kept_faces = call(
        functools.partial(step_inner_kernel, geo),
        [kept_scalar, far(state.shape), far(rate_block)],
        [("R", block), ("R", faces_shape), ("D", faces_shape)],
        [geo.tall],
        work,
    )(mats, state, rate)
    first_ghosts, inner, faces = lax.optimization_barrier((first_ghosts, inner, faces))
    gathered = lax.all_gather(first_ghosts[:, :some], "ckpt", axis=0)
    next_state, next_faces, kept_next_faces, sent, ghosts = call(
        functools.partial(step_edge_kernel, geo, True),
        grouped + [kept_scalar] + [kept_near] * 3 + [near],
        [("R", block), ("R", faces_shape), ("D", faces_shape), ("B", whole), far(faces_shape)],
        [faces_shape, faces_shape[1:], (parts,) + faces_shape[1:]],
        few,
        aliases={5: 0},
    )(*fixed, inner, faces, rate_faces, gathered)

    arrived = swap(sent)
    inner = adjoint_inner(next_state, kept_near, grads, far(block))
    arrived, inner = lax.optimization_barrier((arrived, inner))
    leaving = route(arrived)
    later_state, leaving = lax.optimization_barrier((next_state, leaving))
    next_ghosts = swap(leaving)
    final_inner, weight_ghosts, weight_faces = call(
        functools.partial(turn_weights_kernel, geo),
        [kept_scalar, kept_near, far(rate_block)] + grouped + [near, ("P", None)],
        [far(block), ("R", faces_shape), ("R", faces_shape)],
        [geo.tall, faces_shape],
        work,
        fetch=((8, 2),),
    )(mats, later_state, rate, *table, first_ghosts, weight_faces)
    next_ghosts, final_inner, weight_ghosts, weight_faces = lax.optimization_barrier(
        (next_ghosts, final_inner, weight_ghosts, weight_faces)
    )
    grads_now, next_weight_faces, sent, turned = call(
        functools.partial(adjoint_edge_kernel, geo, False),
        grouped + [kept_scalar] + [kept_near] * 4 + [near, kept_near],
        [("R", block), ("R", faces_shape), ("B", whole), far(faces_shape)],
        [faces_shape],
        few,
        aliases={5: 0},
    )(*fixed, inner, next_faces, weight_faces, rate_faces, next_ghosts, weight_ghosts)

    arrived = swap(sent)
    inner = adjoint_inner(state, far(state.shape), grads_now, kept_near)
    arrived, inner = lax.optimization_barrier((arrived, inner))
    leaving = route(arrived)
    final_inner, leaving = lax.optimization_barrier((final_inner, leaving))
    last_ghosts = swap(leaving)
    final, faces, ghosts = call(
        functools.partial(step_edge_kernel, geo, False),
        grouped + [kept_scalar] + [far(block), far(faces_shape), kept_near, far(faces_shape), ("P", None), ("P", None)],
        [("V", block), ("R", faces_shape), ("R", faces_shape)],
        [],
        work,
        fetch=((9, 1), (10, 2)),
    )(*fixed, final_inner, kept_next_faces, rate_faces, turned, kept_faces, ghosts)
    last_ghosts, final, faces, ghosts = lax.optimization_barrier((last_ghosts, final, faces, ghosts))
    (adjoint,) = call(
        functools.partial(adjoint_edge_kernel, geo, True),
        grouped + [kept_scalar] + [kept_near] * 4 + [near],
        [("B", block)],
        [faces_shape] * 2,
        few,
    )(*fixed, inner, faces, next_weight_faces, ghosts, last_ghosts)
    return (adjoint[None, None], final[None])


def solution(mesh):
    return jax.shard_map(
        functools.partial(on_device, mesh.shape["space"], mesh.shape["ckpt"]),
        mesh=mesh,
        in_specs=(
            P("space", None, "ckpt", None, None),
            P("ckpt", "space", None, None, None, None),
            P("space", None, None, None),
            P(),
            P(),
            P(),
            P(),
        ),
        out_specs=(P("ckpt", "space", None, None, None, None), P("space", None, None, None, None)),
        check_vma=False,
    )
```

```python
import functools

import jax
import jax.numpy as jnp
from jax import lax
from jax.experimental import pallas as pl
from jax.experimental.pallas import tpu as pltpu
from jax.sharding import PartitionSpec as P

STEPS = 2
time_step = 0.05
damping = 0.015

PAD = 8
VMEM = pl.BlockSpec(memory_space=pltpu.VMEM)
SMEM = pl.BlockSpec(memory_space=pltpu.SMEM)
VMEM_LIMIT = 16 * 1024 * 1024


class Pieces:
    def __init__(self, rows, count):
        self.rows = rows
        self.runs = [-(-length // count) for length in rows]
        self.starts = [sum(self.runs[:index]) for index in range(len(rows))]
        self.total = sum(self.runs)


class Geometry:
    def __init__(self, nvars, cx, cy, cz, count, parts):
        self.v, self.x, self.y, self.z, self.n, self.parts = nvars, cx, cy, cz, count, parts
        self.depth = cx // parts
        self.rows = [nvars * cy] * 2 + [nvars * cx] * 2 + [cy] * 2
        self.whole = Pieces(self.rows, count)
        self.part = Pieces([nvars * cy] + [nvars * self.depth] * 2 + [cy], count)
        self.face_rows = -(-max(run * count for run in self.whole.runs) // 8) * 8
        self.block = (nvars, cx, cy, cz)
        self.tall = (nvars, cx, cy + 2 * PAD, cz)
        self.faces = (6, self.face_rows, cz)
        self.rate_faces = (6, max(cx, cy), cz)

    def buffer(self, rows):
        return (self.n, -(-rows // 8) * 8, self.z)


def take_z_faces(geo, load, variables=None):
    v, x, y, z = geo.block
    lane = lax.broadcasted_iota(jnp.int32, (y, z), 1)
    high = jnp.zeros((y, z), jnp.float32)
    low = jnp.zeros((y, z), jnp.float32)
    for var in range(variables or v):
        for plane in range(x):
            place = var * x + plane
            tile = pltpu.roll(load(var, plane), place + 1, 1)
            high = jnp.where(lane == place, tile, high)
            low = jnp.where(lane == place + 1, tile, low)
    return high, pltpu.roll(low, z - 1, 1)


def repeat_lanes(geo, layer):
    total = layer
    for var in range(1, geo.v):
        total = total + pltpu.roll(layer, var * geo.x, 1)
    return total


def take_xy_faces(geo, source, faces):
    v, x, y, z = geo.block
    faces[0, : v * y] = source[:, x - 1].reshape(v * y, z)
    faces[1, : v * y] = source[:, 0].reshape(v * y, z)
    for var in range(v):
        faces[2, var * x : (var + 1) * x] = source[var, :, y - 1, :]
        faces[3, var * x : (var + 1) * x] = source[var, :, 0, :]


def cut(geo, pieces, faces, buffer, base, leave=None):
    for slot in range(geo.n):
        for index, (run, start) in enumerate(zip(pieces.runs, pieces.starts)):
            buffer[slot, base + start : base + start + run] = faces[index, slot * run : (slot + 1) * run]
        if leave:
            leave(slot)


class Table:
    def __init__(self, geo, refs):
        self.n = geo.n
        self.places, self.owner, self.neighbours, self.orientation = refs

    def codes(self):
        own = jnp.int32(0)
        for block in range(self.n):
            own = jnp.where(self.owner[block] == self.places[0], block, own)
        return [self.orientation[own, side] for side in range(6)]

    def part(self):
        return self.places[1]

    def target(self, block):
        return self.owner[block]

    def source(self, block, side):
        return self.owner[self.neighbours[block, side]]


def flip_rows(values, flag, length):
    rows, z = values.shape
    grouped = values.reshape(rows // length, length // 8, 8, z)
    index = lax.broadcasted_iota(jnp.int32, (8, z), 0)
    index = jnp.where(flag == 1, 7 - index, index)
    tiles = length // 8
    out = []
    for group in range(rows // length):
        for tile in range(tiles):
            picked = jnp.where(flag == 1, grouped[group, tiles - 1 - tile], grouped[group, tile])
            out.append(jnp.take_along_axis(picked, index, axis=0))
    return jnp.stack(out).reshape(rows, z)


def flip_lanes(values, flag, length):
    rows, z = values.shape
    lane = lax.broadcasted_iota(jnp.int32, (8, z), 1)
    within = lax.rem(lane, length)
    index = jnp.where(flag == 1, lane + (length - 1) - 2 * within, lane)
    index = jnp.minimum(index, z - 1)
    tiles = values.reshape(rows // 8, 8, z)
    return jnp.stack(
        [jnp.take_along_axis(tiles[tile], index, axis=1) for tile in range(rows // 8)]
    ).reshape(rows, z)


def join(geo, buffer, raw, base=0):
    for side in range(6):
        run, start = geo.whole.runs[side], base + geo.whole.starts[side]
        for slot in range(geo.n):
            raw[side, slot * run : (slot + 1) * run] = buffer[slot, start : start + run]


def part_of_lane(geo, rows):
    lane = lax.broadcasted_iota(jnp.int32, (rows, geo.z), 1)
    return lax.rem(lane, geo.x) // geo.depth


def join_parts(geo, buffer, raw, piece, zpiece):
    for side in range(6):
        index = 0 if side < 2 else min(side - 1, 3)
        run, start = geo.part.runs[index], geo.part.starts[index]
        if side < 2:
            part = 0 if side == 0 else geo.parts - 1
            for slot in range(geo.n):
                raw[side, slot * run : (slot + 1) * run] = buffer[part, slot, start : start + run]
        elif side < 4:
            for part in range(geo.parts):
                for slot in range(geo.n):
                    piece[slot * run : (slot + 1) * run] = buffer[part, slot, start : start + run]
                for var in range(geo.v):
                    row = var * geo.x + part * geo.depth
                    raw[side, row : row + geo.depth] = piece[var * geo.depth : (var + 1) * geo.depth]
        else:
            lanes = part_of_lane(geo, geo.y)
            total = jnp.zeros((geo.y, geo.z), jnp.float32)
            for part in range(geo.parts):
                if side == 4:
                    for slot in range(geo.n):
                        zpiece[part, slot * run : (slot + 1) * run] = buffer[part, slot, start : start + run]
                    rows = zpiece[part, : geo.y]
                    after = (part + 1) % geo.parts
                    rows = jnp.where(lanes == after, rows, 0.0)
                    total = total + pltpu.roll(rows, geo.z - geo.depth if after else geo.x - geo.depth, 1)
                else:
                    total = total + jnp.where(lanes == part, zpiece[part, : geo.y], 0.0)
            raw[side, : geo.y] = total


def turn(geo, codes, raw, ghosts):
    v, x, y, z = geo.block
    for side in range(6):
        first, second = codes[side] & 1, (codes[side] >> 1) & 1
        layer = raw[side, : geo.rows[side]]
        if side < 4:
            layer = flip_lanes(flip_rows(layer, first, y if side < 2 else x), second, z)
        else:
            layer = flip_lanes(flip_rows(layer, second, y), first, x)
        ghosts[side, : geo.rows[side]] = layer


def face_values(geo, faces, side):
    v, x, y, z = geo.block
    if side < 4:
        depth = y if side < 2 else x
        return [faces[side, var * depth : (var + 1) * depth] for var in range(v)]
    layer = faces[side, :y]
    return [layer] + [pltpu.roll(layer, z - var * x, 1) for var in range(1, v)]


def fill_tall(geo, source, tall):
    v, x, y, z = geo.block
    if len(source.shape) == 5:
        depth = geo.depth
        for part in range(geo.parts):
            tall[:, part * depth : (part + 1) * depth, PAD : PAD + y, :] = source[part]
    else:
        tall[:, :, PAD : PAD + y, :] = source[...]
    for var in range(v):
        tall[var, :, PAD - 1, :] = tall[var, :, PAD, :]
        tall[var, :, PAD + y, :] = tall[var, :, PAD + y - 1, :]


def around(geo, tall, plane):
    v, x, y, z = geo.block
    lane = lax.broadcasted_iota(jnp.int32, (y, z), 1)
    before, after = jnp.maximum(plane - 1, 0), jnp.minimum(plane + 1, x - 1)
    cells, low, high = [], [[], [], []], [[], [], []]
    for var in range(v):
        mid = tall[var, plane, PAD : PAD + y]
        cells.append(mid)
        low[0].append(tall[var, before, PAD : PAD + y])
        high[0].append(tall[var, after, PAD : PAD + y])
        low[1].append(tall[var, plane, PAD - 1 : PAD - 1 + y])
        high[1].append(tall[var, plane, PAD + 1 : PAD + 1 + y])
        low[2].append(jnp.where(lane == 0, mid, pltpu.roll(mid, 1, 1)))
        high[2].append(jnp.where(lane == z - 1, mid, pltpu.roll(mid, z - 1, 1)))
    return cells, low, high


def flux_entry(geo, mats, direction, row, column):
    return mats[direction, row, column]


def step_plane(geo, mats, cells, low, high, rate):
    v = geo.v
    total = [None] * v
    for direction in range(3):
        lows, highs = low[direction], high[direction]
        mean_low = 0.5 * (lows[0] + cells[0])
        mean_high = 0.5 * (cells[0] + highs[0])
        square_low = 1.0 + mean_low * mean_low
        square_high = 1.0 + mean_high * mean_high
        spread_low = square_low * lax.rsqrt(square_low)
        spread_high = square_high * lax.rsqrt(square_high)
        slopes = [highs[var] - lows[var] for var in range(v)]
        for var in range(v):
            term = spread_low * (cells[var] - lows[var]) - spread_high * (highs[var] - cells[var])
            for column in range(v):
                term = term + flux_entry(geo, mats, direction, var, column) * slopes[column]
            total[var] = term if total[var] is None else total[var] + term
    scale = (0.5 * time_step) * rate
    return [cells[var] - scale * total[var] - damping * jnp.tanh(cells[var]) for var in range(v)]


def adjoint_plane(geo, mats, cells, low, high, grads, weight, weight_low, weight_high):
    v = geo.v
    total = [None] * v
    extra = None
    for direction in range(3):
        spreads, steps = [], []
        for lower, upper, lower_weight, upper_weight in (
            (low[direction], cells, weight_low[direction], weight),
            (cells, high[direction], weight, weight_high[direction]),
        ):
            mean = 0.5 * (lower[0] + upper[0])
            square = 1.0 + mean * mean
            inverse = lax.rsqrt(square)
            jump = [lower_weight[var] - upper_weight[var] for var in range(v)]
            product = jump[0] * (upper[0] - lower[0])
            for var in range(1, v):
                product = product + jump[var] * (upper[var] - lower[var])
            product = product * (mean * inverse)
            extra = product if extra is None else extra + product
            spreads.append(square * inverse)
            steps.append(jump)
        slopes = [steps[0][var] + steps[1][var] for var in range(v)]
        for var in range(v):
            term = spreads[1] * steps[1][var] - spreads[0] * steps[0][var]
            for row in range(v):
                term = term + flux_entry(geo, mats, direction, row, var) * slopes[row]
            total[var] = term if total[var] is None else total[var] + term
    total[0] = total[0] - 0.5 * extra
    out = []
    for var in range(v):
        bend = jnp.tanh(cells[var])
        slope = (1.0 - damping) + damping * (bend * bend)
        out.append(grads[var] * slope - (0.5 * time_step) * total[var])
    return out


def step_face(geo, mats, side, cells, ghosts, rate):
    v = geo.v
    mean = 0.5 * (cells[0] + ghosts[0])
    square = 1.0 + mean * mean
    spread = square * lax.rsqrt(square)
    gap = [ghosts[var] - cells[var] for var in range(v)]
    scale = (0.5 * time_step) * rate
    out = []
    for var in range(v):
        total = flux_entry(geo, mats, side // 2, var, 0) * gap[0]
        for column in range(1, v):
            total = total + flux_entry(geo, mats, side // 2, var, column) * gap[column]
        if side % 2 == 0:
            out.append(scale * (spread * gap[var] - total))
        else:
            out.append(scale * (spread * gap[var] + total))
    return out


def adjoint_face(geo, mats, side, cells, ghosts, weight, ghost_weight):
    v = geo.v
    mean = 0.5 * (cells[0] + ghosts[0])
    square = 1.0 + mean * mean
    inverse = lax.rsqrt(square)
    spread = square * inverse
    jump = [weight[var] - ghost_weight[var] for var in range(v)]
    product = jump[0] * (ghosts[0] - cells[0])
    for var in range(1, v):
        product = product + jump[var] * (ghosts[var] - cells[var])
    product = (0.5 * product) * (mean * inverse)
    out = []
    for var in range(v):
        total = flux_entry(geo, mats, side // 2, 0, var) * jump[0]
        for row in range(1, v):
            total = total + flux_entry(geo, mats, side // 2, row, var) * jump[row]
        if side % 2 == 0:
            total = spread * jump[var] + total
        else:
            total = spread * jump[var] - total
        if var == 0:
            total = total - product
        out.append((-0.5 * time_step) * total)
    return out


def pack_kernel(geo, late, part, place, stored, grads, rate, *rest):
    weight_faces, rate_faces, buffer, places, pieces = rest
    places[0] = place[0]
    places[1] = part[0]
    v, x, y, z = geo.block
    depth = geo.depth
    late.wait(2)
    lane = lax.broadcasted_iota(jnp.int32, (y, z), 1)
    plane = jnp.where(part[0] == geo.parts - 1, depth - 1, 0)
    high = jnp.zeros((y, z), jnp.float32)
    low = jnp.zeros((y, z), jnp.float32)
    for var in range(v):
        pieces[0, var * y : (var + 1) * y] = stored[var, plane]
        pieces[1, var * depth : (var + 1) * depth] = stored[var, :, y - 1, :]
        pieces[2, var * depth : (var + 1) * depth] = stored[var, :, 0, :]
        for step in range(depth):
            place_now = var * x + part[0] * depth + step
            tile = pltpu.roll(stored[var, step], place_now + 1, 1)
            high = jnp.where(lane == place_now, tile, high)
            low = jnp.where(lane == place_now + 1, tile, low)
    shift = jnp.where(part[0] == geo.parts - 1, z - x + depth, depth)
    pieces[3, :y] = high + pltpu.roll(low, lax.rem(shift + z - 1, z), 1)
    cut(geo, geo.part, pieces, buffer, 0)
    late.wait(3)
    late.wait(4)
    rate_faces[0, :y] = rate[x - 1]
    rate_faces[1, :y] = rate[0]
    rate_faces[2, :x] = rate[:, y - 1, :]
    rate_faces[3, :x] = rate[:, 0, :]
    high, low = take_z_faces(geo, lambda var, plane: rate[plane], 1)
    rate_faces[4, :y] = repeat_lanes(geo, high)
    rate_faces[5, :y] = repeat_lanes(geo, low)
    take_weight_faces(geo, grads, rate_faces, weight_faces)
    late.leave(0)
    cut(geo, geo.whole, weight_faces, buffer, geo.part.total, functools.partial(late.leave, 2))


def take_weight_faces(geo, grads, rate_faces, faces):
    v, x, y, z = geo.block
    lane = lax.broadcasted_iota(jnp.int32, (y, z), 1)
    high = jnp.zeros((y, z), jnp.float32)
    low = jnp.zeros((y, z), jnp.float32)
    for var in range(v):
        faces[0, var * y : (var + 1) * y] = grads[var, x - 1] * rate_faces[0, :y]
        faces[1, var * y : (var + 1) * y] = grads[var, 0] * rate_faces[1, :y]
        faces[2, var * x : (var + 1) * x] = grads[var, :, y - 1, :] * rate_faces[2, :x]
        faces[3, var * x : (var + 1) * x] = grads[var, :, 0, :] * rate_faces[3, :x]
        for plane in range(x):
            place = var * x + plane
            tile = pltpu.roll(grads[var, plane], place + 1, 1)
            high = jnp.where(lane == place, tile, high)
            low = jnp.where(lane == place + 1, tile, low)
    faces[4, :y] = high * rate_faces[4, :y]
    faces[5, :y] = pltpu.roll(low, z - 1, 1) * rate_faces[5, :y]


def route_whole(geo, links, block, arrived, leaving, base):
    for side in range(6):
        source = links.source(block, side)
        run, start, far = geo.whole.runs[side], base + geo.whole.starts[side], base + geo.whole.starts[side ^ 1]
        leaving[links.target(block), start : start + run] = arrived[source, far : far + run]


def route_kernel(geo, late, table, arrived, leaving):
    links = Table(geo, table)
    for block in range(geo.n):
        route_whole(geo, links, block, arrived, leaving, 0)
        late.leave(0, links.target(block))


def route_first_kernel(geo, late, table, arrived, leaving):
    links = Table(geo, table)
    x_side = jnp.where(links.part() == geo.parts - 1, 1, 0)
    for block in range(geo.n):
        route_whole(geo, links, block, arrived, leaving, geo.part.total)
        for index in range(3):
            side, far_index = (x_side, 0) if index == 0 else (index + 1, 3 - index)
            source = links.source(block, side)
            run, start, far = geo.part.runs[index], geo.part.starts[index], geo.part.starts[far_index]
            leaving[links.target(block), start : start + run] = arrived[source, far : far + run]
        run, start = geo.part.runs[3], geo.part.starts[3]
        from_low = arrived[links.source(block, 4), start : start + run]
        from_high = arrived[links.source(block, 5), start : start + run]
        own_lanes = part_of_lane(geo, run) == links.part()
        leaving[links.target(block), start : start + run] = jnp.where(own_lanes, from_high, from_low)
        late.leave(0, links.target(block))


def turn_weights_kernel(geo, late, mats, block, rate, table, buffer, result, ghosts, tall, raw):
    join(geo, buffer, raw, geo.part.total)
    turn(geo, Table(geo, table).codes(), raw, ghosts)
    step_inner_kernel(geo, late, mats, block, rate, result, tall)


def step_inner_kernel(geo, late, mats, block, rate, result, *rest):
    tall = rest[-1]
    late.wait(1)
    late.wait(2)
    fill_tall(geo, block, tall)

    def body(plane, carry):
        cells, low, high = around(geo, tall, plane)
        for var, value in enumerate(step_plane(geo, mats, cells, low, high, rate[plane])):
            result[var, plane] = value
        return carry

    lax.fori_loop(0, geo.x, body, 0)
    late.leave(0)
    if len(rest) == 2:
        faces = rest[0]
        v, x, y, z = geo.block
        for var in range(v):
            faces[0, var * y : (var + 1) * y] = tall[var, x - 1, PAD : PAD + y]
            faces[1, var * y : (var + 1) * y] = tall[var, 0, PAD : PAD + y]
            faces[2, var * x : (var + 1) * x] = tall[var, :, PAD + y - 1, :]
            faces[3, var * x : (var + 1) * x] = tall[var, :, PAD, :]
        high, low = take_z_faces(geo, lambda var, plane: tall[var, plane, PAD : PAD + y])
        faces[4, :y] = high
        faces[5, :y] = low
        late.leave(2)


def adjoint_inner_kernel(geo, late, mats, block, grads, rate, result, tall, weights):
    v, x, y, z = geo.block
    for index in range(1, 4):
        late.wait(index)
    fill_tall(geo, block, tall)

    def scale(plane, carry):
        for var in range(v):
            weights[var, plane, PAD : PAD + y] = rate[plane] * grads[var, plane]
        return carry

    lax.fori_loop(0, x, scale, 0)
    for var in range(v):
        weights[var, :, PAD - 1, :] = weights[var, :, PAD, :]
        weights[var, :, PAD + y, :] = weights[var, :, PAD + y - 1, :]

    def body(plane, carry):
        cells, low, high = around(geo, tall, plane)
        weight, weight_low, weight_high = around(geo, weights, plane)
        here = [grads[var, plane] for var in range(v)]
        values = adjoint_plane(geo, mats, cells, low, high, here, weight, weight_low, weight_high)
        for var, value in enumerate(values):
            result[var, plane] = value
        return carry

    lax.fori_loop(0, x, body, 0)


def add_terms(geo, values, inner, result, leave=None):
    v, x, y, z = geo.block
    lane = lax.broadcasted_iota(jnp.int32, (y, z), 1)
    zero = jnp.zeros((y, z), jnp.float32)
    ends = (lane == 0) | (lane == z - 1)
    even = lane % 2 == 0
    for var in range(v):
        high, low = values[4][var], pltpu.roll(values[5][var], 1, 1)
        mixed = (jnp.where(even, high, low), jnp.where(even, low, high))
        for plane in range(x):
            change = jnp.where(ends, pltpu.roll(mixed[plane % 2], z - 1 - plane, 1), zero)
            if plane == 0:
                change = change + values[1][var]
            if plane == x - 1:
                change = change + values[0][var]
            result[var, plane] = inner[var, plane] + change
        result[var, :, y - 1, :] = result[var, :, y - 1, :] + values[2][var]
        result[var, :, 0, :] = result[var, :, 0, :] + values[3][var]
        if leave:
            leave(var)


def step_edge_kernel(geo, first, late, table, mats, inner, faces, rate_faces, arrived, result, *rest):
    v, x, y, z = geo.block
    if first:
        new_faces, sent, ghosts, raw, piece, zpiece = rest
        join_parts(geo, arrived, raw, piece, zpiece)
        turn(geo, Table(geo, table).codes(), raw, ghosts)
        late.leave(4)
    else:
        ghosts = arrived
        late.wait(5)
        late.wait(8)
    late.wait(6)
    values = []
    for side in range(6):
        depth = y if side < 2 or side > 3 else x
        cells, outer = face_values(geo, faces, side), face_values(geo, ghosts, side)
        values.append(step_face(geo, mats, side, cells, outer, rate_faces[side, :depth]))
    add_terms(geo, values, inner, result)
    if first:
        take_xy_faces(geo, result, new_faces)
        high, low = take_z_faces(geo, lambda var, plane: result[var, plane])
        new_faces[4, :y] = high
        new_faces[5, :y] = low
        late.leave(2)
        cut(geo, geo.whole, new_faces, sent, 0, functools.partial(late.leave, 3))


def adjoint_edge_kernel(geo, last, late, table, mats, inner, faces, weight_faces, *rest):
    v, x, y, z = geo.block
    codes = Table(geo, table).codes()
    if last:
        ghosts, weight_buffer, result, raw, weight_ghosts = rest
        join(geo, weight_buffer, raw)
        turn(geo, codes, raw, weight_ghosts)
    else:
        rate_faces, buffer, weight_ghosts, result, new_faces, sent, ghosts, raw = rest
        join(geo, buffer, raw)
        turn(geo, codes, raw, ghosts)
        late.leave(3)
    values = []
    for side in range(6):
        views = [face_values(geo, field, side) for field in (faces, ghosts, weight_faces, weight_ghosts)]
        values.append(adjoint_face(geo, mats, side, *views))
    add_terms(geo, values, inner, result, functools.partial(late.leave, 0) if last else None)
    if not last:
        take_weight_faces(geo, result, rate_faces, new_faces)
        cut(geo, geo.whole, new_faces, sent, 0, functools.partial(late.leave, 2))


class Late:
    def __init__(self, arrivals, departures, sems):
        self.arrivals, self.departures, self.sems, self.started = arrivals, departures, sems, []

    def wait(self, index):
        if index in self.arrivals:
            self.arrivals[index].wait()

    def leave(self, index, slot=None):
        if index in self.departures:
            source, target = self.departures[index]
            if slot is not None:
                source, target = source.at[slot], target.at[slot]
            copy = pltpu.make_async_copy(source, target, self.sems.at[len(self.started)])
            copy.start()
            self.started.append(copy)


def call(kernel, ins, outs, scratch, flops, fetch=(), aliases=None):
    late_in = [(index, shape) for index, (kind, shape) in enumerate(ins) if kind == "H"]
    late_out = [(index, shape) for index, (kind, shape) in enumerate(outs) if kind in "HB"]
    count_in, count_out = len(late_in), len(late_out)
    sends = sum(shape[0] if kind == "B" else 1 for kind, shape in outs if kind in "HBD")

    def body(*refs):
        given = list(refs[: len(ins)])
        made = list(refs[len(ins) : len(ins) + len(outs)])
        rest = list(refs[len(ins) + len(outs) :])
        own = rest[: len(scratch)]
        stage = rest[len(scratch) : len(scratch) + count_in + count_out]
        sems_in = rest[len(scratch) + count_in + count_out] if count_in or fetch else None
        sems_out = rest[-1] if sends else None
        arrivals, departures = {}, {}
        for slot, (index, _) in enumerate(late_in):
            copy = pltpu.make_async_copy(given[index], stage[slot], sems_in.at[slot])
            copy.start()
            arrivals[index] = copy
            given[index] = stage[slot]
        for slot, (index, _) in enumerate(late_out):
            departures[index] = (stage[count_in + slot], made[index])
            made[index] = stage[count_in + slot]
        for index, (kind, _) in enumerate(outs):
            if kind == "D":
                departures[index] = (made[index - 1], made[index])
        fetched = []
        for slot, (source, target) in enumerate(fetch):
            copy = pltpu.make_async_copy(given[source], made[target], sems_in.at[count_in + slot])
            copy.start()
            fetched.append(copy)
        late = Late(arrivals, departures, sems_out)
        hidden_in = {source for source, _ in fetch}
        hidden_out = {target for _, target in fetch}
        operands, group = [], []
        for index, ref in enumerate(given):
            if ins[index][0] == "G":
                group.append(ref)
                if len(group) == 1:
                    operands.append(group)
            elif index not in hidden_in:
                operands.append(ref)
        kernel(
            late,
            *operands,
            *[ref for index, ref in enumerate(made) if index not in hidden_out and outs[index][0] != "D"],
            *own,
        )
        assert len(late.started) == sends
        for copy in fetched + late.started:
            copy.wait()

    hbm = pl.BlockSpec(memory_space=pltpu.HBM)
    specs = {"G": SMEM, "S": SMEM, "V": VMEM, "R": VMEM, "H": hbm, "B": hbm, "D": hbm, "P": hbm, "M": SMEM, "I": SMEM}
    scratch_shapes = [pltpu.VMEM(shape, jnp.float32) for shape in scratch]
    scratch_shapes += [pltpu.VMEM(shape, jnp.float32) for _, shape in late_in + late_out]
    if count_in or fetch:
        scratch_shapes.append(pltpu.SemaphoreType.DMA((count_in + len(fetch),)))
    if sends:
        scratch_shapes.append(pltpu.SemaphoreType.DMA((sends,)))
    shapes = {"V": jax.ShapeDtypeStruct, "R": pltpu.VMEM, "H": pltpu.HBM, "B": pltpu.HBM, "D": pltpu.HBM}
    shapes.update({"M": pltpu.SMEM, "I": pltpu.SMEM})
    invoke = pl.pallas_call(
        body,
        in_specs=[specs[kind] for kind, _ in ins],
        out_specs=[specs[kind] for kind, _ in outs],
        out_shape=[shapes[kind](shape, jnp.int32 if kind == "I" else jnp.float32) for kind, shape in outs],
        scratch_shapes=scratch_shapes,
        input_output_aliases=aliases or {},
        compiler_params=pltpu.CompilerParams(vmem_limit_bytes=VMEM_LIMIT),
        cost_estimate=pl.CostEstimate(flops=flops, bytes_accessed=3 << 20, transcendentals=0),
    )

    def run(*operands):
        placed = {"G": pltpu.SMEM, "M": pltpu.SMEM, "H": pltpu.HBM, "R": pltpu.VMEM, "P": pltpu.HBM}
        return invoke(
            *[
                pltpu.with_memory_space_constraint(operand, placed[kind]) if kind in placed else operand
                for operand, (kind, _) in zip(operands, ins)
            ]
        )

    return run


def on_device(count, parts, checkpoint, seeds, cell_rate, flux_mats, owner, neighbours, orientation):
    nvars, cx, cy, cz = seeds.shape[2:]
    geo = Geometry(nvars, cx, cy, cz, count, parts)
    rate = cell_rate[0]
    grads = seeds[0, 0]
    place = lax.axis_index("space").astype(jnp.int32).reshape(1)
    part = lax.axis_index("ckpt").astype(jnp.int32).reshape(1)
    work = nvars * nvars * 3 * 4 * cx * cy * cz
    few = work // 16
    whole, both = geo.buffer(geo.whole.total), geo.buffer(geo.part.total + geo.whole.total)
    some = -(-geo.part.total // 8) * 8

    stored_shape, block, faces_shape = checkpoint.shape[1:], geo.block, geo.faces
    rate_block = cell_rate.shape[1:]
    scalar, near, kept_near, kept_scalar = ("S", None), ("V", None), ("R", None), ("M", None)

    grouped = [("G", None)] * 4

    def far(shape):
        return ("H", shape)

    def swap(buffer):
        return lax.all_to_all(buffer, "space", 0, 0, tiled=True)

    def route(arrived):
        return call(functools.partial(route_kernel, geo), grouped + [near], [("B", whole)], [], few)(
            *table, arrived
        )[0]

    def adjoint_inner(state, state_kind, grads, grads_kind):
        return call(
            functools.partial(adjoint_inner_kernel, geo),
            [kept_scalar, state_kind, grads_kind, far(rate_block)],
            [("R", block)],
            [geo.tall] * 2,
            2 * work,
        )(mats, state, grads, rate)[0]

    links = (owner, neighbours, orientation)
    weight_faces, rate_faces, sent, *table, mats = call(
        functools.partial(pack_kernel, geo),
        [scalar] * 2 + [far(stored_shape), far(block), far(rate_block)] + [("P", None)] * 4,
        [far(faces_shape), ("R", geo.rate_faces), ("B", both), ("I", (2,))]
        + [("I", link.shape) for link in links]
        + [("M", flux_mats.shape)],
        [faces_shape],
        few,
        fetch=((5, 4), (6, 5), (7, 6), (8, 7)),
    )(part, place, checkpoint[0], grads, rate, *links, flux_mats)
    fixed = (*table, mats)
    kept, sent = lax.optimization_barrier((checkpoint[0], sent))
    arrived = swap(sent)
    state = lax.all_gather(kept, "ckpt", axis=0)
    arrived, state = lax.optimization_barrier((arrived, state))
    (leaving,) = call(functools.partial(route_first_kernel, geo), grouped + [near], [("B", both)], [], few)(
        *table, arrived
    )
    first_ghosts = swap(leaving)
    inner, faces, kept_faces = call(
        functools.partial(step_inner_kernel, geo),
        [kept_scalar, far(state.shape), far(rate_block)],
        [("R", block), ("R", faces_shape), ("D", faces_shape)],
        [geo.tall],
        work,
    )(mats, state, rate)
    first_ghosts, inner, faces = lax.optimization_barrier((first_ghosts, inner, faces))
    gathered = lax.all_gather(first_ghosts[:, :some], "ckpt", axis=0)
    next_state, next_faces, kept_next_faces, sent, ghosts = call(
        functools.partial(step_edge_kernel, geo, True),
        grouped + [kept_scalar] + [kept_near] * 3 + [near],
        [("R", block), ("R", faces_shape), ("D", faces_shape), ("B", whole), far(faces_shape)],
        [faces_shape, faces_shape[1:], (parts,) + faces_shape[1:]],
        few,
        aliases={5: 0},
    )(*fixed, inner, faces, rate_faces, gathered)

    arrived = swap(sent)
    inner = adjoint_inner(next_state, kept_near, grads, far(block))
    arrived, inner = lax.optimization_barrier((arrived, inner))
    leaving = route(arrived)
    later_state, leaving = lax.optimization_barrier((next_state, leaving))
    next_ghosts = swap(leaving)
    final_inner, weight_ghosts, weight_faces = call(
        functools.partial(turn_weights_kernel, geo),
        [kept_scalar, kept_near, far(rate_block)] + grouped + [near, ("P", None)],
        [far(block), ("R", faces_shape), ("R", faces_shape)],
        [geo.tall, faces_shape],
        work,
        fetch=((8, 2),),
    )(mats, later_state, rate, *table, first_ghosts, weight_faces)
    next_ghosts, final_inner, weight_ghosts, weight_faces = lax.optimization_barrier(
        (next_ghosts, final_inner, weight_ghosts, weight_faces)
    )
    grads_now, next_weight_faces, sent, turned = call(
        functools.partial(adjoint_edge_kernel, geo, False),
        grouped + [kept_scalar] + [kept_near] * 4 + [near, kept_near],
        [("R", block), ("R", faces_shape), ("B", whole), far(faces_shape)],
        [faces_shape],
        few,
        aliases={5: 0},
    )(*fixed, inner, next_faces, weight_faces, rate_faces, next_ghosts, weight_ghosts)

    arrived = swap(sent)
    inner = adjoint_inner(state, far(state.shape), grads_now, kept_near)
    arrived, inner = lax.optimization_barrier((arrived, inner))
    leaving = route(arrived)
    final_inner, leaving = lax.optimization_barrier((final_inner, leaving))
    last_ghosts = swap(leaving)
    final, faces, ghosts = call(
        functools.partial(step_edge_kernel, geo, False),
        grouped + [kept_scalar] + [far(block), far(faces_shape), kept_near, far(faces_shape), ("P", None), ("P", None)],
        [("V", block), ("R", faces_shape), ("R", faces_shape)],
        [],
        work,
        fetch=((9, 1), (10, 2)),
    )(*fixed, final_inner, kept_next_faces, rate_faces, turned, kept_faces, ghosts)
    last_ghosts, final, faces, ghosts = lax.optimization_barrier((last_ghosts, final, faces, ghosts))
    (adjoint,) = call(
        functools.partial(adjoint_edge_kernel, geo, True),
        grouped + [kept_scalar] + [kept_near] * 4 + [near],
        [("B", block)],
        [faces_shape] * 2,
        few,
    )(*fixed, inner, faces, next_weight_faces, ghosts, last_ghosts)
    return (adjoint[None, None], final[None])


def solution(mesh):
    return jax.shard_map(
        functools.partial(on_device, mesh.shape["space"], mesh.shape["ckpt"]),
        mesh=mesh,
        in_specs=(
            P("space", None, "ckpt", None, None),
            P("ckpt", "space", None, None, None, None),
            P("space", None, None, None),
            P(),
            P(),
            P(),
            P(),
        ),
        out_specs=(P("ckpt", "space", None, None, None, None), P("space", None, None, None, None)),
        check_vma=False,
    )
```

```python
import functools

import jax
import jax.numpy as jnp
from jax import lax
from jax.experimental import pallas as pl
from jax.experimental.pallas import tpu as pltpu
from jax.sharding import PartitionSpec as P

STEPS = 2
time_step = 0.05
damping = 0.015

PAD = 8
VMEM = pl.BlockSpec(memory_space=pltpu.VMEM)
SMEM = pl.BlockSpec(memory_space=pltpu.SMEM)
VMEM_LIMIT = 16 * 1024 * 1024


class Pieces:
    def __init__(self, rows, count):
        self.rows = rows
        self.runs = [-(-length // count) for length in rows]
        self.starts = [sum(self.runs[:index]) for index in range(len(rows))]
        self.total = sum(self.runs)


class Geometry:
    def __init__(self, nvars, cx, cy, cz, count, parts):
        self.v, self.x, self.y, self.z, self.n, self.parts = nvars, cx, cy, cz, count, parts
        self.depth = cx // parts
        self.rows = [nvars * cy] * 2 + [nvars * cx] * 2 + [cy] * 2
        self.whole = Pieces(self.rows, count)
        self.part = Pieces([nvars * cy] + [nvars * self.depth] * 2 + [cy], count)
        self.face_rows = -(-max(run * count for run in self.whole.runs) // 8) * 8
        self.block = (nvars, cx, cy, cz)
        self.tall = (nvars, cx, cy + 2 * PAD, cz)
        self.faces = (6, self.face_rows, cz)
        self.rate_faces = (6, max(cx, cy), cz)

    def buffer(self, rows):
        return (self.n, -(-rows // 8) * 8, self.z)


def take_z_faces(geo, load, variables=None):
    v, x, y, z = geo.block
    lane = lax.broadcasted_iota(jnp.int32, (y, z), 1)
    high = jnp.zeros((y, z), jnp.float32)
    low = jnp.zeros((y, z), jnp.float32)
    for var in range(variables or v):
        for plane in range(x):
            place = var * x + plane
            tile = pltpu.roll(load(var, plane), place + 1, 1)
            high = jnp.where(lane == place, tile, high)
            low = jnp.where(lane == place + 1, tile, low)
    return high, pltpu.roll(low, z - 1, 1)


def repeat_lanes(geo, layer):
    total = layer
    for var in range(1, geo.v):
        total = total + pltpu.roll(layer, var * geo.x, 1)
    return total


def take_xy_faces(geo, source, faces):
    v, x, y, z = geo.block
    faces[0, : v * y] = source[:, x - 1].reshape(v * y, z)
    faces[1, : v * y] = source[:, 0].reshape(v * y, z)
    for var in range(v):
        faces[2, var * x : (var + 1) * x] = source[var, :, y - 1, :]
        faces[3, var * x : (var + 1) * x] = source[var, :, 0, :]


def cut(geo, pieces, faces, buffer, base, leave=None):
    for slot in range(geo.n):
        for index, (run, start) in enumerate(zip(pieces.runs, pieces.starts)):
            buffer[slot, base + start : base + start + run] = faces[index, slot * run : (slot + 1) * run]
        if leave:
            leave(slot)


class Table:
    def __init__(self, geo, refs):
        self.n = geo.n
        self.places, self.owner, self.neighbours, self.orientation = refs

    def codes(self):
        own = jnp.int32(0)
        for block in range(self.n):
            own = jnp.where(self.owner[block] == self.places[0], block, own)
        return [self.orientation[own, side] for side in range(6)]

    def part(self):
        return self.places[1]

    def slot(self, place):
        half = place >> 1
        return jnp.where((place & 1) == 1, self.n - 1 - half, half)

    def target(self, block):
        return self.slot(self.owner[block])

    def source(self, block, side):
        return self.slot(self.owner[self.neighbours[block, side]])


def flip_rows(values, flag, length):
    rows, z = values.shape
    grouped = values.reshape(rows // length, length // 8, 8, z)
    index = lax.broadcasted_iota(jnp.int32, (8, z), 0)
    index = jnp.where(flag == 1, 7 - index, index)
    tiles = length // 8
    out = []
    for group in range(rows // length):
        for tile in range(tiles):
            picked = jnp.where(flag == 1, grouped[group, tiles - 1 - tile], grouped[group, tile])
            out.append(jnp.take_along_axis(picked, index, axis=0))
    return jnp.stack(out).reshape(rows, z)


def flip_lanes(values, flag, length):
    rows, z = values.shape
    lane = lax.broadcasted_iota(jnp.int32, (8, z), 1)
    within = lax.rem(lane, length)
    index = jnp.where(flag == 1, lane + (length - 1) - 2 * within, lane)
    index = jnp.minimum(index, z - 1)
    tiles = values.reshape(rows // 8, 8, z)
    return jnp.stack(
        [jnp.take_along_axis(tiles[tile], index, axis=1) for tile in range(rows // 8)]
    ).reshape(rows, z)


def join(geo, buffer, raw, base=0):
    for side in range(6):
        run, start = geo.whole.runs[side], base + geo.whole.starts[side]
        for slot in range(geo.n):
            raw[side, slot * run : (slot + 1) * run] = buffer[slot, start : start + run]


def part_of_lane(geo, rows):
    lane = lax.broadcasted_iota(jnp.int32, (rows, geo.z), 1)
    return lax.rem(lane, geo.x) // geo.depth


def join_parts(geo, buffer, raw, piece, zpiece):
    for side in range(6):
        index = 0 if side < 2 else min(side - 1, 3)
        run, start = geo.part.runs[index], geo.part.starts[index]
        if side < 2:
            part = 0 if side == 0 else geo.parts - 1
            for slot in range(geo.n):
                raw[side, slot * run : (slot + 1) * run] = buffer[part, slot, start : start + run]
        elif side < 4:
            for part in range(geo.parts):
                for slot in range(geo.n):
                    piece[slot * run : (slot + 1) * run] = buffer[part, slot, start : start + run]
                for var in range(geo.v):
                    row = var * geo.x + part * geo.depth
                    raw[side, row : row + geo.depth] = piece[var * geo.depth : (var + 1) * geo.depth]
        else:
            lanes = part_of_lane(geo, geo.y)
            total = jnp.zeros((geo.y, geo.z), jnp.float32)
            for part in range(geo.parts):
                if side == 4:
                    for slot in range(geo.n):
                        zpiece[part, slot * run : (slot + 1) * run] = buffer[part, slot, start : start + run]
                    rows = zpiece[part, : geo.y]
                    after = (part + 1) % geo.parts
                    rows = jnp.where(lanes == after, rows, 0.0)
                    total = total + pltpu.roll(rows, geo.z - geo.depth if after else geo.x - geo.depth, 1)
                else:
                    total = total + jnp.where(lanes == part, zpiece[part, : geo.y], 0.0)
            raw[side, : geo.y] = total


def turn(geo, codes, raw, ghosts):
    v, x, y, z = geo.block
    for side in range(6):
        first, second = codes[side] & 1, (codes[side] >> 1) & 1
        layer = raw[side, : geo.rows[side]]
        if side < 4:
            layer = flip_lanes(flip_rows(layer, first, y if side < 2 else x), second, z)
        else:
            layer = flip_lanes(flip_rows(layer, second, y), first, x)
        ghosts[side, : geo.rows[side]] = layer


def face_values(geo, faces, side):
    v, x, y, z = geo.block
    if side < 4:
        depth = y if side < 2 else x
        return [faces[side, var * depth : (var + 1) * depth] for var in range(v)]
    layer = faces[side, :y]
    return [layer] + [pltpu.roll(layer, z - var * x, 1) for var in range(1, v)]


def fill_tall(geo, source, tall):
    v, x, y, z = geo.block
    if len(source.shape) == 5:
        depth = geo.depth
        for part in range(geo.parts):
            tall[:, part * depth : (part + 1) * depth, PAD : PAD + y, :] = source[part]
    else:
        tall[:, :, PAD : PAD + y, :] = source[...]
    for var in range(v):
        tall[var, :, PAD - 1, :] = tall[var, :, PAD, :]
        tall[var, :, PAD + y, :] = tall[var, :, PAD + y - 1, :]


def around(geo, tall, plane):
    v, x, y, z = geo.block
    lane = lax.broadcasted_iota(jnp.int32, (y, z), 1)
    before, after = jnp.maximum(plane - 1, 0), jnp.minimum(plane + 1, x - 1)
    cells, low, high = [], [[], [], []], [[], [], []]
    for var in range(v):
        mid = tall[var, plane, PAD : PAD + y]
        cells.append(mid)
        low[0].append(tall[var, before, PAD : PAD + y])
        high[0].append(tall[var, after, PAD : PAD + y])
        low[1].append(tall[var, plane, PAD - 1 : PAD - 1 + y])
        high[1].append(tall[var, plane, PAD + 1 : PAD + 1 + y])
        low[2].append(jnp.where(lane == 0, mid, pltpu.roll(mid, 1, 1)))
        high[2].append(jnp.where(lane == z - 1, mid, pltpu.roll(mid, z - 1, 1)))
    return cells, low, high


def flux_entry(geo, mats, direction, row, column):
    return mats[direction, row, column]


def step_plane(geo, mats, cells, low, high, rate):
    v = geo.v
    total = [None] * v
    for direction in range(3):
        lows, highs = low[direction], high[direction]
        mean_low = 0.5 * (lows[0] + cells[0])
        mean_high = 0.5 * (cells[0] + highs[0])
        square_low = 1.0 + mean_low * mean_low
        square_high = 1.0 + mean_high * mean_high
        spread_low = square_low * lax.rsqrt(square_low)
        spread_high = square_high * lax.rsqrt(square_high)
        slopes = [highs[var] - lows[var] for var in range(v)]
        for var in range(v):
            term = spread_low * (cells[var] - lows[var]) - spread_high * (highs[var] - cells[var])
            for column in range(v):
                term = term + flux_entry(geo, mats, direction, var, column) * slopes[column]
            total[var] = term if total[var] is None else total[var] + term
    scale = (0.5 * time_step) * rate
    return [cells[var] - scale * total[var] - damping * jnp.tanh(cells[var]) for var in range(v)]


def adjoint_plane(geo, mats, cells, low, high, grads, weight, weight_low, weight_high):
    v = geo.v
    total = [None] * v
    extra = None
    for direction in range(3):
        spreads, steps = [], []
        for lower, upper, lower_weight, upper_weight in (
            (low[direction], cells, weight_low[direction], weight),
            (cells, high[direction], weight, weight_high[direction]),
        ):
            mean = 0.5 * (lower[0] + upper[0])
            square = 1.0 + mean * mean
            inverse = lax.rsqrt(square)
            jump = [lower_weight[var] - upper_weight[var] for var in range(v)]
            product = jump[0] * (upper[0] - lower[0])
            for var in range(1, v):
                product = product + jump[var] * (upper[var] - lower[var])
            product = product * (mean * inverse)
            extra = product if extra is None else extra + product
            spreads.append(square * inverse)
            steps.append(jump)
        slopes = [steps[0][var] + steps[1][var] for var in range(v)]
        for var in range(v):
            term = spreads[1] * steps[1][var] - spreads[0] * steps[0][var]
            for row in range(v):
                term = term + flux_entry(geo, mats, direction, row, var) * slopes[row]
            total[var] = term if total[var] is None else total[var] + term
    total[0] = total[0] - 0.5 * extra
    out = []
    for var in range(v):
        bend = jnp.tanh(cells[var])
        slope = (1.0 - damping) + damping * (bend * bend)
        out.append(grads[var] * slope - (0.5 * time_step) * total[var])
    return out


def step_face(geo, mats, side, cells, ghosts, rate):
    v = geo.v
    mean = 0.5 * (cells[0] + ghosts[0])
    square = 1.0 + mean * mean
    spread = square * lax.rsqrt(square)
    gap = [ghosts[var] - cells[var] for var in range(v)]
    scale = (0.5 * time_step) * rate
    out = []
    for var in range(v):
        total = flux_entry(geo, mats, side // 2, var, 0) * gap[0]
        for column in range(1, v):
            total = total + flux_entry(geo, mats, side // 2, var, column) * gap[column]
        if side % 2 == 0:
            out.append(scale * (spread * gap[var] - total))
        else:
            out.append(scale * (spread * gap[var] + total))
    return out


def adjoint_face(geo, mats, side, cells, ghosts, weight, ghost_weight):
    v = geo.v
    mean = 0.5 * (cells[0] + ghosts[0])
    square = 1.0 + mean * mean
    inverse = lax.rsqrt(square)
    spread = square * inverse
    jump = [weight[var] - ghost_weight[var] for var in range(v)]
    product = jump[0] * (ghosts[0] - cells[0])
    for var in range(1, v):
        product = product + jump[var] * (ghosts[var] - cells[var])
    product = (0.5 * product) * (mean * inverse)
    out = []
    for var in range(v):
        total = flux_entry(geo, mats, side // 2, 0, var) * jump[0]
        for row in range(1, v):
            total = total + flux_entry(geo, mats, side // 2, row, var) * jump[row]
        if side % 2 == 0:
            total = spread * jump[var] + total
        else:
            total = spread * jump[var] - total
        if var == 0:
            total = total - product
        out.append((-0.5 * time_step) * total)
    return out


def pack_kernel(geo, late, part, place, stored, grads, rate, *rest):
    weight_faces, rate_faces, buffer, places, pieces = rest
    places[0] = place[0]
    places[1] = part[0]
    v, x, y, z = geo.block
    depth = geo.depth
    late.wait(2)
    lane = lax.broadcasted_iota(jnp.int32, (y, z), 1)
    plane = jnp.where(part[0] == geo.parts - 1, depth - 1, 0)
    high = jnp.zeros((y, z), jnp.float32)
    low = jnp.zeros((y, z), jnp.float32)
    for var in range(v):
        pieces[0, var * y : (var + 1) * y] = stored[var, plane]
        pieces[1, var * depth : (var + 1) * depth] = stored[var, :, y - 1, :]
        pieces[2, var * depth : (var + 1) * depth] = stored[var, :, 0, :]
        for step in range(depth):
            place_now = var * x + part[0] * depth + step
            tile = pltpu.roll(stored[var, step], place_now + 1, 1)
            high = jnp.where(lane == place_now, tile, high)
            low = jnp.where(lane == place_now + 1, tile, low)
    shift = jnp.where(part[0] == geo.parts - 1, z - x + depth, depth)
    pieces[3, :y] = high + pltpu.roll(low, lax.rem(shift + z - 1, z), 1)
    cut(geo, geo.part, pieces, buffer, 0)
    late.wait(3)
    late.wait(4)
    rate_faces[0, :y] = rate[x - 1]
    rate_faces[1, :y] = rate[0]
    rate_faces[2, :x] = rate[:, y - 1, :]
    rate_faces[3, :x] = rate[:, 0, :]
    high, low = take_z_faces(geo, lambda var, plane: rate[plane], 1)
    rate_faces[4, :y] = repeat_lanes(geo, high)
    rate_faces[5, :y] = repeat_lanes(geo, low)
    take_weight_faces(geo, grads, rate_faces, weight_faces)
    late.leave(0)
    cut(geo, geo.whole, weight_faces, buffer, geo.part.total, functools.partial(late.leave, 2))


def take_weight_faces(geo, grads, rate_faces, faces):
    v, x, y, z = geo.block
    lane = lax.broadcasted_iota(jnp.int32, (y, z), 1)
    high = jnp.zeros((y, z), jnp.float32)
    low = jnp.zeros((y, z), jnp.float32)
    for var in range(v):
        faces[0, var * y : (var + 1) * y] = grads[var, x - 1] * rate_faces[0, :y]
        faces[1, var * y : (var + 1) * y] = grads[var, 0] * rate_faces[1, :y]
        faces[2, var * x : (var + 1) * x] = grads[var, :, y - 1, :] * rate_faces[2, :x]
        faces[3, var * x : (var + 1) * x] = grads[var, :, 0, :] * rate_faces[3, :x]
        for plane in range(x):
            place = var * x + plane
            tile = pltpu.roll(grads[var, plane], place + 1, 1)
            high = jnp.where(lane == place, tile, high)
            low = jnp.where(lane == place + 1, tile, low)
    faces[4, :y] = high * rate_faces[4, :y]
    faces[5, :y] = pltpu.roll(low, z - 1, 1) * rate_faces[5, :y]


def route_whole(geo, links, block, arrived, leaving, base):
    for side in range(6):
        source = links.source(block, side)
        run, start, far = geo.whole.runs[side], base + geo.whole.starts[side], base + geo.whole.starts[side ^ 1]
        leaving[links.target(block), start : start + run] = arrived[source, far : far + run]


def route_kernel(geo, late, table, arrived, leaving):
    links = Table(geo, table)
    for block in range(geo.n):
        route_whole(geo, links, block, arrived, leaving, 0)
        late.leave(0, links.target(block))


def route_first_kernel(geo, late, table, arrived, leaving):
    links = Table(geo, table)
    x_side = jnp.where(links.part() == geo.parts - 1, 1, 0)
    for block in range(geo.n):
        route_whole(geo, links, block, arrived, leaving, geo.part.total)
        for index in range(3):
            side, far_index = (x_side, 0) if index == 0 else (index + 1, 3 - index)
            source = links.source(block, side)
            run, start, far = geo.part.runs[index], geo.part.starts[index], geo.part.starts[far_index]
            leaving[links.target(block), start : start + run] = arrived[source, far : far + run]
        run, start = geo.part.runs[3], geo.part.starts[3]
        from_low = arrived[links.source(block, 4), start : start + run]
        from_high = arrived[links.source(block, 5), start : start + run]
        own_lanes = part_of_lane(geo, run) == links.part()
        leaving[links.target(block), start : start + run] = jnp.where(own_lanes, from_high, from_low)
        late.leave(0, links.target(block))


def turn_weights_kernel(geo, late, mats, block, rate, table, buffer, result, ghosts, tall, raw):
    join(geo, buffer, raw, geo.part.total)
    turn(geo, Table(geo, table).codes(), raw, ghosts)
    step_inner_kernel(geo, late, mats, block, rate, result, tall)


def step_inner_kernel(geo, late, mats, block, rate, result, *rest):
    tall = rest[-1]
    late.wait(1)
    late.wait(2)
    fill_tall(geo, block, tall)

    def body(plane, carry):
        cells, low, high = around(geo, tall, plane)
        for var, value in enumerate(step_plane(geo, mats, cells, low, high, rate[plane])):
            result[var, plane] = value
        return carry

    lax.fori_loop(0, geo.x, body, 0)
    late.leave(0)
    if len(rest) == 2:
        faces = rest[0]
        v, x, y, z = geo.block
        for var in range(v):
            faces[0, var * y : (var + 1) * y] = tall[var, x - 1, PAD : PAD + y]
            faces[1, var * y : (var + 1) * y] = tall[var, 0, PAD : PAD + y]
            faces[2, var * x : (var + 1) * x] = tall[var, :, PAD + y - 1, :]
            faces[3, var * x : (var + 1) * x] = tall[var, :, PAD, :]
        high, low = take_z_faces(geo, lambda var, plane: tall[var, plane, PAD : PAD + y])
        faces[4, :y] = high
        faces[5, :y] = low
        late.leave(2)


def adjoint_inner_kernel(geo, late, mats, block, grads, rate, result, tall, weights):
    v, x, y, z = geo.block
    for index in range(1, 4):
        late.wait(index)
    fill_tall(geo, block, tall)

    def scale(plane, carry):
        for var in range(v):
            weights[var, plane, PAD : PAD + y] = rate[plane] * grads[var, plane]
        return carry

    lax.fori_loop(0, x, scale, 0)
    for var in range(v):
        weights[var, :, PAD - 1, :] = weights[var, :, PAD, :]
        weights[var, :, PAD + y, :] = weights[var, :, PAD + y - 1, :]

    def body(plane, carry):
        cells, low, high = around(geo, tall, plane)
        weight, weight_low, weight_high = around(geo, weights, plane)
        here = [grads[var, plane] for var in range(v)]
        values = adjoint_plane(geo, mats, cells, low, high, here, weight, weight_low, weight_high)
        for var, value in enumerate(values):
            result[var, plane] = value
        return carry

    lax.fori_loop(0, x, body, 0)


def add_terms(geo, values, inner, result, leave=None):
    v, x, y, z = geo.block
    lane = lax.broadcasted_iota(jnp.int32, (y, z), 1)
    zero = jnp.zeros((y, z), jnp.float32)
    ends = (lane == 0) | (lane == z - 1)
    even = lane % 2 == 0
    for var in range(v):
        high, low = values[4][var], pltpu.roll(values[5][var], 1, 1)
        mixed = (jnp.where(even, high, low), jnp.where(even, low, high))
        for plane in range(x):
            change = jnp.where(ends, pltpu.roll(mixed[plane % 2], z - 1 - plane, 1), zero)
            if plane == 0:
                change = change + values[1][var]
            if plane == x - 1:
                change = change + values[0][var]
            result[var, plane] = inner[var, plane] + change
        result[var, :, y - 1, :] = result[var, :, y - 1, :] + values[2][var]
        result[var, :, 0, :] = result[var, :, 0, :] + values[3][var]
        if leave:
            leave(var)


def step_edge_kernel(geo, first, late, table, mats, inner, faces, rate_faces, arrived, result, *rest):
    v, x, y, z = geo.block
    if first:
        new_faces, sent, ghosts, raw, piece, zpiece = rest
        join_parts(geo, arrived, raw, piece, zpiece)
        turn(geo, Table(geo, table).codes(), raw, ghosts)
        late.leave(4)
    else:
        ghosts = arrived
        late.wait(5)
        late.wait(8)
    late.wait(6)
    values = []
    for side in range(6):
        depth = y if side < 2 or side > 3 else x
        cells, outer = face_values(geo, faces, side), face_values(geo, ghosts, side)
        values.append(step_face(geo, mats, side, cells, outer, rate_faces[side, :depth]))
    add_terms(geo, values, inner, result)
    if first:
        take_xy_faces(geo, result, new_faces)
        high, low = take_z_faces(geo, lambda var, plane: result[var, plane])
        new_faces[4, :y] = high
        new_faces[5, :y] = low
        late.leave(2)
        cut(geo, geo.whole, new_faces, sent, 0, functools.partial(late.leave, 3))


def adjoint_edge_kernel(geo, last, late, table, mats, inner, faces, weight_faces, *rest):
    v, x, y, z = geo.block
    codes = Table(geo, table).codes()
    if last:
        ghosts, weight_buffer, result, raw, weight_ghosts = rest
        join(geo, weight_buffer, raw)
        turn(geo, codes, raw, weight_ghosts)
    else:
        rate_faces, buffer, weight_ghosts, result, new_faces, sent, ghosts, raw = rest
        join(geo, buffer, raw)
        turn(geo, codes, raw, ghosts)
        late.leave(3)
    values = []
    for side in range(6):
        views = [face_values(geo, field, side) for field in (faces, ghosts, weight_faces, weight_ghosts)]
        values.append(adjoint_face(geo, mats, side, *views))
    add_terms(geo, values, inner, result, functools.partial(late.leave, 0) if last else None)
    if not last:
        take_weight_faces(geo, result, rate_faces, new_faces)
        cut(geo, geo.whole, new_faces, sent, 0, functools.partial(late.leave, 2))


class Late:
    def __init__(self, arrivals, departures, sems):
        self.arrivals, self.departures, self.sems, self.started = arrivals, departures, sems, []

    def wait(self, index):
        if index in self.arrivals:
            self.arrivals[index].wait()

    def leave(self, index, slot=None):
        if index in self.departures:
            source, target = self.departures[index]
            if slot is not None:
                source, target = source.at[slot], target.at[slot]
            copy = pltpu.make_async_copy(source, target, self.sems.at[len(self.started)])
            copy.start()
            self.started.append(copy)


def call(kernel, ins, outs, scratch, flops, fetch=(), aliases=None):
    late_in = [(index, shape) for index, (kind, shape) in enumerate(ins) if kind == "H"]
    late_out = [(index, shape) for index, (kind, shape) in enumerate(outs) if kind in "HB"]
    count_in, count_out = len(late_in), len(late_out)
    sends = sum(shape[0] if kind == "B" else 1 for kind, shape in outs if kind in "HBD")

    def body(*refs):
        given = list(refs[: len(ins)])
        made = list(refs[len(ins) : len(ins) + len(outs)])
        rest = list(refs[len(ins) + len(outs) :])
        own = rest[: len(scratch)]
        stage = rest[len(scratch) : len(scratch) + count_in + count_out]
        sems_in = rest[len(scratch) + count_in + count_out] if count_in or fetch else None
        sems_out = rest[-1] if sends else None
        arrivals, departures = {}, {}
        for slot, (index, _) in enumerate(late_in):
            copy = pltpu.make_async_copy(given[index], stage[slot], sems_in.at[slot])
            copy.start()
            arrivals[index] = copy
            given[index] = stage[slot]
        for slot, (index, _) in enumerate(late_out):
            departures[index] = (stage[count_in + slot], made[index])
            made[index] = stage[count_in + slot]
        for index, (kind, _) in enumerate(outs):
            if kind == "D":
                departures[index] = (made[index - 1], made[index])
        fetched = []
        for slot, (source, target) in enumerate(fetch):
            copy = pltpu.make_async_copy(given[source], made[target], sems_in.at[count_in + slot])
            copy.start()
            fetched.append(copy)
        late = Late(arrivals, departures, sems_out)
        hidden_in = {source for source, _ in fetch}
        hidden_out = {target for _, target in fetch}
        operands, group = [], []
        for index, ref in enumerate(given):
            if ins[index][0] == "G":
                group.append(ref)
                if len(group) == 1:
                    operands.append(group)
            elif index not in hidden_in:
                operands.append(ref)
        kernel(
            late,
            *operands,
            *[ref for index, ref in enumerate(made) if index not in hidden_out and outs[index][0] != "D"],
            *own,
        )
        assert len(late.started) == sends
        for copy in fetched + late.started:
            copy.wait()

    hbm = pl.BlockSpec(memory_space=pltpu.HBM)
    specs = {"G": SMEM, "S": SMEM, "V": VMEM, "R": VMEM, "H": hbm, "B": hbm, "D": hbm, "P": hbm, "M": SMEM, "I": SMEM}
    scratch_shapes = [pltpu.VMEM(shape, jnp.float32) for shape in scratch]
    scratch_shapes += [pltpu.VMEM(shape, jnp.float32) for _, shape in late_in + late_out]
    if count_in or fetch:
        scratch_shapes.append(pltpu.SemaphoreType.DMA((count_in + len(fetch),)))
    if sends:
        scratch_shapes.append(pltpu.SemaphoreType.DMA((sends,)))
    shapes = {"V": jax.ShapeDtypeStruct, "R": pltpu.VMEM, "H": pltpu.HBM, "B": pltpu.HBM, "D": pltpu.HBM}
    shapes.update({"M": pltpu.SMEM, "I": pltpu.SMEM})
    invoke = pl.pallas_call(
        body,
        in_specs=[specs[kind] for kind, _ in ins],
        out_specs=[specs[kind] for kind, _ in outs],
        out_shape=[shapes[kind](shape, jnp.int32 if kind == "I" else jnp.float32) for kind, shape in outs],
        scratch_shapes=scratch_shapes,
        input_output_aliases=aliases or {},
        compiler_params=pltpu.CompilerParams(vmem_limit_bytes=VMEM_LIMIT),
        cost_estimate=pl.CostEstimate(flops=flops, bytes_accessed=3 << 20, transcendentals=0),
    )

    def run(*operands):
        placed = {"G": pltpu.SMEM, "M": pltpu.SMEM, "H": pltpu.HBM, "R": pltpu.VMEM, "P": pltpu.HBM}
        return invoke(
            *[
                pltpu.with_memory_space_constraint(operand, placed[kind]) if kind in placed else operand
                for operand, (kind, _) in zip(operands, ins)
            ]
        )

    return run


def on_device(count, parts, checkpoint, seeds, cell_rate, flux_mats, owner, neighbours, orientation):
    nvars, cx, cy, cz = seeds.shape[2:]
    geo = Geometry(nvars, cx, cy, cz, count, parts)
    rate = cell_rate[0]
    grads = seeds[0, 0]
    place = lax.axis_index("space").astype(jnp.int32).reshape(1)
    part = lax.axis_index("ckpt").astype(jnp.int32).reshape(1)
    work = nvars * nvars * 3 * 4 * cx * cy * cz
    few = work // 16
    whole, both = geo.buffer(geo.whole.total), geo.buffer(geo.part.total + geo.whole.total)
    some = -(-geo.part.total // 8) * 8

    stored_shape, block, faces_shape = checkpoint.shape[1:], geo.block, geo.faces
    rate_block = cell_rate.shape[1:]
    scalar, near, kept_near, kept_scalar = ("S", None), ("V", None), ("R", None), ("M", None)

    grouped = [("G", None)] * 4

    def far(shape):
        return ("H", shape)

    def swap(buffer):
        ring = list(range(0, count, 2)) + list(range(count - 1, 0, -2))
        return lax.all_to_all(buffer, "space", 0, 0, axis_index_groups=[ring], tiled=True)

    def route(arrived):
        return call(functools.partial(route_kernel, geo), grouped + [near], [("B", whole)], [], few)(
            *table, arrived
        )[0]

    def adjoint_inner(state, state_kind, grads, grads_kind):
        return call(
            functools.partial(adjoint_inner_kernel, geo),
            [kept_scalar, state_kind, grads_kind, far(rate_block)],
            [("R", block)],
            [geo.tall] * 2,
            2 * work,
        )(mats, state, grads, rate)[0]

    links = (owner, neighbours, orientation)
    weight_faces, rate_faces, sent, *table, mats = call(
        functools.partial(pack_kernel, geo),
        [scalar] * 2 + [far(stored_shape), far(block), far(rate_block)] + [("P", None)] * 4,
        [far(faces_shape), ("R", geo.rate_faces), ("B", both), ("I", (2,))]
        + [("I", link.shape) for link in links]
        + [("M", flux_mats.shape)],
        [faces_shape],
        few,
        fetch=((5, 4), (6, 5), (7, 6), (8, 7)),
    )(part, place, checkpoint[0], grads, rate, *links, flux_mats)
    fixed = (*table, mats)
    kept, sent = lax.optimization_barrier((checkpoint[0], sent))
    arrived = swap(sent)
    state = lax.all_gather(kept, "ckpt", axis=0)
    arrived, state = lax.optimization_barrier((arrived, state))
    (leaving,) = call(functools.partial(route_first_kernel, geo), grouped + [near], [("B", both)], [], few)(
        *table, arrived
    )
    first_ghosts = swap(leaving)
    inner, faces, kept_faces = call(
        functools.partial(step_inner_kernel, geo),
        [kept_scalar, far(state.shape), far(rate_block)],
        [("R", block), ("R", faces_shape), ("D", faces_shape)],
        [geo.tall],
        work,
    )(mats, state, rate)
    first_ghosts, inner, faces = lax.optimization_barrier((first_ghosts, inner, faces))
    gathered = lax.all_gather(first_ghosts[:, :some], "ckpt", axis=0)
    next_state, next_faces, kept_next_faces, sent, ghosts = call(
        functools.partial(step_edge_kernel, geo, True),
        grouped + [kept_scalar] + [kept_near] * 3 + [near],
        [("R", block), ("R", faces_shape), ("D", faces_shape), ("B", whole), far(faces_shape)],
        [faces_shape, faces_shape[1:], (parts,) + faces_shape[1:]],
        few,
        aliases={5: 0},
    )(*fixed, inner, faces, rate_faces, gathered)

    arrived = swap(sent)
    inner = adjoint_inner(next_state, kept_near, grads, far(block))
    arrived, inner = lax.optimization_barrier((arrived, inner))
    leaving = route(arrived)
    later_state, leaving = lax.optimization_barrier((next_state, leaving))
    next_ghosts = swap(leaving)
    final_inner, weight_ghosts, weight_faces = call(
        functools.partial(turn_weights_kernel, geo),
        [kept_scalar, kept_near, far(rate_block)] + grouped + [near, ("P", None)],
        [far(block), ("R", faces_shape), ("R", faces_shape)],
        [geo.tall, faces_shape],
        work,
        fetch=((8, 2),),
    )(mats, later_state, rate, *table, first_ghosts, weight_faces)
    next_ghosts, final_inner, weight_ghosts, weight_faces = lax.optimization_barrier(
        (next_ghosts, final_inner, weight_ghosts, weight_faces)
    )
    grads_now, next_weight_faces, sent, turned = call(
        functools.partial(adjoint_edge_kernel, geo, False),
        grouped + [kept_scalar] + [kept_near] * 4 + [near, kept_near],
        [("R", block), ("R", faces_shape), ("B", whole), far(faces_shape)],
        [faces_shape],
        few,
        aliases={5: 0},
    )(*fixed, inner, next_faces, weight_faces, rate_faces, next_ghosts, weight_ghosts)

    arrived = swap(sent)
    inner = adjoint_inner(state, far(state.shape), grads_now, kept_near)
    arrived, inner = lax.optimization_barrier((arrived, inner))
    leaving = route(arrived)
    final_inner, leaving = lax.optimization_barrier((final_inner, leaving))
    last_ghosts = swap(leaving)
    final, faces, ghosts = call(
        functools.partial(step_edge_kernel, geo, False),
        grouped + [kept_scalar] + [far(block), far(faces_shape), kept_near, far(faces_shape), ("P", None), ("P", None)],
        [("V", block), ("R", faces_shape), ("R", faces_shape)],
        [],
        work,
        fetch=((9, 1), (10, 2)),
    )(*fixed, final_inner, kept_next_faces, rate_faces, turned, kept_faces, ghosts)
    last_ghosts, final, faces, ghosts = lax.optimization_barrier((last_ghosts, final, faces, ghosts))
    (adjoint,) = call(
        functools.partial(adjoint_edge_kernel, geo, True),
        grouped + [kept_scalar] + [kept_near] * 4 + [near],
        [("B", block)],
        [faces_shape] * 2,
        few,
    )(*fixed, inner, faces, next_weight_faces, ghosts, last_ghosts)
    return (adjoint[None, None], final[None])


def solution(mesh):
    return jax.shard_map(
        functools.partial(on_device, mesh.shape["space"], mesh.shape["ckpt"]),
        mesh=mesh,
        in_specs=(
            P("space", None, "ckpt", None, None),
            P("ckpt", "space", None, None, None, None),
            P("space", None, None, None),
            P(),
            P(),
            P(),
            P(),
        ),
        out_specs=(P("ckpt", "space", None, None, None, None), P("space", None, None, None, None)),
        check_vma=False,
    )
```

```python
import functools

import jax
import jax.numpy as jnp
from jax import lax
from jax.experimental import pallas as pl
from jax.experimental.pallas import tpu as pltpu
from jax.sharding import PartitionSpec as P

STEPS = 2
time_step = 0.05
damping = 0.015

PAD = 8
VMEM = pl.BlockSpec(memory_space=pltpu.VMEM)
SMEM = pl.BlockSpec(memory_space=pltpu.SMEM)
VMEM_LIMIT = 16 * 1024 * 1024


class Pieces:
    def __init__(self, rows, count):
        self.rows = rows
        self.runs = [-(-length // count) for length in rows]
        self.starts = [sum(self.runs[:index]) for index in range(len(rows))]
        self.total = sum(self.runs)


class Geometry:
    def __init__(self, nvars, cx, cy, cz, count, parts):
        self.v, self.x, self.y, self.z, self.n, self.parts = nvars, cx, cy, cz, count, parts
        self.depth = cx // parts
        self.rows = [nvars * cy] * 2 + [nvars * cx] * 2 + [cy] * 2
        self.whole = Pieces(self.rows, count)
        self.part = Pieces([nvars * cy] + [nvars * self.depth] * 2 + [cy], count)
        self.face_rows = -(-max(run * count for run in self.whole.runs) // 8) * 8
        self.block = (nvars, cx, cy, cz)
        self.tall = (nvars, cx, cy + 2 * PAD, cz)
        self.faces = (6, self.face_rows, cz)
        self.rate_faces = (6, max(cx, cy), cz)

    def buffer(self, rows):
        return (self.n, -(-rows // 8) * 8, self.z)


def take_z_faces(geo, load, variables=None):
    v, x, y, z = geo.block
    lane = lax.broadcasted_iota(jnp.int32, (y, z), 1)
    high = jnp.zeros((y, z), jnp.float32)
    low = jnp.zeros((y, z), jnp.float32)
    for var in range(variables or v):
        for plane in range(x):
            place = var * x + plane
            tile = pltpu.roll(load(var, plane), place + 1, 1)
            high = jnp.where(lane == place, tile, high)
            low = jnp.where(lane == place + 1, tile, low)
    return high, pltpu.roll(low, z - 1, 1)


def repeat_lanes(geo, layer):
    total = layer
    for var in range(1, geo.v):
        total = total + pltpu.roll(layer, var * geo.x, 1)
    return total


def take_xy_faces(geo, source, faces):
    v, x, y, z = geo.block
    faces[0, : v * y] = source[:, x - 1].reshape(v * y, z)
    faces[1, : v * y] = source[:, 0].reshape(v * y, z)
    for var in range(v):
        faces[2, var * x : (var + 1) * x] = source[var, :, y - 1, :]
        faces[3, var * x : (var + 1) * x] = source[var, :, 0, :]


def cut(geo, pieces, faces, buffer, base, leave=None):
    for slot in range(geo.n):
        for index, (run, start) in enumerate(zip(pieces.runs, pieces.starts)):
            buffer[slot, base + start : base + start + run] = faces[index, slot * run : (slot + 1) * run]
        if leave:
            leave(slot)


class Table:
    def __init__(self, geo, refs):
        self.n = geo.n
        self.places, self.owner, self.neighbours, self.orientation = refs

    def codes(self):
        own = jnp.int32(0)
        for block in range(self.n):
            own = jnp.where(self.owner[block] == self.places[0], block, own)
        return [self.orientation[own, side] for side in range(6)]

    def part(self):
        return self.places[1]

    def target(self, block):
        return self.owner[block]

    def source(self, block, side):
        return self.owner[self.neighbours[block, side]]


def flip_rows(values, flag, length):
    rows, z = values.shape
    grouped = values.reshape(rows // length, length // 8, 8, z)
    index = lax.broadcasted_iota(jnp.int32, (8, z), 0)
    index = jnp.where(flag == 1, 7 - index, index)
    tiles = length // 8
    out = []
    for group in range(rows // length):
        for tile in range(tiles):
            picked = jnp.where(flag == 1, grouped[group, tiles - 1 - tile], grouped[group, tile])
            out.append(jnp.take_along_axis(picked, index, axis=0))
    return jnp.stack(out).reshape(rows, z)


def flip_lanes(values, flag, length):
    rows, z = values.shape
    lane = lax.broadcasted_iota(jnp.int32, (8, z), 1)
    within = lax.rem(lane, length)
    index = jnp.where(flag == 1, lane + (length - 1) - 2 * within, lane)
    index = jnp.minimum(index, z - 1)
    tiles = values.reshape(rows // 8, 8, z)
    return jnp.stack(
        [jnp.take_along_axis(tiles[tile], index, axis=1) for tile in range(rows // 8)]
    ).reshape(rows, z)


def join(geo, buffer, raw, base=0):
    for side in range(6):
        run, start = geo.whole.runs[side], base + geo.whole.starts[side]
        for slot in range(geo.n):
            raw[side, slot * run : (slot + 1) * run] = buffer[slot, start : start + run]


def part_of_lane(geo, rows):
    lane = lax.broadcasted_iota(jnp.int32, (rows, geo.z), 1)
    return lax.rem(lane, geo.x) // geo.depth


def join_parts(geo, buffer, raw, piece, zpiece):
    for side in range(6):
        index = 0 if side < 2 else min(side - 1, 3)
        run, start = geo.part.runs[index], geo.part.starts[index]
        if side < 2:
            part = 0 if side == 0 else geo.parts - 1
            for slot in range(geo.n):
                raw[side, slot * run : (slot + 1) * run] = buffer[part, slot, start : start + run]
        elif side < 4:
            for part in range(geo.parts):
                for slot in range(geo.n):
                    piece[slot * run : (slot + 1) * run] = buffer[part, slot, start : start + run]
                for var in range(geo.v):
                    row = var * geo.x + part * geo.depth
                    raw[side, row : row + geo.depth] = piece[var * geo.depth : (var + 1) * geo.depth]
        else:
            lanes = part_of_lane(geo, geo.y)
            total = jnp.zeros((geo.y, geo.z), jnp.float32)
            for part in range(geo.parts):
                if side == 4:
                    for slot in range(geo.n):
                        zpiece[part, slot * run : (slot + 1) * run] = buffer[part, slot, start : start + run]
                    rows = zpiece[part, : geo.y]
                    after = (part + 1) % geo.parts
                    rows = jnp.where(lanes == after, rows, 0.0)
                    total = total + pltpu.roll(rows, geo.z - geo.depth if after else geo.x - geo.depth, 1)
                else:
                    total = total + jnp.where(lanes == part, zpiece[part, : geo.y], 0.0)
            raw[side, : geo.y] = total


def turn(geo, codes, raw, ghosts):
    v, x, y, z = geo.block
    for side in range(6):
        first, second = codes[side] & 1, (codes[side] >> 1) & 1
        layer = raw[side, : geo.rows[side]]
        if side < 4:
            layer = flip_lanes(flip_rows(layer, first, y if side < 2 else x), second, z)
        else:
            layer = flip_lanes(flip_rows(layer, second, y), first, x)
        ghosts[side, : geo.rows[side]] = layer


def face_values(geo, faces, side):
    v, x, y, z = geo.block
    if side < 4:
        depth = y if side < 2 else x
        return [faces[side, var * depth : (var + 1) * depth] for var in range(v)]
    layer = faces[side, :y]
    return [layer] + [pltpu.roll(layer, z - var * x, 1) for var in range(1, v)]


def fill_tall(geo, source, tall):
    v, x, y, z = geo.block
    if len(source.shape) == 5:
        depth = geo.depth
        for part in range(geo.parts):
            tall[:, part * depth : (part + 1) * depth, PAD : PAD + y, :] = source[part]
    else:
        tall[:, :, PAD : PAD + y, :] = source[...]
    for var in range(v):
        tall[var, :, PAD - 1, :] = tall[var, :, PAD, :]
        tall[var, :, PAD + y, :] = tall[var, :, PAD + y - 1, :]


def around(geo, tall, plane):
    v, x, y, z = geo.block
    lane = lax.broadcasted_iota(jnp.int32, (y, z), 1)
    before, after = jnp.maximum(plane - 1, 0), jnp.minimum(plane + 1, x - 1)
    cells, low, high = [], [[], [], []], [[], [], []]
    for var in range(v):
        mid = tall[var, plane, PAD : PAD + y]
        cells.append(mid)
        low[0].append(tall[var, before, PAD : PAD + y])
        high[0].append(tall[var, after, PAD : PAD + y])
        low[1].append(tall[var, plane, PAD - 1 : PAD - 1 + y])
        high[1].append(tall[var, plane, PAD + 1 : PAD + 1 + y])
        low[2].append(jnp.where(lane == 0, mid, pltpu.roll(mid, 1, 1)))
        high[2].append(jnp.where(lane == z - 1, mid, pltpu.roll(mid, z - 1, 1)))
    return cells, low, high


def flux_entry(geo, mats, direction, row, column):
    return mats[direction, row, column]


def step_plane(geo, mats, cells, low, high, rate):
    v = geo.v
    total = [None] * v
    for direction in range(3):
        lows, highs = low[direction], high[direction]
        mean_low = 0.5 * (lows[0] + cells[0])
        mean_high = 0.5 * (cells[0] + highs[0])
        square_low = 1.0 + mean_low * mean_low
        square_high = 1.0 + mean_high * mean_high
        spread_low = square_low * lax.rsqrt(square_low)
        spread_high = square_high * lax.rsqrt(square_high)
        slopes = [highs[var] - lows[var] for var in range(v)]
        for var in range(v):
            term = spread_low * (cells[var] - lows[var]) - spread_high * (highs[var] - cells[var])
            for column in range(v):
                term = term + flux_entry(geo, mats, direction, var, column) * slopes[column]
            total[var] = term if total[var] is None else total[var] + term
    scale = (0.5 * time_step) * rate
    return [cells[var] - scale * total[var] - damping * jnp.tanh(cells[var]) for var in range(v)]


def adjoint_plane(geo, mats, cells, low, high, grads, weight, weight_low, weight_high):
    v = geo.v
    total = [None] * v
    extra = None
    for direction in range(3):
        spreads, steps = [], []
        for lower, upper, lower_weight, upper_weight in (
            (low[direction], cells, weight_low[direction], weight),
            (cells, high[direction], weight, weight_high[direction]),
        ):
            mean = 0.5 * (lower[0] + upper[0])
            square = 1.0 + mean * mean
            inverse = lax.rsqrt(square)
            jump = [lower_weight[var] - upper_weight[var] for var in range(v)]
            product = jump[0] * (upper[0] - lower[0])
            for var in range(1, v):
                product = product + jump[var] * (upper[var] - lower[var])
            product = product * (mean * inverse)
            extra = product if extra is None else extra + product
            spreads.append(square * inverse)
            steps.append(jump)
        slopes = [steps[0][var] + steps[1][var] for var in range(v)]
        for var in range(v):
            term = spreads[1] * steps[1][var] - spreads[0] * steps[0][var]
            for row in range(v):
                term = term + flux_entry(geo, mats, direction, row, var) * slopes[row]
            total[var] = term if total[var] is None else total[var] + term
    total[0] = total[0] - 0.5 * extra
    out = []
    for var in range(v):
        bend = jnp.tanh(cells[var])
        slope = (1.0 - damping) + damping * (bend * bend)
        out.append(grads[var] * slope - (0.5 * time_step) * total[var])
    return out


def step_face(geo, mats, side, cells, ghosts, rate):
    v = geo.v
    mean = 0.5 * (cells[0] + ghosts[0])
    square = 1.0 + mean * mean
    spread = square * lax.rsqrt(square)
    gap = [ghosts[var] - cells[var] for var in range(v)]
    scale = (0.5 * time_step) * rate
    out = []
    for var in range(v):
        total = flux_entry(geo, mats, side // 2, var, 0) * gap[0]
        for column in range(1, v):
            total = total + flux_entry(geo, mats, side // 2, var, column) * gap[column]
        if side % 2 == 0:
            out.append(scale * (spread * gap[var] - total))
        else:
            out.append(scale * (spread * gap[var] + total))
    return out


def adjoint_face(geo, mats, side, cells, ghosts, weight, ghost_weight):
    v = geo.v
    mean = 0.5 * (cells[0] + ghosts[0])
    square = 1.0 + mean * mean
    inverse = lax.rsqrt(square)
    spread = square * inverse
    jump = [weight[var] - ghost_weight[var] for var in range(v)]
    product = jump[0] * (ghosts[0] - cells[0])
    for var in range(1, v):
        product = product + jump[var] * (ghosts[var] - cells[var])
    product = (0.5 * product) * (mean * inverse)
    out = []
    for var in range(v):
        total = flux_entry(geo, mats, side // 2, 0, var) * jump[0]
        for row in range(1, v):
            total = total + flux_entry(geo, mats, side // 2, row, var) * jump[row]
        if side % 2 == 0:
            total = spread * jump[var] + total
        else:
            total = spread * jump[var] - total
        if var == 0:
            total = total - product
        out.append((-0.5 * time_step) * total)
    return out


def pack_kernel(geo, late, part, place, stored, grads, rate, *rest):
    weight_faces, rate_faces, buffer, places, pieces = rest
    places[0] = place[0]
    places[1] = part[0]
    v, x, y, z = geo.block
    depth = geo.depth
    late.wait(2)
    lane = lax.broadcasted_iota(jnp.int32, (y, z), 1)
    plane = jnp.where(part[0] == geo.parts - 1, depth - 1, 0)
    high = jnp.zeros((y, z), jnp.float32)
    low = jnp.zeros((y, z), jnp.float32)
    for var in range(v):
        pieces[0, var * y : (var + 1) * y] = stored[var, plane]
        pieces[1, var * depth : (var + 1) * depth] = stored[var, :, y - 1, :]
        pieces[2, var * depth : (var + 1) * depth] = stored[var, :, 0, :]
        for step in range(depth):
            place_now = var * x + part[0] * depth + step
            tile = pltpu.roll(stored[var, step], place_now + 1, 1)
            high = jnp.where(lane == place_now, tile, high)
            low = jnp.where(lane == place_now + 1, tile, low)
    shift = jnp.where(part[0] == geo.parts - 1, z - x + depth, depth)
    pieces[3, :y] = high + pltpu.roll(low, lax.rem(shift + z - 1, z), 1)
    cut(geo, geo.part, pieces, buffer, 0)
    late.wait(3)
    late.wait(4)
    rate_faces[0, :y] = rate[x - 1]
    rate_faces[1, :y] = rate[0]
    rate_faces[2, :x] = rate[:, y - 1, :]
    rate_faces[3, :x] = rate[:, 0, :]
    high, low = take_z_faces(geo, lambda var, plane: rate[plane], 1)
    rate_faces[4, :y] = repeat_lanes(geo, high)
    rate_faces[5, :y] = repeat_lanes(geo, low)
    take_weight_faces(geo, grads, rate_faces, weight_faces)
    late.leave(0)
    cut(geo, geo.whole, weight_faces, buffer, geo.part.total, functools.partial(late.leave, 2))


def take_weight_faces(geo, grads, rate_faces, faces):
    v, x, y, z = geo.block
    lane = lax.broadcasted_iota(jnp.int32, (y, z), 1)
    high = jnp.zeros((y, z), jnp.float32)
    low = jnp.zeros((y, z), jnp.float32)
    for var in range(v):
        faces[0, var * y : (var + 1) * y] = grads[var, x - 1] * rate_faces[0, :y]
        faces[1, var * y : (var + 1) * y] = grads[var, 0] * rate_faces[1, :y]
        faces[2, var * x : (var + 1) * x] = grads[var, :, y - 1, :] * rate_faces[2, :x]
        faces[3, var * x : (var + 1) * x] = grads[var, :, 0, :] * rate_faces[3, :x]
        for plane in range(x):
            place = var * x + plane
            tile = pltpu.roll(grads[var, plane], place + 1, 1)
            high = jnp.where(lane == place, tile, high)
            low = jnp.where(lane == place + 1, tile, low)
    faces[4, :y] = high * rate_faces[4, :y]
    faces[5, :y] = pltpu.roll(low, z - 1, 1) * rate_faces[5, :y]


def route_whole(geo, links, block, arrived, leaving, base):
    for side in range(6):
        source = links.source(block, side)
        run, start, far = geo.whole.runs[side], base + geo.whole.starts[side], base + geo.whole.starts[side ^ 1]
        leaving[links.target(block), start : start + run] = arrived[source, far : far + run]


def route_kernel(geo, late, table, arrived, leaving):
    links = Table(geo, table)
    for block in range(geo.n):
        route_whole(geo, links, block, arrived, leaving, 0)
        late.leave(0, links.target(block))


def route_first_kernel(geo, late, table, arrived, leaving):
    links = Table(geo, table)
    x_side = jnp.where(links.part() == geo.parts - 1, 1, 0)
    for block in range(geo.n):
        route_whole(geo, links, block, arrived, leaving, geo.part.total)
        for index in range(3):
            side, far_index = (x_side, 0) if index == 0 else (index + 1, 3 - index)
            source = links.source(block, side)
            run, start, far = geo.part.runs[index], geo.part.starts[index], geo.part.starts[far_index]
            leaving[links.target(block), start : start + run] = arrived[source, far : far + run]
        run, start = geo.part.runs[3], geo.part.starts[3]
        from_low = arrived[links.source(block, 4), start : start + run]
        from_high = arrived[links.source(block, 5), start : start + run]
        own_lanes = part_of_lane(geo, run) == links.part()
        leaving[links.target(block), start : start + run] = jnp.where(own_lanes, from_high, from_low)
        late.leave(0, links.target(block))


def turn_weights_kernel(geo, late, mats, block, rate, table, buffer, result, ghosts, tall, raw):
    join(geo, buffer, raw, geo.part.total)
    turn(geo, Table(geo, table).codes(), raw, ghosts)
    step_inner_kernel(geo, late, mats, block, rate, result, tall)


def step_inner_kernel(geo, late, mats, block, rate, result, *rest):
    tall = rest[-1]
    late.wait(1)
    late.wait(2)
    fill_tall(geo, block, tall)

    def body(plane, carry):
        cells, low, high = around(geo, tall, plane)
        for var, value in enumerate(step_plane(geo, mats, cells, low, high, rate[plane])):
            result[var, plane] = value
        return carry

    lax.fori_loop(0, geo.x, body, 0)
    late.leave(0)
    if len(rest) == 2:
        faces = rest[0]
        v, x, y, z = geo.block
        for var in range(v):
            faces[0, var * y : (var + 1) * y] = tall[var, x - 1, PAD : PAD + y]
            faces[1, var * y : (var + 1) * y] = tall[var, 0, PAD : PAD + y]
            faces[2, var * x : (var + 1) * x] = tall[var, :, PAD + y - 1, :]
            faces[3, var * x : (var + 1) * x] = tall[var, :, PAD, :]
        high, low = take_z_faces(geo, lambda var, plane: tall[var, plane, PAD : PAD + y])
        faces[4, :y] = high
        faces[5, :y] = low
        late.leave(2)


def adjoint_inner_kernel(geo, late, mats, block, grads, rate, result, tall, weights):
    v, x, y, z = geo.block
    for index in range(1, 4):
        late.wait(index)
    fill_tall(geo, block, tall)

    def scale(plane, carry):
        for var in range(v):
            weights[var, plane, PAD : PAD + y] = rate[plane] * grads[var, plane]
        return carry

    lax.fori_loop(0, x, scale, 0)
    for var in range(v):
        weights[var, :, PAD - 1, :] = weights[var, :, PAD, :]
        weights[var, :, PAD + y, :] = weights[var, :, PAD + y - 1, :]

    def body(plane, carry):
        cells, low, high = around(geo, tall, plane)
        weight, weight_low, weight_high = around(geo, weights, plane)
        here = [grads[var, plane] for var in range(v)]
        values = adjoint_plane(geo, mats, cells, low, high, here, weight, weight_low, weight_high)
        for var, value in enumerate(values):
            result[var, plane] = value
        return carry

    lax.fori_loop(0, x, body, 0)


def add_terms(geo, values, inner, result, leave=None):
    v, x, y, z = geo.block
    lane = lax.broadcasted_iota(jnp.int32, (y, z), 1)
    zero = jnp.zeros((y, z), jnp.float32)
    ends = (lane == 0) | (lane == z - 1)
    even = lane % 2 == 0
    for var in range(v):
        high, low = values[4][var], pltpu.roll(values[5][var], 1, 1)
        mixed = (jnp.where(even, high, low), jnp.where(even, low, high))
        for plane in range(x):
            change = jnp.where(ends, pltpu.roll(mixed[plane % 2], z - 1 - plane, 1), zero)
            if plane == 0:
                change = change + values[1][var]
            if plane == x - 1:
                change = change + values[0][var]
            result[var, plane] = inner[var, plane] + change
        result[var, :, y - 1, :] = result[var, :, y - 1, :] + values[2][var]
        result[var, :, 0, :] = result[var, :, 0, :] + values[3][var]
        if leave:
            leave(var)


def step_edge_kernel(geo, first, late, table, mats, inner, faces, rate_faces, arrived, result, *rest):
    v, x, y, z = geo.block
    if first:
        new_faces, sent, ghosts, raw, piece, zpiece = rest
        join_parts(geo, arrived, raw, piece, zpiece)
        turn(geo, Table(geo, table).codes(), raw, ghosts)
        late.leave(4)
    else:
        ghosts = arrived
        late.wait(5)
        late.wait(8)
    late.wait(6)
    values = []
    for side in range(6):
        depth = y if side < 2 or side > 3 else x
        cells, outer = face_values(geo, faces, side), face_values(geo, ghosts, side)
        values.append(step_face(geo, mats, side, cells, outer, rate_faces[side, :depth]))
    add_terms(geo, values, inner, result)
    if first:
        take_xy_faces(geo, result, new_faces)
        high, low = take_z_faces(geo, lambda var, plane: result[var, plane])
        new_faces[4, :y] = high
        new_faces[5, :y] = low
        cut(geo, geo.whole, new_faces, sent, 0, functools.partial(late.leave, 3))
        late.leave(2)


def adjoint_edge_kernel(geo, last, late, table, mats, inner, faces, weight_faces, *rest):
    v, x, y, z = geo.block
    codes = Table(geo, table).codes()
    if last:
        ghosts, weight_buffer, result, raw, weight_ghosts = rest
        join(geo, weight_buffer, raw)
        turn(geo, codes, raw, weight_ghosts)
    else:
        rate_faces, buffer, weight_ghosts, result, new_faces, sent, ghosts, raw = rest
        join(geo, buffer, raw)
        turn(geo, codes, raw, ghosts)
        late.leave(3)
    values = []
    for side in range(6):
        views = [face_values(geo, field, side) for field in (faces, ghosts, weight_faces, weight_ghosts)]
        values.append(adjoint_face(geo, mats, side, *views))
    add_terms(geo, values, inner, result, functools.partial(late.leave, 0) if last else None)
    if not last:
        take_weight_faces(geo, result, rate_faces, new_faces)
        cut(geo, geo.whole, new_faces, sent, 0, functools.partial(late.leave, 2))


class Late:
    def __init__(self, arrivals, departures, sems):
        self.arrivals, self.departures, self.sems, self.started = arrivals, departures, sems, []

    def wait(self, index):
        if index in self.arrivals:
            self.arrivals[index].wait()

    def leave(self, index, slot=None):
        if index in self.departures:
            source, target = self.departures[index]
            if slot is not None:
                source, target = source.at[slot], target.at[slot]
            copy = pltpu.make_async_copy(source, target, self.sems.at[len(self.started)])
            copy.start()
            self.started.append(copy)


def call(kernel, ins, outs, scratch, flops, fetch=(), aliases=None):
    late_in = [(index, shape) for index, (kind, shape) in enumerate(ins) if kind == "H"]
    late_out = [(index, shape) for index, (kind, shape) in enumerate(outs) if kind in "HB"]
    count_in, count_out = len(late_in), len(late_out)
    sends = sum(shape[0] if kind == "B" else 1 for kind, shape in outs if kind in "HBD")

    def body(*refs):
        given = list(refs[: len(ins)])
        made = list(refs[len(ins) : len(ins) + len(outs)])
        rest = list(refs[len(ins) + len(outs) :])
        own = rest[: len(scratch)]
        stage = rest[len(scratch) : len(scratch) + count_in + count_out]
        sems_in = rest[len(scratch) + count_in + count_out] if count_in or fetch else None
        sems_out = rest[-1] if sends else None
        arrivals, departures = {}, {}
        for slot, (index, _) in enumerate(late_in):
            copy = pltpu.make_async_copy(given[index], stage[slot], sems_in.at[slot])
            copy.start()
            arrivals[index] = copy
            given[index] = stage[slot]
        for slot, (index, _) in enumerate(late_out):
            departures[index] = (stage[count_in + slot], made[index])
            made[index] = stage[count_in + slot]
        for index, (kind, _) in enumerate(outs):
            if kind == "D":
                departures[index] = (made[index - 1], made[index])
        fetched = []
        for slot, (source, target) in enumerate(fetch):
            copy = pltpu.make_async_copy(given[source], made[target], sems_in.at[count_in + slot])
            copy.start()
            fetched.append(copy)
        late = Late(arrivals, departures, sems_out)
        hidden_in = {source for source, _ in fetch}
        hidden_out = {target for _, target in fetch}
        operands, group = [], []
        for index, ref in enumerate(given):
            if ins[index][0] == "G":
                group.append(ref)
                if len(group) == 1:
                    operands.append(group)
            elif index not in hidden_in:
                operands.append(ref)
        kernel(
            late,
            *operands,
            *[ref for index, ref in enumerate(made) if index not in hidden_out and outs[index][0] != "D"],
            *own,
        )
        assert len(late.started) == sends
        for copy in fetched + late.started:
            copy.wait()

    hbm = pl.BlockSpec(memory_space=pltpu.HBM)
    specs = {"G": SMEM, "S": SMEM, "V": VMEM, "R": VMEM, "H": hbm, "B": hbm, "D": hbm, "P": hbm, "M": SMEM, "I": SMEM}
    scratch_shapes = [pltpu.VMEM(shape, jnp.float32) for shape in scratch]
    scratch_shapes += [pltpu.VMEM(shape, jnp.float32) for _, shape in late_in + late_out]
    if count_in or fetch:
        scratch_shapes.append(pltpu.SemaphoreType.DMA((count_in + len(fetch),)))
    if sends:
        scratch_shapes.append(pltpu.SemaphoreType.DMA((sends,)))
    shapes = {"V": jax.ShapeDtypeStruct, "R": pltpu.VMEM, "H": pltpu.HBM, "B": pltpu.HBM, "D": pltpu.HBM}
    shapes.update({"M": pltpu.SMEM, "I": pltpu.SMEM})
    invoke = pl.pallas_call(
        body,
        in_specs=[specs[kind] for kind, _ in ins],
        out_specs=[specs[kind] for kind, _ in outs],
        out_shape=[shapes[kind](shape, jnp.int32 if kind == "I" else jnp.float32) for kind, shape in outs],
        scratch_shapes=scratch_shapes,
        input_output_aliases=aliases or {},
        compiler_params=pltpu.CompilerParams(vmem_limit_bytes=VMEM_LIMIT),
        cost_estimate=pl.CostEstimate(flops=flops, bytes_accessed=3 << 20, transcendentals=0),
    )

    def run(*operands):
        placed = {"G": pltpu.SMEM, "M": pltpu.SMEM, "H": pltpu.HBM, "R": pltpu.VMEM, "P": pltpu.HBM}
        return invoke(
            *[
                pltpu.with_memory_space_constraint(operand, placed[kind]) if kind in placed else operand
                for operand, (kind, _) in zip(operands, ins)
            ]
        )

    return run


def on_device(count, parts, checkpoint, seeds, cell_rate, flux_mats, owner, neighbours, orientation):
    nvars, cx, cy, cz = seeds.shape[2:]
    geo = Geometry(nvars, cx, cy, cz, count, parts)
    rate = cell_rate[0]
    grads = seeds[0, 0]
    place = lax.axis_index("space").astype(jnp.int32).reshape(1)
    part = lax.axis_index("ckpt").astype(jnp.int32).reshape(1)
    work = nvars * nvars * 3 * 4 * cx * cy * cz
    few = work // 16
    whole, both = geo.buffer(geo.whole.total), geo.buffer(geo.part.total + geo.whole.total)
    some = -(-geo.part.total // 8) * 8

    stored_shape, block, faces_shape = checkpoint.shape[1:], geo.block, geo.faces
    rate_block = cell_rate.shape[1:]
    scalar, near, kept_near, kept_scalar = ("S", None), ("V", None), ("R", None), ("M", None)

    grouped = [("G", None)] * 4

    def far(shape):
        return ("H", shape)

    def swap(buffer):
        return lax.all_to_all(buffer, "space", 0, 0, tiled=True)

    def route(arrived):
        return call(functools.partial(route_kernel, geo), grouped + [near], [("B", whole)], [], few)(
            *table, arrived
        )[0]

    def adjoint_inner(state, state_kind, grads, grads_kind):
        return call(
            functools.partial(adjoint_inner_kernel, geo),
            [kept_scalar, state_kind, grads_kind, far(rate_block)],
            [("R", block)],
            [geo.tall] * 2,
            2 * work,
        )(mats, state, grads, rate)[0]

    links = (owner, neighbours, orientation)
    weight_faces, rate_faces, sent, *table, mats = call(
        functools.partial(pack_kernel, geo),
        [scalar] * 2 + [far(stored_shape), far(block), far(rate_block)] + [("P", None)] * 4,
        [far(faces_shape), ("R", geo.rate_faces), ("B", both), ("I", (2,))]
        + [("I", link.shape) for link in links]
        + [("M", flux_mats.shape)],
        [faces_shape],
        few,
        fetch=((5, 4), (6, 5), (7, 6), (8, 7)),
    )(part, place, checkpoint[0], grads, rate, *links, flux_mats)
    fixed = (*table, mats)
    kept, sent = lax.optimization_barrier((checkpoint[0], sent))
    arrived = swap(sent)
    state = lax.all_gather(kept, "ckpt", axis=0)
    arrived, state = lax.optimization_barrier((arrived, state))
    (leaving,) = call(functools.partial(route_first_kernel, geo), grouped + [near], [("B", both)], [], few)(
        *table, arrived
    )
    first_ghosts = swap(leaving)
    inner, faces, kept_faces = call(
        functools.partial(step_inner_kernel, geo),
        [kept_scalar, far(state.shape), far(rate_block)],
        [("R", block), ("R", faces_shape), ("D", faces_shape)],
        [geo.tall],
        work,
    )(mats, state, rate)
    first_ghosts, inner, faces = lax.optimization_barrier((first_ghosts, inner, faces))
    gathered = lax.all_gather(first_ghosts[:, :some], "ckpt", axis=0)
    next_state, next_faces, kept_next_faces, sent, ghosts = call(
        functools.partial(step_edge_kernel, geo, True),
        grouped + [kept_scalar] + [kept_near] * 3 + [near],
        [("R", block), ("R", faces_shape), ("D", faces_shape), ("B", whole), far(faces_shape)],
        [faces_shape, faces_shape[1:], (parts,) + faces_shape[1:]],
        few,
        aliases={5: 0},
    )(*fixed, inner, faces, rate_faces, gathered)

    arrived = swap(sent)
    inner = adjoint_inner(next_state, kept_near, grads, far(block))
    arrived, inner = lax.optimization_barrier((arrived, inner))
    leaving = route(arrived)
    later_state, leaving = lax.optimization_barrier((next_state, leaving))
    next_ghosts = swap(leaving)
    final_inner, weight_ghosts, weight_faces = call(
        functools.partial(turn_weights_kernel, geo),
        [kept_scalar, kept_near, far(rate_block)] + grouped + [near, ("P", None)],
        [far(block), ("R", faces_shape), ("R", faces_shape)],
        [geo.tall, faces_shape],
        work,
        fetch=((8, 2),),
    )(mats, later_state, rate, *table, first_ghosts, weight_faces)
    next_ghosts, final_inner, weight_ghosts, weight_faces = lax.optimization_barrier(
        (next_ghosts, final_inner, weight_ghosts, weight_faces)
    )
    grads_now, next_weight_faces, sent, turned = call(
        functools.partial(adjoint_edge_kernel, geo, False),
        grouped + [kept_scalar] + [kept_near] * 4 + [near, kept_near],
        [("R", block), ("R", faces_shape), ("B", whole), far(faces_shape)],
        [faces_shape],
        few,
        aliases={5: 0},
    )(*fixed, inner, next_faces, weight_faces, rate_faces, next_ghosts, weight_ghosts)

    arrived = swap(sent)
    inner = adjoint_inner(state, far(state.shape), grads_now, kept_near)
    arrived, inner = lax.optimization_barrier((arrived, inner))
    leaving = route(arrived)
    final_inner, leaving = lax.optimization_barrier((final_inner, leaving))
    last_ghosts = swap(leaving)
    final, faces, ghosts = call(
        functools.partial(step_edge_kernel, geo, False),
        grouped + [kept_scalar] + [far(block), far(faces_shape), kept_near, far(faces_shape), ("P", None), ("P", None)],
        [("V", block), ("R", faces_shape), ("R", faces_shape)],
        [],
        work,
        fetch=((9, 1), (10, 2)),
    )(*fixed, final_inner, kept_next_faces, rate_faces, turned, kept_faces, ghosts)
    last_ghosts, final, faces, ghosts = lax.optimization_barrier((last_ghosts, final, faces, ghosts))
    (adjoint,) = call(
        functools.partial(adjoint_edge_kernel, geo, True),
        grouped + [kept_scalar] + [kept_near] * 4 + [near],
        [("B", block)],
        [faces_shape] * 2,
        few,
    )(*fixed, inner, faces, next_weight_faces, ghosts, last_ghosts)
    return (adjoint[None, None], final[None])


def solution(mesh):
    return jax.shard_map(
        functools.partial(on_device, mesh.shape["space"], mesh.shape["ckpt"]),
        mesh=mesh,
        in_specs=(
            P("space", None, "ckpt", None, None),
            P("ckpt", "space", None, None, None, None),
            P("space", None, None, None),
            P(),
            P(),
            P(),
            P(),
        ),
        out_specs=(P("ckpt", "space", None, None, None, None), P("space", None, None, None, None)),
        check_vma=False,
    )
```
